128 devices in a mesh: dp: 16 (over y, z_hi, core), tensor: 8 (over x, z_lo).
Axes of the slice: x: 4, y: 4, z: 4 (z_hi: 2, z_lo: 2; z = z_hi * 2 + z_lo), core: 2. Of those that a mesh axis runs over, the one named last changes fastest.
Arguments:
- tokens: bfloat16 [16384, 2048], P(('dp', 'tensor')), may hold values from -6 to 6
- starts: int32 [16], P('dp'), may hold values from 0 to 768, as said below
- w_query: bfloat16 [2048, 2048], P('dp', 'tensor'), may hold values from -0.125 to 0.125
- w_key: bfloat16 [2048, 2048], P('dp', 'tensor'), may hold values from -0.125 to 0.125
- w_value: bfloat16 [2048, 2048], P('dp', 'tensor'), may hold values from -0.125 to 0.125
- w_out: bfloat16 [2048, 2048], P('tensor', 'dp'), may hold values from -2 to 2
- w_gate: bfloat16 [2048, 5504], P('dp', 'tensor'), may hold values from -0.125 to 0.125
- w_up: bfloat16 [2048, 5504], P('dp', 'tensor'), may hold values from -0.125 to 0.125
- w_down: bfloat16 [5504, 2048], P('tensor', 'dp'), may hold values from -0.078125 to 0.078125
- gain_attn: float32 [2048], P(('dp', 'tensor')), may hold values from 0.5 to 1.5
- gain_mlp: float32 [2048], P(('dp', 'tensor')), may hold values from 0.5 to 1.5
- cotangent: bfloat16 [16384, 2048], P(('dp', 'tensor')), may hold values from -6 to 6
Outputs:
- output: bfloat16 [16384, 2048], P(('dp', 'tensor'))
- grad_tokens: bfloat16 [16384, 2048], P(('dp', 'tensor'))
- grad_query: float32 [2048, 2048], P('dp', 'tensor')
- grad_key: float32 [2048, 2048], P('dp', 'tensor')
- grad_value: float32 [2048, 2048], P('dp', 'tensor')
- grad_out: float32 [2048, 2048], P('tensor', 'dp')
- grad_gate: float32 [2048, 5504], P('dp', 'tensor')
- grad_up: float32 [2048, 5504], P('dp', 'tensor')
- grad_down: float32 [5504, 2048], P('tensor', 'dp')
- grad_gain_attn: float32 [2048], P(('dp', 'tensor'))
- grad_gain_mlp: float32 [2048], P(('dp', 'tensor'))
The draws below stay inside these ranges and needn't reach their ends.
Inputs may be any that keep to these rules, and one draw needn't show every extreme that they name: `starts`: the start of the one picture piece of each sequence; its 256 positions attend to each other both ways.
All inputs are finite; a program needn't handle non-finite values.
Results may differ from the reference program's by a relative error of at most 0.03.
Values may be sent and summed in bfloat16 or wider, within the bound.
A program may use at most 128 MiB of HBM per device.

```python
import math
import jax
import jax.numpy as jnp
from jax import lax

D = 2048
H = 16
HD = 128
FF = 5504
PIECE = 256
SEQ_LEN = 1024
SEQS = 16
TOKENS = 16384


def draw_starts(key, part):
    key = jax.random.fold_in(key, 7)
    first_key, second_key, third_key = jax.random.split(key, 3)
    room = SEQ_LEN - PIECE
    base = jax.random.randint(first_key, (SEQS,), 0, room + 1)
    top_row = jax.random.randint(second_key, (), 0, SEQS)
    bottom_row = (top_row + 1 + jax.random.randint(third_key, (), 0, SEQS - 1)) % SEQS
    rows = jnp.arange(SEQS)
    base = jnp.where(rows == top_row, room, base)
    base = jnp.where(rows == bottom_row, 0, base)
    return base.astype(jnp.int32)


def block_levels(own_key, extent, shards, low, top_value):
    gain, own = 1.0, jax.random.fold_in(own_key, 6)
    for dim, parts in shards:
        heights = jnp.exp(jax.random.uniform(jax.random.fold_in(own, dim), (parts,), jnp.float32, low / len(shards), top_value / len(shards)))
        gain = gain * jnp.repeat(heights, extent[dim] // parts).reshape([-1 if axis == dim else 1 for axis in range(len(extent))])
    return gain


def gaussian(own_key, dims, spread, most, cuts=(), dtype=jnp.bfloat16):
    array = jax.random.normal(own_key, dims, jnp.float32) * spread
    if len(cuts) > 0:
        array = block_levels(own_key, dims, cuts, -0.22, 0.18) * array
    return jnp.clip(array, min=-most, max=most).astype(dtype)


def setup_inputs(seed: int = 0) -> dict:
    streams_of = jax.random.split(jax.random.key(seed), 13)
    return {
        "tokens": gaussian(streams_of[0], (TOKENS, D), 1.0, 6.0, ((0, 128),)),
        "starts": draw_starts(jax.random.fold_in(streams_of[12], 71), 0),
        "w_query": gaussian(streams_of[2], (D, D), D ** -0.5, 0.125, ((0, 16), (1, 8))),
        "w_key": gaussian(streams_of[3], (D, D), D ** -0.5, 0.125, ((0, 16), (1, 8))),
        "w_value": gaussian(streams_of[4], (D, D), D ** -0.5, 0.125, ((0, 16), (1, 8))),
        "w_out": gaussian(streams_of[5], (D, D), (max(1, 4 * D // SEQ_LEN)) ** -0.5, 2.0, ((0, 8), (1, 16))),
        "w_gate": gaussian(streams_of[6], (D, FF), D ** -0.5, 0.125, ((0, 16), (1, 8))),
        "w_up": gaussian(streams_of[7], (D, FF), D ** -0.5, 0.125, ((0, 16), (1, 8))),
        "w_down": gaussian(streams_of[8], (FF, D), FF ** -0.5, 0.078125, ((0, 8), (1, 16))),
        "gain_attn": jnp.clip(1.0 + 0.1 * jax.random.normal(streams_of[9], (D,), jnp.float32), 0.5, 1.5),
        "gain_mlp": jnp.clip(1.0 + 0.1 * jax.random.normal(streams_of[10], (D,), jnp.float32), 0.5, 1.5),
        "cotangent": gaussian(streams_of[11], (TOKENS, D), 1.0, 6.0, ((0, 128),)),
    }


EPS = 1e-05

@jax.custom_vjp
def low(v):
    return lax.optimization_barrier(v.astype(jnp.bfloat16)).astype(jnp.float32)

@jax.custom_vjp
def low_back(v):
    return v

def low_keep(v):
    return (low(v), None)

def low_pass(kept, incoming_gradient):
    return (incoming_gradient,)

def back_keep(v):
    return (v, None)

def back_low(kept, incoming_gradient):
    return (low(incoming_gradient),)
low.defvjp(low_keep, low_pass)
low_back.defvjp(back_keep, back_low)

def matmul(left, right):
    return jnp.dot(left, right, precision=lax.Precision.HIGHEST, preferred_element_type=jnp.float32)

def rope_parts(length):
    half = HD // 2
    index = jnp.arange(half).astype(jnp.float32)
    freq = jnp.exp(index * (-2.0 * math.log(10000.0) / HD))
    angle = jnp.arange(length).astype(jnp.float32)[:, None] * freq[None, :]
    return (jnp.cos(angle), jnp.sin(angle))

def rotate(field, cosine, sine):
    half = HD // 2
    first = field[..., :half]
    second = field[..., half:]
    cosine = cosine[:, None, :]
    sine = sine[:, None, :]
    return jnp.concatenate([first * cosine - second * sine, second * cosine + first * sine], axis=-1)

def make_allowed(start):
    positions = jnp.arange(SEQ_LEN).astype(jnp.int32)
    inside = (positions >= start) & (positions < start + PIECE)
    return (positions[None, :] <= positions[:, None]) | inside[:, None] & inside[None, :]

def forward(xf, w_query, w_key, w_value, w_out, w_gate, w_up, w_down, gain_attn, gain_mlp, allowed):
    length = xf.shape[0]
    scale = HD ** (-0.5)
    r_one = lax.rsqrt(lax.optimization_barrier(jnp.mean(xf * xf, axis=-1, keepdims=True)) + EPS)
    h_one = low(xf * r_one * gain_attn)
    cosine, sine = rope_parts(length)
    raw_q = low_back(matmul(h_one, w_query)).reshape(length, H, HD)
    raw_k = low_back(matmul(h_one, w_key)).reshape(length, H, HD)
    raw_v = low_back(matmul(h_one, w_value)).reshape(length, H, HD)
    query = low(rotate(raw_q, cosine, sine))
    keys = low(rotate(raw_k, cosine, sine))
    value_rows = low(raw_v)

    def one_head(item):
        q_head, k_head, v_head = item
        scores = low_back(matmul(q_head, k_head.T)) * scale
        scores = jnp.where(allowed, scores, -1e+30)
        top = lax.optimization_barrier(jnp.max(scores, axis=-1, keepdims=True))
        expo = jnp.exp(scores - top)
        probs = low(expo / lax.optimization_barrier(jnp.sum(expo, axis=-1, keepdims=True)))
        return low(low_back(matmul(probs, v_head)))
    heads = lax.map(jax.checkpoint(one_head), (query.transpose(1, 0, 2), keys.transpose(1, 0, 2), value_rows.transpose(1, 0, 2)))
    heads_out = heads.transpose(1, 0, 2).reshape(length, D)
    y_one = xf + low_back(matmul(heads_out, w_out))
    r_two = lax.rsqrt(lax.optimization_barrier(jnp.mean(y_one * y_one, axis=-1, keepdims=True)) + EPS)
    h_two = low(y_one * r_two * gain_mlp)
    gate = low_back(matmul(h_two, w_gate))
    up = low_back(matmul(h_two, w_up))
    act = low(jax.nn.silu(gate) * up)
    return y_one + low_back(matmul(act, w_down))

def reference(tokens, starts, w_query, w_key, w_value, w_out, w_gate, w_up, w_down, gain_attn, gain_mlp, cotangent):
    params = (w_query.astype(jnp.float32), w_key.astype(jnp.float32), w_value.astype(jnp.float32), w_out.astype(jnp.float32), w_gate.astype(jnp.float32), w_up.astype(jnp.float32), w_down.astype(jnp.float32), gain_attn.astype(jnp.float32), gain_mlp.astype(jnp.float32))
    inputs = tokens.astype(jnp.float32).reshape(SEQS, SEQ_LEN, D)
    grads_in = cotangent.astype(jnp.float32).reshape(SEQS, SEQ_LEN, D)

    def one_sequence(totals, item):
        x_seq, ct_seq, start = item
        allowed = make_allowed(start)

        def run(xf, *weights):
            return forward(xf, *weights, allowed)
        result, pull = jax.vjp(run, x_seq, *params)
        grads = pull(ct_seq)
        totals = tuple((total + incoming_gradient for total, incoming_gradient in zip(totals, grads[1:])))
        return (totals, (result.astype(jnp.bfloat16), grads[0].astype(jnp.bfloat16)))
    zeros = tuple((jnp.zeros_like(p) for p in params))
    totals, (outs, grad_x) = lax.scan(one_sequence, zeros, (inputs, grads_in, starts))
    return (outs.reshape(TOKENS, D), grad_x.reshape(TOKENS, D), totals[0], totals[1], totals[2], totals[3], totals[4], totals[5], totals[6], totals[7], totals[8])
```

```python
import functools
import math
import types

import jax
import jax.numpy as jnp
import numpy as np
from jax import lax
from jax.experimental import pallas as pl
from jax.experimental.pallas import tpu as pltpu
from jax.sharding import PartitionSpec as P

HD = 128
PIECE = 256
EPS = 1e-05
NEG = -1e30
SCALE = HD ** (-0.5)
D = 2048
SEQ = 1024
UNITS = 688
BF = jnp.bfloat16
F32 = jnp.float32
MESH = pl.DeviceIdType.MESH
VMEM_BYTES = 60 * 1024 * 1024
ALL = slice(None)


def dot_nn(left, right):
    return jnp.dot(left, right, preferred_element_type=F32)


def dot_nt(left, right):
    return lax.dot_general(left, right, (((1,), (1,)), ((), ())), preferred_element_type=F32)


def dot_tn(left, right):
    return lax.dot_general(left, right, (((0,), (0,)), ((), ())), preferred_element_type=F32)


def rem4(value):
    return lax.rem(value, 4)


def place():
    dp = lax.axis_index("dp")
    tp = lax.axis_index("tensor")
    zh = lax.rem(lax.div(dp, 2), 2)
    zl = lax.rem(tp, 2)
    return types.SimpleNamespace(
        y=lax.div(dp, 4), zh=zh, zl=zl, z=zh * 2 + zl, x=lax.div(tp, 2), core=lax.rem(dp, 2)
    )


def device(me, **moved):
    at = types.SimpleNamespace(**{**vars(me), **moved})
    zh, zl = lax.div(at.z, 2), lax.rem(at.z, 2)
    return (at.y * 4 + zh * 2 + at.core, at.x * 2 + zl)


def near(me, axis, step):
    return device(me, **{axis: rem4(getattr(me, axis) + step)})


def sibling(me):
    return device(me, core=1 - me.core)


def partner(me):
    return device(me, z=me.zh * 2 + 1 - me.zl)


def greet(me, axes):
    others = [near(me, axis, step) for axis in axes for step in (1, 3)] + [sibling(me)]
    barrier = pltpu.get_barrier_semaphore()
    for other in others:
        pl.semaphore_signal(barrier, inc=1, device_id=other, device_id_type=MESH)
    pl.semaphore_wait(barrier, len(others))


class Wire:
    def __init__(self, send, recv, local):
        self.send, self.recv, self.local = send, recv, local
        self.used, self.used_local = 0, 0
        self.sent = []

    def put(self, source, target, to):
        index = self.used
        self.used += 1
        copy = pltpu.make_async_remote_copy(
            src_ref=source,
            dst_ref=target,
            send_sem=self.send.at[index],
            recv_sem=self.recv.at[index],
            device_id=to,
            device_id_type=MESH,
        )
        copy.start()
        self.sent.append(copy)
        return copy

    def move(self, source, target):
        index = self.used_local
        self.used_local += 1
        copy = pltpu.make_async_copy(source, target, self.local.at[index])
        copy.start()
        return copy

    def settle(self, copies):
        for copy in copies:
            copy.wait_send()
        done = {id(copy) for copy in copies}
        self.sent = [copy for copy in self.sent if id(copy) not in done]

    def drain(self):
        for copy in self.sent:
            copy.wait_send()
        self.sent = []


class Ring:
    def __init__(self, wire, me, axis, view, own=None):
        self.wire, self.view = wire, view
        self.at = getattr(me, axis)
        self.right, self.left = near(me, axis, 1), near(me, axis, 3)
        self.own = view(self.at, None) if own is None else own

    def start(self):
        target = self.view(self.at, None)
        self.to_right = self.wire.put(self.own, target, self.right)
        self.to_left = self.wire.put(self.own, target, self.left)
        return self

    def relay(self, halves=True):
        before, after = rem4(self.at + 3), rem4(self.at + 1)
        self.to_right.wait_recv()
        piece = self.view(before, 0 if halves else None)
        self.far = [self.wire.put(piece, piece, self.right)]
        self.to_left.wait_recv()
        if halves:
            piece = self.view(after, 1)
            self.far.append(self.wire.put(piece, piece, self.left))
        return self

    def finish(self):
        for copy in self.far:
            copy.wait_recv()
        return self


def add_rows(target, terms, rows, step):
    def body(index, carry):
        span = pl.ds(pl.multiple_of(index * step, step), step)
        total = terms[0][span, :].astype(F32)
        for term in terms[1:]:
            total = total + term[span, :].astype(F32)
        target[span, :] = total.astype(target.dtype)
        return carry

    lax.fori_loop(0, rows // step, body, 0)


class RingSum:
    def __init__(self, wire, me, axis, part, from_left, from_right, whole_left, whole_right, add):
        self.wire, self.part, self.add = wire, part, add
        self.at = getattr(me, axis)
        self.right, self.left = near(me, axis, 1), near(me, axis, 3)
        self.near_bufs = (from_left, from_right)
        self.whole = (whole_left, whole_right)

    def start(self, halves=(0, 1)):
        far = rem4(self.at + 2)
        if 0 in halves:
            self.first = self.wire.put(self.part(far, 0), self.near_bufs[0], self.right)
        if 1 in halves:
            self.second = self.wire.put(self.part(far, 1), self.near_bufs[1], self.left)
        return self

    def relay(self):
        after, before = rem4(self.at + 1), rem4(self.at + 3)
        self.first.wait_recv()
        self.add(self.part(after, 0), self.near_bufs[0])
        self.to_right = self.wire.put(self.part(after, None), self.whole[0], self.right)
        self.second.wait_recv()
        self.add(self.part(before, 1), self.near_bufs[1])
        self.to_left = self.wire.put(self.part(before, None), self.whole[1], self.left)
        return self

    def finish(self):
        self.to_right.wait_recv()
        self.to_left.wait_recv()
        return self


class Spread:
    def __init__(self, wire, me, ref, lead, row, rows, first, cut, source):
        self.wire, self.me, self.first = wire, me, first
        head = (ALL,) * lead

        def view(y, z, part):
            zl, zh = (ALL, ALL) if z is None else (lax.rem(z, 2), lax.div(z, 2))
            start, size = row, rows
            if part == 0:
                size = cut
            if part == 1:
                start, size = row + cut, rows - cut
            yy = ALL if y is None else y
            return ref.at[head + (zl, yy, zh, me.core, pl.ds(start, size), ALL)]

        self.view = view
        own = source.at[head + (pl.ds(row, rows), ALL)]
        if first == "y":
            self.one = Ring(wire, me, "y", lambda slot, part: view(slot, me.z, part), own)
            self.two = Ring(wire, me, "z", lambda slot, part: view(None, slot, part))
        else:
            self.one = Ring(wire, me, "z", lambda slot, part: view(me.y, slot, part), own)
            self.two = Ring(wire, me, "y", lambda slot, part: view(slot, None, part))

    def core(self):
        piece = self.view(None, None, None)
        self.last = self.wire.put(piece, piece, sibling(self.me))
        return self


def norm_rows(source, target, gain, rows, step=32):
    def body(index, carry):
        span = pl.ds(pl.multiple_of(index * step, step), step)
        value = source[span, :].astype(F32)
        scale = lax.rsqrt(jnp.mean(value * value, axis=-1, keepdims=True) + EPS)
        target[span, :] = (value * scale * gain).astype(BF)
        return carry

    lax.fori_loop(0, rows // step, body, 0)


def fill_bias(bias, me, start):
    row = lax.broadcasted_iota(jnp.int32, (128, 512), 0)
    column = lax.broadcasted_iota(jnp.int32, (128, 512), 1)
    query = lax.div(column, 128) * 256 + me.zl * 128 + lax.rem(column, 128)
    query_in = (query >= start) & (query < start + PIECE)

    def body(block, carry):
        pair, other = lax.div(block, 2), lax.rem(block, 2)
        parity = me.zl + other * (1 - 2 * me.zl)
        key = (pair * 2 + parity) * 128 + row
        key_in = (key >= start) & (key < start + PIECE)
        allowed = (key <= query) | (query_in & key_in)
        bias[pl.ds(pl.multiple_of(block * 128, 128), 128), :] = jnp.where(allowed, 0.0, NEG)
        return carry

    lax.fori_loop(0, 8, body, 0)


def turn(field, cosine, sine):
    return field * cosine + pltpu.roll(field, HD // 2, 1) * sine


def kernel_attend(
    tokens_in, cotangent_in, start_in, qkv_in, out_in, wide_in, down_in, tile_in, tables_in,
    qkv_out, wo_out, wide_out, down_out, cot_out, turned_out,
    query_out, keys_out, values_out, heads_out, lse_out, y_out, h_out, gains_out,
    tok, h_one, w_qkv, w_o, tables, bias, part, near_left, near_right, whole_left, whole_right,
    turned, gain_x, gain_z, gain_y, gain_c,
    send, recv, local,
):
    me = place()
    wire = Wire(send, recv, local)
    greet(me, ("x", "y", "z"))
    one = rem4(me.x + 1)
    three = rem4(me.x + 3)

    rows_x = Ring(
        wire, me, "x",
        lambda slot, half: tok.at[slot, 0] if half is None else tok.at[slot, 0, pl.ds(half * 64, 64)],
        tokens_in,
    ).start()
    rows_z = wire.put(tokens_in, tok.at[me.x, 1], partner(me))
    gain_ring_x = Ring(wire, me, "x", lambda slot, half: gain_x.at[slot], tile_in).start()
    qkv = [
        Spread(wire, me, w_qkv, 1, 0, 64, "y", 32, qkv_in),
        Spread(wire, me, w_qkv, 1, 64, 64, "z", 32, qkv_in),
    ]
    for item in qkv:
        item.one.start()
    own = [
        wire.move(tokens_in, tok.at[me.x, 0]),
        wire.move(tile_in, gain_x.at[me.x]),
        wire.move(qkv_in, w_qkv.at[:, me.zl, me.y, me.zh, me.core]),
        wire.move(out_in, w_o.at[me.zl, me.y, me.zh, me.core]),
        wire.move(wide_in, wide_out.at[:, me.zl, me.y, me.zh, me.core]),
        wire.move(down_in, down_out.at[me.zl, me.y, me.zh, me.core]),
        wire.move(tables_in.at[me.zl], tables),
        wire.move(cotangent_in, cot_out.at[me.x]),
    ]
    fill_bias(bias, me, start_in[0])
    for copy in own:
        copy.wait()

    gain_ring_x.relay(False)
    rows_x.relay()
    rows_z.wait_recv()
    other_right = wire.put(tok.at[me.x, 1], tok.at[me.x, 1], near(me, "x", 1))
    other_left = wire.put(tok.at[me.x, 1], tok.at[me.x, 1], near(me, "x", 3))
    for item in qkv:
        item.one.relay()
    gain_ring_x.finish()
    gain_z[me.z] = gain_x[0] + gain_x[1] + gain_x[2] + gain_x[3]
    gain_ring_z = Ring(wire, me, "z", lambda slot, half: gain_z.at[slot]).start()
    for item in qkv:
        item.one.finish()
        item.two.start()
    later = [
        Spread(wire, me, w_o, 0, 0, 128, "y", 64, out_in),
        Spread(wire, me, w_o, 0, 128, 128, "z", 64, out_in),
        Spread(wire, me, wide_out, 1, 0, 64, "y", 32, wide_in),
        Spread(wire, me, wide_out, 1, 64, 64, "z", 32, wide_in),
        Spread(wire, me, down_out, 0, 0, 352, "y", 176, down_in),
        Spread(wire, me, down_out, 0, 352, 336, "z", 176, down_in),
    ]
    for item in later:
        item.one.start()
    gain_ring_z.relay(False).finish()
    gain_y[me.y, 0] = gain_z[0] + gain_z[1]
    gain_y[me.y, 1] = gain_z[2] + gain_z[3]
    gain_ring_y = Ring(wire, me, "y", lambda slot, half: gain_y.at[slot]).start()
    gain_ring_y.relay(False).finish()
    gain_c[me.core] = gain_y[...]
    piece = gain_c.at[me.core]
    wire.put(piece, piece, sibling(me)).wait_recv()
    for y in range(4):
        for zh in range(2):
            for core in range(2):
                column = (y * 4 + zh * 2 + core) * 128
                gains_out[:, column : column + 128] = gain_c[core, y, zh]
    gain_one, gain_two = gains_out[0:1, :], gains_out[1:2, :]

    norm_rows(tok.at[me.x, 0], h_one.at[me.x, 0], gain_one, 128)
    norm_rows(tok.at[me.x, 1], h_one.at[me.x, 1], gain_one, 128)
    norm_rows(tok.at[one, 0], h_one.at[one, 0], gain_one, 128)
    norm_rows(tok.at[three, 0], h_one.at[three, 0], gain_one, 128)
    for item in qkv:
        item.two.relay()
    rows_x.finish()
    far = rem4(me.x + 2)
    far_z = wire.put(tok.at[far, 0], tok.at[far, 1], partner(me))
    norm_rows(tok.at[far, 0], h_one.at[far, 0], gain_one, 128)
    other_right.wait_recv()
    other_left.wait_recv()
    norm_rows(tok.at[one, 1], h_one.at[one, 1], gain_one, 128)
    norm_rows(tok.at[three, 1], h_one.at[three, 1], gain_one, 128)
    cot_x = Ring(
        wire, me, "x",
        lambda slot, half: cot_out.at[slot] if half is None else cot_out.at[slot, pl.ds(half * 64, 64)],
        cotangent_in,
    ).start()
    for item in qkv:
        item.two.finish()
        item.core()
    for item in later:
        item.one.relay()
    far_z.wait_recv()
    norm_rows(tok.at[far, 1], h_one.at[far, 1], gain_one, 128)
    for item in qkv:
        item.last.wait_recv()
    kept = [wire.move(w_qkv, qkv_out)]
    for item in later:
        item.one.finish()
        item.two.start()

    def project(pair, carry):
        def weight(which):
            return w_qkv[which, pair].reshape(D, 256)

        raw = dot_nn(h_one[:, 0].reshape(512, D), weight(0))
        for j in range(2):
            cosine = tables[0, :, 0].reshape(512, HD)
            sine = tables[1, :, 0].reshape(512, HD)
            query_out[pair * 2 + j] = turn(raw[:, j * HD : (j + 1) * HD], cosine, sine).astype(BF)
        for half in range(2):
            rows = h_one[2 * half : 2 * half + 2].reshape(512, D)
            span = slice(half * 512, half * 512 + 512)
            raw = dot_nn(rows, weight(1))
            cosine = tables[0, 2 * half : 2 * half + 2].reshape(512, HD)
            sine = tables[1, 2 * half : 2 * half + 2].reshape(512, HD)
            for j in range(2):
                keys_out[pair * 2 + j, span, :] = turn(
                    raw[:, j * HD : (j + 1) * HD], cosine, sine
                ).astype(BF)
            raw = dot_nn(rows, weight(2))
            for j in range(2):
                values_out[pair * 2 + j, span, :] = raw[:, j * HD : (j + 1) * HD].astype(BF)
        return carry

    lax.fori_loop(0, 2, project, 0)
    cot_x.relay()

    def attend(head, carry):
        for half, span in ((0, 768), (1, 1024)):
            rows = slice(half * 256, half * 256 + 256)
            scores = dot_nt(keys_out[head, 0:span, :], query_out[head, rows, :]) * SCALE
            scores = scores + bias[0:span, rows]
            top = jnp.max(scores, axis=0, keepdims=True)
            expo = jnp.exp(scores - top)
            total = jnp.sum(expo, axis=0, keepdims=True)
            probs = (expo * (1.0 / total)).astype(BF)
            result = dot_tn(values_out[head, 0:span, :], probs)
            heads_out[rows, pl.ds(pl.multiple_of(head * HD, HD), HD)] = result.T.astype(BF)
            lse_out[head, :, rows] = top + jnp.log(total)
        return carry

    lax.fori_loop(0, 4, attend, 0)
    for item in later:
        item.two.relay()

    def project_out(block, carry):
        y, zh = lax.div(block, 2), lax.rem(block, 2)
        weight = jnp.concatenate(
            [
                jnp.concatenate([w_o[zl, y, zh, 0], w_o[zl, y, zh, 1]], axis=1)
                for zl in range(2)
            ],
            axis=0,
        )
        result = dot_nn(heads_out[...], weight).astype(BF).reshape(4, 128, 256)
        part[:, :, pl.ds(pl.multiple_of(block * 256, 256), 256)] = result
        return carry

    later[0].two.finish()
    later[1].two.finish()
    later[0].core()
    later[1].core()
    later[0].last.wait_recv()
    later[1].last.wait_recv()
    kept.append(wire.move(w_o, wo_out))
    cot_x.finish()

    def halves(ref):
        def view(slot, half):
            if half is None:
                return ref.at[slot]
            return ref.at[slot, :, pl.ds(half * 1024, 1024)]

        return view

    total = RingSum(
        wire, me, "x", halves(part), near_left, near_right, whole_left, whole_right,
        lambda target, term: add_rows(target, [target, term], 128, 32),
    )
    lax.fori_loop(0, 4, project_out, 0)
    total.start((0,))
    lax.fori_loop(4, 8, project_out, 0)
    total.start((1,))

    def flip(block, carry):
        column = pl.ds(pl.multiple_of(block * 128, 128), 128)
        rows = h_one[:, :, :, column].reshape(SEQ, 128)
        turned[lax.rem(block, 2), lax.div(block, 2)] = rows.T
        return carry

    lax.fori_loop(0, 8, flip, 0)
    total.relay()
    lax.fori_loop(8, 16, flip, 0)
    kept.append(wire.move(turned.at[me.core], turned_out.at[0]))
    turned_far = wire.put(turned.at[1 - me.core], turned_out.at[1], sibling(me))
    for item in later[2:]:
        item.two.finish()
        item.core()
    total.finish()

    def finish(index, carry):
        span = pl.ds(pl.multiple_of(index * 32, 32), 32)
        value = tok[me.x, 0, span, :].astype(F32) + (
            part[me.x, span, :].astype(F32)
            + whole_left[span, :].astype(F32)
            + whole_right[span, :].astype(F32)
        )
        scale = lax.rsqrt(jnp.mean(value * value, axis=-1, keepdims=True) + EPS)
        y_out[span, :] = value
        h_out[span, :] = (value * scale * gain_two).astype(BF)
        return carry

    lax.fori_loop(0, 4, finish, 0)
    for item in later[2:]:
        item.last.wait_recv()
    turned_far.wait_recv()
    for copy in kept:
        copy.wait()
    wire.drain()


def anywhere():
    return pl.BlockSpec(memory_space=pl.ANY)


def in_vmem():
    return pl.BlockSpec(memory_space=pltpu.VMEM)


def call_attend(tokens, cotangent, starts, qkv, w_out, wide, w_down, tile, tables):
    shape = jax.ShapeDtypeStruct
    return pl.pallas_call(
        kernel_attend,
        name="attend",
        in_specs=[anywhere(), anywhere(), pl.BlockSpec(memory_space=pltpu.SMEM)] + [anywhere()] * 6,
        out_specs=[anywhere()] * 6 + [in_vmem()] * 8,
        out_shape=[
            shape((3, 2, 4, 2, 2, 128, 256), BF),
            shape((2, 4, 2, 2, 256, 128), BF),
            shape((2, 2, 4, 2, 2, 128, UNITS), BF),
            shape((2, 4, 2, 2, UNITS, 128), BF),
            shape((4, 128, D), BF),
            shape((2, 8, 128, SEQ), BF),
            shape((4, 512, HD), BF),
            shape((4, SEQ, HD), BF),
            shape((4, SEQ, HD), BF),
            shape((512, 512), BF),
            shape((4, 1, 512), F32),
            shape((128, D), F32),
            shape((128, D), BF),
            shape((8, D), F32),
        ],
        scratch_shapes=[
            pltpu.VMEM((4, 2, 128, D), BF),
            pltpu.VMEM((4, 2, 128, D), BF),
            pltpu.VMEM((3, 2, 4, 2, 2, 128, 256), BF),
            pltpu.VMEM((2, 4, 2, 2, 256, 128), BF),
            pltpu.VMEM((2, 4, 2, 128, HD), F32),
            pltpu.VMEM((SEQ, 512), F32),
            pltpu.VMEM((4, 128, D), BF),
            pltpu.VMEM((128, D // 2), BF),
            pltpu.VMEM((128, D // 2), BF),
            pltpu.VMEM((128, D), BF),
            pltpu.VMEM((128, D), BF),
            pltpu.VMEM((2, 8, 128, SEQ), BF),
            pltpu.VMEM((4, 8, 128), F32),
            pltpu.VMEM((4, 8, 128), F32),
            pltpu.VMEM((4, 2, 8, 128), F32),
            pltpu.VMEM((2, 4, 2, 8, 128), F32),
            pltpu.SemaphoreType.DMA((110,)),
            pltpu.SemaphoreType.DMA((110,)),
            pltpu.SemaphoreType.DMA((16,)),
        ],
        compiler_params=pltpu.CompilerParams(
            collective_id=0, has_side_effects=True, vmem_limit_bytes=VMEM_BYTES
        ),
    )(tokens, cotangent, starts, qkv, w_out, wide, w_down, tile, tables)


def rope_tables():
    half = HD // 2
    freq = np.exp(np.arange(half, dtype=np.float32) * np.float32(-2.0 * math.log(10000.0) / HD))
    order = np.array(
        [
            [[(2 * pair + (zl + other) % 2) * 128 + np.arange(128) for other in range(2)] for pair in range(4)]
            for zl in range(2)
        ]
    )
    angle = order.astype(np.float32)[..., None] * freq.astype(np.float32)
    cosine, sine = np.cos(angle.astype(np.float64)), np.sin(angle.astype(np.float64))
    both = np.stack(
        [np.concatenate([cosine, cosine], -1), np.concatenate([-sine, sine], -1)], axis=1
    )
    return both.astype(np.float32)


def gain_tile(gain_attn, gain_mlp):
    column = lax.axis_index("tensor") * 16
    both = jnp.stack([gain_attn, gain_mlp])
    return lax.dynamic_update_slice(jnp.zeros((8, 128), F32), both, (0, column))


def add_into(target, terms, result=None):
    shape = target.shape
    lead, rows, columns = shape[:-2], shape[-2], shape[-1]
    step = rows
    while step * columns > 33000:
        step = next(s for s in range(step - 16, 0, -16) if rows % s == 0)
    cuts = rows // step
    result = target if result is None else result

    def body(index, carry):
        where, rest = [], lax.div(index, cuts)
        for extent in reversed(lead):
            where.insert(0, lax.rem(rest, extent))
            rest = lax.div(rest, extent)
        where = tuple(where) + (
            pl.ds(pl.multiple_of(lax.rem(index, cuts) * step, 16), step), ALL
        )
        total = target[where].astype(F32)
        for term in terms:
            total = total + term[where].astype(F32)
        result[where] = total.astype(result.dtype)
        return carry

    lax.fori_loop(0, math.prod(lead) * cuts, body, 0)


def columns_of(ref):
    def view(slot, half):
        if half is None:
            return ref.at[slot]
        return ref.at[slot, :, pl.ds(half * (D // 2), D // 2)]

    return view


def rows_of(ref):
    def view(slot, half):
        return ref.at[slot] if half is None else ref.at[slot, pl.ds(half * 64, 64)]

    return view


def fold_view(ref, me, lead, axis, row, rows, cut):
    head = (ALL,) * lead

    def view(slot, part):
        start, size = row, rows
        if part == 0:
            size = cut
        if part == 1:
            start, size = row + cut, rows - cut
        if axis == "y":
            where = (ALL, slot, ALL)
        else:
            where = (lax.rem(slot, 2), ALL, lax.div(slot, 2))
        return ref.at[head + where + (pl.ds(start, size), ALL)]

    return view


def kernel_feed(
    h_in, cot_in, wide_in, down_in, y_in, gains_in,
    part_out, dattn_out, wide_y_out, wide_z_out, down_y_out, down_z_out, dy_out, gain_out,
    w_wide, w_down, h_two, cot, gate_s, up_s, act_s, d_wide, act, act_t, d_wide_far, act_t_far,
    h_t, h_t_far, cot_far, part, near_left, near_right, whole_left, whole_right, d_attn,
    wy_near_left, wy_near_right, wy_left, wy_right, wz_near_left, wz_near_right, wz_left, wz_right,
    dy_near_left, dy_near_right, dy_left, dy_right, dz_near_left, dz_near_right, dz_left, dz_right,
    send, recv, local,
):
    me = place()
    wire = Wire(send, recv, local)
    greet(me, ("x", "y", "z"))
    h_ring = Ring(wire, me, "x", rows_of(h_two), h_in).start()
    loads = [
        wire.move(cot_in, cot),
        wire.move(down_in, w_down),
        wire.move(h_in, h_two.at[me.x]),
        wire.move(wide_in, w_wide),
    ]
    loads[0].wait()
    cot_puts = []
    for block in range(8):
        column = pl.ds(pl.multiple_of((block * 2 + 1 - me.core) * 128, 128), 128)
        cot_puts.append(wire.put(cot.at[:, :, column], cot_far.at[block], sibling(me)))
    loads[1].wait()

    def back_act(zl, carry):
        weight = jnp.concatenate(
            [w_down[zl, y, zh, c] for y in range(4) for zh in range(2) for c in range(2)], axis=1
        )
        act_s[zl] = dot_nt(cot[...].reshape(512, D), weight)
        return carry

    lax.fori_loop(0, 1, back_act, 0)
    h_ring.relay()
    lax.fori_loop(1, 2, back_act, 0)
    loads[2].wait()
    loads[3].wait()
    h_ring.finish()

    def forward(zl, carry):
        rows = h_two[...].reshape(512, D)
        gate_s[...] = dot_nn(rows, w_wide[0, zl].reshape(D, UNITS))
        up_s[...] = dot_nn(rows, w_wide[1, zl].reshape(D, UNITS))

        def inner(index, carry):
            span = pl.ds(pl.multiple_of(index * 32, 32), 32)
            gate, up, d_act = gate_s[span, :], up_s[span, :], act_s[zl, span, :]
            sigma = 1.0 / (1.0 + jnp.exp(-gate))
            act[zl, span, :] = (gate * sigma * up).astype(BF)
            d_wide[0, zl, span, :] = (d_act * up * sigma * (1.0 + gate * (1.0 - sigma))).astype(BF)
            d_wide[1, zl, span, :] = (d_act * gate * sigma).astype(BF)
            return carry

        lax.fori_loop(0, 16, inner, 0)
        act_t[zl] = act[zl].T
        return carry

    lax.fori_loop(0, 2, forward, 0)

    def flip(block, carry):
        column = pl.ds(pl.multiple_of(block * 128, 128), 128)
        h_t[lax.rem(block, 2), lax.div(block, 2)] = h_two[:, :, column].reshape(512, 128).T
        return carry

    lax.fori_loop(0, 16, flip, 0)
    far = [
        wire.put(h_t.at[1 - me.core], h_t_far, sibling(me)),
        wire.put(d_wide, d_wide_far, sibling(me)),
        wire.put(act_t, act_t_far, sibling(me)),
    ]

    def back_h(block, carry):
        y, zh = lax.div(block, 2), lax.rem(block, 2)
        total = None
        for which in range(2):
            for zl in range(2):
                weight = w_wide[which, zl, y, zh].reshape(256, UNITS)
                term = dot_nt(d_wide[which, zl], weight)
                total = term if total is None else total + term
        part[:, :, pl.ds(pl.multiple_of(block * 256, 256), 256)] = total.astype(BF).reshape(4, 128, 256)
        return carry

    total = RingSum(
        wire, me, "x", columns_of(part), near_left, near_right, whole_left, whole_right,
        lambda target, term: add_into(target, [term]),
    )
    lax.fori_loop(0, 4, back_h, 0)
    total.start((0,))
    lax.fori_loop(4, 8, back_h, 0)
    total.start((1,))
    wire.settle((h_ring.to_right, h_ring.to_left, *h_ring.far))

    def forward_down(block, carry):
        y, zh = lax.div(block, 2), lax.rem(block, 2)
        result = None
        for zl in range(2):
            weight = jnp.concatenate([w_down[zl, y, zh, 0], w_down[zl, y, zh, 1]], axis=1)
            term = dot_nn(act[zl], weight)
            result = term if result is None else result + term
        h_two[:, :, pl.ds(pl.multiple_of(block * 256, 256), 256)] = result.astype(BF).reshape(4, 128, 256)
        return carry

    lax.fori_loop(0, 8, forward_down, 0)
    kept = [wire.move(h_two, part_out)]
    total.relay()
    for copy in far[:2]:
        copy.wait_recv()

    def grad_wide(index, carry):
        which, rest = lax.div(index, 4), lax.rem(index, 4)
        zl, pair = lax.div(rest, 2), lax.rem(rest, 2)
        blocks = pl.ds(pair * 4, 4)
        result = dot_nn(h_t[me.core, blocks].reshape(512, 512), d_wide[which, zl]) + dot_nn(
            h_t_far[blocks].reshape(512, 512), d_wide_far[which, zl]
        )
        w_wide[which, zl, pl.ds(pair * 2, 2), :, 0] = result.astype(BF).reshape(2, 2, 128, UNITS)
        return carry

    lax.fori_loop(0, 8, grad_wide, 0)
    g_wide = w_wide.at[:, :, :, :, 0]
    g_down = w_down.at[:, :, :, 0]

    def add(target, term):
        add_into(target, [term])

    sums = [
        RingSum(wire, me, "y", fold_view(g_wide, me, 1, "y", 0, 64, 32),
                wy_near_left, wy_near_right, wy_left, wy_right, add),
        RingSum(wire, me, "z", fold_view(g_wide, me, 1, "z", 64, 64, 32),
                wz_near_left, wz_near_right, wz_left, wz_right, add),
    ]
    for item in sums:
        item.start()
    total.finish()

    gain_two = gains_in[1:2, :]

    def back_norm(index, carry):
        span = pl.ds(pl.multiple_of(index * 16, 16), 16)
        d_h = (
            part[me.x, span, :].astype(F32)
            + whole_left[span, :].astype(F32)
            + whole_right[span, :].astype(F32)
        )
        value = y_in[span, :]
        scale = lax.rsqrt(jnp.mean(value * value, axis=-1, keepdims=True) + EPS)
        normed = value * scale
        e_two = d_h * gain_two
        inner = jnp.mean(e_two * normed, axis=-1, keepdims=True)
        d_y = cot[me.x, span, :].astype(F32) + scale * (e_two - normed * inner)
        dy_out[span, :] = d_y
        d_attn[span, :] = d_y.astype(BF)
        return carry + jnp.sum(d_h * normed, axis=0, keepdims=True)

    gain_out[0:1, :] = lax.fori_loop(0, 8, back_norm, jnp.zeros((1, D), F32))
    d_ring = Ring(wire, me, "x", rows_of(dattn_out), d_attn).start()
    kept.append(wire.move(d_attn, dattn_out.at[me.x]))
    far[2].wait_recv()
    for copy in cot_puts:
        copy.wait_recv()

    def grad_down(index, carry):
        zl, y = lax.div(index, 4), lax.rem(index, 4)
        mine = jnp.concatenate(
            [
                cot[:, :, pl.ds(pl.multiple_of(((y * 2 + zh) * 2 + me.core) * 128, 128), 128)]
                .reshape(512, 128)
                for zh in range(2)
            ],
            axis=1,
        )
        other = jnp.concatenate(
            [cot_far[y * 2 + zh].reshape(512, 128) for zh in range(2)], axis=1
        )
        result = (dot_nn(act_t[zl], mine) + dot_nn(act_t_far[zl], other)).astype(BF)
        w_down[zl, y, 0, 0] = result[:, 0:128]
        w_down[zl, y, 1, 0] = result[:, 128:256]
        return carry

    lax.fori_loop(0, 8, grad_down, 0)
    sums += [
        RingSum(wire, me, "y", fold_view(g_down, me, 0, "y", 0, 352, 176),
                dy_near_left, dy_near_right, dy_left, dy_right, add),
        RingSum(wire, me, "z", fold_view(g_down, me, 0, "z", 352, 336, 176),
                dz_near_left, dz_near_right, dz_left, dz_right, add),
    ]
    for item in sums[2:]:
        item.start()
    for item in sums[:2]:
        item.relay()
    d_ring.relay()
    for item in sums[2:]:
        item.relay()
    outs = (wide_y_out, wide_z_out, down_y_out, down_z_out)
    for item, out in zip(sums, outs):
        item.finish()
        mine = item.part(item.at, None)
        add_into(mine, list(item.whole))
        kept.append(wire.move(mine, out))
    d_ring.finish()
    for copy in kept:
        copy.wait()
    wire.drain()


def call_feed(h_two, cot, wide, down, y_one, gains):
    shape = jax.ShapeDtypeStruct
    return pl.pallas_call(
        kernel_feed,
        name="feed",
        in_specs=[anywhere()] * 4 + [in_vmem()] * 2,
        out_specs=[anywhere()] * 6 + [in_vmem()] * 2,
        out_shape=[
            shape((4, 128, D), BF),
            shape((4, 128, D), BF),
            shape((2, 2, 2, 64, UNITS), BF),
            shape((2, 4, 64, UNITS), BF),
            shape((2, 2, 352, 128), BF),
            shape((4, 336, 128), BF),
            shape((128, D), F32),
            shape((1, D), F32),
        ],
        scratch_shapes=[
            pltpu.VMEM((2, 2, 4, 2, 2, 128, UNITS), BF),
            pltpu.VMEM((2, 4, 2, 2, UNITS, 128), BF),
            pltpu.VMEM((4, 128, D), BF),
            pltpu.VMEM((4, 128, D), BF),
            pltpu.VMEM((512, UNITS), F32),
            pltpu.VMEM((512, UNITS), F32),
            pltpu.VMEM((2, 512, UNITS), F32),
            pltpu.VMEM((2, 2, 512, UNITS), BF),
            pltpu.VMEM((2, 512, UNITS), BF),
            pltpu.VMEM((2, UNITS, 512), BF),
            pltpu.VMEM((2, 2, 512, UNITS), BF),
            pltpu.VMEM((2, UNITS, 512), BF),
            pltpu.VMEM((2, 8, 128, 512), BF),
            pltpu.VMEM((8, 128, 512), BF),
            pltpu.VMEM((8, 4, 128, 128), BF),
            pltpu.VMEM((4, 128, D), BF),
            pltpu.VMEM((128, D // 2), BF),
            pltpu.VMEM((128, D // 2), BF),
            pltpu.VMEM((128, D), BF),
            pltpu.VMEM((128, D), BF),
            pltpu.VMEM((128, D), BF),
            pltpu.VMEM((2, 2, 2, 32, UNITS), BF),
            pltpu.VMEM((2, 2, 2, 32, UNITS), BF),
            pltpu.VMEM((2, 2, 2, 64, UNITS), BF),
            pltpu.VMEM((2, 2, 2, 64, UNITS), BF),
            pltpu.VMEM((2, 4, 32, UNITS), BF),
            pltpu.VMEM((2, 4, 32, UNITS), BF),
            pltpu.VMEM((2, 4, 64, UNITS), BF),
            pltpu.VMEM((2, 4, 64, UNITS), BF),
            pltpu.VMEM((2, 2, 176, 128), BF),
            pltpu.VMEM((2, 2, 176, 128), BF),
            pltpu.VMEM((2, 2, 352, 128), BF),
            pltpu.VMEM((2, 2, 352, 128), BF),
            pltpu.VMEM((4, 176, 128), BF),
            pltpu.VMEM((4, 160, 128), BF),
            pltpu.VMEM((4, 336, 128), BF),
            pltpu.VMEM((4, 336, 128), BF),
            pltpu.SemaphoreType.DMA((60,)),
            pltpu.SemaphoreType.DMA((60,)),
            pltpu.SemaphoreType.DMA((16,)),
        ],
        compiler_params=pltpu.CompilerParams(
            collective_id=1, has_side_effects=True, vmem_limit_bytes=VMEM_BYTES
        ),
    )(h_two, cot, wide, down, y_one, gains)


class Fold:
    def __init__(self, wire, me, view_one, axes, bufs, view_two, bufs_two):
        def add(target, term):
            add_into(target, [term])

        self.wire, self.me, self.axes, self.add = wire, me, axes, add
        self.view_two, self.bufs_two = view_two, bufs_two
        self.one = None
        if view_one is not None:
            self.one = RingSum(wire, me, axes[0], view_one, *bufs, add)

    def start(self):
        self.one.start()

    def relay(self):
        self.one.relay()

    def turn(self):
        if self.one is not None:
            self.one.finish()
            add_into(self.one.part(self.one.at, None), list(self.one.whole))
        self.two = RingSum(self.wire, self.me, self.axes[1], self.view_two, *self.bufs_two, self.add)
        self.two.start()

    def relay_two(self):
        self.two.relay()

    def finish(self, result):
        self.two.finish()
        add_into(self.two.part(self.two.at, None), list(self.two.whole), result)


def crossed_view(ref, me, lead, axis, row, rows, cut):
    head = (ALL,) * lead

    def view(slot, part):
        start, size = row, rows
        if part == 0:
            size = cut
        if part == 1:
            start, size = row + cut, rows - cut
        if axis == "z":
            where = (lax.rem(slot, 2), me.y, lax.div(slot, 2))
        else:
            where = (me.zl, slot, me.zh)
        return ref.at[head + where + (pl.ds(start, size), ALL)]

    return view


def held_view(ref, lead, axis, rows, cut):
    head = (ALL,) * lead

    def view(slot, part):
        start, size = 0, rows
        if part == 0:
            size = cut
        if part == 1:
            start, size = cut, rows - cut
        where = (lax.rem(slot, 2), lax.div(slot, 2)) if axis == "z" else (slot,)
        return ref.at[head + where + (pl.ds(start, size), ALL)]

    return view


def fold_shapes(lead, count, rows, cut, columns):
    return [
        pltpu.VMEM((*lead, *count, cut, columns), BF),
        pltpu.VMEM((*lead, *count, rows - cut, columns), BF),
        pltpu.VMEM((*lead, *count, rows, columns), BF),
        pltpu.VMEM((*lead, *count, rows, columns), BF),
    ]


def kernel_back(
    start_in, tokens_in, dattn_in, part_in, qkv_in, wo_in, query_in, keys_in, values_in, heads_in,
    lse_in, turned_in, tables_in, gains_in, y_in, dy_in, gain_in, wide_y_in, wide_z_in, down_y_in, down_z_in,
    result_out, tokens_out, g_qkv_out, g_o_out, g_wide_out, g_down_out, gains_out,
    w_qkv, w_o, d_attn, out_part, tables, bias, tok, turned, d_heads, d_query, d_keys, d_values,
    d_query_far, d_keys_far, d_values_far, sum_keys, sum_values, heads_t, heads_t_far, attn_far,
    d_h, far_one, side_left, side_right, last_z,
    near_left, near_right, whole_left, whole_right,
    out_near_left, out_near_right, out_whole_left, out_whole_right,
    g_qkv, g_o, wide_y, wide_z, down_y, down_z, gain_t, gain_x, gain_y, gain_z, gain_c,
    *rest,
):
    bufs, (send, recv, local) = list(rest[:-3]), rest[-3:]
    bufs = [tuple(bufs[4 * i : 4 * i + 4]) for i in range(len(bufs) // 4)]
    me = place()
    wire = Wire(send, recv, local)
    greet(me, ("x", "y", "z"))
    loads = [
        wire.move(dattn_in, d_attn),
        wire.move(wo_in, w_o),
        wire.move(wide_y_in, wide_y),
        wire.move(wide_z_in, wide_z),
        wire.move(down_y_in, down_y),
        wire.move(down_z_in, down_z),
        wire.move(part_in, out_part),
        wire.move(tables_in.at[me.zl], tables),
        wire.move(qkv_in, w_qkv),
        wire.move(tokens_in, tok),
        wire.move(turned_in, turned),
    ]
    for copy in loads[2:6]:
        copy.wait()
    feed = [
        Fold(wire, me, None, ("y", "z"), None, held_view(wide_y, 2 - 1, "z", 64, 32), bufs[0]),
        Fold(wire, me, None, ("z", "y"), None, held_view(wide_z, 1, "y", 64, 32), bufs[1]),
        Fold(wire, me, None, ("y", "z"), None, held_view(down_y, 0, "z", 352, 176), bufs[2]),
        Fold(wire, me, None, ("z", "y"), None, held_view(down_z, 0, "y", 336, 176), bufs[3]),
    ]
    for item in feed:
        item.turn()
    loads[0].wait()
    attn_puts = []
    for block in range(8):
        column = pl.ds(pl.multiple_of((block * 2 + 1 - me.core) * 128, 128), 128)
        attn_puts.append(wire.put(d_attn.at[:, :, column], attn_far.at[block], sibling(me)))
    heads_t[...] = heads_in[...].T
    heads_put = wire.put(heads_t, heads_t_far, sibling(me))
    loads[6].wait()

    def add(target, term):
        add_into(target, [term])

    total = RingSum(
        wire, me, "x", columns_of(out_part), out_near_left, out_near_right, out_whole_left,
        out_whole_right, add,
    ).start()
    loads[1].wait()

    def back_heads(zl, carry):
        weight = jnp.concatenate(
            [w_o[zl, y, zh, c] for y in range(4) for zh in range(2) for c in range(2)], axis=1
        )
        result = dot_nt(d_attn[...].reshape(512, D), weight).astype(BF)
        d_heads[zl * 2] = result[:, 0:HD]
        d_heads[zl * 2 + 1] = result[:, HD : 2 * HD]
        return carry

    lax.fori_loop(0, 2, back_heads, 0)
    fill_bias(bias, me, start_in[0])
    loads[7].wait()

    def grad_o(index, carry):
        zl, y = lax.div(index, 4), lax.rem(index, 4)
        mine = jnp.concatenate(
            [
                d_attn[:, :, pl.ds(pl.multiple_of(((y * 2 + zh) * 2 + me.core) * 128, 128), 128)]
                .reshape(512, 128)
                for zh in range(2)
            ],
            axis=1,
        )
        other = jnp.concatenate(
            [attn_far[y * 2 + zh].reshape(512, 128) for zh in range(2)], axis=1
        )
        rows = pl.ds(pl.multiple_of(zl * 256, 256), 256)
        result = (dot_nn(heads_t[rows, :], mine) + dot_nn(heads_t_far[rows, :], other)).astype(BF)
        g_o[zl, y, 0] = result[:, 0:128]
        g_o[zl, y, 1] = result[:, 128:256]
        return carry

    heads_put.wait_recv()
    for copy in attn_puts:
        copy.wait_recv()
    lax.fori_loop(0, 8, grad_o, 0)
    attn = [
        Fold(wire, me, fold_view(g_o, me, 0, "y", 0, 128, 64), ("y", "z"), bufs[4],
             crossed_view(g_o, me, 0, "z", 0, 128, 64), bufs[5]),
        Fold(wire, me, fold_view(g_o, me, 0, "z", 128, 128, 64), ("z", "y"), bufs[6],
             crossed_view(g_o, me, 0, "y", 128, 128, 64), bufs[7]),
    ]
    for item in attn:
        item.start()
    total.relay()
    for item in feed:
        item.relay_two()

    def back_attend(head, carry):
        for half, span in ((1, 1024), (0, 768)):
            rows = slice(half * 256, half * 256 + 256)
            key, value = keys_in[head, 0:span, :], values_in[head, 0:span, :]
            query, d_head = query_in[head, rows, :], d_heads[head, rows, :]
            scores = dot_nt(key, query) * SCALE + bias[0:span, rows]
            probs = jnp.exp(scores - lse_in[head, :, rows])
            d_probs = dot_nt(value, d_head)
            delta = jnp.sum(probs * d_probs, axis=0, keepdims=True)
            d_scores = (probs * (d_probs - delta) * SCALE).astype(BF)
            d_key = dot_nn(d_scores, query)
            d_value = dot_nn(probs.astype(BF), d_head)
            if half == 1:
                sum_keys[...] = d_key
                sum_values[...] = d_value
            else:
                sum_keys[0:span, :] += d_key
                sum_values[0:span, :] += d_value
            raw = dot_tn(key, d_scores).T
            cosine = tables[0, 2 * half : 2 * half + 2, 0].reshape(256, HD)
            sine = tables[1, 2 * half : 2 * half + 2, 0].reshape(256, HD)
            column = pl.ds(pl.multiple_of(head * HD, HD), HD)
            d_query[rows, column] = turn(raw, cosine, -sine).astype(BF)
        cosine, sine = tables[0].reshape(SEQ, HD), tables[1].reshape(SEQ, HD)
        d_keys[:, column] = turn(sum_keys[...], cosine, -sine).astype(BF)
        d_values[:, column] = sum_values[...].astype(BF)
        return carry

    lax.fori_loop(0, 2, back_attend, 0)
    for item in attn:
        item.relay()
    for item, out in zip(feed[:2], (g_wide_out.at[:, 0:64, :], g_wide_out.at[:, 64:128, :])):
        item.finish(out)
    for item, out in zip(feed[2:], (g_down_out.at[0:352, :], g_down_out.at[352:UNITS, :])):
        item.finish(out)
    lax.fori_loop(2, 4, back_attend, 0)
    grads_put = [
        wire.put(d_query, d_query_far, sibling(me)),
        wire.put(d_keys, d_keys_far, sibling(me)),
        wire.put(d_values, d_values_far, sibling(me)),
    ]
    for item in attn:
        item.turn()
    for copy in loads[8:]:
        copy.wait()

    def back_h(block, carry):
        y, zh = lax.div(block, 2), lax.rem(block, 2)

        def weight(which):
            return jnp.concatenate(
                [w_qkv[which, 0, y, zh].reshape(256, 256), w_qkv[which, 1, y, zh].reshape(256, 256)],
                axis=1,
            )

        column = pl.ds(pl.multiple_of(block * 256, 256), 256)
        both = dot_nt(d_keys[...], weight(1)) + dot_nt(d_values[...], weight(2))
        both = both.reshape(4, 2, 128, 256)
        own = dot_nt(d_query[...], weight(0)).reshape(4, 128, 256) + both[:, 0]
        d_h[:, 0, :, column] = own.astype(BF)
        d_h[:, 1, :, column] = both[:, 1].astype(BF)
        return carry

    lax.fori_loop(0, 8, back_h, 0)
    one, far, three = rem4(me.x + 1), rem4(me.x + 2), rem4(me.x + 3)
    to_z = wire.put(d_h.at[far, 1], far_one, partner(me))
    to_right = wire.put(d_h.at[one, 1], side_left, near(me, "x", 1))
    to_left = wire.put(d_h.at[three, 1], side_right, near(me, "x", 3))

    total.finish()

    def finish_out(index, carry):
        span = pl.ds(pl.multiple_of(index * 16, 16), 16)
        result_out[span, :] = (
            y_in[span, :]
            + (
                out_part[me.x, span, :].astype(F32)
                + out_whole_left[span, :].astype(F32)
                + out_whole_right[span, :].astype(F32)
            )
        ).astype(BF)
        return carry

    lax.fori_loop(0, 8, finish_out, 0)
    for copy in grads_put:
        copy.wait_recv()

    def blocks(which, pair):
        return turned[which, pl.ds(pair * 4, 4)].reshape(512, SEQ)

    def own_rows(value):
        return jnp.concatenate([value[:, i * 256 : i * 256 + 128] for i in range(4)], axis=1)

    def grad_qkv(index, carry):
        zl, pair = lax.div(index, 2), lax.rem(index, 2)
        column = pl.ds(pl.multiple_of(zl * 256, 256), 256)
        mine, other = blocks(0, pair), blocks(1, pair)
        result = dot_nn(own_rows(mine), d_query[:, column])
        result = result + dot_nn(own_rows(other), d_query_far[:, column])
        g_qkv[0, zl, pl.ds(pair * 2, 2)] = result.astype(BF).reshape(2, 2, 128, 256)
        result = dot_nn(mine, d_keys[:, column]) + dot_nn(other, d_keys_far[:, column])
        g_qkv[1, zl, pl.ds(pair * 2, 2)] = result.astype(BF).reshape(2, 2, 128, 256)
        result = dot_nn(mine, d_values[:, column]) + dot_nn(other, d_values_far[:, column])
        g_qkv[2, zl, pl.ds(pair * 2, 2)] = result.astype(BF).reshape(2, 2, 128, 256)
        return carry

    lax.fori_loop(0, 4, grad_qkv, 0)
    more = [
        Fold(wire, me, fold_view(g_qkv, me, 1, "y", 0, 64, 32), ("y", "z"), bufs[8],
             crossed_view(g_qkv, me, 1, "z", 0, 64, 32), bufs[9]),
        Fold(wire, me, fold_view(g_qkv, me, 1, "z", 64, 64, 32), ("z", "y"), bufs[10],
             crossed_view(g_qkv, me, 1, "y", 64, 64, 32), bufs[11]),
    ]
    for item in more:
        item.start()

    to_z.wait_recv()
    add_into(d_h.at[far, 0], [far_one])
    own_part = RingSum(
        wire, me, "x",
        lambda slot, half: d_h.at[slot, 0] if half is None else d_h.at[slot, 0, :, pl.ds(half * 1024, 1024)],
        near_left, near_right, whole_left, whole_right, add,
    ).start()
    to_right.wait_recv()
    to_left.wait_recv()
    add_into(d_h.at[me.x, 1], [side_left, side_right])
    to_z = wire.put(d_h.at[me.x, 1], last_z, partner(me))
    for item in attn:
        item.relay_two()
    own_part.relay()
    for item in more:
        item.relay()
    for item, out in zip(attn, (g_o_out.at[0:128, :], g_o_out.at[128:256, :])):
        item.finish(out)
    for item in more:
        item.turn()
    own_part.finish()
    to_z.wait_recv()

    gain_one = gains_in[0:1, :]

    def back_norm(index, carry):
        span = pl.ds(pl.multiple_of(index * 16, 16), 16)
        d_h_one = (
            d_h[me.x, 0, span, :].astype(F32)
            + whole_left[span, :].astype(F32)
            + whole_right[span, :].astype(F32)
            + last_z[span, :].astype(F32)
        )
        value = tok[span, :].astype(F32)
        scale = lax.rsqrt(jnp.mean(value * value, axis=-1, keepdims=True) + EPS)
        normed = value * scale
        e_one = d_h_one * gain_one
        inner = jnp.mean(e_one * normed, axis=-1, keepdims=True)
        tokens_out[span, :] = (dy_in[span, :] + scale * (e_one - normed * inner)).astype(BF)
        return carry + jnp.sum(d_h_one * normed, axis=0, keepdims=True)

    gain_t[0:1, :] = lax.fori_loop(0, 8, back_norm, jnp.zeros((1, D), F32))
    gain_t[1:2, :] = gain_in[...]
    for row in range(2):
        for block in range(16):
            gain_x[me.x, row * 16 + block : row * 16 + block + 1, :] = gain_t[
                row : row + 1, block * 128 : block * 128 + 128
            ]
    ring = Ring(wire, me, "x", lambda slot, half: gain_x.at[slot]).start()
    for item in more:
        item.relay_two()
    ring.relay(False).finish()
    gain_z[me.z] = gain_x[0] + gain_x[1] + gain_x[2] + gain_x[3]
    Ring(wire, me, "z", lambda slot, half: gain_z.at[slot]).start().relay(False).finish()
    gain_y[me.y] = gain_z[0] + gain_z[1] + gain_z[2] + gain_z[3]
    Ring(wire, me, "y", lambda slot, half: gain_y.at[slot]).start().relay(False).finish()
    gain_c[me.core] = gain_y[0] + gain_y[1] + gain_y[2] + gain_y[3]
    piece = gain_c.at[me.core]
    wire.put(piece, piece, sibling(me)).wait_recv()
    gains_out[...] = gain_c[0] + gain_c[1]
    for item, out in zip(more, (g_qkv_out.at[:, 0:64, :], g_qkv_out.at[:, 64:128, :])):
        item.finish(out)
    wire.drain()


def call_back(starts, tokens, d_attn, out_part, qkv, w_out, query, keys, values, heads, lse, turned,
              tables, gains, y_one, d_y, gain_two, wide_y, wide_z, down_y, down_z):
    shape = jax.ShapeDtypeStruct
    bufs = (
        fold_shapes((2,), (), 64, 32, UNITS)
        + fold_shapes((2,), (), 64, 32, UNITS)
        + fold_shapes((), (), 352, 176, 128)
        + fold_shapes((), (), 336, 176, 128)
        + fold_shapes((), (2, 2), 128, 64, 128)
        + fold_shapes((), (), 128, 64, 128)
        + fold_shapes((), (4,), 128, 64, 128)
        + fold_shapes((), (), 128, 64, 128)
        + fold_shapes((3,), (2, 2), 64, 32, 256)
        + fold_shapes((3,), (), 64, 32, 256)
        + fold_shapes((3,), (4,), 64, 32, 256)
        + fold_shapes((3,), (), 64, 32, 256)
    )
    return pl.pallas_call(
        kernel_back,
        name="back",
        in_specs=[pl.BlockSpec(memory_space=pltpu.SMEM)]
        + [anywhere()] * 5
        + [in_vmem()] * 5
        + [anywhere()] * 2
        + [in_vmem()] * 4
        + [anywhere()] * 4,
        out_specs=[in_vmem()] * 7,
        out_shape=[
            shape((128, D), BF),
            shape((128, D), BF),
            shape((3, 128, 256), F32),
            shape((256, 128), F32),
            shape((2, 128, UNITS), F32),
            shape((UNITS, 128), F32),
            shape((32, 128), F32),
        ],
        scratch_shapes=[
            pltpu.VMEM((3, 2, 4, 2, 2, 128, 256), BF),
            pltpu.VMEM((2, 4, 2, 2, 256, 128), BF),
            pltpu.VMEM((4, 128, D), BF),
            pltpu.VMEM((4, 128, D), BF),
            pltpu.VMEM((2, 4, 2, 128, HD), F32),
            pltpu.VMEM((SEQ, 512), F32),
            pltpu.VMEM((128, D), BF),
            pltpu.VMEM((2, 8, 128, SEQ), BF),
            pltpu.VMEM((4, 512, HD), BF),
            pltpu.VMEM((512, 512), BF),
            pltpu.VMEM((SEQ, 512), BF),
            pltpu.VMEM((SEQ, 512), BF),
            pltpu.VMEM((512, 512), BF),
            pltpu.VMEM((SEQ, 512), BF),
            pltpu.VMEM((SEQ, 512), BF),
            pltpu.VMEM((SEQ, HD), F32),
            pltpu.VMEM((SEQ, HD), F32),
            pltpu.VMEM((512, 512), BF),
            pltpu.VMEM((512, 512), BF),
            pltpu.VMEM((8, 4, 128, 128), BF),
            pltpu.VMEM((4, 2, 128, D), BF),
        ]
        + [pltpu.VMEM((128, D), BF)] * 4
        + [
            pltpu.VMEM((128, D // 2), BF),
            pltpu.VMEM((128, D // 2), BF),
            pltpu.VMEM((128, D), BF),
            pltpu.VMEM((128, D), BF),
        ]
        * 2
        + [
            pltpu.VMEM((3, 2, 4, 2, 128, 256), BF),
            pltpu.VMEM((2, 4, 2, 256, 128), BF),
            pltpu.VMEM((2, 2, 2, 64, UNITS), BF),
            pltpu.VMEM((2, 4, 64, UNITS), BF),
            pltpu.VMEM((2, 2, 352, 128), BF),
            pltpu.VMEM((4, 336, 128), BF),
            pltpu.VMEM((2, D), F32),
            pltpu.VMEM((4, 32, 128), F32),
            pltpu.VMEM((4, 32, 128), F32),
            pltpu.VMEM((4, 32, 128), F32),
            pltpu.VMEM((2, 32, 128), F32),
        ]
        + bufs
        + [
            pltpu.SemaphoreType.DMA((90,)),
            pltpu.SemaphoreType.DMA((90,)),
            pltpu.SemaphoreType.DMA((16,)),
        ],
        compiler_params=pltpu.CompilerParams(
            collective_id=2, has_side_effects=True, vmem_limit_bytes=VMEM_BYTES
        ),
    )(starts, tokens, d_attn, out_part, qkv, w_out, query, keys, values, heads, lse, turned,
      tables, gains, y_one, d_y, gain_two, wide_y, wide_z, down_y, down_z)


def on_device(tables, tokens, starts, w_query, w_key, w_value, w_out, w_gate, w_up, w_down,
              gain_attn, gain_mlp, cotangent):
    qkv = jnp.stack([w_query, w_key, w_value])
    wide = jnp.stack([w_gate, w_up])
    tile = gain_tile(gain_attn, gain_mlp)
    (qkv, w_o, wide, down, cot, turned, query, keys, values, heads, lse, y_one, h_two, gains) = (
        call_attend(tokens, cotangent, starts, qkv, w_out, wide, w_down, tile, tables)
    )
    (out_part, d_attn, wide_y, wide_z, down_y, down_z, d_y, gain_two) = call_feed(
        h_two, cot, wide, down, y_one, gains
    )
    result, grad_tokens, g_qkv, g_o, g_wide, g_down, g_gains = call_back(
        starts, tokens, d_attn, out_part, qkv, w_o, query, keys, values, heads, lse, turned,
        tables, gains, y_one, d_y, gain_two, wide_y, wide_z, down_y, down_z,
    )
    dp, tp = lax.axis_index("dp"), lax.axis_index("tensor")
    grad_attn = lax.dynamic_slice(g_gains, (dp, tp * 16), (1, 16))[0]
    grad_mlp = lax.dynamic_slice(g_gains, (16 + dp, tp * 16), (1, 16))[0]
    return (
        result, grad_tokens, g_qkv[0], g_qkv[1], g_qkv[2], g_o, g_wide[0], g_wide[1], g_down,
        grad_attn, grad_mlp,
    )


def solution(mesh):
    both = ("dp", "tensor")
    rows, wide, tall = P(both, None), P("dp", "tensor"), P("tensor", "dp")
    in_specs = (
        rows, P("dp"), wide, wide, wide, tall, wide, wide, tall, P(both), P(both), rows,
    )
    out_specs = (
        rows, rows, wide, wide, wide, tall, wide, wide, tall, P(both), P(both),
    )
    return jax.shard_map(
        functools.partial(on_device, rope_tables()), mesh=mesh, in_specs=in_specs,
        out_specs=out_specs, check_vma=False,
    )
```

```python
import functools
import math
import types

import jax
import jax.numpy as jnp
import numpy as np
from jax import lax
from jax.experimental import pallas as pl
from jax.experimental.pallas import tpu as pltpu
from jax.sharding import PartitionSpec as P

HD = 128
PIECE = 256
EPS = 1e-05
NEG = -1e30
SCALE = HD ** (-0.5)
D = 2048
SEQ = 1024
UNITS = 688
BF = jnp.bfloat16
F32 = jnp.float32
MESH = pl.DeviceIdType.MESH
VMEM_BYTES = 60 * 1024 * 1024
ALL = slice(None)


def dot_nn(left, right):
    return jnp.dot(left, right, preferred_element_type=F32)


def dot_nt(left, right):
    return lax.dot_general(left, right, (((1,), (1,)), ((), ())), preferred_element_type=F32)


def dot_tn(left, right):
    return lax.dot_general(left, right, (((0,), (0,)), ((), ())), preferred_element_type=F32)


def rem4(value):
    return lax.rem(value, 4)


def place():
    dp = lax.axis_index("dp")
    tp = lax.axis_index("tensor")
    zh = lax.rem(lax.div(dp, 2), 2)
    zl = lax.rem(tp, 2)
    return types.SimpleNamespace(
        y=lax.div(dp, 4), zh=zh, zl=zl, z=zh * 2 + zl, x=lax.div(tp, 2), core=lax.rem(dp, 2)
    )


def device(me, **moved):
    at = types.SimpleNamespace(**{**vars(me), **moved})
    zh, zl = lax.div(at.z, 2), lax.rem(at.z, 2)
    return (at.y * 4 + zh * 2 + at.core, at.x * 2 + zl)


def near(me, axis, step):
    return device(me, **{axis: rem4(getattr(me, axis) + step)})


def sibling(me):
    return device(me, core=1 - me.core)


def partner(me):
    return device(me, z=me.zh * 2 + 1 - me.zl)


def greet(me, wide):
    others = [near(me, axis, step) for axis in ("x", "y", "z") for step in (1, 3)] + [sibling(me)]
    if wide:
        others += [near(me, axis, 2) for axis in ("x", "y", "z")]
        others += [crossed(me, step) for step in (1, 2, 3)]
    barrier = pltpu.get_barrier_semaphore()
    for other in others:
        pl.semaphore_signal(barrier, inc=1, device_id=other, device_id_type=MESH)
    pl.semaphore_wait(barrier, len(others))


def crossed(me, step):
    return device(me, y=rem4(me.y + step), core=1 - me.core)


class Wire:
    def __init__(self, send, recv, local):
        self.send, self.recv, self.local = send, recv, local
        self.used, self.used_local = 0, 0
        self.sent = []

    def put(self, source, target, to):
        index = self.used
        self.used += 1
        copy = pltpu.make_async_remote_copy(
            src_ref=source,
            dst_ref=target,
            send_sem=self.send.at[index],
            recv_sem=self.recv.at[index],
            device_id=to,
            device_id_type=MESH,
        )
        copy.start()
        self.sent.append(copy)
        return copy

    def move(self, source, target):
        index = self.used_local
        self.used_local += 1
        copy = pltpu.make_async_copy(source, target, self.local.at[index])
        copy.start()
        return copy

    def settle(self, copies):
        for copy in copies:
            copy.wait_send()
        done = {id(copy) for copy in copies}
        self.sent = [copy for copy in self.sent if id(copy) not in done]

    def drain(self):
        for copy in self.sent:
            copy.wait_send()
        self.sent = []


class Ring:
    def __init__(self, wire, me, axis, view):
        self.wire, self.view = wire, view
        self.at = getattr(me, axis)
        self.right, self.left = near(me, axis, 1), near(me, axis, 3)

    def put(self, slot, part, to):
        piece = self.view(slot, part)
        return self.wire.put(piece, piece, to)

    def start(self):
        self.right_one = self.put(self.at, 0, self.right)
        self.left_one = self.put(self.at, 1, self.left)
        self.right_two = self.put(self.at, 1, self.right)
        self.left_two = self.put(self.at, 0, self.left)
        return self

    def relay(self):
        self.right_one.wait_recv()
        self.far_right = self.put(rem4(self.at + 3), 0, self.right)
        self.left_one.wait_recv()
        self.far_left = self.put(rem4(self.at + 1), 1, self.left)
        return self

    def close(self):
        self.right_two.wait_recv()
        self.left_two.wait_recv()
        return self

    def finish(self):
        self.far_right.wait_recv()
        self.far_left.wait_recv()
        return self


class Meet:
    def __init__(self, wire, me, axis, ref):
        piece = ref.at[getattr(me, axis)]
        self.copies = [wire.put(piece, piece, near(me, axis, step)) for step in (1, 2, 3)]

    def finish(self):
        for copy in self.copies:
            copy.wait_recv()


class MeetCores:
    def __init__(self, wire, me, ref):
        piece = ref.at[me.core, me.y]
        others = [near(me, "y", step) for step in (1, 2, 3)] + [sibling(me)]
        others += [crossed(me, step) for step in (1, 2, 3)]
        self.copies = [wire.put(piece, piece, other) for other in others]

    finish = Meet.finish


class RingSum:
    def __init__(self, wire, me, axis, part, from_left, from_right, whole_left, whole_right, split, add):
        self.wire, self.part, self.split, self.add = wire, part, split, add
        self.at = getattr(me, axis)
        self.right, self.left = near(me, axis, 1), near(me, axis, 3)
        self.near_bufs = (from_left, from_right)
        self.whole = (whole_left, whole_right)

    def start(self, halves=(0, 1)):
        after, far, before = rem4(self.at + 1), rem4(self.at + 2), rem4(self.at + 3)
        put, part, split = self.wire.put, self.part, self.split
        if 0 in halves:
            self.first = put(part(far, 0), self.near_bufs[0], self.right)
        if 1 in halves:
            self.second = put(part(far, 1), self.near_bufs[1], self.left)
        if 0 in halves:
            self.left_whole = put(part(before, 0), split(self.whole[1], 0), self.left)
        if 1 in halves:
            self.right_whole = put(part(after, 1), split(self.whole[0], 1), self.right)
        return self

    def relay(self):
        after, before = rem4(self.at + 1), rem4(self.at + 3)
        self.first.wait_recv()
        self.add(self.part(after, 0), self.near_bufs[0])
        self.to_right = self.wire.put(self.part(after, 0), self.split(self.whole[0], 0), self.right)
        self.second.wait_recv()
        self.add(self.part(before, 1), self.near_bufs[1])
        self.to_left = self.wire.put(self.part(before, 1), self.split(self.whole[1], 1), self.left)
        return self

    def finish(self):
        for copy in (self.left_whole, self.right_whole, self.to_right, self.to_left):
            copy.wait_recv()
        return self


def split_columns(ref, half):
    return ref.at[:, pl.ds(half * (D // 2), D // 2)]


def split_rows(cut):
    def split(ref, half):
        rows = ref.shape[-2]
        span = pl.ds(0, cut) if half == 0 else pl.ds(cut, rows - cut)
        return ref.at[(ALL,) * (len(ref.shape) - 2) + (span, ALL)]

    return split


class Spread:
    def __init__(self, wire, me, ref, lead, row, rows, first, cut):
        self.wire, self.me = wire, me
        head = (ALL,) * lead

        def view(y, z, part):
            zl, zh = (ALL, ALL) if z is None else (lax.rem(z, 2), lax.div(z, 2))
            start, size = row, rows
            if part == 0:
                size = cut
            if part == 1:
                start, size = row + cut, rows - cut
            yy = ALL if y is None else y
            return ref.at[head + (zl, yy, zh, me.core, pl.ds(start, size), ALL)]

        self.view = view
        if first == "y":
            self.one = Ring(wire, me, "y", lambda slot, part: view(slot, me.z, part))
            self.two = Ring(wire, me, "z", lambda slot, part: view(None, slot, part))
        else:
            self.one = Ring(wire, me, "z", lambda slot, part: view(me.y, slot, part))
            self.two = Ring(wire, me, "y", lambda slot, part: view(slot, None, part))
        self.shared = []

    def share(self, slot):
        piece = self.two.view(slot, None)
        self.shared.append(self.wire.put(piece, piece, sibling(self.me)))

    def turn(self):
        self.one.close().finish()
        self.two.start()
        self.share(self.two.at)

    def relay(self):
        self.two.relay()

    def finish(self):
        self.two.close()
        self.share(rem4(self.two.at + 3))
        self.share(rem4(self.two.at + 1))
        self.two.finish()
        self.share(rem4(self.two.at + 2))

    def wait(self):
        for copy in self.shared:
            copy.wait_recv()


def norm_rows(source, target, gain, rows, step=32):
    def body(index, carry):
        span = pl.ds(pl.multiple_of(index * step, step), step)
        value = source[span, :].astype(F32)
        scale = lax.rsqrt(jnp.mean(value * value, axis=-1, keepdims=True) + EPS)
        target[span, :] = (value * scale * gain).astype(BF)
        return carry

    lax.fori_loop(0, rows // step, body, 0)


def fill_bias(bias, me, start):
    row = lax.broadcasted_iota(jnp.int32, (128, 512), 0)
    column = lax.broadcasted_iota(jnp.int32, (128, 512), 1)
    query = lax.div(column, 128) * 256 + me.zl * 128 + lax.rem(column, 128)
    query_in = (query >= start) & (query < start + PIECE)

    def body(block, carry):
        pair, other = lax.div(block, 2), lax.rem(block, 2)
        parity = me.zl + other * (1 - 2 * me.zl)
        key = (pair * 2 + parity) * 128 + row
        key_in = (key >= start) & (key < start + PIECE)
        allowed = (key <= query) | (query_in & key_in)
        bias[pl.ds(pl.multiple_of(block * 128, 128), 128), :] = jnp.where(allowed, 0.0, NEG)
        return carry

    lax.fori_loop(0, 8, body, 0)


def turn(field, cosine, sine):
    return field * cosine + pltpu.roll(field, HD // 2, 1) * sine


def add_into(target, terms, result=None):
    shape = target.shape
    lead, rows, columns = shape[:-2], shape[-2], shape[-1]
    step = rows
    while step * columns > 33000:
        step = next(s for s in range(step - 16, 0, -16) if rows % s == 0)
    cuts = rows // step
    result = target if result is None else result

    def body(index, carry):
        where, rest = [], lax.div(index, cuts)
        for extent in reversed(lead):
            where.insert(0, lax.rem(rest, extent))
            rest = lax.div(rest, extent)
        where = tuple(where) + (
            pl.ds(pl.multiple_of(lax.rem(index, cuts) * step, 16), step), ALL
        )
        total = target[where].astype(F32)
        for term in terms:
            total = total + term[where].astype(F32)
        result[where] = total.astype(result.dtype)
        return carry

    lax.fori_loop(0, math.prod(lead) * cuts, body, 0)


def columns_of(ref):
    def view(slot, half):
        if half is None:
            return ref.at[slot]
        return ref.at[slot, :, pl.ds(half * (D // 2), D // 2)]

    return view


def rows_of(ref):
    def view(slot, half):
        return ref.at[slot] if half is None else ref.at[slot, pl.ds(half * 64, 64)]

    return view


def kernel_attend(
    tokens_in, cotangent_in, start_in, query_w, key_w, value_w, out_w, gate_w, up_w, down_w,
    gain_one_in, gain_two_in, tables_in,
    qkv_out, wo_out, mlp_out, cot_out, turned_out, query_out, keys_out, values_out, heads_out,
    h_out, lse_out, y_out, gains_out,
    tok, h_one, w_qkv, w_o, w_mlp, tables, bias, query, keys, values, heads, cot, h_two,
    part, near_left, near_right, whole_left, whole_right,
    turned, gain_x, gain_z, gain_c,
    send, recv, local,
):
    me = place()
    wire = Wire(send, recv, local)
    own = [wire.move(tokens_in, tok.at[me.x, 0])]
    for index, ref in enumerate((query_w, key_w, value_w)):
        own.append(wire.move(ref, w_qkv.at[index, me.zl, me.y, me.zh, me.core]))
    own.append(wire.move(out_w, w_o.at[me.zl, me.y, me.zh, me.core]))
    for index, ref in enumerate((gate_w, up_w, down_w)):
        own.append(wire.move(ref, w_mlp.at[index, me.zl, me.y, me.zh, me.core]))
    own.append(wire.move(tables_in.at[me.zl], tables))
    own.append(wire.move(cotangent_in, cot.at[me.x]))
    lane = lax.div(lax.broadcasted_iota(jnp.int32, (1, 128), 1), 16)
    tensor = me.x * 2 + me.zl
    gain_x[me.x] = jnp.concatenate(
        [
            jnp.where(lane == tensor, jnp.concatenate([ref[...]] * 8, axis=1), 0.0)
            for ref in (gain_one_in, gain_two_in)
        ]
        + [jnp.zeros((6, 128), F32)],
        axis=0,
    )
    greet(me, True)
    one, far, three = rem4(me.x + 1), rem4(me.x + 2), rem4(me.x + 3)
    meet = Meet(wire, me, "x", gain_x)

    own[0].wait()
    rows_x = Ring(
        wire, me, "x",
        lambda slot, half: tok.at[slot, 0] if half is None else tok.at[slot, 0, pl.ds(half * 64, 64)],
    ).start()
    rows_z = wire.put(tok.at[me.x, 0], tok.at[me.x, 1], partner(me))
    for copy in own[1:5]:
        copy.wait()
    qkv = [
        Spread(wire, me, w_qkv, 1, 0, 64, "y", 32),
        Spread(wire, me, w_qkv, 1, 64, 64, "z", 32),
    ]
    outs = [
        Spread(wire, me, w_o, 0, 0, 128, "y", 64),
        Spread(wire, me, w_o, 0, 128, 128, "z", 64),
    ]
    mlp = [
        Spread(wire, me, w_mlp, 1, 0, 352, "y", 176),
        Spread(wire, me, w_mlp, 1, 352, 336, "z", 176),
    ]
    for item in qkv + outs:
        item.one.start()
    meet.finish()
    gain_z[me.z] = gain_x[0] + gain_x[1] + gain_x[2] + gain_x[3]
    meet = Meet(wire, me, "z", gain_z)
    for item in qkv + outs:
        item.one.relay()
    meet.finish()
    gain_c[me.core, me.y, 0] = gain_z[0] + gain_z[1]
    gain_c[me.core, me.y, 1] = gain_z[2] + gain_z[3]
    meet = MeetCores(wire, me, gain_c)
    for item in qkv:
        item.turn()
    for copy in own[5:]:
        copy.wait()
    fill_bias(bias, me, start_in[0])
    meet.finish()
    for y in range(4):
        for zh in range(2):
            for core in range(2):
                column = (y * 4 + zh * 2 + core) * 128
                gains_out[:, column : column + 128] = gain_c[core, y, zh]
    rows_x.relay()
    rows_z.wait_recv()
    other_right = wire.put(tok.at[me.x, 1], tok.at[me.x, 1], near(me, "x", 1))
    other_left = wire.put(tok.at[me.x, 1], tok.at[me.x, 1], near(me, "x", 3))
    gain_one, gain_two = gains_out[0:1, :], gains_out[1:2, :]

    norm_rows(tok.at[me.x, 0], h_one.at[me.x, 0], gain_one, 128)
    norm_rows(tok.at[me.x, 1], h_one.at[me.x, 1], gain_one, 128)
    rows_x.close()
    norm_rows(tok.at[one, 0], h_one.at[one, 0], gain_one, 128)
    norm_rows(tok.at[three, 0], h_one.at[three, 0], gain_one, 128)
    for item in qkv:
        item.relay()
    for item in outs:
        item.turn()
    for item in mlp:
        item.one.start()
    rows_x.finish()
    far_z = wire.put(tok.at[far, 0], tok.at[far, 1], partner(me))
    norm_rows(tok.at[far, 0], h_one.at[far, 0], gain_one, 128)
    for item in qkv:
        item.finish()
    for item in outs:
        item.relay()
    for item in mlp:
        item.one.relay()
    for item in qkv:
        item.wait()
    kept = [wire.move(w_qkv, qkv_out)]

    def project(zl, carry):
        rows = h_one[:, 0].reshape(512, D)
        cosine, sine = tables[0, :, 0].reshape(512, HD), tables[1, :, 0].reshape(512, HD)
        raw = dot_nn(rows, w_qkv[0, zl].reshape(D, 256))
        for j in range(2):
            query[zl * 2 + j] = turn(raw[:, j * HD : (j + 1) * HD], cosine, sine).astype(BF)
        raw = dot_nn(rows, w_qkv[1, zl].reshape(D, 256))
        for j in range(2):
            keys[zl * 2 + j, :, 0] = (
                turn(raw[:, j * HD : (j + 1) * HD], cosine, sine).astype(BF).reshape(4, 128, HD)
            )
        raw = dot_nn(rows, w_qkv[2, zl].reshape(D, 256))
        for j in range(2):
            values[zl * 2 + j, :, 0] = raw[:, j * HD : (j + 1) * HD].astype(BF).reshape(4, 128, HD)
        return carry

    lax.fori_loop(0, 2, project, 0)
    kept.append(wire.move(query, query_out))
    other_right.wait_recv()
    other_left.wait_recv()
    norm_rows(tok.at[one, 1], h_one.at[one, 1], gain_one, 128)
    norm_rows(tok.at[three, 1], h_one.at[three, 1], gain_one, 128)
    far_z.wait_recv()
    cot_x = Ring(wire, me, "x", rows_of(cot)).start()
    norm_rows(tok.at[far, 1], h_one.at[far, 1], gain_one, 128)

    def project_other(zl, carry):
        rows = h_one[:, 1].reshape(512, D)
        cosine, sine = tables[0, :, 1].reshape(512, HD), tables[1, :, 1].reshape(512, HD)
        raw = dot_nn(rows, w_qkv[1, zl].reshape(D, 256))
        for j in range(2):
            keys[zl * 2 + j, :, 1] = (
                turn(raw[:, j * HD : (j + 1) * HD], cosine, sine).astype(BF).reshape(4, 128, HD)
            )
        raw = dot_nn(rows, w_qkv[2, zl].reshape(D, 256))
        for j in range(2):
            values[zl * 2 + j, :, 1] = raw[:, j * HD : (j + 1) * HD].astype(BF).reshape(4, 128, HD)
        return carry

    lax.fori_loop(0, 2, project_other, 0)
    kept += [wire.move(keys, keys_out), wire.move(values, values_out)]
    for item in outs:
        item.finish()
    for item in mlp:
        item.turn()

    def attend(head, carry):
        for half, pairs in ((0, 3), (1, 4)):
            span = pairs * 256
            rows = slice(half * 256, half * 256 + 256)
            scores = dot_nt(keys[head, 0:pairs].reshape(span, HD), query[head, rows, :]) * SCALE
            scores = scores + bias[0:span, rows]
            top = jnp.max(scores, axis=0, keepdims=True)
            expo = jnp.exp(scores - top)
            total = jnp.sum(expo, axis=0, keepdims=True)
            probs = (expo * (1.0 / total)).astype(BF)
            result = dot_tn(values[head, 0:pairs].reshape(span, HD), probs)
            heads[rows, pl.ds(pl.multiple_of(head * HD, HD), HD)] = result.T.astype(BF)
            lse_out[head, :, rows] = top + jnp.log(total)
        return carry

    lax.fori_loop(0, 4, attend, 0)
    kept.append(wire.move(heads, heads_out))
    for item in outs:
        item.wait()
    kept.append(wire.move(w_o, wo_out))

    def project_out(block, carry):
        y, zh = lax.div(block, 2), lax.rem(block, 2)
        weight = jnp.concatenate(
            [
                jnp.concatenate([w_o[zl, y, zh, 0], w_o[zl, y, zh, 1]], axis=1)
                for zl in range(2)
            ],
            axis=0,
        )
        result = dot_nn(heads[...], weight).astype(BF).reshape(4, 128, 256)
        part[:, :, pl.ds(pl.multiple_of(block * 256, 256), 256)] = result
        return carry

    total = RingSum(
        wire, me, "x", columns_of(part), near_left, near_right, whole_left, whole_right,
        split_columns, lambda target, term: add_into(target, [term]),
    )
    lax.fori_loop(0, 4, project_out, 0)
    total.start((0,))
    lax.fori_loop(4, 8, project_out, 0)
    total.start((1,))
    cot_x.relay()

    def flip(block, carry):
        column = pl.ds(pl.multiple_of(block * 128, 128), 128)
        rows = h_one[:, :, :, column].reshape(SEQ, 128)
        turned[lax.rem(block, 2), lax.div(block, 2)] = rows.T
        return carry

    lax.fori_loop(0, 8, flip, 0)
    total.relay()
    for item in mlp:
        item.relay()
    lax.fori_loop(8, 16, flip, 0)
    kept.append(wire.move(turned.at[me.core], turned_out.at[0]))
    turned_far = wire.put(turned.at[1 - me.core], turned_out.at[1], sibling(me))
    cot_x.close().finish()
    kept.append(wire.move(cot, cot_out))
    total.finish()

    def finish(index, carry):
        span = pl.ds(pl.multiple_of(index * 32, 32), 32)
        value = tok[me.x, 0, span, :].astype(F32) + (
            part[me.x, span, :].astype(F32)
            + whole_left[span, :].astype(F32)
            + whole_right[span, :].astype(F32)
        )
        scale = lax.rsqrt(jnp.mean(value * value, axis=-1, keepdims=True) + EPS)
        y_out[span, :] = value
        h_two[me.x, span, :] = (value * scale * gain_two).astype(BF)
        return carry

    lax.fori_loop(0, 4, finish, 0)
    h_ring = Ring(wire, me, "x", rows_of(h_two)).start()
    for item in mlp:
        item.finish()
    for item, rows in zip(mlp, (pl.ds(0, 352), pl.ds(352, 336))):
        item.wait()
        kept.append(wire.move(w_mlp.at[:, :, :, :, :, rows], mlp_out.at[:, :, :, :, :, rows]))
    h_ring.relay()
    turned_far.wait_recv()
    h_ring.close().finish()
    kept.append(wire.move(h_two, h_out))
    for copy in kept:
        copy.wait()
    wire.drain()


def anywhere():
    return pl.BlockSpec(memory_space=pl.ANY)


def in_vmem():
    return pl.BlockSpec(memory_space=pltpu.VMEM)


def call_attend(tokens, cotangent, starts, weights, gain_attn, gain_mlp, tables):
    shape = jax.ShapeDtypeStruct
    hbm = [
        shape((3, 2, 4, 2, 2, 128, 256), BF),
        shape((2, 4, 2, 2, 256, 128), BF),
        shape((3, 2, 4, 2, 2, UNITS, 128), BF),
        shape((4, 128, D), BF),
        shape((2, 8, 128, SEQ), BF),
        shape((4, 512, HD), BF),
        shape((4, 4, 2, 128, HD), BF),
        shape((4, 4, 2, 128, HD), BF),
        shape((512, 512), BF),
        shape((4, 128, D), BF),
    ]
    vmem = [shape((4, 1, 512), F32), shape((128, D), F32), shape((8, D), F32)]
    return pl.pallas_call(
        kernel_attend,
        name="attend",
        in_specs=[anywhere(), anywhere(), pl.BlockSpec(memory_space=pltpu.SMEM)]
        + [anywhere()] * 7
        + [in_vmem()] * 2
        + [anywhere()],
        out_specs=[anywhere()] * len(hbm) + [in_vmem()] * len(vmem),
        out_shape=hbm + vmem,
        scratch_shapes=[
            pltpu.VMEM((4, 2, 128, D), BF),
            pltpu.VMEM((4, 2, 128, D), BF),
            pltpu.VMEM((3, 2, 4, 2, 2, 128, 256), BF),
            pltpu.VMEM((2, 4, 2, 2, 256, 128), BF),
            pltpu.VMEM((3, 2, 4, 2, 2, UNITS, 128), BF),
            pltpu.VMEM((2, 4, 2, 128, HD), F32),
            pltpu.VMEM((SEQ, 512), F32),
            pltpu.VMEM((4, 512, HD), BF),
            pltpu.VMEM((4, 4, 2, 128, HD), BF),
            pltpu.VMEM((4, 4, 2, 128, HD), BF),
            pltpu.VMEM((512, 512), BF),
            pltpu.VMEM((4, 128, D), BF),
            pltpu.VMEM((4, 128, D), BF),
            pltpu.VMEM((4, 128, D), BF),
            pltpu.VMEM((128, D // 2), BF),
            pltpu.VMEM((128, D // 2), BF),
            pltpu.VMEM((128, D), BF),
            pltpu.VMEM((128, D), BF),
            pltpu.VMEM((2, 8, 128, SEQ), BF),
            pltpu.VMEM((4, 8, 128), F32),
            pltpu.VMEM((4, 8, 128), F32),
            pltpu.VMEM((2, 4, 2, 8, 128), F32),
            pltpu.SemaphoreType.DMA((140,)),
            pltpu.SemaphoreType.DMA((140,)),
            pltpu.SemaphoreType.DMA((24,)),
        ],
        compiler_params=pltpu.CompilerParams(
            collective_id=0, has_side_effects=True, vmem_limit_bytes=VMEM_BYTES
        ),
    )(tokens, cotangent, starts, *weights, gain_attn, gain_mlp, tables)


def rope_tables():
    half = HD // 2
    freq = np.exp(np.arange(half, dtype=np.float32) * np.float32(-2.0 * math.log(10000.0) / HD))
    order = np.array(
        [
            [[(2 * pair + (zl + other) % 2) * 128 + np.arange(128) for other in range(2)] for pair in range(4)]
            for zl in range(2)
        ]
    )
    angle = order.astype(np.float32)[..., None] * freq.astype(np.float32)
    cosine, sine = np.cos(angle.astype(np.float64)), np.sin(angle.astype(np.float64))
    both = np.stack(
        [np.concatenate([cosine, cosine], -1), np.concatenate([-sine, sine], -1)], axis=1
    )
    return both.astype(np.float32)


def fold_view(ref, me, lead, axis, row, rows, cut):
    head = (ALL,) * lead

    def view(slot, part):
        start, size = row, rows
        if part == 0:
            size = cut
        if part == 1:
            start, size = row + cut, rows - cut
        if axis == "y":
            where = (ALL, slot, ALL)
        else:
            where = (lax.rem(slot, 2), ALL, lax.div(slot, 2))
        return ref.at[head + where + (pl.ds(start, size), ALL)]

    return view


def kernel_feed(
    h_in, cot_in, mlp_in, y_in, gains_in,
    part_out, dattn_out, fold_y_out, fold_z_out, dy_out, gain_out,
    w_mlp, h_two, cot, gate_s, up_s, act_s, d_gate, d_up, act, flipped, flipped_far,
    h_far, cot_far, part, near_left, near_right, whole_left, whole_right, d_attn, out_part,
    *rest,
):
    bufs, (send, recv, local) = list(rest[:-3]), rest[-3:]
    bufs = [tuple(bufs[4 * i : 4 * i + 4]) for i in range(len(bufs) // 4)]
    me = place()
    wire = Wire(send, recv, local)
    loads = [
        wire.move(h_in, h_two),
        wire.move(mlp_in.at[0], w_mlp.at[0]),
        wire.move(mlp_in.at[1], w_mlp.at[1]),
        wire.move(cot_in, cot),
        wire.move(mlp_in.at[2], w_mlp.at[2]),
    ]
    greet(me, False)

    def whole(which, zl):
        return jnp.concatenate(
            [
                w_mlp[which, zl, y, zh, core]
                for y in range(4)
                for zh in range(2)
                for core in range(2)
            ],
            axis=1,
        )

    def share(source, target):
        return [
            wire.put(
                source.at[:, :, pl.ds(pl.multiple_of((block * 2 + 1 - me.core) * 128, 128), 128)],
                target.at[block],
                sibling(me),
            )
            for block in range(8)
        ]

    loads[0].wait()
    h_puts = share(h_two, h_far)
    loads[1].wait()
    gate_s[...] = dot_nt(h_two[...].reshape(512, D), whole(0, 0))
    loads[2].wait()
    up_s[...] = dot_nt(h_two[...].reshape(512, D), whole(1, 0))
    loads[3].wait()
    cot_puts = share(cot, cot_far)
    loads[4].wait()
    far = []

    def forward(zl):
        act_s[...] = dot_nt(cot[...].reshape(512, D), whole(2, zl))

        def inner(index, carry):
            span = pl.ds(pl.multiple_of(index * 32, 32), 32)
            gate, up, d_act = gate_s[span, :], up_s[span, :], act_s[span, :]
            sigma = 1.0 / (1.0 + jnp.exp(-gate))
            act[zl, span, :] = (gate * sigma * up).astype(BF)
            d_gate[zl, span, :] = (d_act * up * sigma * (1.0 + gate * (1.0 - sigma))).astype(BF)
            d_up[zl, span, :] = (d_act * gate * sigma).astype(BF)
            return carry

        lax.fori_loop(0, 16, inner, 0)

    forward(0)
    gate_s[...] = dot_nt(h_two[...].reshape(512, D), whole(0, 1))
    up_s[...] = dot_nt(h_two[...].reshape(512, D), whole(1, 1))
    forward(1)

    def back_h(block, carry):
        y, zh = lax.div(block, 2), lax.rem(block, 2)
        total = None
        for which, left in ((0, d_gate), (1, d_up)):
            for zl in range(2):
                weight = jnp.concatenate(
                    [w_mlp[which, zl, y, zh, 0], w_mlp[which, zl, y, zh, 1]], axis=1
                )
                term = dot_nn(left[zl], weight)
                total = term if total is None else total + term
        part[:, :, pl.ds(pl.multiple_of(block * 256, 256), 256)] = total.astype(BF).reshape(4, 128, 256)
        return carry

    total = RingSum(
        wire, me, "x", columns_of(part), near_left, near_right, whole_left, whole_right,
        split_columns, lambda target, term: add_into(target, [term]),
    )
    lax.fori_loop(0, 4, back_h, 0)
    total.start((0,))
    lax.fori_loop(4, 8, back_h, 0)
    total.start((1,))

    for which, source in enumerate((d_gate, d_up, act)):
        for zl in range(2):
            flipped[which, zl] = source[zl].T
        far.append(wire.put(flipped.at[which], flipped_far.at[which], sibling(me)))

    def forward_down(block, carry):
        y, zh = lax.div(block, 2), lax.rem(block, 2)
        result = None
        for zl in range(2):
            weight = jnp.concatenate([w_mlp[2, zl, y, zh, 0], w_mlp[2, zl, y, zh, 1]], axis=1)
            term = dot_nn(act[zl], weight)
            result = term if result is None else result + term
        out_part[:, :, pl.ds(pl.multiple_of(block * 256, 256), 256)] = result.astype(BF).reshape(4, 128, 256)
        return carry

    lax.fori_loop(0, 8, forward_down, 0)
    kept = [wire.move(out_part, part_out)]
    total.relay()

    def grad(which, rows, rows_far):
        def body(index, carry):
            zl, y = lax.div(index, 4), lax.rem(index, 4)
            mine = jnp.concatenate(
                [
                    rows[:, :, pl.ds(pl.multiple_of(((y * 2 + zh) * 2 + me.core) * 128, 128), 128)]
                    .reshape(512, 128)
                    for zh in range(2)
                ],
                axis=1,
            )
            other = jnp.concatenate(
                [rows_far[y * 2 + zh].reshape(512, 128) for zh in range(2)], axis=1
            )
            result = dot_nn(flipped[which, zl], mine) + dot_nn(flipped_far[which, zl], other)
            result = result.astype(BF)
            w_mlp[which, zl, y, 0, 0] = result[:, 0:128]
            w_mlp[which, zl, y, 1, 0] = result[:, 128:256]
            return carry

        return body

    def add(target, term):
        add_into(target, [term])

    sums = []

    def start_sums(which):
        ref = w_mlp.at[which, :, :, :, 0]
        pair = [
            RingSum(wire, me, "y", fold_view(ref, me, 0, "y", 0, 352, 176), *bufs[2 * which],
                    split_rows(176), add),
            RingSum(wire, me, "z", fold_view(ref, me, 0, "z", 352, 336, 176), *bufs[2 * which + 1],
                    split_rows(176), add),
        ]
        for item in pair:
            item.start()
        sums.append(pair)

    for copy in h_puts:
        copy.wait_recv()
    far[0].wait_recv()
    lax.fori_loop(0, 8, grad(0, h_two, h_far), 0)
    start_sums(0)
    far[1].wait_recv()
    lax.fori_loop(0, 8, grad(1, h_two, h_far), 0)
    start_sums(1)
    total.finish()

    gain_two = gains_in[1:2, :]

    def back_norm(index, carry):
        span = pl.ds(pl.multiple_of(index * 16, 16), 16)
        d_h = (
            part[me.x, span, :].astype(F32)
            + whole_left[span, :].astype(F32)
            + whole_right[span, :].astype(F32)
        )
        value = y_in[span, :]
        scale = lax.rsqrt(jnp.mean(value * value, axis=-1, keepdims=True) + EPS)
        normed = value * scale
        e_two = d_h * gain_two
        inner = jnp.mean(e_two * normed, axis=-1, keepdims=True)
        d_y = cot[me.x, span, :].astype(F32) + scale * (e_two - normed * inner)
        dy_out[span, :] = d_y
        d_attn[me.x, span, :] = d_y.astype(BF)
        return carry + jnp.sum(d_h * normed, axis=0, keepdims=True)

    gain_out[...] = lax.fori_loop(0, 8, back_norm, jnp.zeros((1, D), F32))
    d_ring = Ring(wire, me, "x", rows_of(d_attn)).start()
    far[2].wait_recv()
    for copy in cot_puts:
        copy.wait_recv()
    lax.fori_loop(0, 8, grad(2, cot, cot_far), 0)
    start_sums(2)
    for item in sums[0] + sums[1]:
        item.relay()
    d_ring.relay()
    for item in sums[2]:
        item.relay()
    for which, pair in enumerate(sums):
        for item, out in zip(pair, (fold_y_out, fold_z_out)):
            item.finish()
            mine = item.part(item.at, None)
            add_into(mine, list(item.whole))
            kept.append(wire.move(mine, out.at[which]))
    d_ring.close().finish()
    kept.append(wire.move(d_attn, dattn_out))
    for copy in kept:
        copy.wait()
    wire.drain()


def fold_shapes(lead, count, rows, cut, columns):
    return [
        pltpu.VMEM((*lead, *count, cut, columns), BF),
        pltpu.VMEM((*lead, *count, rows - cut, columns), BF),
        pltpu.VMEM((*lead, *count, rows, columns), BF),
        pltpu.VMEM((*lead, *count, rows, columns), BF),
    ]


def call_feed(h_two, cot, mlp, y_one, gains):
    shape = jax.ShapeDtypeStruct
    bufs = (fold_shapes((), (2, 2), 352, 176, 128) + fold_shapes((), (4,), 336, 176, 128)) * 3
    return pl.pallas_call(
        kernel_feed,
        name="feed",
        in_specs=[anywhere()] * 3 + [in_vmem()] * 2,
        out_specs=[anywhere()] * 4 + [in_vmem()] * 2,
        out_shape=[
            shape((4, 128, D), BF),
            shape((4, 128, D), BF),
            shape((3, 2, 2, 352, 128), BF),
            shape((3, 4, 336, 128), BF),
            shape((128, D), F32),
            shape((1, D), F32),
        ],
        scratch_shapes=[
            pltpu.VMEM((3, 2, 4, 2, 2, UNITS, 128), BF),
            pltpu.VMEM((4, 128, D), BF),
            pltpu.VMEM((4, 128, D), BF),
            pltpu.VMEM((512, UNITS), F32),
            pltpu.VMEM((512, UNITS), F32),
            pltpu.VMEM((512, UNITS), F32),
            pltpu.VMEM((2, 512, UNITS), BF),
            pltpu.VMEM((2, 512, UNITS), BF),
            pltpu.VMEM((2, 512, UNITS), BF),
            pltpu.VMEM((3, 2, UNITS, 512), BF),
            pltpu.VMEM((3, 2, UNITS, 512), BF),
            pltpu.VMEM((8, 4, 128, 128), BF),
            pltpu.VMEM((8, 4, 128, 128), BF),
            pltpu.VMEM((4, 128, D), BF),
            pltpu.VMEM((128, D // 2), BF),
            pltpu.VMEM((128, D // 2), BF),
            pltpu.VMEM((128, D), BF),
            pltpu.VMEM((128, D), BF),
            pltpu.VMEM((4, 128, D), BF),
            pltpu.VMEM((4, 128, D), BF),
        ]
        + bufs
        + [
            pltpu.SemaphoreType.DMA((100,)),
            pltpu.SemaphoreType.DMA((100,)),
            pltpu.SemaphoreType.DMA((24,)),
        ],
        compiler_params=pltpu.CompilerParams(
            collective_id=1, has_side_effects=True, vmem_limit_bytes=VMEM_BYTES
        ),
    )(h_two, cot, mlp, y_one, gains)


class Fold:
    def __init__(self, wire, me, cut, view_one, axes, bufs, view_two, bufs_two):
        def add(target, term):
            add_into(target, [term])

        self.wire, self.me, self.axes, self.add = wire, me, axes, add
        self.view_two, self.bufs_two = view_two, bufs_two
        self.one, self.split = None, split_rows(cut)
        if view_one is not None:
            self.one = RingSum(wire, me, axes[0], view_one, *bufs, self.split, add)

    def start(self):
        self.one.start()

    def relay(self):
        self.one.relay()

    def turn(self):
        if self.one is not None:
            self.one.finish()
            add_into(self.one.part(self.one.at, None), list(self.one.whole))
        self.two = RingSum(self.wire, self.me, self.axes[1], self.view_two, *self.bufs_two, self.split, self.add)
        self.two.start()

    def relay_two(self):
        self.two.relay()

    def finish(self, result):
        self.two.finish()
        add_into(self.two.part(self.two.at, None), list(self.two.whole), result)


def crossed_view(ref, me, lead, axis, row, rows, cut):
    head = (ALL,) * lead

    def view(slot, part):
        start, size = row, rows
        if part == 0:
            size = cut
        if part == 1:
            start, size = row + cut, rows - cut
        if axis == "z":
            where = (lax.rem(slot, 2), me.y, lax.div(slot, 2))
        else:
            where = (me.zl, slot, me.zh)
        return ref.at[head + where + (pl.ds(start, size), ALL)]

    return view


def held_view(ref, lead, axis, rows, cut):
    head = (ALL,) * lead

    def view(slot, part):
        start, size = 0, rows
        if part == 0:
            size = cut
        if part == 1:
            start, size = cut, rows - cut
        where = (lax.rem(slot, 2), lax.div(slot, 2)) if axis == "z" else (slot,)
        return ref.at[head + where + (pl.ds(start, size), ALL)]

    return view


def kernel_back(
    start_in, tokens_in, dattn_in, part_in, qkv_in, wo_in, query_in, keys_in, values_in, heads_in,
    lse_in, turned_in, tables_in, gains_in, y_in, dy_in, gain_in, fold_y_in, fold_z_in,
    result_out, tokens_out, g_qkv_out, g_o_out, g_mlp_out, gains_out,
    w_qkv, w_o, d_attn, out_part, tables, bias, tok, turned, d_heads, d_query, d_keys, d_values,
    d_query_far, d_keys_far, d_values_far, sum_keys, sum_values, heads_t, heads_t_far, attn_far,
    d_h, far_one, side_left, side_right, last_z,
    near_left, near_right, whole_left, whole_right,
    out_near_left, out_near_right, out_whole_left, out_whole_right,
    g_qkv, g_o, fold_y, fold_z, gain_t, gain_x, gain_z, gain_c,
    *rest,
):
    bufs, (send, recv, local) = list(rest[:-3]), rest[-3:]
    bufs = [tuple(bufs[4 * i : 4 * i + 4]) for i in range(len(bufs) // 4)]
    me = place()
    wire = Wire(send, recv, local)
    greet(me, True)
    loads = [
        wire.move(dattn_in, d_attn),
        wire.move(wo_in, w_o),
        wire.move(fold_y_in, fold_y),
        wire.move(fold_z_in, fold_z),
        wire.move(part_in, out_part),
        wire.move(tables_in.at[me.zl], tables),
        wire.move(qkv_in, w_qkv),
        wire.move(tokens_in, tok),
        wire.move(turned_in, turned),
    ]
    for copy in loads[2:4]:
        copy.wait()
    feed = [
        Fold(wire, me, 176, None, ("y", "z"), None, held_view(fold_y, 1, "z", 352, 176), bufs[0]),
        Fold(wire, me, 176, None, ("z", "y"), None, held_view(fold_z, 1, "y", 336, 176), bufs[1]),
    ]
    for item in feed:
        item.turn()
    loads[0].wait()
    attn_puts = []
    for block in range(8):
        column = pl.ds(pl.multiple_of((block * 2 + 1 - me.core) * 128, 128), 128)
        attn_puts.append(wire.put(d_attn.at[:, :, column], attn_far.at[block], sibling(me)))
    heads_t[...] = heads_in[...].T
    heads_put = wire.put(heads_t, heads_t_far, sibling(me))
    loads[4].wait()

    def add(target, term):
        add_into(target, [term])

    total = RingSum(
        wire, me, "x", columns_of(out_part), out_near_left, out_near_right, out_whole_left,
        out_whole_right, split_columns, add,
    ).start()
    loads[1].wait()

    def back_heads(zl, carry):
        weight = jnp.concatenate(
            [w_o[zl, y, zh, c] for y in range(4) for zh in range(2) for c in range(2)], axis=1
        )
        result = dot_nt(d_attn[...].reshape(512, D), weight).astype(BF)
        d_heads[zl * 2] = result[:, 0:HD]
        d_heads[zl * 2 + 1] = result[:, HD : 2 * HD]
        return carry

    lax.fori_loop(0, 2, back_heads, 0)
    fill_bias(bias, me, start_in[0])
    loads[5].wait()

    def grad_o(index, carry):
        zl, y = lax.div(index, 4), lax.rem(index, 4)
        mine = jnp.concatenate(
            [
                d_attn[:, :, pl.ds(pl.multiple_of(((y * 2 + zh) * 2 + me.core) * 128, 128), 128)]
                .reshape(512, 128)
                for zh in range(2)
            ],
            axis=1,
        )
        other = jnp.concatenate(
            [attn_far[y * 2 + zh].reshape(512, 128) for zh in range(2)], axis=1
        )
        rows = pl.ds(pl.multiple_of(zl * 256, 256), 256)
        result = (dot_nn(heads_t[rows, :], mine) + dot_nn(heads_t_far[rows, :], other)).astype(BF)
        g_o[zl, y, 0] = result[:, 0:128]
        g_o[zl, y, 1] = result[:, 128:256]
        return carry

    heads_put.wait_recv()
    for copy in attn_puts:
        copy.wait_recv()
    lax.fori_loop(0, 8, grad_o, 0)
    attn = [
        Fold(wire, me, 64, fold_view(g_o, me, 0, "y", 0, 128, 64), ("y", "z"), bufs[2],
             crossed_view(g_o, me, 0, "z", 0, 128, 64), bufs[3]),
        Fold(wire, me, 64, fold_view(g_o, me, 0, "z", 128, 128, 64), ("z", "y"), bufs[4],
             crossed_view(g_o, me, 0, "y", 128, 128, 64), bufs[5]),
    ]
    for item in attn:
        item.start()
    total.relay()
    for item in feed:
        item.relay_two()

    def back_attend(head, carry):
        for half, pairs in ((1, 4), (0, 3)):
            span = pairs * 256
            rows = slice(half * 256, half * 256 + 256)
            key = keys_in[head, 0:pairs].reshape(span, HD)
            value = values_in[head, 0:pairs].reshape(span, HD)
            query, d_head = query_in[head, rows, :], d_heads[head, rows, :]
            scores = dot_nt(key, query) * SCALE + bias[0:span, rows]
            probs = jnp.exp(scores - lse_in[head, :, rows])
            d_probs = dot_nt(value, d_head)
            delta = jnp.sum(probs * d_probs, axis=0, keepdims=True)
            d_scores = (probs * (d_probs - delta) * SCALE).astype(BF)
            d_key = dot_nn(d_scores, query)
            d_value = dot_nn(probs.astype(BF), d_head)
            if half == 1:
                sum_keys[...] = d_key
                sum_values[...] = d_value
            else:
                sum_keys[0:span, :] += d_key
                sum_values[0:span, :] += d_value
            raw = dot_tn(key, d_scores).T
            cosine = tables[0, 2 * half : 2 * half + 2, 0].reshape(256, HD)
            sine = tables[1, 2 * half : 2 * half + 2, 0].reshape(256, HD)
            column = pl.ds(pl.multiple_of(head * HD, HD), HD)
            d_query[rows, column] = turn(raw, cosine, -sine).astype(BF)
        cosine, sine = tables[0].reshape(SEQ, HD), tables[1].reshape(SEQ, HD)
        d_keys[:, column] = turn(sum_keys[...], cosine, -sine).astype(BF)
        d_values[:, column] = sum_values[...].astype(BF)
        return carry

    lax.fori_loop(0, 2, back_attend, 0)
    for item in attn:
        item.relay()
    for item, out in zip(feed, (g_mlp_out.at[:, 0:352, :], g_mlp_out.at[:, 352:UNITS, :])):
        item.finish(out)
    lax.fori_loop(2, 4, back_attend, 0)
    grads_put = [
        wire.put(d_query, d_query_far, sibling(me)),
        wire.put(d_keys, d_keys_far, sibling(me)),
        wire.put(d_values, d_values_far, sibling(me)),
    ]
    for item in attn:
        item.turn()
    for copy in loads[6:]:
        copy.wait()

    def back_h(block, carry):
        y, zh = lax.div(block, 2), lax.rem(block, 2)

        def weight(which):
            return jnp.concatenate(
                [w_qkv[which, 0, y, zh].reshape(256, 256), w_qkv[which, 1, y, zh].reshape(256, 256)],
                axis=1,
            )

        column = pl.ds(pl.multiple_of(block * 256, 256), 256)
        both = dot_nt(d_keys[...], weight(1)) + dot_nt(d_values[...], weight(2))
        both = both.reshape(4, 2, 128, 256)
        own = dot_nt(d_query[...], weight(0)).reshape(4, 128, 256) + both[:, 0]
        d_h[:, 0, :, column] = own.astype(BF)
        d_h[:, 1, :, column] = both[:, 1].astype(BF)
        return carry

    lax.fori_loop(0, 8, back_h, 0)
    one, far, three = rem4(me.x + 1), rem4(me.x + 2), rem4(me.x + 3)
    to_z = wire.put(d_h.at[far, 1], far_one, partner(me))
    to_right = wire.put(d_h.at[one, 1], side_left, near(me, "x", 1))
    to_left = wire.put(d_h.at[three, 1], side_right, near(me, "x", 3))

    total.finish()

    def finish_out(index, carry):
        span = pl.ds(pl.multiple_of(index * 16, 16), 16)
        result_out[span, :] = (
            y_in[span, :]
            + (
                out_part[me.x, span, :].astype(F32)
                + out_whole_left[span, :].astype(F32)
                + out_whole_right[span, :].astype(F32)
            )
        ).astype(BF)
        return carry

    lax.fori_loop(0, 8, finish_out, 0)
    for copy in grads_put:
        copy.wait_recv()

    def blocks(which, pair):
        return turned[which, pl.ds(pair * 4, 4)].reshape(512, SEQ)

    def own_rows(value):
        return jnp.concatenate([value[:, i * 256 : i * 256 + 128] for i in range(4)], axis=1)

    def grad_qkv(index, carry):
        zl, pair = lax.div(index, 2), lax.rem(index, 2)
        column = pl.ds(pl.multiple_of(zl * 256, 256), 256)
        mine, other = blocks(0, pair), blocks(1, pair)
        result = dot_nn(own_rows(mine), d_query[:, column])
        result = result + dot_nn(own_rows(other), d_query_far[:, column])
        g_qkv[0, zl, pl.ds(pair * 2, 2)] = result.astype(BF).reshape(2, 2, 128, 256)
        result = dot_nn(mine, d_keys[:, column]) + dot_nn(other, d_keys_far[:, column])
        g_qkv[1, zl, pl.ds(pair * 2, 2)] = result.astype(BF).reshape(2, 2, 128, 256)
        result = dot_nn(mine, d_values[:, column]) + dot_nn(other, d_values_far[:, column])
        g_qkv[2, zl, pl.ds(pair * 2, 2)] = result.astype(BF).reshape(2, 2, 128, 256)
        return carry

    lax.fori_loop(0, 4, grad_qkv, 0)
    more = [
        Fold(wire, me, 32, fold_view(g_qkv, me, 1, "y", 0, 64, 32), ("y", "z"), bufs[6],
             crossed_view(g_qkv, me, 1, "z", 0, 64, 32), bufs[7]),
        Fold(wire, me, 32, fold_view(g_qkv, me, 1, "z", 64, 64, 32), ("z", "y"), bufs[8],
             crossed_view(g_qkv, me, 1, "y", 64, 64, 32), bufs[9]),
    ]
    for item in more:
        item.start()

    to_z.wait_recv()
    add_into(d_h.at[far, 0], [far_one])
    own_part = RingSum(
        wire, me, "x",
        lambda slot, half: d_h.at[slot, 0] if half is None else d_h.at[slot, 0, :, pl.ds(half * 1024, 1024)],
        near_left, near_right, whole_left, whole_right, split_columns, add,
    ).start()
    to_right.wait_recv()
    to_left.wait_recv()
    add_into(d_h.at[me.x, 1], [side_left, side_right])
    to_z = wire.put(d_h.at[me.x, 1], last_z, partner(me))
    for item in attn:
        item.relay_two()
    own_part.relay()
    for item in more:
        item.relay()
    for item, out in zip(attn, (g_o_out.at[0:128, :], g_o_out.at[128:256, :])):
        item.finish(out)
    for item in more:
        item.turn()
    own_part.finish()
    to_z.wait_recv()

    gain_one = gains_in[0:1, :]

    def back_norm(index, carry):
        span = pl.ds(pl.multiple_of(index * 16, 16), 16)
        d_h_one = (
            d_h[me.x, 0, span, :].astype(F32)
            + whole_left[span, :].astype(F32)
            + whole_right[span, :].astype(F32)
            + last_z[span, :].astype(F32)
        )
        value = tok[span, :].astype(F32)
        scale = lax.rsqrt(jnp.mean(value * value, axis=-1, keepdims=True) + EPS)
        normed = value * scale
        e_one = d_h_one * gain_one
        inner = jnp.mean(e_one * normed, axis=-1, keepdims=True)
        tokens_out[span, :] = (dy_in[span, :] + scale * (e_one - normed * inner)).astype(BF)
        return carry + jnp.sum(d_h_one * normed, axis=0, keepdims=True)

    gain_t[0:1, :] = lax.fori_loop(0, 8, back_norm, jnp.zeros((1, D), F32))
    gain_t[1:2, :] = gain_in[...]
    for row in range(2):
        for block in range(16):
            gain_x[me.x, row * 16 + block : row * 16 + block + 1, :] = gain_t[
                row : row + 1, block * 128 : block * 128 + 128
            ]
    meet = Meet(wire, me, "x", gain_x)
    for item in more:
        item.relay_two()
    meet.finish()
    gain_z[me.z] = gain_x[0] + gain_x[1] + gain_x[2] + gain_x[3]
    Meet(wire, me, "z", gain_z).finish()
    gain_c[me.core, me.y] = gain_z[0] + gain_z[1] + gain_z[2] + gain_z[3]
    MeetCores(wire, me, gain_c).finish()
    total = gain_c[0, 0]
    for core, y in ((0, 1), (0, 2), (0, 3), (1, 0), (1, 1), (1, 2), (1, 3)):
        total = total + gain_c[core, y]
    gains_out[...] = total
    for item, out in zip(more, (g_qkv_out.at[:, 0:64, :], g_qkv_out.at[:, 64:128, :])):
        item.finish(out)
    wire.drain()


def call_back(starts, tokens, d_attn, out_part, qkv, w_out, query, keys, values, heads, lse, turned,
              tables, gains, y_one, d_y, gain_two, fold_y, fold_z):
    shape = jax.ShapeDtypeStruct
    bufs = (
        fold_shapes((3,), (), 352, 176, 128)
        + fold_shapes((3,), (), 336, 176, 128)
        + fold_shapes((), (2, 2), 128, 64, 128)
        + fold_shapes((), (), 128, 64, 128)
        + fold_shapes((), (4,), 128, 64, 128)
        + fold_shapes((), (), 128, 64, 128)
        + fold_shapes((3,), (2, 2), 64, 32, 256)
        + fold_shapes((3,), (), 64, 32, 256)
        + fold_shapes((3,), (4,), 64, 32, 256)
        + fold_shapes((3,), (), 64, 32, 256)
    )
    return pl.pallas_call(
        kernel_back,
        name="back",
        in_specs=[pl.BlockSpec(memory_space=pltpu.SMEM)]
        + [anywhere()] * 5
        + [in_vmem()] * 5
        + [anywhere()] * 2
        + [in_vmem()] * 4
        + [anywhere()] * 2,
        out_specs=[in_vmem()] * 6,
        out_shape=[
            shape((128, D), BF),
            shape((128, D), BF),
            shape((3, 128, 256), F32),
            shape((256, 128), F32),
            shape((3, UNITS, 128), F32),
            shape((32, 128), F32),
        ],
        scratch_shapes=[
            pltpu.VMEM((3, 2, 4, 2, 2, 128, 256), BF),
            pltpu.VMEM((2, 4, 2, 2, 256, 128), BF),
            pltpu.VMEM((4, 128, D), BF),
            pltpu.VMEM((4, 128, D), BF),
            pltpu.VMEM((2, 4, 2, 128, HD), F32),
            pltpu.VMEM((SEQ, 512), F32),
            pltpu.VMEM((128, D), BF),
            pltpu.VMEM((2, 8, 128, SEQ), BF),
            pltpu.VMEM((4, 512, HD), BF),
            pltpu.VMEM((512, 512), BF),
            pltpu.VMEM((SEQ, 512), BF),
            pltpu.VMEM((SEQ, 512), BF),
            pltpu.VMEM((512, 512), BF),
            pltpu.VMEM((SEQ, 512), BF),
            pltpu.VMEM((SEQ, 512), BF),
            pltpu.VMEM((SEQ, HD), F32),
            pltpu.VMEM((SEQ, HD), F32),
            pltpu.VMEM((512, 512), BF),
            pltpu.VMEM((512, 512), BF),
            pltpu.VMEM((8, 4, 128, 128), BF),
            pltpu.VMEM((4, 2, 128, D), BF),
        ]
        + [pltpu.VMEM((128, D), BF)] * 4
        + [
            pltpu.VMEM((128, D // 2), BF),
            pltpu.VMEM((128, D // 2), BF),
            pltpu.VMEM((128, D), BF),
            pltpu.VMEM((128, D), BF),
        ]
        * 2
        + [
            pltpu.VMEM((3, 2, 4, 2, 128, 256), BF),
            pltpu.VMEM((2, 4, 2, 256, 128), BF),
            pltpu.VMEM((3, 2, 2, 352, 128), BF),
            pltpu.VMEM((3, 4, 336, 128), BF),
            pltpu.VMEM((2, D), F32),
            pltpu.VMEM((4, 32, 128), F32),
            pltpu.VMEM((4, 32, 128), F32),
            pltpu.VMEM((2, 4, 32, 128), F32),
        ]
        + bufs
        + [
            pltpu.SemaphoreType.DMA((140,)),
            pltpu.SemaphoreType.DMA((140,)),
            pltpu.SemaphoreType.DMA((16,)),
        ],
        compiler_params=pltpu.CompilerParams(
            collective_id=2, has_side_effects=True, vmem_limit_bytes=VMEM_BYTES
        ),
    )(starts, tokens, d_attn, out_part, qkv, w_out, query, keys, values, heads, lse, turned,
      tables, gains, y_one, d_y, gain_two, fold_y, fold_z)


def kernel_settle(result_in, tokens_in, qkv_in, o_in, mlp_in, gains_in,
                  result, tokens, query, key, value, out, gate, up, down, attn, feed):
    dp, tp = lax.axis_index("dp"), lax.axis_index("tensor")
    result[...] = result_in[...]
    tokens[...] = tokens_in[...]
    for index, target in enumerate((query, key, value)):
        target[...] = qkv_in[index]
    out[...] = o_in[...]
    for index, target in enumerate((gate, up, down)):
        target[...] = mlp_in[index]
    for index, target in enumerate((attn, feed)):
        row = gains_in[pl.ds(index * 16 + dp, 1), :]
        target[...] = pltpu.roll(row, lax.rem(128 - tp * 16, 128), 1)[:, 0:16]


def call_settle(*arrays):
    shape = jax.ShapeDtypeStruct
    return pl.pallas_call(
        kernel_settle,
        name="settle",
        in_specs=[in_vmem()] * 6,
        out_specs=[in_vmem()] * 11,
        out_shape=[shape((128, D), BF)] * 2
        + [shape((128, 256), F32)] * 3
        + [shape((256, 128), F32)]
        + [shape((UNITS, 128), F32)] * 3
        + [shape((1, 16), F32)] * 2,
        compiler_params=pltpu.CompilerParams(vmem_limit_bytes=VMEM_BYTES),
    )(*arrays)


def on_device(tables, tokens, starts, w_query, w_key, w_value, w_out, w_gate, w_up, w_down,
              gain_attn, gain_mlp, cotangent):
    weights = (w_query, w_key, w_value, w_out, w_gate.T, w_up.T, w_down)
    (qkv, w_o, mlp, cot, turned, query, keys, values, heads, h_two, lse, y_one, gains) = call_attend(
        tokens, cotangent, starts, weights, gain_attn.reshape(1, 16), gain_mlp.reshape(1, 16), tables
    )
    out_part, d_attn, fold_y, fold_z, d_y, gain_two = call_feed(h_two, cot, mlp, y_one, gains)
    sums = call_back(
        starts, tokens, d_attn, out_part, qkv, w_o, query, keys, values, heads, lse, turned,
        tables, gains, y_one, d_y, gain_two, fold_y, fold_z,
    )
    result, grad_tokens, query, key, value, out, gate, up, down, attn, feed = call_settle(*sums)
    return (
        result, grad_tokens, query, key, value, out, gate.T, up.T, down,
        attn.reshape(16), feed.reshape(16),
    )


def solution(mesh):
    both = ("dp", "tensor")
    rows, wide, tall = P(both, None), P("dp", "tensor"), P("tensor", "dp")
    in_specs = (
        rows, P("dp"), wide, wide, wide, tall, wide, wide, tall, P(both), P(both), rows,
    )
    out_specs = (
        rows, rows, wide, wide, wide, tall, wide, wide, tall, P(both), P(both),
    )
    return jax.shard_map(
        functools.partial(on_device, rope_tables()), mesh=mesh, in_specs=in_specs,
        out_specs=out_specs, check_vma=False,
    )
```

```python
import functools
import math
import types

import jax
import jax.numpy as jnp
import numpy as np
from jax import lax
from jax.experimental import pallas as pl
from jax.experimental.pallas import tpu as pltpu
from jax.sharding import PartitionSpec as P

HD = 128
PIECE = 256
EPS = 1e-05
NEG = -1e30
SCALE = HD ** (-0.5)
D = 2048
SEQ = 1024
UNITS = 688
BF = jnp.bfloat16
F32 = jnp.float32
MESH = pl.DeviceIdType.MESH
VMEM_BYTES = 60 * 1024 * 1024
ALL = slice(None)


def dot_nn(left, right):
    return jnp.dot(left, right, preferred_element_type=F32)


def dot_nt(left, right):
    return lax.dot_general(left, right, (((1,), (1,)), ((), ())), preferred_element_type=F32)


def dot_tn(left, right):
    return lax.dot_general(left, right, (((0,), (0,)), ((), ())), preferred_element_type=F32)


def rem4(value):
    return lax.rem(value, 4)


def place():
    dp = lax.axis_index("dp")
    tp = lax.axis_index("tensor")
    zh = lax.rem(lax.div(dp, 2), 2)
    zl = lax.rem(tp, 2)
    return types.SimpleNamespace(
        y=lax.div(dp, 4), zh=zh, zl=zl, z=zh * 2 + zl, x=lax.div(tp, 2), core=lax.rem(dp, 2)
    )


def device(me, **moved):
    at = types.SimpleNamespace(**{**vars(me), **moved})
    zh, zl = lax.div(at.z, 2), lax.rem(at.z, 2)
    return (at.y * 4 + zh * 2 + at.core, at.x * 2 + zl)


def near(me, axis, step):
    return device(me, **{axis: rem4(getattr(me, axis) + step)})


def sibling(me):
    return device(me, core=1 - me.core)


def partner(me):
    return device(me, z=me.zh * 2 + 1 - me.zl)


def across(me):
    return device(me, z=rem4(me.z + 3 + 2 * me.zl))


def greet(me, wide, meanwhile=()):
    others = [near(me, axis, step) for axis in ("x", "y", "z") for step in (1, 3)] + [sibling(me)]
    if wide:
        others += [near(me, axis, 2) for axis in ("x", "y", "z")]
        others += [crossed(me, step) for step in (1, 2, 3)]
    barrier = pltpu.get_barrier_semaphore()
    for other in others:
        pl.semaphore_signal(barrier, inc=1, device_id=other, device_id_type=MESH)
    for copy in meanwhile:
        copy.wait()
    pl.semaphore_wait(barrier, len(others))


def crossed(me, step):
    return device(me, y=rem4(me.y + step), core=1 - me.core)


class Plan:
    def __init__(self):
        self.steps = {}

    def add(self, name, run, waits=tuple, after=(), rank=5):
        self.steps[name] = types.SimpleNamespace(run=run, waits=waits, after=after, rank=rank)

    def go(self, order):
        assert sorted(order) == sorted(self.steps)
        for name in order:
            step = self.steps[name]
            for copy in step.waits():
                copy.wait_recv()
            step.run()


class Once:
    def __init__(self, copy, remote):
        self.copy, self.remote = copy, remote
        self.received = self.left = False

    def wait_recv(self):
        if not self.received:
            self.received = True
            if self.remote:
                self.copy.wait_recv()
            else:
                self.copy.wait()

    wait = wait_recv

    def wait_send(self):
        if not self.left:
            self.left = True
            self.copy.wait_send()


class Wire:
    def __init__(self, send, recv, local):
        self.send, self.recv, self.local = send, recv, local
        self.used, self.used_local = 0, 0
        self.sent = []

    def put(self, source, target, to):
        index = self.used
        self.used += 1
        assert index < self.send.shape[0]
        copy = pltpu.make_async_remote_copy(
            src_ref=source,
            dst_ref=target,
            send_sem=self.send.at[index],
            recv_sem=self.recv.at[index],
            device_id=to,
            device_id_type=MESH,
        )
        copy.start()
        copy = Once(copy, True)
        self.sent.append(copy)
        return copy

    def move(self, source, target):
        index = self.used_local
        self.used_local += 1
        assert index < self.local.shape[0]
        copy = pltpu.make_async_copy(source, target, self.local.at[index])
        copy.start()
        return Once(copy, False)

    def drain(self):
        for copy in self.sent:
            copy.wait_send()
        self.sent = []


class Ring:
    def __init__(self, wire, me, axis, view):
        self.wire, self.view = wire, view
        self.at = getattr(me, axis)
        self.right, self.left = near(me, axis, 1), near(me, axis, 3)

    def put(self, slot, part, to):
        piece = self.view(slot, part)
        return self.wire.put(piece, piece, to)

    def start(self):
        self.right_one = self.put(self.at, 0, self.right)
        self.left_one = self.put(self.at, 1, self.left)
        self.right_two = self.put(self.at, 1, self.right)
        self.left_two = self.put(self.at, 0, self.left)

    def plan(self, plan, name, after, rank):
        plan.add(name + ".go", self.start, after=after, rank=rank)
        plan.add(name + ".r", self.relay_right, lambda: [self.right_one], (name + ".go",), rank)
        plan.add(name + ".l", self.relay_left, lambda: [self.left_one], (name + ".go",), rank)
        plan.add(
            name + ".near", lambda: None, lambda: [self.right_two, self.left_two],
            (name + ".r", name + ".l"), rank,
        )
        plan.add(
            name + ".far", lambda: None, lambda: [self.far_right, self.far_left], (name + ".near",), rank
        )

    def relay_right(self):
        self.far_right = self.put(rem4(self.at + 3), 0, self.right)

    def relay_left(self):
        self.far_left = self.put(rem4(self.at + 1), 1, self.left)

    def closed(self):
        return rem4(self.at + 3), rem4(self.at + 1)


class PairRing:
    def __init__(self, wire, me, view):
        self.wire, self.view, self.me = wire, view, me
        self.at = me.z
        self.mate, self.beyond = me.zh * 2 + 1 - me.zl, rem4(me.z + 3 + 2 * me.zl)

    def put(self, slot, to):
        piece = self.view(slot, None)
        return self.wire.put(piece, piece, to)

    def start(self):
        self.to_mate = self.put(self.at, partner(self.me))
        self.to_beyond = self.put(self.at, across(self.me))

    def plan(self, plan, name, after, rank):
        plan.add(name + ".go", self.start, after=after, rank=rank)
        plan.add(name + ".r", self.relay, lambda: [self.to_mate], (name + ".go",), rank)
        plan.add(name + ".near", lambda: None, lambda: [self.to_beyond], (name + ".r",), rank)
        plan.add(name + ".far", lambda: None, lambda: [self.far], (name + ".near",), rank)

    def relay(self):
        self.far = self.put(self.mate, across(self.me))

    def closed(self):
        return self.mate, self.beyond


class Meet:
    def __init__(self, wire, me, axis, ref):
        piece = ref.at[getattr(me, axis)]
        self.copies = [wire.put(piece, piece, near(me, axis, step)) for step in (1, 2, 3)]


class MeetCores:
    def __init__(self, wire, me, ref):
        piece = ref.at[me.core, me.y]
        others = [near(me, "y", step) for step in (1, 2, 3)] + [sibling(me)]
        others += [crossed(me, step) for step in (1, 2, 3)]
        self.copies = [wire.put(piece, piece, other) for other in others]


class RingSum:
    def __init__(self, wire, me, axis, part, from_left, from_right, whole_left, whole_right, split, add):
        self.wire, self.part, self.split, self.add = wire, part, split, add
        self.at = getattr(me, axis)
        self.right, self.left = near(me, axis, 1), near(me, axis, 3)
        self.near_bufs = (from_left, from_right)
        self.whole = (whole_left, whole_right)

    def start_near(self, half):
        piece = self.part(rem4(self.at + 2), half)
        to = self.left if half else self.right
        copy = self.wire.put(piece, self.near_bufs[half], to)
        if half:
            self.second = copy
        else:
            self.first = copy

    def start_whole(self, half):
        if half:
            self.right_whole = self.wire.put(
                self.part(rem4(self.at + 1), 1), self.split(self.whole[0], 1), self.right
            )
        else:
            self.left_whole = self.wire.put(
                self.part(rem4(self.at + 3), 0), self.split(self.whole[1], 0), self.left
            )

    def start(self, halves=(0, 1)):
        for half in halves:
            self.start_near(half)
        if 1 in halves:
            self.start_whole(1)
            self.start_whole(0)

    def plan(self, plan, name, after, rank, go=True):
        if go:
            plan.add(name + ".go", self.start, after=after, rank=rank)
        plan.add(name + ".r", self.relay_right, lambda: [self.first], (name + ".go",), rank)
        plan.add(name + ".l", self.relay_left, lambda: [self.second], (name + ".go",), rank)
        plan.add(
            name + ".far",
            lambda: None,
            lambda: [self.left_whole, self.right_whole, self.to_right, self.to_left],
            (name + ".r", name + ".l"),
            rank,
        )

    def relay_right(self):
        after = rem4(self.at + 1)
        self.add(self.part(after, 0), self.near_bufs[0])
        self.to_right = self.wire.put(self.part(after, 0), self.split(self.whole[0], 0), self.right)

    def relay_left(self):
        before = rem4(self.at + 3)
        self.add(self.part(before, 1), self.near_bufs[1])
        self.to_left = self.wire.put(self.part(before, 1), self.split(self.whole[1], 1), self.left)


class PairSum:
    def __init__(self, wire, me, part, from_beyond, for_mate, from_mate, add):
        self.wire, self.me, self.part, self.add = wire, me, part, add
        self.at = me.z
        self.mate, self.beyond = me.zh * 2 + 1 - me.zl, rem4(me.z + 3 + 2 * me.zl)
        self.for_mate, self.whole = for_mate, (from_beyond, from_mate)

    def start(self):
        far = rem4(self.at + 2)
        self.first = self.wire.put(self.part(far, None), self.for_mate, across(self.me))
        self.second = self.wire.put(self.part(self.beyond, None), self.whole[0], across(self.me))

    def plan(self, plan, name, after, rank):
        plan.add(name + ".go", self.start, after=after, rank=rank)
        plan.add(name + ".r", self.relay, lambda: [self.first], (name + ".go",), rank)
        plan.add(
            name + ".far", lambda: None, lambda: [self.second, self.to_mate], (name + ".r",), rank
        )

    def relay(self):
        self.add(self.part(self.mate, None), self.for_mate)
        self.to_mate = self.wire.put(self.part(self.mate, None), self.whole[1], partner(self.me))


def split_columns(ref, half):
    return ref.at[:, pl.ds(half * (D // 2), D // 2)]


def split_rows(cut):
    def split(ref, half):
        rows = ref.shape[-2]
        span = pl.ds(0, cut) if half == 0 else pl.ds(cut, rows - cut)
        return ref.at[(ALL,) * (len(ref.shape) - 2) + (span, ALL)]

    return split


class Spread:
    def __init__(self, wire, me, ref, lead, row, rows, first, cut, cuts=(ALL,)):
        self.wire, self.me = wire, me
        head = (ALL,) * lead

        def view(y, z, part, low=ALL):
            zl, zh = (low, ALL) if z is None else (lax.rem(z, 2), lax.div(z, 2))
            start, size = row, rows
            if part == 0:
                size = cut
            if part == 1:
                start, size = row + cut, rows - cut
            yy = ALL if y is None else y
            return ref.at[head + (zl, yy, zh, me.core, pl.ds(start, size), ALL)]

        if first == "y":
            self.one = Ring(wire, me, "y", lambda slot, part: view(slot, me.z, part))
            self.twos = [PairRing(wire, me, lambda slot, part: view(None, slot, part))]
        else:
            self.one = PairRing(wire, me, lambda slot, part: view(me.y, slot, part))
            self.twos = [
                Ring(wire, me, "y", lambda slot, part, low=low: view(slot, None, part, low))
                for low in cuts
            ]

    def plan(self, plan, name, after, turn_after, rank):
        self.one.plan(plan, name + ".a", after, rank)
        done = [name + ".a.far", *turn_after]
        for index, two in enumerate(self.twos):
            tail = str(index) if len(self.twos) > 1 else ""
            self.plan_two(plan, two, name, tail, tuple(done), rank + 0.01 * index)
            done += [name + ".b" + tail + ".r", name + ".b" + tail + ".l"] if tail else []

    def plan_two(self, plan, two, name, tail, after, rank):
        shared = []

        def share(slots):
            for slot in slots:
                piece = two.view(slot, None)
                shared.append(self.wire.put(piece, piece, sibling(self.me)))

        def go():
            two.start()
            share([two.at])

        step = name + ".b" + tail
        two.plan(plan, step, after, rank)
        plan.steps[step + ".go"].run = go
        plan.add(name + ".s" + tail, lambda: share(two.closed()), after=(step + ".near",), rank=rank)
        plan.add(
            name + ".t" + tail, lambda: share([rem4(two.at + 2)]),
            after=(name + ".s" + tail, step + ".far"), rank=rank,
        )
        plan.add(name + ".all" + tail, lambda: None, lambda: shared, (name + ".t" + tail,), rank)
MLP_Y, MLP_CUT, MLP_REST = 368, 192, 160
MZ_AFTER, MZ_TURN = ("tz", "qz.a.r"), ("oz.b.l", "oz.b.r")
MY_AFTER, MY_TURN = ("qz.a.go",), ("oy.b.r", "mz.a.r")
ORDER_ATTEND = (
    "gx", "tx.go", "qz.a.go", "my.a.go", "bias", "gz", "tz", "my.a.l", "my.a.r", "gy", "qz.a.r",
    "oz.a.go", "oy.a.go", "qz.a.near", "mz.a.go", "tx.r", "tx.l", "my.a.near", "my.a.far",
    "gains", "n0", "oy.a.l", "oy.a.r", "oy.a.near", "qz.a.far", "qz.b0.go", "tx.near", "n1",
    "oy.a.far", "oy.b.go", "to", "cx.go", "n3", "oz.a.r", "oz.a.near", "tx.far", "tf", "n2",
    "qz.b0.r", "qz.b0.l", "qz.b1.go", "oz.a.far", "qz.b0.near", "qz.s0", "mz.a.r", "mz.a.near",
    "oy.b.r", "oy.b.near", "oy.s", "my.b.go", "qz.b0.far", "qz.t0", "qz.all0", "proj0", "qz.b1.r",
    "qz.b1.l", "oz.b.go", "mz.a.far", "n4", "oy.b.far", "oy.t", "oy.all", "qz.b1.near", "qz.s1",
    "cx.r", "cx.l", "n5", "rest0", "att0", "oz.b.r", "oz.b.l", "qz.b1.far", "qz.t1", "mz.b.go",
    "cx.near", "oz.b.near", "oz.s", "qz.all1", "proj1", "oz.b.far", "oz.t", "rest1", "att2",
    "oz.all", "cx.far", "ck", "po", "ys.go", "flip", "flip2", "mz.b.r", "mz.b.l", "ys.r", "flip3",
    "my.b.r", "my.b.near", "my.s", "ys.l", "mz.b.near", "mz.s", "ys.far", "fin", "hx.go",
    "mz.b.far", "mz.t", "mz0", "mz.all", "mz1", "hx.r", "hx.l", "hx.near", "my.b.far", "my.t",
    "my0", "my.all", "my1", "hx.far", "hk",
)


def norm_rows(source, target, gain, rows, step=32):
    def body(index, carry):
        span = pl.ds(pl.multiple_of(index * step, step), step)
        value = source[span, :].astype(F32)
        scale = lax.rsqrt(jnp.mean(value * value, axis=-1, keepdims=True) + EPS)
        target[span, :] = (value * scale * gain).astype(BF)
        return carry

    lax.fori_loop(0, rows // step, body, 0)


def fill_bias(bias, me, start):
    row = lax.broadcasted_iota(jnp.int32, (128, 512), 0)
    column = lax.broadcasted_iota(jnp.int32, (128, 512), 1)
    query = lax.div(column, 128) * 256 + me.zl * 128 + lax.rem(column, 128)
    query_in = (query >= start) & (query < start + PIECE)

    def body(block, carry):
        pair, other = lax.div(block, 2), lax.rem(block, 2)
        parity = me.zl + other * (1 - 2 * me.zl)
        key = (pair * 2 + parity) * 128 + row
        key_in = (key >= start) & (key < start + PIECE)
        allowed = (key <= query) | (query_in & key_in)
        bias[pl.ds(pl.multiple_of(block * 128, 128), 128), :] = jnp.where(allowed, 0.0, NEG)
        return carry

    lax.fori_loop(0, 8, body, 0)


def turn(field, cosine, sine):
    return field * cosine + pltpu.roll(field, HD // 2, 1) * sine


def add_into(target, terms, result=None):
    shape = target.shape
    lead, rows, columns = shape[:-2], shape[-2], shape[-1]
    step = rows
    while step * columns > 33000:
        step = next(s for s in range(step - 16, 0, -16) if rows % s == 0)
    cuts = rows // step
    result = target if result is None else result

    def body(index, carry):
        where, rest = [], lax.div(index, cuts)
        for extent in reversed(lead):
            where.insert(0, lax.rem(rest, extent))
            rest = lax.div(rest, extent)
        where = tuple(where) + (
            pl.ds(pl.multiple_of(lax.rem(index, cuts) * step, 16), step), ALL
        )
        total = target[where].astype(F32)
        for term in terms:
            total = total + term[where].astype(F32)
        result[where] = total.astype(result.dtype)
        return carry

    lax.fori_loop(0, math.prod(lead) * cuts, body, 0)


def columns_of(ref):
    def view(slot, half):
        if half is None:
            return ref.at[slot]
        return ref.at[slot, :, pl.ds(half * (D // 2), D // 2)]

    return view


def rows_of(ref):
    def view(slot, half):
        return ref.at[slot] if half is None else ref.at[slot, pl.ds(half * 64, 64)]

    return view


def kernel_attend(
    tokens_in, cotangent_in, start_in, query_w, key_w, value_w, out_w, gate_w, up_w, down_w,
    gain_one_in, gain_two_in, tables_in,
    qkv_out, wo_out, mlp_out, cot_out, turned_out, query_out, keys_out, values_out, heads_out,
    h_out, lse_out, y_out, gains_out,
    tok, h_one, w_qkv, w_o, w_mlp, tables, bias, query, keys, values, heads, cot, h_two,
    part, near_left, near_right, whole_left, whole_right,
    turned, gain_x, gain_z, gain_c,
    send, recv, local,
):
    me = place()
    wire = Wire(send, recv, local)
    own = [wire.move(tokens_in, tok.at[me.x, 0])]
    for index, ref in enumerate((query_w, key_w, value_w)):
        own.append(wire.move(ref, w_qkv.at[index, me.zl, me.y, me.zh, me.core]))
    own.append(wire.move(out_w, w_o.at[me.zl, me.y, me.zh, me.core]))
    for index, ref in enumerate((gate_w, up_w, down_w)):
        own.append(wire.move(ref, w_mlp.at[index, me.zl, me.y, me.zh, me.core]))
    own.append(wire.move(tables_in.at[me.zl], tables))
    own.append(wire.move(cotangent_in, cot.at[me.x]))
    lane = lax.div(lax.broadcasted_iota(jnp.int32, (1, 128), 1), 16)
    tensor = me.x * 2 + me.zl
    gain_x[me.x] = jnp.concatenate(
        [
            jnp.where(lane == tensor, jnp.concatenate([ref[...]] * 8, axis=1), 0.0)
            for ref in (gain_one_in, gain_two_in)
        ]
        + [jnp.zeros((6, 128), F32)],
        axis=0,
    )
    greet(me, True, own)
    plan = Plan()
    at = types.SimpleNamespace()
    one, far, three = rem4(me.x + 1), rem4(me.x + 2), rem4(me.x + 3)
    kept = []

    def keep(source, target):
        kept.append(wire.move(source, target))

    def gains_x():
        at.gains = Meet(wire, me, "x", gain_x).copies

    def gains_z():
        gain_z[me.z] = gain_x[0] + gain_x[1] + gain_x[2] + gain_x[3]
        at.gains = Meet(wire, me, "z", gain_z).copies

    def gains_y():
        gain_c[me.core, me.y, 0] = gain_z[0] + gain_z[1]
        gain_c[me.core, me.y, 1] = gain_z[2] + gain_z[3]
        at.gains = MeetCores(wire, me, gain_c).copies

    def gains_all():
        for y in range(4):
            for zh in range(2):
                for core in range(2):
                    column = (y * 4 + zh * 2 + core) * 128
                    gains_out[:, column : column + 128] = gain_c[core, y, zh]

    plan.add("gx", gains_x, rank=0)
    plan.add("gz", gains_z, lambda: at.gains, ("gx",), 0)
    plan.add("gy", gains_y, lambda: at.gains, ("gz",), 0)
    plan.add("gains", gains_all, lambda: at.gains, ("gy",), 1)

    def tokens_z():
        at.rows_z = wire.put(tok.at[me.x, 0], tok.at[me.x, 1], partner(me))

    def tokens_on():
        at.on = [
            wire.put(tok.at[me.x, 1], tok.at[me.x, 1], near(me, "x", step)) for step in (1, 3)
        ]

    def tokens_far():
        at.far_z = wire.put(tok.at[far, 0], tok.at[far, 1], partner(me))

    Ring(
        wire, me, "x",
        lambda slot, half: tok.at[slot, 0] if half is None else tok.at[slot, 0, pl.ds(half * 64, 64)],
    ).plan(plan, "tx", ("gx",), 0)
    plan.add("tz", tokens_z, after=("qz.a.go", "gz"), rank=0)
    plan.add("to", tokens_on, lambda: [at.rows_z], ("tz", "tx.r", "tx.l"), 0)
    plan.add("tf", tokens_far, after=("tx.far",), rank=0)

    def norm(*blocks):
        def run():
            for slot, p in blocks:
                norm_rows(tok.at[slot, p], h_one.at[slot, p], gains_out[0:1, :], 128)

        return run

    plan.add("n0", norm((me.x, 0)), after=("gains",), rank=2)
    plan.add("n1", norm((one, 0), (three, 0)), after=("gains", "tx.near"), rank=2)
    plan.add("n2", norm((far, 0)), after=("gains", "tx.far"), rank=2)
    plan.add("n3", norm((me.x, 1)), after=("gains", "to"), rank=3)
    plan.add("n4", norm((one, 1), (three, 1)), lambda: at.on, ("gains", "to"), 3)
    plan.add("n5", norm((far, 1)), lambda: [at.far_z], ("gains", "tf"), 2)

    Spread(wire, me, w_qkv, 1, 0, 128, "z", 64, (0, 1)).plan(plan, "qz", ("tx.go",), (), 1)
    Spread(wire, me, w_o, 0, 96, 160, "z", 80).plan(plan, "oz", ("tz", "qz.a.r"), ("qz.b1.l", "qz.b1.r"), 1)
    Spread(wire, me, w_o, 0, 0, 96, "y", 48).plan(plan, "oy", ("tz", "qz.a.r"), (), 1)
    mlp_z = Spread(wire, me, w_mlp, 1, MLP_Y, UNITS - MLP_Y, "z", MLP_REST)
    mlp_y = Spread(wire, me, w_mlp, 1, 0, MLP_Y, "y", MLP_CUT)
    mlp_z.plan(plan, "mz", MZ_AFTER, MZ_TURN, 1.5)
    mlp_y.plan(plan, "my", MY_AFTER, MY_TURN, 1.5)
    plan.add("bias", lambda: fill_bias(bias, me, start_in[0]), rank=6)

    def project(zl, carry):
        rows = h_one[:, 0].reshape(512, D)
        cosine, sine = tables[0, :, 0].reshape(512, HD), tables[1, :, 0].reshape(512, HD)
        raw = dot_nn(rows, w_qkv[0, zl].reshape(D, 256))
        for j in range(2):
            query[zl * 2 + j] = turn(raw[:, j * HD : (j + 1) * HD], cosine, sine).astype(BF)
        raw = dot_nn(rows, w_qkv[1, zl].reshape(D, 256))
        for j in range(2):
            keys[zl * 2 + j, :, 0] = (
                turn(raw[:, j * HD : (j + 1) * HD], cosine, sine).astype(BF).reshape(4, 128, HD)
            )
        raw = dot_nn(rows, w_qkv[2, zl].reshape(D, 256))
        for j in range(2):
            values[zl * 2 + j, :, 0] = raw[:, j * HD : (j + 1) * HD].astype(BF).reshape(4, 128, HD)
        return carry

    def project_other(zl, carry):
        rows = h_one[:, 1].reshape(512, D)
        cosine, sine = tables[0, :, 1].reshape(512, HD), tables[1, :, 1].reshape(512, HD)
        raw = dot_nn(rows, w_qkv[1, zl].reshape(D, 256))
        for j in range(2):
            keys[zl * 2 + j, :, 1] = (
                turn(raw[:, j * HD : (j + 1) * HD], cosine, sine).astype(BF).reshape(4, 128, HD)
            )
        raw = dot_nn(rows, w_qkv[2, zl].reshape(D, 256))
        for j in range(2):
            values[zl * 2 + j, :, 1] = raw[:, j * HD : (j + 1) * HD].astype(BF).reshape(4, 128, HD)
        return carry

    def project_half(zl):
        def run():
            lax.fori_loop(zl, zl + 1, project, 0)
            if zl == 1:
                keep(w_qkv, qkv_out)
                keep(query, query_out)

        return run

    def other_half(zl):
        def run():
            lax.fori_loop(zl, zl + 1, project_other, 0)
            if zl == 1:
                keep(keys, keys_out)
                keep(values, values_out)

        return run

    plan.add("proj0", project_half(0), after=("n0", "n1", "n2", "qz.all0"), rank=2)
    plan.add("rest0", other_half(0), after=("n3", "n4", "n5", "proj0"), rank=2)
    plan.add("proj1", project_half(1), after=("n0", "n1", "n2", "qz.all1"), rank=2.1)
    plan.add("rest1", other_half(1), after=("n3", "n4", "n5", "proj1"), rank=2.1)

    def attend(head, carry):
        for half, pairs in ((0, 3), (1, 4)):
            span = pairs * 256
            rows = slice(half * 256, half * 256 + 256)
            scores = dot_nt(keys[head, 0:pairs].reshape(span, HD), query[head, rows, :]) * SCALE
            scores = scores + bias[0:span, rows]
            top = jnp.max(scores, axis=0, keepdims=True)
            expo = jnp.exp(scores - top)
            total = jnp.sum(expo, axis=0, keepdims=True)
            probs = (expo * (1.0 / total)).astype(BF)
            result = dot_tn(values[head, 0:pairs].reshape(span, HD), probs)
            heads[rows, pl.ds(pl.multiple_of(head * HD, HD), HD)] = result.T.astype(BF)
            lse_out[head, :, rows] = top + jnp.log(total)
        return carry

    def attend_rest():
        lax.fori_loop(2, 4, attend, 0)
        keep(heads, heads_out)

    plan.add("att0", lambda: lax.fori_loop(0, 2, attend, 0), after=("rest0", "bias"), rank=2)
    plan.add("att2", attend_rest, after=("rest1", "bias"), rank=2.1)

    def project_out(block, carry):
        y, zh = lax.div(block, 2), lax.rem(block, 2)
        weight = jnp.concatenate(
            [
                jnp.concatenate([w_o[zl, y, zh, 0], w_o[zl, y, zh, 1]], axis=1)
                for zl in range(2)
            ],
            axis=0,
        )
        result = dot_nn(heads[...], weight).astype(BF).reshape(4, 128, 256)
        part[:, :, pl.ds(pl.multiple_of(block * 256, 256), 256)] = result
        return carry

    total = RingSum(
        wire, me, "x", columns_of(part), near_left, near_right, whole_left, whole_right,
        split_columns, lambda target, term: add_into(target, [term]),
    )

    def out_one():
        keep(w_o, wo_out)
        lax.fori_loop(0, 4, project_out, 0)
        total.start((0,))

    def out_two():
        lax.fori_loop(4, 8, project_out, 0)
        total.start((1,))

    plan.add("po", out_one, after=("att0", "att2", "oz.all", "oy.all"), rank=2)
    plan.add("ys.go", out_two, after=("po",), rank=2)
    total.plan(plan, "ys", (), 1, go=False)

    def finish(index, carry):
        span = pl.ds(pl.multiple_of(index * 32, 32), 32)
        value = tok[me.x, 0, span, :].astype(F32) + (
            part[me.x, span, :].astype(F32)
            + whole_left[span, :].astype(F32)
            + whole_right[span, :].astype(F32)
        )
        scale = lax.rsqrt(jnp.mean(value * value, axis=-1, keepdims=True) + EPS)
        y_out[span, :] = value
        h_two[me.x, span, :] = (value * scale * gains_out[1:2, :]).astype(BF)
        return carry

    plan.add("fin", lambda: lax.fori_loop(0, 4, finish, 0), after=("ys.far",), rank=0)
    Ring(wire, me, "x", rows_of(h_two)).plan(plan, "hx", ("fin",), 0)
    plan.add("hk", lambda: keep(h_two, h_out), after=("hx.far",), rank=0)
    Ring(wire, me, "x", rows_of(cot)).plan(plan, "cx", ("to",), 1.6)
    plan.add("ck", lambda: keep(cot, cot_out), after=("cx.far",), rank=1.8)

    def flip(block, carry):
        column = pl.ds(pl.multiple_of(block * 128, 128), 128)
        rows = h_one[:, :, :, column].reshape(SEQ, 128)
        turned[lax.rem(block, 2), lax.div(block, 2)] = rows.T
        return carry

    def flip_rest():
        lax.fori_loop(8, 16, flip, 0)
        keep(turned.at[me.core], turned_out.at[0])
        at.turned = wire.put(turned.at[1 - me.core], turned_out.at[1], sibling(me))

    plan.add("flip", lambda: lax.fori_loop(0, 8, flip, 0), after=("rest1", "ys.go"), rank=7)
    plan.add("flip2", flip_rest, after=("flip",), rank=7)
    plan.add("flip3", lambda: None, lambda: [at.turned], ("flip2",), 9)

    def keep_mlp(mine, start, size):
        def run():
            core = me.core if mine else 1 - me.core
            piece = (ALL, ALL, ALL, ALL, core, pl.ds(start, size), ALL)
            keep(w_mlp.at[piece], mlp_out.at[piece])

        return run

    plan.add("my0", keep_mlp(True, 0, MLP_Y), after=("my.t",), rank=1.8)
    plan.add("my1", keep_mlp(False, 0, MLP_Y), after=("my.all",), rank=1.8)
    plan.add("mz0", keep_mlp(True, MLP_Y, UNITS - MLP_Y), after=("mz.t",), rank=1.8)
    plan.add("mz1", keep_mlp(False, MLP_Y, UNITS - MLP_Y), after=("mz.all",), rank=1.8)

    plan.go(ORDER_ATTEND)
    for copy in kept:
        copy.wait()
    wire.drain()


def anywhere():
    return pl.BlockSpec(memory_space=pl.ANY)


def in_vmem():
    return pl.BlockSpec(memory_space=pltpu.VMEM)


def call_attend(tokens, cotangent, starts, weights, gain_attn, gain_mlp, tables):
    shape = jax.ShapeDtypeStruct
    hbm = [
        shape((3, 2, 4, 2, 2, 128, 256), BF),
        shape((2, 4, 2, 2, 256, 128), BF),
        shape((3, 2, 4, 2, 2, UNITS, 128), BF),
        shape((4, 128, D), BF),
        shape((2, 8, 128, SEQ), BF),
        shape((4, 512, HD), BF),
        shape((4, 4, 2, 128, HD), BF),
        shape((4, 4, 2, 128, HD), BF),
        shape((512, 512), BF),
        shape((4, 128, D), BF),
    ]
    vmem = [shape((4, 1, 512), F32), shape((128, D), F32), shape((8, D), F32)]
    return pl.pallas_call(
        kernel_attend,
        name="attend",
        in_specs=[anywhere(), anywhere(), pl.BlockSpec(memory_space=pltpu.SMEM)]
        + [anywhere()] * 7
        + [in_vmem()] * 2
        + [anywhere()],
        out_specs=[anywhere()] * len(hbm) + [in_vmem()] * len(vmem),
        out_shape=hbm + vmem,
        scratch_shapes=[
            pltpu.VMEM((4, 2, 128, D), BF),
            pltpu.VMEM((4, 2, 128, D), BF),
            pltpu.VMEM((3, 2, 4, 2, 2, 128, 256), BF),
            pltpu.VMEM((2, 4, 2, 2, 256, 128), BF),
            pltpu.VMEM((3, 2, 4, 2, 2, UNITS, 128), BF),
            pltpu.VMEM((2, 4, 2, 128, HD), F32),
            pltpu.VMEM((SEQ, 512), F32),
            pltpu.VMEM((4, 512, HD), BF),
            pltpu.VMEM((4, 4, 2, 128, HD), BF),
            pltpu.VMEM((4, 4, 2, 128, HD), BF),
            pltpu.VMEM((512, 512), BF),
            pltpu.VMEM((4, 128, D), BF),
            pltpu.VMEM((4, 128, D), BF),
            pltpu.VMEM((4, 128, D), BF),
            pltpu.VMEM((128, D // 2), BF),
            pltpu.VMEM((128, D // 2), BF),
            pltpu.VMEM((128, D), BF),
            pltpu.VMEM((128, D), BF),
            pltpu.VMEM((2, 8, 128, SEQ), BF),
            pltpu.VMEM((4, 8, 128), F32),
            pltpu.VMEM((4, 8, 128), F32),
            pltpu.VMEM((2, 4, 2, 8, 128), F32),
            pltpu.SemaphoreType.DMA((140,)),
            pltpu.SemaphoreType.DMA((140,)),
            pltpu.SemaphoreType.DMA((24,)),
        ],
        compiler_params=pltpu.CompilerParams(
            collective_id=0, has_side_effects=True, vmem_limit_bytes=VMEM_BYTES
        ),
    )(tokens, cotangent, starts, *weights, gain_attn, gain_mlp, tables)


def rope_tables():
    half = HD // 2
    freq = np.exp(np.arange(half, dtype=np.float32) * np.float32(-2.0 * math.log(10000.0) / HD))
    order = np.array(
        [
            [[(2 * pair + (zl + other) % 2) * 128 + np.arange(128) for other in range(2)] for pair in range(4)]
            for zl in range(2)
        ]
    )
    angle = order.astype(np.float32)[..., None] * freq.astype(np.float32)
    cosine, sine = np.cos(angle.astype(np.float64)), np.sin(angle.astype(np.float64))
    both = np.stack(
        [np.concatenate([cosine, cosine], -1), np.concatenate([-sine, sine], -1)], axis=1
    )
    return both.astype(np.float32)
SUM_Y, SUM_CUT = 400, 208
ORDER_FEED = (
    "hs", "g0", "u0", "cs", "f0", "g1", "u1", "f1", "bh", "ds.go", "t0", "t1", "t2", "fd0", "fd1",
    "ds.r", "gr0a", "gr0b", "ds.l", "s0y.go", "s0z.go", "gr1a", "gr1b", "s1y.go", "s1z.go",
    "gr2a", "s0y.l", "s0y.r", "gr2b", "ds.far", "bn", "dx.go", "s0z.r", "dg", "s1y.l", "s1y.r",
    "dx.r", "dx.l", "s0z.far", "s0z.k", "s1z.r", "s0y.far", "s0y.k", "dx.near", "s1y.far",
    "s1y.k", "dx.far", "dk", "s1z.far", "s1z.k",
)


def fold_view(ref, me, lead, axis, row, rows, cut):
    head = (ALL,) * lead

    def view(slot, part):
        start, size = row, rows
        if part == 0:
            size = cut
        if part == 1:
            start, size = row + cut, rows - cut
        if axis == "y":
            where = (ALL, slot, ALL)
        else:
            where = (lax.rem(slot, 2), ALL, lax.div(slot, 2))
        return ref.at[head + where + (pl.ds(start, size), ALL)]

    return view


def kernel_feed(
    h_in, cot_in, mlp_in, y_in, gains_in,
    part_out, dattn_out, fold_y_out, fold_z_out, down_out, dy_out, gain_out,
    w_mlp, h_two, cot, gate_s, up_s, act_s, d_gate, d_up, act, flipped, flipped_far,
    h_far, cot_far, part, near_left, near_right, whole_left, whole_right, d_attn, out_part,
    *rest,
):
    bufs, (send, recv, local) = list(rest[:-3]), rest[-3:]
    bufs = [tuple(bufs[a:b]) for a, b in ((0, 4), (4, 7), (7, 11), (11, 14))]
    me = place()
    wire = Wire(send, recv, local)
    loads = [
        wire.move(h_in, h_two),
        wire.move(mlp_in.at[0], w_mlp.at[0]),
        wire.move(mlp_in.at[1], w_mlp.at[1]),
        wire.move(cot_in, cot),
        wire.move(mlp_in.at[2], w_mlp.at[2]),
    ]
    greet(me, False)
    plan = Plan()
    at = types.SimpleNamespace()
    kept = []

    def keep(source, target):
        kept.append(wire.move(source, target))

    def whole(which, zl):
        return jnp.concatenate(
            [
                w_mlp[which, zl, y, zh, core]
                for y in range(4)
                for zh in range(2)
                for core in range(2)
            ],
            axis=1,
        )

    def share(source, target):
        return [
            wire.put(
                source.at[:, :, pl.ds(pl.multiple_of((block * 2 + 1 - me.core) * 128, 128), 128)],
                target.at[block],
                sibling(me),
            )
            for block in range(8)
        ]

    def share_h():
        at.h_puts = share(h_two, h_far)

    def share_cot():
        at.cot_puts = share(cot, cot_far)

    def gate(zl):
        def run():
            gate_s[...] = dot_nt(h_two[...].reshape(512, D), whole(0, zl))

        return run

    def up(zl):
        def run():
            up_s[...] = dot_nt(h_two[...].reshape(512, D), whole(1, zl))

        return run

    def forward(zl):
        def inner(index, carry):
            span = pl.ds(pl.multiple_of(index * 32, 32), 32)
            gate, up, d_act = gate_s[span, :], up_s[span, :], act_s[span, :]
            sigma = 1.0 / (1.0 + jnp.exp(-gate))
            act[zl, span, :] = (gate * sigma * up).astype(BF)
            d_gate[zl, span, :] = (d_act * up * sigma * (1.0 + gate * (1.0 - sigma))).astype(BF)
            d_up[zl, span, :] = (d_act * gate * sigma).astype(BF)
            return carry

        def run():
            act_s[...] = dot_nt(cot[...].reshape(512, D), whole(2, zl))
            lax.fori_loop(0, 16, inner, 0)

        return run

    plan.add("hs", share_h, lambda: [loads[0]], rank=1)
    plan.add("cs", share_cot, lambda: [loads[3]], rank=5)
    plan.add("g0", gate(0), lambda: loads[:2], rank=2)
    plan.add("u0", up(0), lambda: [loads[2]], ("g0",), 2)
    plan.add("f0", forward(0), lambda: loads[3:], ("u0",), 2)
    plan.add("g1", gate(1), after=("f0",), rank=2)
    plan.add("u1", up(1), after=("f0",), rank=2)
    plan.add("f1", forward(1), after=("g1", "u1"), rank=2)

    def back_h(block, carry):
        y, zh = lax.div(block, 2), lax.rem(block, 2)
        total = None
        for which, left in ((0, d_gate), (1, d_up)):
            for zl in range(2):
                weight = jnp.concatenate(
                    [w_mlp[which, zl, y, zh, 0], w_mlp[which, zl, y, zh, 1]], axis=1
                )
                term = dot_nn(left[zl], weight)
                total = term if total is None else total + term
        part[:, :, pl.ds(pl.multiple_of(block * 256, 256), 256)] = total.astype(BF).reshape(4, 128, 256)
        return carry

    total = RingSum(
        wire, me, "x", columns_of(part), near_left, near_right, whole_left, whole_right,
        split_columns, lambda target, term: add_into(target, [term]),
    )
    def back_one():
        lax.fori_loop(0, 4, back_h, 0)
        total.start((0,))

    def back_two():
        lax.fori_loop(4, 8, back_h, 0)
        total.start((1,))

    plan.add("bh", back_one, after=("f1",), rank=2)
    plan.add("ds.go", back_two, after=("bh",), rank=2)
    total.plan(plan, "ds", (), 0, go=False)

    def add(target, term):
        add_into(target, [term])

    at.far = {}

    def turn_over(which, source):
        def run():
            for zl in range(2):
                flipped[which, zl] = source[zl].T
            at.far[which] = wire.put(flipped.at[which], flipped_far.at[which], sibling(me))

        return run

    for which, source in enumerate((d_gate, d_up, act)):
        plan.add("t%d" % which, turn_over(which, source), after=("ds.go",), rank=2 + which * 0.2)

    def forward_down(block, carry):
        y, zh = lax.div(block, 2), lax.rem(block, 2)
        result = None
        for zl in range(2):
            weight = jnp.concatenate([w_mlp[2, zl, y, zh, 0], w_mlp[2, zl, y, zh, 1]], axis=1)
            term = dot_nn(act[zl], weight)
            result = term if result is None else result + term
        out_part[:, :, pl.ds(pl.multiple_of(block * 256, 256), 256)] = result.astype(BF).reshape(4, 128, 256)
        return carry

    def down_rest():
        lax.fori_loop(4, 8, forward_down, 0)
        keep(out_part, part_out)

    plan.add("fd0", lambda: lax.fori_loop(0, 4, forward_down, 0), after=("t2",), rank=4)
    plan.add("fd1", down_rest, after=("fd0",), rank=4)

    def grad(which, rows, rows_far):
        def body(index, carry):
            zl, y = lax.div(index, 4), lax.rem(index, 4)
            mine = jnp.concatenate(
                [
                    rows[:, :, pl.ds(pl.multiple_of(((y * 2 + zh) * 2 + me.core) * 128, 128), 128)]
                    .reshape(512, 128)
                    for zh in range(2)
                ],
                axis=1,
            )
            other = jnp.concatenate(
                [rows_far[y * 2 + zh].reshape(512, 128) for zh in range(2)], axis=1
            )
            result = dot_nn(flipped[which, zl], mine) + dot_nn(flipped_far[which, zl], other)
            result = result.astype(BF)
            w_mlp[which, zl, y, 0, 0] = result[:, 0:128]
            w_mlp[which, zl, y, 1, 0] = result[:, 128:256]
            return carry

        return body

    def add(target, term):
        add_into(target, [term])

    sums = []

    def start_sums(which):
        ref = w_mlp.at[which, :, :, :, 0]
        pair = [
            RingSum(wire, me, "y", fold_view(ref, me, 0, "y", 0, SUM_Y, SUM_CUT), *bufs[2 * which],
                    split_rows(SUM_CUT), add),
            PairSum(wire, me, fold_view(ref, me, 0, "z", SUM_Y, UNITS - SUM_Y, 0),
                    *bufs[2 * which + 1], add),
        ]
        for item, out, axis in zip(pair, (fold_y_out, fold_z_out), "yz"):
            name = "s%d%s" % (which, axis)
            item.plan(plan, name, ("gr%db" % which,), 1)
            plan.add(name + ".k", close_sum(item, out.at[which]), after=(name + ".far",), rank=3)

    def close_sum(item, out):
        def run():
            mine = item.part(item.at, None)
            add_into(mine, list(item.whole))
            keep(mine, out)

        return run

    rows_of_step = ((h_two, h_far), (h_two, h_far), (cot, cot_far))
    for which in range(3):
        body = grad(which, *rows_of_step[which])

        def waits(which=which):
            return [at.far[which]] + (at.cot_puts if which == 2 else at.h_puts)

        before = ("t%d" % which, "cs", "hs") + (("fd1",) if which == 2 else ())
        plan.add("gr%da" % which, lambda body=body: lax.fori_loop(0, 4, body, 0), waits, before, 3)
        plan.add(
            "gr%db" % which, lambda body=body: lax.fori_loop(4, 8, body, 0),
            after=("gr%da" % which,), rank=3,
        )
        if which < 2:
            start_sums(which)
    plan.add("dg", lambda: keep(w_mlp.at[2, :, :, :, 0], down_out), after=("gr2b",), rank=2)

    def back_norm(index, carry):
        span = pl.ds(pl.multiple_of(index * 16, 16), 16)
        d_h = (
            part[me.x, span, :].astype(F32)
            + whole_left[span, :].astype(F32)
            + whole_right[span, :].astype(F32)
        )
        value = y_in[span, :]
        scale = lax.rsqrt(jnp.mean(value * value, axis=-1, keepdims=True) + EPS)
        normed = value * scale
        e_two = d_h * gains_in[1:2, :]
        inner = jnp.mean(e_two * normed, axis=-1, keepdims=True)
        d_y = cot[me.x, span, :].astype(F32) + scale * (e_two - normed * inner)
        dy_out[span, :] = d_y
        d_attn[me.x, span, :] = d_y.astype(BF)
        return carry + jnp.sum(d_h * normed, axis=0, keepdims=True)

    def back_all():
        gain_out[...] = lax.fori_loop(0, 8, back_norm, jnp.zeros((1, D), F32))

    plan.add("bn", back_all, after=("ds.far",), rank=0)
    Ring(wire, me, "x", rows_of(d_attn)).plan(plan, "dx", ("bn",), 0)
    plan.add("dk", lambda: keep(d_attn, dattn_out), after=("dx.far",), rank=0)
    plan.go(ORDER_FEED)
    for copy in kept:
        copy.wait()
    wire.drain()


def fold_shapes(lead, count, rows, cut, columns):
    return [
        pltpu.VMEM((*lead, *count, cut, columns), BF),
        pltpu.VMEM((*lead, *count, rows - cut, columns), BF),
        pltpu.VMEM((*lead, *count, rows, columns), BF),
        pltpu.VMEM((*lead, *count, rows, columns), BF),
    ]


def call_feed(h_two, cot, mlp, y_one, gains):
    shape = jax.ShapeDtypeStruct
    bufs = (
        fold_shapes((), (2, 2), SUM_Y, SUM_CUT, 128)
        + [pltpu.VMEM((4, UNITS - SUM_Y, 128), BF)] * 3
    ) * 2
    return pl.pallas_call(
        kernel_feed,
        name="feed",
        in_specs=[anywhere()] * 3 + [in_vmem()] * 2,
        out_specs=[anywhere()] * 5 + [in_vmem()] * 2,
        out_shape=[
            shape((4, 128, D), BF),
            shape((4, 128, D), BF),
            shape((2, 2, 2, SUM_Y, 128), BF),
            shape((2, 4, UNITS - SUM_Y, 128), BF),
            shape((2, 4, 2, UNITS, 128), BF),
            shape((128, D), F32),
            shape((1, D), F32),
        ],
        scratch_shapes=[
            pltpu.VMEM((3, 2, 4, 2, 2, UNITS, 128), BF),
            pltpu.VMEM((4, 128, D), BF),
            pltpu.VMEM((4, 128, D), BF),
            pltpu.VMEM((512, UNITS), F32),
            pltpu.VMEM((512, UNITS), F32),
            pltpu.VMEM((512, UNITS), F32),
            pltpu.VMEM((2, 512, UNITS), BF),
            pltpu.VMEM((2, 512, UNITS), BF),
            pltpu.VMEM((2, 512, UNITS), BF),
            pltpu.VMEM((3, 2, UNITS, 512), BF),
            pltpu.VMEM((3, 2, UNITS, 512), BF),
            pltpu.VMEM((8, 4, 128, 128), BF),
            pltpu.VMEM((8, 4, 128, 128), BF),
            pltpu.VMEM((4, 128, D), BF),
            pltpu.VMEM((128, D // 2), BF),
            pltpu.VMEM((128, D // 2), BF),
            pltpu.VMEM((128, D), BF),
            pltpu.VMEM((128, D), BF),
            pltpu.VMEM((4, 128, D), BF),
            pltpu.VMEM((4, 128, D), BF),
        ]
        + bufs
        + [
            pltpu.SemaphoreType.DMA((100,)),
            pltpu.SemaphoreType.DMA((100,)),
            pltpu.SemaphoreType.DMA((24,)),
        ],
        compiler_params=pltpu.CompilerParams(
            collective_id=1, has_side_effects=True, vmem_limit_bytes=VMEM_BYTES
        ),
    )(h_two, cot, mlp, y_one, gains)
BACK_GROUPS = (3, 4, 4, 3, 3, 4, 4, 3, 3, 4, 4, 3, 3, 4)
ORDER_BACK = (
    "bias", "os.go", "my.b.go", "mz.b.go", "ht", "as", "wy.a.go", "wz.a.go", "dh", "ba0",
    "mz.b.r", "mz.b.l", "my.b.r", "os.r", "os.l", "ba2", "wy.a.l", "wy.a.r", "bh0", "my.b.far",
    "mz.b.far", "my.k", "wz.a.r", "mz.k", "bh1", "os.far", "wy.a.far", "wy.b.go", "go", "dn0",
    "dl0", "oy.a.go", "oz.a.go", "gq0", "wy.b.r", "oy.a.r", "oy.a.l", "wz.a.far", "wz.b.go",
    "gq1", "qy.a.go", "qz.a.go", "wz.b.r", "wz.b.l", "oz.a.r", "oy.a.far", "oy.b.go", "dl1", "fo",
    "dn1", "ds.go", "qy.a.r", "ds.r", "qy.a.l", "wy.b.far", "wy.k", "ds.l", "qz.a.r", "wz.b.far",
    "wz.k", "oz.a.far", "oz.b.go", "qy.a.far", "qy.b.go", "oz.b.r", "oz.b.l", "ds.far", "gx",
    "oz.b.far", "oy.b.r", "oz.k", "qy.b.r", "gz", "gy", "qz.a.far", "qz.b.go", "oy.b.far", "oy.k",
    "qy.b.far", "qy.k", "gains", "qz.b.r", "qz.b.l", "qz.b.far", "qz.k",
)
DOWN_AFTER = ("my.b.go", "mz.b.go")


class Fold:
    def __init__(self, wire, me, cut, view_one, axes, bufs, view_two, bufs_two):
        def add(target, term):
            add_into(target, [term])

        self.wire, self.me, self.add, self.split = wire, me, add, split_rows(cut)
        self.one = None
        if view_one is not None:
            self.one = self.sum(axes[0], view_one, bufs)
        self.two = self.sum(axes[1], view_two, bufs_two)

    def sum(self, axis, view, bufs):
        if axis == "z":
            return PairSum(self.wire, self.me, view, *bufs, self.add)
        return RingSum(self.wire, self.me, "y", view, *bufs, self.split, self.add)

    def turn(self):
        add_into(self.one.part(self.one.at, None), list(self.one.whole))
        self.two.start()

    def close(self, result):
        add_into(self.two.part(self.two.at, None), list(self.two.whole), result)

    def plan(self, plan, name, waits, after, rank, result):
        if self.one is None:
            self.two.plan(plan, name + ".b", after, rank)
            plan.steps[name + ".b.go"].waits = waits
        else:
            self.one.plan(plan, name + ".a", after, rank)
            plan.steps[name + ".a.go"].waits = waits
            self.two.plan(plan, name + ".b", (name + ".a.far",), rank)
            plan.steps[name + ".b.go"].run = self.turn
        plan.add(name + ".k", lambda: self.close(result), after=(name + ".b.far",), rank=rank + 0.5)


def crossed_view(ref, me, lead, axis, row, rows, cut):
    head = (ALL,) * lead

    def view(slot, part):
        start, size = row, rows
        if part == 0:
            size = cut
        if part == 1:
            start, size = row + cut, rows - cut
        if axis == "z":
            where = (lax.rem(slot, 2), me.y, lax.div(slot, 2))
        else:
            where = (me.zl, slot, me.zh)
        return ref.at[head + where + (pl.ds(start, size), ALL)]

    return view


def held_view(ref, lead, axis, rows, cut):
    head = (ALL,) * lead

    def view(slot, part):
        start, size = 0, rows
        if part == 0:
            size = cut
        if part == 1:
            start, size = cut, rows - cut
        where = (lax.rem(slot, 2), lax.div(slot, 2)) if axis == "z" else (slot,)
        return ref.at[head + where + (pl.ds(start, size), ALL)]

    return view


def kernel_back(
    start_in, tokens_in, dattn_in, part_in, qkv_in, wo_in, query_in, keys_in, values_in, heads_in,
    lse_in, turned_in, tables_in, gains_in, y_in, dy_in, gain_in, fold_y_in, fold_z_in, down_in,
    result_out, tokens_out, g_qkv_out, g_o_out, g_mlp_out, gains_out,
    w_qkv, w_o, d_attn, out_part, tables, bias, tok, turned, d_heads, d_query, d_keys, d_values,
    d_query_far, d_keys_far, d_values_far, sum_keys, sum_values, heads_t, heads_t_far, attn_far,
    d_h, far_one, side_left, side_right, last_z,
    near_left, near_right, whole_left, whole_right,
    out_near_left, out_near_right, out_whole_left, out_whole_right,
    fold_y, fold_z, g_down, gain_t, gain_x, gain_z, gain_c,
    *rest,
):
    bufs, (send, recv, local) = list(rest[:-3]), rest[-3:]
    groups = []
    for size in BACK_GROUPS:
        groups.append(tuple(bufs[:size]))
        bufs = bufs[size:]
    me = place()
    wire = Wire(send, recv, local)
    loads = {
        name: wire.move(source, target)
        for name, source, target in (
            ("attn", dattn_in, d_attn),
            ("o", wo_in, w_o),
            ("part", part_in, out_part),
            ("tables", tables_in.at[me.zl], tables),
            ("fold_y", fold_y_in, fold_y),
            ("fold_z", fold_z_in, fold_z),
            ("down", down_in, g_down),
            ("qkv", qkv_in, w_qkv),
            ("tok", tokens_in, tok),
            ("turned", turned_in, turned),
        )
    }
    greet(me, True)
    plan = Plan()
    at = types.SimpleNamespace()
    one, far, three = rem4(me.x + 1), rem4(me.x + 2), rem4(me.x + 3)
    right, left = near(me, "x", 1), near(me, "x", 3)

    def add(target, term):
        add_into(target, [term])

    def loaded(*names):
        return lambda: [loads[name] for name in names]

    def share_attn():
        at.attn = [
            wire.put(
                d_attn.at[:, :, pl.ds(pl.multiple_of((block * 2 + 1 - me.core) * 128, 128), 128)],
                attn_far.at[block],
                sibling(me),
            )
            for block in range(8)
        ]

    def share_heads():
        heads_t[...] = heads_in[...].T
        at.heads = wire.put(heads_t, heads_t_far, sibling(me))

    plan.add("as", share_attn, loaded("attn"), rank=1.5)
    plan.add("ht", share_heads, rank=1.5)

    total = RingSum(
        wire, me, "x", columns_of(out_part), out_near_left, out_near_right, out_whole_left,
        out_whole_right, split_columns, add,
    )
    total.plan(plan, "os", (), 1)
    plan.steps["os.go"].waits = loaded("part")

    def finish_out(index, carry):
        span = pl.ds(pl.multiple_of(index * 16, 16), 16)
        result_out[span, :] = (
            y_in[span, :]
            + (
                out_part[me.x, span, :].astype(F32)
                + out_whole_left[span, :].astype(F32)
                + out_whole_right[span, :].astype(F32)
            )
        ).astype(BF)
        return carry

    plan.add("fo", lambda: lax.fori_loop(0, 8, finish_out, 0), after=("os.far",), rank=6)

    def back_heads(zl, carry):
        weight = jnp.concatenate(
            [w_o[zl, y, zh, c] for y in range(4) for zh in range(2) for c in range(2)], axis=1
        )
        result = dot_nt(d_attn[...].reshape(512, D), weight).astype(BF)
        d_heads[zl * 2] = result[:, 0:HD]
        d_heads[zl * 2 + 1] = result[:, HD : 2 * HD]
        return carry

    plan.add("dh", lambda: lax.fori_loop(0, 2, back_heads, 0), loaded("attn", "o"), rank=2)
    plan.add("bias", lambda: fill_bias(bias, me, start_in[0]), rank=1)

    def back_attend(head, carry):
        for half, pairs in ((1, 4), (0, 3)):
            span = pairs * 256
            rows = slice(half * 256, half * 256 + 256)
            key = keys_in[head, 0:pairs].reshape(span, HD)
            value = values_in[head, 0:pairs].reshape(span, HD)
            query, d_head = query_in[head, rows, :], d_heads[head, rows, :]
            scores = dot_nt(key, query) * SCALE + bias[0:span, rows]
            probs = jnp.exp(scores - lse_in[head, :, rows])
            d_probs = dot_nt(value, d_head)
            delta = jnp.sum(probs * d_probs, axis=0, keepdims=True)
            d_scores = (probs * (d_probs - delta) * SCALE).astype(BF)
            d_key = dot_nn(d_scores, query)
            d_value = dot_nn(probs.astype(BF), d_head)
            if half == 1:
                sum_keys[...] = d_key
                sum_values[...] = d_value
            else:
                sum_keys[0:span, :] += d_key
                sum_values[0:span, :] += d_value
            raw = dot_tn(key, d_scores).T
            cosine = tables[0, 2 * half : 2 * half + 2, 0].reshape(256, HD)
            sine = tables[1, 2 * half : 2 * half + 2, 0].reshape(256, HD)
            column = pl.ds(pl.multiple_of(head * HD, HD), HD)
            d_query[rows, column] = turn(raw, cosine, -sine).astype(BF)
        cosine, sine = tables[0].reshape(SEQ, HD), tables[1].reshape(SEQ, HD)
        d_keys[:, column] = turn(sum_keys[...], cosine, -sine).astype(BF)
        d_values[:, column] = sum_values[...].astype(BF)
        return carry

    def attend_rest():
        lax.fori_loop(2, 4, back_attend, 0)
        at.grads = [
            wire.put(d_query, d_query_far, sibling(me)),
            wire.put(d_keys, d_keys_far, sibling(me)),
            wire.put(d_values, d_values_far, sibling(me)),
        ]

    plan.add(
        "ba0", lambda: lax.fori_loop(0, 2, back_attend, 0), loaded("tables"), ("dh", "bias"), 2
    )
    plan.add("ba2", attend_rest, after=("ba0",), rank=2)

    def back_h(block, carry):
        y, zh = lax.div(block, 2), lax.rem(block, 2)

        def weight(which):
            return jnp.concatenate(
                [w_qkv[which, 0, y, zh].reshape(256, 256), w_qkv[which, 1, y, zh].reshape(256, 256)],
                axis=1,
            )

        column = pl.ds(pl.multiple_of(block * 256, 256), 256)
        both = dot_nt(d_keys[...], weight(1)) + dot_nt(d_values[...], weight(2))
        both = both.reshape(4, 2, 128, 256)
        own = dot_nt(d_query[...], weight(0)).reshape(4, 128, 256) + both[:, 0]
        d_h[:, 0, :, column] = own.astype(BF)
        d_h[:, 1, :, column] = both[:, 1].astype(BF)
        return carry

    own = RingSum(
        wire, me, "x",
        lambda slot, half: d_h.at[slot, 0] if half is None else d_h.at[slot, 0, :, pl.ds(half * 1024, 1024)],
        near_left, near_right, whole_left, whole_right, split_columns, add,
    )
    at.far_z, at.sides, at.last = {}, {}, {}

    def cut(ref, half):
        return ref.at[:, pl.ds(half * 1024, 1024)]

    def back_half(half):
        def run():
            lax.fori_loop(half * 4, half * 4 + 4, back_h, 0)
            at.far_z[half] = wire.put(cut(d_h.at[far, 1], half), cut(far_one, half), partner(me))
            at.sides[half] = [
                wire.put(cut(d_h.at[one, 1], half), cut(side_left, half), right),
                wire.put(cut(d_h.at[three, 1], half), cut(side_right, half), left),
            ]
            own.start_whole(half)

        return run

    def near_half(half):
        def run():
            add_into(cut(d_h.at[far, 0], half), [cut(far_one, half)])
            own.start_near(half)

        return run

    def last_half(half):
        def run():
            add_into(cut(d_h.at[me.x, 1], half), [cut(side_left, half), cut(side_right, half)])
            at.last[half] = wire.put(cut(d_h.at[me.x, 1], half), cut(last_z, half), partner(me))

        return run

    plan.add("bh0", back_half(0), loaded("qkv"), ("ba2",), 2)
    plan.add("bh1", back_half(1), after=("bh0",), rank=2)
    for half in range(2):
        name = "%d" % half
        plan.add("dn" + name, near_half(half), lambda half=half: [at.far_z[half]], ("bh" + name,), 0)
        plan.add("dl" + name, last_half(half), lambda half=half: at.sides[half], ("bh" + name,), 0.5)
    plan.add("ds.go", lambda: None, after=("dn0", "dn1"), rank=0)
    own.plan(plan, "ds", (), 0, go=False)

    def grad_o(index, carry):
        zl, y = lax.div(index, 4), lax.rem(index, 4)
        mine = jnp.concatenate(
            [
                d_attn[:, :, pl.ds(pl.multiple_of(((y * 2 + zh) * 2 + me.core) * 128, 128), 128)]
                .reshape(512, 128)
                for zh in range(2)
            ],
            axis=1,
        )
        other = jnp.concatenate(
            [attn_far[y * 2 + zh].reshape(512, 128) for zh in range(2)], axis=1
        )
        rows = pl.ds(pl.multiple_of(zl * 256, 256), 256)
        result = (dot_nn(heads_t[rows, :], mine) + dot_nn(heads_t_far[rows, :], other)).astype(BF)
        w_o[zl, y, 0, 0] = result[:, 0:128]
        w_o[zl, y, 1, 0] = result[:, 128:256]
        return carry

    plan.add("go", lambda: lax.fori_loop(0, 8, grad_o, 0), lambda: [at.heads, *at.attn], ("as", "ht", "dh"), 3)

    def blocks(which, pair):
        return turned[which, pl.ds(pair * 4, 4)].reshape(512, SEQ)

    def own_rows(value):
        return jnp.concatenate([value[:, i * 256 : i * 256 + 128] for i in range(4)], axis=1)

    def grad_qkv(index, carry):
        zl, pair = lax.div(index, 2), lax.rem(index, 2)
        column = pl.ds(pl.multiple_of(zl * 256, 256), 256)
        mine, other = blocks(0, pair), blocks(1, pair)
        result = dot_nn(own_rows(mine), d_query[:, column])
        result = result + dot_nn(own_rows(other), d_query_far[:, column])
        w_qkv[0, zl, pl.ds(pair * 2, 2), :, 0] = result.astype(BF).reshape(2, 2, 128, 256)
        result = dot_nn(mine, d_keys[:, column]) + dot_nn(other, d_keys_far[:, column])
        w_qkv[1, zl, pl.ds(pair * 2, 2), :, 0] = result.astype(BF).reshape(2, 2, 128, 256)
        result = dot_nn(mine, d_values[:, column]) + dot_nn(other, d_values_far[:, column])
        w_qkv[2, zl, pl.ds(pair * 2, 2), :, 0] = result.astype(BF).reshape(2, 2, 128, 256)
        return carry

    plan.add(
        "gq0", lambda: lax.fori_loop(0, 2, grad_qkv, 0),
        lambda: [loads["turned"], *at.grads], ("bh1",), 3,
    )
    plan.add("gq1", lambda: lax.fori_loop(2, 4, grad_qkv, 0), after=("gq0",), rank=3)

    g_qkv, g_o = w_qkv.at[:, :, :, :, 0], w_o.at[:, :, :, 0]
    rest = UNITS - SUM_Y
    for name, fold, waits, after, rank, result in (
        ("my", Fold(wire, me, 0, None, ("y", "z"), None, held_view(fold_y, 1, "z", SUM_Y, 0), groups[0]),
         loaded("fold_y"), (), 1.2, g_mlp_out.at[0:2, 0:SUM_Y, :]),
        ("mz", Fold(wire, me, 144, None, ("z", "y"), None, held_view(fold_z, 1, "y", rest, 144), groups[1]),
         loaded("fold_z"), (), 1.2, g_mlp_out.at[0:2, SUM_Y:UNITS, :]),
        ("oy", Fold(wire, me, 64, fold_view(g_o, me, 0, "y", 0, 128, 64), ("y", "z"), groups[2],
                    crossed_view(g_o, me, 0, "z", 0, 128, 64), groups[3]),
         tuple, ("go",), 1.4, g_o_out.at[0:128, :]),
        ("oz", Fold(wire, me, 64, fold_view(g_o, me, 0, "z", 128, 128, 64), ("z", "y"), groups[4],
                    crossed_view(g_o, me, 0, "y", 128, 128, 64), groups[5]),
         tuple, ("go",), 1.4, g_o_out.at[128:256, :]),
        ("qy", Fold(wire, me, 32, fold_view(g_qkv, me, 1, "y", 0, 64, 32), ("y", "z"), groups[6],
                    crossed_view(g_qkv, me, 1, "z", 0, 64, 32), groups[7]),
         tuple, ("gq1",), 1, g_qkv_out.at[:, 0:64, :]),
        ("qz", Fold(wire, me, 32, fold_view(g_qkv, me, 1, "z", 64, 64, 32), ("z", "y"), groups[8],
                    crossed_view(g_qkv, me, 1, "y", 64, 64, 32), groups[9]),
         tuple, ("gq1",), 1, g_qkv_out.at[:, 64:128, :]),
        ("wy", Fold(wire, me, SUM_CUT, fold_view(g_down, me, 0, "y", 0, SUM_Y, SUM_CUT), ("y", "z"),
                    groups[10], crossed_view(g_down, me, 0, "z", 0, SUM_Y, 0), groups[11]),
         loaded("down"), DOWN_AFTER, 1.3, g_mlp_out.at[2, 0:SUM_Y, :]),
        ("wz", Fold(wire, me, 144, fold_view(g_down, me, 0, "z", SUM_Y, rest, 0), ("z", "y"),
                    groups[12], crossed_view(g_down, me, 0, "y", SUM_Y, rest, 144), groups[13]),
         loaded("down"), DOWN_AFTER, 1.3, g_mlp_out.at[2, SUM_Y:UNITS, :]),
    ):
        fold.plan(plan, name, waits, after, rank, result)

    def back_norm(index, carry):
        span = pl.ds(pl.multiple_of(index * 16, 16), 16)
        d_h_one = (
            d_h[me.x, 0, span, :].astype(F32)
            + whole_left[span, :].astype(F32)
            + whole_right[span, :].astype(F32)
            + last_z[span, :].astype(F32)
        )
        value = tok[span, :].astype(F32)
        scale = lax.rsqrt(jnp.mean(value * value, axis=-1, keepdims=True) + EPS)
        normed = value * scale
        e_one = d_h_one * gains_in[0:1, :]
        inner = jnp.mean(e_one * normed, axis=-1, keepdims=True)
        tokens_out[span, :] = (dy_in[span, :] + scale * (e_one - normed * inner)).astype(BF)
        return carry + jnp.sum(d_h_one * normed, axis=0, keepdims=True)

    def gains_x():
        gain_t[0:1, :] = lax.fori_loop(0, 8, back_norm, jnp.zeros((1, D), F32))
        gain_t[1:2, :] = gain_in[...]
        for row in range(2):
            for block in range(16):
                gain_x[me.x, row * 16 + block : row * 16 + block + 1, :] = gain_t[
                    row : row + 1, block * 128 : block * 128 + 128
                ]
        at.gains = Meet(wire, me, "x", gain_x).copies

    def gains_z():
        gain_z[me.z] = gain_x[0] + gain_x[1] + gain_x[2] + gain_x[3]
        at.gains = Meet(wire, me, "z", gain_z).copies

    def gains_y():
        gain_c[me.core, me.y] = gain_z[0] + gain_z[1] + gain_z[2] + gain_z[3]
        at.gains = MeetCores(wire, me, gain_c).copies

    def gains_all():
        total = gain_c[0, 0]
        for core, y in ((0, 1), (0, 2), (0, 3), (1, 0), (1, 1), (1, 2), (1, 3)):
            total = total + gain_c[core, y]
        gains_out[...] = total

    plan.add(
        "gx", gains_x, lambda: [loads["tok"], at.last[0], at.last[1]], ("ds.far", "dl0", "dl1"), 0
    )
    plan.add("gz", gains_z, lambda: at.gains, ("gx",), 0)
    plan.add("gy", gains_y, lambda: at.gains, ("gz",), 0)
    plan.add("gains", gains_all, lambda: at.gains, ("gy",), 0)
    plan.go(ORDER_BACK)
    wire.drain()


def call_back(starts, tokens, d_attn, out_part, qkv, w_out, query, keys, values, heads, lse, turned,
              tables, gains, y_one, d_y, gain_two, fold_y, fold_z, down):
    shape = jax.ShapeDtypeStruct

    def three(*dims):
        return [pltpu.VMEM(dims, BF)] * 3

    rest = UNITS - SUM_Y
    bufs = (
        three(2, SUM_Y, 128)
        + fold_shapes((2,), (), rest, 144, 128)
        + fold_shapes((), (2, 2), 128, 64, 128)
        + three(128, 128)
        + three(4, 128, 128)
        + fold_shapes((), (), 128, 64, 128)
        + fold_shapes((3,), (2, 2), 64, 32, 256)
        + three(3, 64, 256)
        + three(3, 4, 64, 256)
        + fold_shapes((3,), (), 64, 32, 256)
        + fold_shapes((), (2, 2), SUM_Y, SUM_CUT, 128)
        + three(SUM_Y, 128)
        + three(4, rest, 128)
        + fold_shapes((), (), rest, 144, 128)
    )
    return pl.pallas_call(
        kernel_back,
        name="back",
        in_specs=[pl.BlockSpec(memory_space=pltpu.SMEM)]
        + [anywhere()] * 5
        + [in_vmem()] * 5
        + [anywhere()] * 2
        + [in_vmem()] * 4
        + [anywhere()] * 3,
        out_specs=[in_vmem()] * 6,
        out_shape=[
            shape((128, D), BF),
            shape((128, D), BF),
            shape((3, 128, 256), F32),
            shape((256, 128), F32),
            shape((3, UNITS, 128), F32),
            shape((32, 128), F32),
        ],
        scratch_shapes=[
            pltpu.VMEM((3, 2, 4, 2, 2, 128, 256), BF),
            pltpu.VMEM((2, 4, 2, 2, 256, 128), BF),
            pltpu.VMEM((4, 128, D), BF),
            pltpu.VMEM((4, 128, D), BF),
            pltpu.VMEM((2, 4, 2, 128, HD), F32),
            pltpu.VMEM((SEQ, 512), F32),
            pltpu.VMEM((128, D), BF),
            pltpu.VMEM((2, 8, 128, SEQ), BF),
            pltpu.VMEM((4, 512, HD), BF),
            pltpu.VMEM((512, 512), BF),
            pltpu.VMEM((SEQ, 512), BF),
            pltpu.VMEM((SEQ, 512), BF),
            pltpu.VMEM((512, 512), BF),
            pltpu.VMEM((SEQ, 512), BF),
            pltpu.VMEM((SEQ, 512), BF),
            pltpu.VMEM((SEQ, HD), F32),
            pltpu.VMEM((SEQ, HD), F32),
            pltpu.VMEM((512, 512), BF),
            pltpu.VMEM((512, 512), BF),
            pltpu.VMEM((8, 4, 128, 128), BF),
            pltpu.VMEM((4, 2, 128, D), BF),
        ]
        + [pltpu.VMEM((128, D), BF)] * 4
        + [
            pltpu.VMEM((128, D // 2), BF),
            pltpu.VMEM((128, D // 2), BF),
            pltpu.VMEM((128, D), BF),
            pltpu.VMEM((128, D), BF),
        ]
        * 2
        + [
            pltpu.VMEM((2, 2, 2, SUM_Y, 128), BF),
            pltpu.VMEM((2, 4, UNITS - SUM_Y, 128), BF),
            pltpu.VMEM((2, 4, 2, UNITS, 128), BF),
            pltpu.VMEM((2, D), F32),
            pltpu.VMEM((4, 32, 128), F32),
            pltpu.VMEM((4, 32, 128), F32),
            pltpu.VMEM((2, 4, 32, 128), F32),
        ]
        + bufs
        + [
            pltpu.SemaphoreType.DMA((140,)),
            pltpu.SemaphoreType.DMA((140,)),
            pltpu.SemaphoreType.DMA((16,)),
        ],
        compiler_params=pltpu.CompilerParams(
            collective_id=2, has_side_effects=True, vmem_limit_bytes=VMEM_BYTES
        ),
    )(starts, tokens, d_attn, out_part, qkv, w_out, query, keys, values, heads, lse, turned,
      tables, gains, y_one, d_y, gain_two, fold_y, fold_z, down)


def kernel_settle(result_in, tokens_in, qkv_in, o_in, mlp_in, gains_in,
                  result, tokens, query, key, value, out, gate, up, down, attn, feed):
    dp, tp = lax.axis_index("dp"), lax.axis_index("tensor")
    result[...] = result_in[...]
    tokens[...] = tokens_in[...]
    for index, target in enumerate((query, key, value)):
        target[...] = qkv_in[index]
    out[...] = o_in[...]
    for index, target in enumerate((gate, up, down)):
        target[...] = mlp_in[index]
    for index, target in enumerate((attn, feed)):
        row = gains_in[pl.ds(index * 16 + dp, 1), :]
        target[...] = pltpu.roll(row, lax.rem(128 - tp * 16, 128), 1)[:, 0:16]


def call_settle(*arrays):
    shape = jax.ShapeDtypeStruct
    return pl.pallas_call(
        kernel_settle,
        name="settle",
        in_specs=[in_vmem()] * 6,
        out_specs=[in_vmem()] * 11,
        out_shape=[shape((128, D), BF)] * 2
        + [shape((128, 256), F32)] * 3
        + [shape((256, 128), F32)]
        + [shape((UNITS, 128), F32)] * 3
        + [shape((1, 16), F32)] * 2,
        compiler_params=pltpu.CompilerParams(vmem_limit_bytes=VMEM_BYTES),
    )(*arrays)


def on_device(tables, tokens, starts, w_query, w_key, w_value, w_out, w_gate, w_up, w_down,
              gain_attn, gain_mlp, cotangent):
    weights = (w_query, w_key, w_value, w_out, w_gate.T, w_up.T, w_down)
    (qkv, w_o, mlp, cot, turned, query, keys, values, heads, h_two, lse, y_one, gains) = call_attend(
        tokens, cotangent, starts, weights, gain_attn.reshape(1, 16), gain_mlp.reshape(1, 16), tables
    )
    out_part, d_attn, fold_y, fold_z, down, d_y, gain_two = call_feed(h_two, cot, mlp, y_one, gains)
    sums = call_back(
        starts, tokens, d_attn, out_part, qkv, w_o, query, keys, values, heads, lse, turned,
        tables, gains, y_one, d_y, gain_two, fold_y, fold_z, down,
    )
    result, grad_tokens, query, key, value, out, gate, up, down, attn, feed = call_settle(*sums)
    return (
        result, grad_tokens, query, key, value, out, gate.T, up.T, down,
        attn.reshape(16), feed.reshape(16),
    )


def solution(mesh):
    both = ("dp", "tensor")
    rows, wide, tall = P(both, None), P("dp", "tensor"), P("tensor", "dp")
    in_specs = (
        rows, P("dp"), wide, wide, wide, tall, wide, wide, tall, P(both), P(both), rows,
    )
    out_specs = (
        rows, rows, wide, wide, wide, tall, wide, wide, tall, P(both), P(both),
    )
    return jax.shard_map(
        functools.partial(on_device, rope_tables()), mesh=mesh, in_specs=in_specs,
        out_specs=out_specs, check_vma=False,
    )
```

```python
import functools
import math
import types

import jax
import jax.numpy as jnp
import numpy as np
from jax import lax
from jax.experimental import pallas as pl
from jax.experimental.pallas import tpu as pltpu
from jax.sharding import PartitionSpec as P

HD = 128
PIECE = 256
EPS = 1e-05
NEG = -1e30
SCALE = HD ** (-0.5)
D = 2048
SEQ = 1024
UNITS = 688
BF = jnp.bfloat16
F32 = jnp.float32
MESH = pl.DeviceIdType.MESH
VMEM_BYTES = 60 * 1024 * 1024
ALL = slice(None)


def dot_nn(left, right):
    return jnp.dot(left, right, preferred_element_type=F32)


def dot_nt(left, right):
    return lax.dot_general(left, right, (((1,), (1,)), ((), ())), preferred_element_type=F32)


def dot_tn(left, right):
    return lax.dot_general(left, right, (((0,), (0,)), ((), ())), preferred_element_type=F32)


def rem4(value):
    return lax.rem(value, 4)


def place():
    dp = lax.axis_index("dp")
    tp = lax.axis_index("tensor")
    zh = lax.rem(lax.div(dp, 2), 2)
    zl = lax.rem(tp, 2)
    return types.SimpleNamespace(
        y=lax.div(dp, 4), zh=zh, zl=zl, z=zh * 2 + zl, x=lax.div(tp, 2), core=lax.rem(dp, 2)
    )


def device(me, **moved):
    at = types.SimpleNamespace(**{**vars(me), **moved})
    zh, zl = lax.div(at.z, 2), lax.rem(at.z, 2)
    return (at.y * 4 + zh * 2 + at.core, at.x * 2 + zl)


def near(me, axis, step):
    return device(me, **{axis: rem4(getattr(me, axis) + step)})


def sibling(me):
    return device(me, core=1 - me.core)


def partner(me):
    return device(me, z=me.zh * 2 + 1 - me.zl)


def across(me):
    return device(me, z=rem4(me.z + 3 + 2 * me.zl))


def greet(me, wide, meanwhile=()):
    others = [near(me, axis, step) for axis in ("x", "y", "z") for step in (1, 3)] + [sibling(me)]
    if wide:
        others += [near(me, axis, 2) for axis in ("x", "y", "z")]
        others += [crossed(me, step) for step in (1, 2, 3)]
    barrier = pltpu.get_barrier_semaphore()
    for other in others:
        pl.semaphore_signal(barrier, inc=1, device_id=other, device_id_type=MESH)
    for copy in meanwhile:
        copy.wait()
    pl.semaphore_wait(barrier, len(others))


def crossed(me, step):
    return device(me, y=rem4(me.y + step), core=1 - me.core)


class Plan:
    def __init__(self):
        self.steps = {}

    def add(self, name, run, waits=tuple, after=(), rank=5):
        self.steps[name] = types.SimpleNamespace(run=run, waits=waits, after=after, rank=rank)

    def go(self, order):
        assert sorted(order) == sorted(self.steps)
        for name in order:
            step = self.steps[name]
            for copy in step.waits():
                copy.wait_recv()
            step.run()


class Once:
    def __init__(self, copy, remote):
        self.copy, self.remote = copy, remote
        self.received = self.left = False

    def wait_recv(self):
        if not self.received:
            self.received = True
            if self.remote:
                self.copy.wait_recv()
            else:
                self.copy.wait()

    wait = wait_recv

    def wait_send(self):
        if not self.left:
            self.left = True
            self.copy.wait_send()


class Wire:
    def __init__(self, send, recv, local):
        self.send, self.recv, self.local = send, recv, local
        self.used, self.used_local = 0, 0
        self.sent = []

    def put(self, source, target, to):
        index = self.used
        self.used += 1
        assert index < self.send.shape[0]
        copy = pltpu.make_async_remote_copy(
            src_ref=source,
            dst_ref=target,
            send_sem=self.send.at[index],
            recv_sem=self.recv.at[index],
            device_id=to,
            device_id_type=MESH,
        )
        copy.start()
        copy = Once(copy, True)
        self.sent.append(copy)
        return copy

    def move(self, source, target):
        index = self.used_local
        self.used_local += 1
        assert index < self.local.shape[0]
        copy = pltpu.make_async_copy(source, target, self.local.at[index])
        copy.start()
        return Once(copy, False)

    def drain(self):
        for copy in self.sent:
            copy.wait_send()
        self.sent = []


class Ring:
    def __init__(self, wire, me, axis, view):
        self.wire, self.view = wire, view
        self.at = getattr(me, axis)
        self.right, self.left = near(me, axis, 1), near(me, axis, 3)

    def put(self, slot, part, to):
        piece = self.view(slot, part)
        return self.wire.put(piece, piece, to)

    def start(self):
        self.right_one = self.put(self.at, 0, self.right)
        self.left_one = self.put(self.at, 1, self.left)
        self.right_two = self.put(self.at, 1, self.right)
        self.left_two = self.put(self.at, 0, self.left)

    def plan(self, plan, name, after, rank):
        plan.add(name + ".go", self.start, after=after, rank=rank)
        plan.add(name + ".r", self.relay_right, lambda: [self.right_one], (name + ".go",), rank)
        plan.add(name + ".l", self.relay_left, lambda: [self.left_one], (name + ".go",), rank)
        plan.add(
            name + ".near", lambda: None, lambda: [self.right_two, self.left_two],
            (name + ".r", name + ".l"), rank,
        )
        plan.add(
            name + ".far", lambda: None, lambda: [self.far_right, self.far_left], (name + ".near",), rank
        )

    def relay_right(self):
        self.far_right = self.put(rem4(self.at + 3), 0, self.right)

    def relay_left(self):
        self.far_left = self.put(rem4(self.at + 1), 1, self.left)

    def closed(self):
        return rem4(self.at + 3), rem4(self.at + 1)


class Direct:
    def __init__(self, wire, me, view):
        self.wire, self.view, self.me, self.at = wire, view, me, me.z

    def start(self):
        piece = self.view(self.at, None)
        others = (partner(self.me), across(self.me), near(self.me, "z", 2))
        self.copies = [self.wire.put(piece, piece, other) for other in others]

    def plan(self, plan, name, after, rank):
        plan.add(name + ".go", self.start, after=after, rank=rank)
        plan.add(name + ".far", lambda: None, lambda: self.copies, (name + ".go",), rank)


class PairRing:
    def __init__(self, wire, me, view):
        self.wire, self.view, self.me = wire, view, me
        self.at = me.z
        self.mate, self.beyond = me.zh * 2 + 1 - me.zl, rem4(me.z + 3 + 2 * me.zl)

    def put(self, slot, to):
        piece = self.view(slot, None)
        return self.wire.put(piece, piece, to)

    def start(self):
        self.to_mate = self.put(self.at, partner(self.me))
        self.to_beyond = self.put(self.at, across(self.me))

    def plan(self, plan, name, after, rank):
        plan.add(name + ".go", self.start, after=after, rank=rank)
        plan.add(name + ".r", self.relay, lambda: [self.to_mate], (name + ".go",), rank)
        plan.add(name + ".near", lambda: None, lambda: [self.to_beyond], (name + ".r",), rank)
        plan.add(name + ".far", lambda: None, lambda: [self.far], (name + ".near",), rank)

    def relay(self):
        self.far = self.put(self.mate, across(self.me))

    def closed(self):
        return self.mate, self.beyond


class Meet:
    def __init__(self, wire, me, axis, ref):
        piece = ref.at[getattr(me, axis)]
        self.copies = [wire.put(piece, piece, near(me, axis, step)) for step in (1, 2, 3)]


class MeetCores:
    def __init__(self, wire, me, ref):
        piece = ref.at[me.core, me.y]
        others = [near(me, "y", step) for step in (1, 2, 3)] + [sibling(me)]
        others += [crossed(me, step) for step in (1, 2, 3)]
        self.copies = [wire.put(piece, piece, other) for other in others]


class RingSum:
    def __init__(self, wire, me, axis, part, from_left, from_right, whole_left, whole_right, split, add):
        self.wire, self.part, self.split, self.add = wire, part, split, add
        self.at = getattr(me, axis)
        self.right, self.left = near(me, axis, 1), near(me, axis, 3)
        self.near_bufs = (from_left, from_right)
        self.whole = (whole_left, whole_right)

    def start_near(self, half):
        piece = self.part(rem4(self.at + 2), half)
        to = self.left if half else self.right
        copy = self.wire.put(piece, self.near_bufs[half], to)
        if half:
            self.second = copy
        else:
            self.first = copy

    def start_whole(self, half):
        if half:
            self.right_whole = self.wire.put(
                self.part(rem4(self.at + 1), 1), self.split(self.whole[0], 1), self.right
            )
        else:
            self.left_whole = self.wire.put(
                self.part(rem4(self.at + 3), 0), self.split(self.whole[1], 0), self.left
            )

    def start(self, halves=(0, 1)):
        for half in halves:
            self.start_near(half)
        if 1 in halves:
            self.start_whole(1)
            self.start_whole(0)

    def plan(self, plan, name, after, rank, go=True):
        if go:
            plan.add(name + ".go", self.start, after=after, rank=rank)
        plan.add(name + ".r", self.relay_right, lambda: [self.first], (name + ".go",), rank)
        plan.add(name + ".l", self.relay_left, lambda: [self.second], (name + ".go",), rank)
        plan.add(
            name + ".far",
            lambda: None,
            lambda: [self.left_whole, self.right_whole, self.to_right, self.to_left],
            (name + ".r", name + ".l"),
            rank,
        )

    def relay_right(self):
        after = rem4(self.at + 1)
        self.add(self.part(after, 0), self.near_bufs[0])
        self.to_right = self.wire.put(self.part(after, 0), self.split(self.whole[0], 0), self.right)

    def relay_left(self):
        before = rem4(self.at + 3)
        self.add(self.part(before, 1), self.near_bufs[1])
        self.to_left = self.wire.put(self.part(before, 1), self.split(self.whole[1], 1), self.left)


class PairSum:
    def __init__(self, wire, me, part, from_beyond, for_mate, from_mate, add):
        self.wire, self.me, self.part, self.add = wire, me, part, add
        self.at = me.z
        self.mate, self.beyond = me.zh * 2 + 1 - me.zl, rem4(me.z + 3 + 2 * me.zl)
        self.for_mate, self.whole = for_mate, (from_beyond, from_mate)

    def start(self):
        far = rem4(self.at + 2)
        self.first = self.wire.put(self.part(far, None), self.for_mate, across(self.me))
        self.second = self.wire.put(self.part(self.beyond, None), self.whole[0], across(self.me))

    def plan(self, plan, name, after, rank):
        plan.add(name + ".go", self.start, after=after, rank=rank)
        plan.add(name + ".r", self.relay, lambda: [self.first], (name + ".go",), rank)
        plan.add(
            name + ".far", lambda: None, lambda: [self.second, self.to_mate], (name + ".r",), rank
        )

    def relay(self):
        self.add(self.part(self.mate, None), self.for_mate)
        self.to_mate = self.wire.put(self.part(self.mate, None), self.whole[1], partner(self.me))


def split_columns(ref, half):
    return ref.at[:, pl.ds(half * (D // 2), D // 2)]


def split_rows(cut):
    def split(ref, half):
        rows = ref.shape[-2]
        span = pl.ds(0, cut) if half == 0 else pl.ds(cut, rows - cut)
        return ref.at[(ALL,) * (len(ref.shape) - 2) + (span, ALL)]

    return split


class Spread:
    def __init__(self, wire, me, ref, lead, row, rows, first, cut, cuts=(ALL,), kind=PairRing):
        self.wire, self.me = wire, me
        head = (ALL,) * lead

        def view(y, z, part, low=ALL):
            zl, zh = (low, ALL) if z is None else (lax.rem(z, 2), lax.div(z, 2))
            start, size = row, rows
            if part == 0:
                size = cut
            if part == 1:
                start, size = row + cut, rows - cut
            yy = ALL if y is None else y
            return ref.at[head + (zl, yy, zh, me.core, pl.ds(start, size), ALL)]

        if first == "y":
            self.one = Ring(wire, me, "y", lambda slot, part: view(slot, me.z, part))
            self.twos = [PairRing(wire, me, lambda slot, part: view(None, slot, part))]
        else:
            self.one = kind(wire, me, lambda slot, part: view(me.y, slot, part))
            self.twos = [
                Ring(wire, me, "y", lambda slot, part, low=low: view(slot, None, part, low))
                for low in cuts
            ]

    def plan(self, plan, name, after, turn_after, rank):
        self.one.plan(plan, name + ".a", after, rank)
        done = [name + ".a.far", *turn_after]
        for index, two in enumerate(self.twos):
            tail = str(index) if len(self.twos) > 1 else ""
            self.plan_two(plan, two, name, tail, tuple(done), rank + 0.01 * index)
            done += [name + ".b" + tail + ".r", name + ".b" + tail + ".l"] if tail else []

    def plan_two(self, plan, two, name, tail, after, rank):
        shared = []

        def share(slots):
            for slot in slots:
                piece = two.view(slot, None)
                shared.append(self.wire.put(piece, piece, sibling(self.me)))

        def go():
            two.start()
            share([two.at])

        step = name + ".b" + tail
        two.plan(plan, step, after, rank)
        plan.steps[step + ".go"].run = go
        plan.add(name + ".s" + tail, lambda: share(two.closed()), after=(step + ".near",), rank=rank)
        plan.add(
            name + ".t" + tail, lambda: share([rem4(two.at + 2)]),
            after=(name + ".s" + tail, step + ".far"), rank=rank,
        )
        plan.add(name + ".all" + tail, lambda: None, lambda: shared, (name + ".t" + tail,), rank)
MLP_Y, MLP_CUT, MLP_REST = 320, 160, 176
QKV_Y, QY_CUT, QZ_CUT = 32, 16, 48
QZ_KIND = PairRing
OUT_Y, OUT_CUT, OUT_REST = 64, 32, 96
MZ_AFTER, MZ_TURN = (), ()
MY_AFTER, MY_TURN = (), ()
ORDER_ATTEND = (
    "qz.a.go", "qy.a.go", "my.a.go", "tz", "gx", "tx.go", "qy.a.r", "qy.a.l", "qy.a.near", "gz",
    "qz.a.r", "qz.a.near", "my.a.r", "my.a.l", "oy.a.go", "tx.r", "tx.l", "my.a.near", "qy.a.far",
    "qy.b.go", "qz.a.far", "qz.b0.go", "oz.a.go", "my.a.far", "oy.a.r", "oy.a.l", "mz.a.go",
    "oy.a.near", "tx.near", "qz.b0.r", "qz.b0.l", "to", "bias", "gy", "qz.b1.go", "qz.b0.near",
    "qz.s0", "oy.a.far", "tx.far", "qy.b.r", "qy.b.near", "qy.s", "oz.a.r", "oz.a.near",
    "qz.b0.far", "qz.t0", "cx.go", "gains", "n2", "n1", "qz.all0", "oy.b.go", "tf", "n0",
    "qz.b1.l", "n3", "qz.b1.r", "qy.b.far", "qy.t", "mz.a.r", "mz.a.near", "oz.a.far", "oz.b.go",
    "qy.all", "proj0", "oy.b.r", "own0", "qz.b1.near", "qz.s1", "qz.b1.far", "qz.t1", "oy.b.near",
    "oy.s", "n4", "rest0", "oz.b.l", "oz.b.r", "my.b.go", "qz.all1", "proj1", "cx.r", "rest1",
    "oz.b.near", "mz.a.far", "oy.b.far", "oy.t", "oz.s", "cx.l", "mz.b.go", "own2", "oy.all",
    "oz.b.far", "oz.t", "n5", "last1", "last0", "cx.near", "att0", "att2", "oz.all", "po",
    "cx.far", "ys.go", "flip", "flip2", "mz.b.l", "mz.b.r", "ys.r", "ck", "ys.l", "flip3",
    "my.b.r", "my.b.near", "my.s", "mz.b.near", "mz.s", "ys.far", "fin", "hx.go", "hx.r", "hx.l",
    "mz.b.far", "mz.t", "mz0", "mz.all", "mz1", "hx.near", "my.b.far", "my.t", "my0", "my.all",
    "my1", "hx.far", "hk",
)


def norm_rows(source, target, gain, rows, step=32):
    def body(index, carry):
        span = pl.ds(pl.multiple_of(index * step, step), step)
        value = source[span, :].astype(F32)
        scale = lax.rsqrt(jnp.mean(value * value, axis=-1, keepdims=True) + EPS)
        target[span, :] = (value * scale * gain).astype(BF)
        return carry

    lax.fori_loop(0, rows // step, body, 0)


def fill_bias(bias, me, start):
    row = lax.broadcasted_iota(jnp.int32, (128, 512), 0)
    column = lax.broadcasted_iota(jnp.int32, (128, 512), 1)
    query = lax.div(column, 128) * 256 + me.zl * 128 + lax.rem(column, 128)
    query_in = (query >= start) & (query < start + PIECE)

    def body(block, carry):
        pair, other = lax.div(block, 2), lax.rem(block, 2)
        parity = me.zl + other * (1 - 2 * me.zl)
        key = (pair * 2 + parity) * 128 + row
        key_in = (key >= start) & (key < start + PIECE)
        allowed = (key <= query) | (query_in & key_in)
        bias[pair, other] = jnp.where(allowed, 0.0, NEG)
        return carry

    lax.fori_loop(0, 8, body, 0)


def turn(field, cosine, sine):
    return field * cosine + pltpu.roll(field, HD // 2, 1) * sine


def add_into(target, terms, result=None):
    shape = target.shape
    lead, rows, columns = shape[:-2], shape[-2], shape[-1]
    step = rows
    while step * columns > 33000:
        step = next(s for s in range(step - 16, 0, -16) if rows % s == 0)
    cuts = rows // step
    result = target if result is None else result

    def body(index, carry):
        where, rest = [], lax.div(index, cuts)
        for extent in reversed(lead):
            where.insert(0, lax.rem(rest, extent))
            rest = lax.div(rest, extent)
        where = tuple(where) + (
            pl.ds(pl.multiple_of(lax.rem(index, cuts) * step, 16), step), ALL
        )
        total = target[where].astype(F32)
        for term in terms:
            total = total + term[where].astype(F32)
        result[where] = total.astype(result.dtype)
        return carry

    lax.fori_loop(0, math.prod(lead) * cuts, body, 0)


def columns_of(ref):
    def view(slot, half):
        if half is None:
            return ref.at[slot]
        return ref.at[slot, :, pl.ds(half * (D // 2), D // 2)]

    return view


def rows_of(ref):
    def view(slot, half):
        return ref.at[slot] if half is None else ref.at[slot, pl.ds(half * 64, 64)]

    return view


def kernel_attend(
    tokens_in, cotangent_in, start_in, query_w, key_w, value_w, out_w, gate_w, up_w, down_w,
    gain_one_in, gain_two_in, tables_in,
    qkv_out, wo_out, mlp_out, cot_out, turned_out, query_out, keys_out, values_out, heads_out,
    h_out, lse_hbm, y_hbm, gains_hbm,
    lse_out, y_out, gains_out, tok, h_one, w_qkv, w_o, w_mlp, tables, bias, query, keys, values, heads, cot, h_two,
    part, near_left, near_right, whole_left, whole_right,
    turned, top_s, total_s, result_s, gain_x, gain_z, gain_c,
    send, recv, local,
):
    me = place()
    wire = Wire(send, recv, local)
    own = [wire.move(tokens_in, tok.at[me.x, 0])]
    for index, ref in enumerate((query_w, key_w, value_w)):
        own.append(wire.move(ref, w_qkv.at[index, me.zl, me.y, me.zh, me.core]))
    own.append(wire.move(out_w, w_o.at[me.zl, me.y, me.zh, me.core]))
    for index, ref in enumerate((gate_w, up_w, down_w)):
        own.append(wire.move(ref, w_mlp.at[index, me.zl, me.y, me.zh, me.core]))
    own.append(wire.move(tables_in.at[me.zl], tables))
    own.append(wire.move(cotangent_in, cot.at[me.x]))
    lane = lax.div(lax.broadcasted_iota(jnp.int32, (1, 128), 1), 16)
    tensor = me.x * 2 + me.zl
    gain_x[me.x] = jnp.concatenate(
        [
            jnp.where(lane == tensor, jnp.concatenate([ref[...]] * 8, axis=1), 0.0)
            for ref in (gain_one_in, gain_two_in)
        ]
        + [jnp.zeros((6, 128), F32)],
        axis=0,
    )
    greet(me, True, own)
    plan = Plan()
    at = types.SimpleNamespace()
    one, far, three = rem4(me.x + 1), rem4(me.x + 2), rem4(me.x + 3)
    kept = []

    def keep(source, target):
        kept.append(wire.move(source, target))

    def gains_x():
        at.gains = Meet(wire, me, "x", gain_x).copies

    def gains_z():
        gain_z[me.z] = gain_x[0] + gain_x[1] + gain_x[2] + gain_x[3]
        at.gains = Meet(wire, me, "z", gain_z).copies

    def gains_y():
        gain_c[me.core, me.y, 0] = gain_z[0] + gain_z[1]
        gain_c[me.core, me.y, 1] = gain_z[2] + gain_z[3]
        at.gains = MeetCores(wire, me, gain_c).copies

    def gains_all():
        for y in range(4):
            for zh in range(2):
                for core in range(2):
                    column = (y * 4 + zh * 2 + core) * 128
                    gains_out[:, column : column + 128] = gain_c[core, y, zh]

    plan.add("gx", gains_x, rank=0)
    plan.add("gz", gains_z, lambda: at.gains, ("gx",), 0)
    plan.add("gy", gains_y, lambda: at.gains, ("gz",), 0)
    plan.add("gains", gains_all, lambda: at.gains, ("gy",), 1)

    def tokens_z():
        at.rows_z = wire.put(tok.at[me.x, 0], tok.at[me.x, 1], partner(me))

    def tokens_on():
        at.on = [
            wire.put(tok.at[me.x, 1], tok.at[me.x, 1], near(me, "x", step)) for step in (1, 3)
        ]

    def tokens_far():
        at.far_z = wire.put(tok.at[far, 0], tok.at[far, 1], partner(me))

    Ring(
        wire, me, "x",
        lambda slot, half: tok.at[slot, 0] if half is None else tok.at[slot, 0, pl.ds(half * 64, 64)],
    ).plan(plan, "tx", (), 0)
    plan.add("tz", tokens_z, rank=0)
    plan.add("to", tokens_on, lambda: [at.rows_z], ("tz",), 0)
    plan.add("tf", tokens_far, after=("tx.far",), rank=0)

    def norm(*blocks):
        def run():
            for slot, p in blocks:
                norm_rows(tok.at[slot, p], h_one.at[slot, p], gains_out[0:1, :], 128)

        return run

    plan.add("n0", norm((me.x, 0)), after=("gains",), rank=2)
    plan.add("n1", norm((one, 0), (three, 0)), after=("gains", "tx.near"), rank=2)
    plan.add("n2", norm((far, 0)), after=("gains", "tx.far"), rank=2)
    plan.add("n3", norm((me.x, 1)), after=("gains", "to"), rank=3)
    plan.add("n4", norm((one, 1), (three, 1)), lambda: at.on, ("gains", "to"), 3)
    plan.add("n5", norm((far, 1)), lambda: [at.far_z], ("gains", "tf"), 2)

    Spread(wire, me, w_qkv, 1, QKV_Y, 128 - QKV_Y, "z", QZ_CUT, (0, 1), QZ_KIND).plan(plan, "qz", (), (), 1)
    Spread(wire, me, w_qkv, 1, 0, QKV_Y, "y", QY_CUT).plan(plan, "qy", (), (), 1)
    Spread(wire, me, w_o, 0, OUT_Y, 256 - OUT_Y, "z", OUT_REST).plan(plan, "oz", (), (), 1)
    Spread(wire, me, w_o, 0, 0, OUT_Y, "y", OUT_CUT).plan(plan, "oy", (), (), 1)
    mlp_z = Spread(wire, me, w_mlp, 1, MLP_Y, UNITS - MLP_Y, "z", MLP_REST)
    mlp_y = Spread(wire, me, w_mlp, 1, 0, MLP_Y, "y", MLP_CUT)
    mlp_z.plan(plan, "mz", MZ_AFTER, MZ_TURN, 1.5)
    mlp_y.plan(plan, "my", MY_AFTER, MY_TURN, 1.5)
    plan.add("bias", lambda: fill_bias(bias, me, start_in[0]), rank=6)

    def project(zl, carry):
        rows = h_one[:, 0].reshape(512, D)
        cosine, sine = tables[0, :, 0].reshape(512, HD), tables[1, :, 0].reshape(512, HD)
        raw = dot_nn(rows, w_qkv[0, zl].reshape(D, 256))
        for j in range(2):
            query[zl * 2 + j] = turn(raw[:, j * HD : (j + 1) * HD], cosine, sine).astype(BF)
        raw = dot_nn(rows, w_qkv[1, zl].reshape(D, 256))
        for j in range(2):
            keys[zl * 2 + j, :, 0] = (
                turn(raw[:, j * HD : (j + 1) * HD], cosine, sine).astype(BF).reshape(4, 128, HD)
            )
        raw = dot_nn(rows, w_qkv[2, zl].reshape(D, 256))
        for j in range(2):
            values[zl * 2 + j, :, 0] = raw[:, j * HD : (j + 1) * HD].astype(BF).reshape(4, 128, HD)
        return carry

    def project_other(zl, slots):
        rows = jnp.concatenate([h_one[slot, 1] for slot in slots], axis=0)
        cosine = jnp.concatenate([tables[0, slot, 1] for slot in slots], axis=0)
        sine = jnp.concatenate([tables[1, slot, 1] for slot in slots], axis=0)
        raw_k = dot_nn(rows, w_qkv[1, zl].reshape(D, 256))
        raw_v = dot_nn(rows, w_qkv[2, zl].reshape(D, 256))
        for j in range(2):
            key = turn(raw_k[:, j * HD : (j + 1) * HD], cosine, sine).astype(BF)
            value = raw_v[:, j * HD : (j + 1) * HD].astype(BF)
            for index, slot in enumerate(slots):
                keys[zl * 2 + j, slot, 1] = key[index * 128 : index * 128 + 128]
                values[zl * 2 + j, slot, 1] = value[index * 128 : index * 128 + 128]

    at.projected = at.rest = 0

    def keep_when_done():
        if at.projected == 2 and at.rest == 4:
            keep(w_qkv, qkv_out)
            keep(query, query_out)
            keep(keys, keys_out)
            keep(values, values_out)

    def project_half(zl):
        def run():
            lax.fori_loop(zl, zl + 1, project, 0)
            at.projected += 1
            keep_when_done()

        return run

    def other(zl, slots):
        def run():
            project_other(zl, slots)
            at.rest += 1
            keep_when_done()

        return run

    for zl in range(2):
        name = "%d" % zl
        plan.add(
            "proj" + name, project_half(zl), after=("n0", "n1", "n2", "qy.all", "qz.all" + name), rank=2 + 0.1 * zl
        )
        plan.add(
            "rest" + name, other(zl, (me.x, one, three)), after=("n3", "n4", "qy.all", "qz.all" + name),
            rank=2.2 + 0.1 * zl,
        )
        plan.add("last" + name, other(zl, (far,)), after=("n5", "qy.all", "qz.all" + name), rank=2.4 + 0.1 * zl)

    def attend_own(head, carry):
        for half, pairs in ((0, 3), (1, 4)):
            span = pairs * 128
            rows = slice(half * 256, half * 256 + 256)
            scores = dot_nt(keys[head, 0:pairs, 0].reshape(span, HD), query[head, rows, :]) * SCALE
            scores = scores + bias[0:pairs, 0, :, rows].reshape(span, 256)
            top = jnp.max(scores, axis=0, keepdims=True)
            expo = jnp.exp(scores - top)
            top_s[head, half] = top
            total_s[head, half] = jnp.sum(expo, axis=0, keepdims=True)
            value = values[head, 0:pairs, 0].reshape(span, HD)
            result_s[head, half] = dot_tn(value, expo.astype(BF))
        return carry

    def attend_other(head, carry):
        for half, pairs in ((0, 3), (1, 4)):
            span = pairs * 128
            rows = slice(half * 256, half * 256 + 256)
            scores = dot_nt(keys[head, 0:pairs, 1].reshape(span, HD), query[head, rows, :]) * SCALE
            scores = scores + bias[0:pairs, 1, :, rows].reshape(span, 256)
            before = top_s[head, half]
            top = jnp.maximum(before, jnp.max(scores, axis=0, keepdims=True))
            fade = jnp.exp(before - top)
            expo = jnp.exp(scores - top)
            total = total_s[head, half] * fade + jnp.sum(expo, axis=0, keepdims=True)
            value = values[head, 0:pairs, 1].reshape(span, HD)
            result = (result_s[head, half] * fade + dot_tn(value, expo.astype(BF))) * (1.0 / total)
            heads[rows, pl.ds(pl.multiple_of(head * HD, HD), HD)] = result.T.astype(BF)
            lse_out[head, :, rows] = top + jnp.log(total)
        return carry

    def attend_rest():
        lax.fori_loop(2, 4, attend_other, 0)
        keep(heads, heads_out)
        keep(lse_out, lse_hbm)

    plan.add("own0", lambda: lax.fori_loop(0, 2, attend_own, 0), after=("proj0", "bias"), rank=2.5)
    plan.add("own2", lambda: lax.fori_loop(2, 4, attend_own, 0), after=("proj1", "bias"), rank=2.5)
    plan.add(
        "att0", lambda: lax.fori_loop(0, 2, attend_other, 0), after=("own0", "rest0", "last0"), rank=2.5
    )
    plan.add("att2", attend_rest, after=("own2", "rest1", "last1", "att0"), rank=2.6)

    def project_out(block, carry):
        y, zh = lax.div(block, 2), lax.rem(block, 2)
        weight = jnp.concatenate(
            [
                jnp.concatenate([w_o[zl, y, zh, 0], w_o[zl, y, zh, 1]], axis=1)
                for zl in range(2)
            ],
            axis=0,
        )
        result = dot_nn(heads[...], weight).astype(BF).reshape(4, 128, 256)
        part[:, :, pl.ds(pl.multiple_of(block * 256, 256), 256)] = result
        return carry

    total = RingSum(
        wire, me, "x", columns_of(part), near_left, near_right, whole_left, whole_right,
        split_columns, lambda target, term: add_into(target, [term]),
    )

    def out_one():
        keep(w_o, wo_out)
        lax.fori_loop(0, 4, project_out, 0)
        total.start((0,))

    def out_two():
        lax.fori_loop(4, 8, project_out, 0)
        total.start((1,))

    plan.add("po", out_one, after=("att0", "att2", "oz.all", "oy.all"), rank=2)
    plan.add("ys.go", out_two, after=("po",), rank=2)
    total.plan(plan, "ys", (), 1, go=False)

    def finish(index, carry):
        span = pl.ds(pl.multiple_of(index * 32, 32), 32)
        value = tok[me.x, 0, span, :].astype(F32) + (
            part[me.x, span, :].astype(F32)
            + whole_left[span, :].astype(F32)
            + whole_right[span, :].astype(F32)
        )
        scale = lax.rsqrt(jnp.mean(value * value, axis=-1, keepdims=True) + EPS)
        y_out[span, :] = value
        h_two[me.x, span, :] = (value * scale * gains_out[1:2, :]).astype(BF)
        return carry

    def finish_all():
        lax.fori_loop(0, 4, finish, 0)
        keep(y_out, y_hbm)
        keep(gains_out, gains_hbm)

    plan.add("fin", finish_all, after=("ys.far",), rank=0)
    Ring(wire, me, "x", rows_of(h_two)).plan(plan, "hx", ("fin",), 0)
    plan.add("hk", lambda: keep(h_two, h_out), after=("hx.far",), rank=0)
    Ring(wire, me, "x", rows_of(cot)).plan(plan, "cx", (), 1.6)
    plan.add("ck", lambda: keep(cot, cot_out), after=("cx.far",), rank=1.8)

    def flip(block, carry):
        column = pl.ds(pl.multiple_of(block * 128, 128), 128)
        rows = h_one[:, :, :, column].reshape(SEQ, 128)
        turned[lax.rem(block, 2), lax.div(block, 2)] = rows.T
        return carry

    def flip_rest():
        lax.fori_loop(8, 16, flip, 0)
        keep(turned.at[me.core], turned_out.at[0])
        at.turned = wire.put(turned.at[1 - me.core], turned_out.at[1], sibling(me))

    plan.add("flip", lambda: lax.fori_loop(0, 8, flip, 0), after=("n0", "n1", "n2", "n3", "n4", "n5"), rank=7)
    plan.add("flip2", flip_rest, after=("flip",), rank=7)
    plan.add("flip3", lambda: None, lambda: [at.turned], ("flip2",), 9)

    def keep_mlp(mine, start, size):
        def run():
            core = me.core if mine else 1 - me.core
            piece = (ALL, ALL, ALL, ALL, core, pl.ds(start, size), ALL)
            keep(w_mlp.at[piece], mlp_out.at[piece])

        return run

    plan.add("my0", keep_mlp(True, 0, MLP_Y), after=("my.t",), rank=1.8)
    plan.add("my1", keep_mlp(False, 0, MLP_Y), after=("my.all",), rank=1.8)
    plan.add("mz0", keep_mlp(True, MLP_Y, UNITS - MLP_Y), after=("mz.t",), rank=1.8)
    plan.add("mz1", keep_mlp(False, MLP_Y, UNITS - MLP_Y), after=("mz.all",), rank=1.8)

    plan.go(ORDER_ATTEND)
    for copy in kept:
        copy.wait()
    wire.drain()


def anywhere():
    return pl.BlockSpec(memory_space=pl.ANY)


def in_vmem():
    return pl.BlockSpec(memory_space=pltpu.VMEM)


def call_attend(tokens, cotangent, starts, weights, gain_attn, gain_mlp, tables):
    shape = jax.ShapeDtypeStruct
    hbm = [
        shape((3, 2, 4, 2, 2, 128, 256), BF),
        shape((2, 4, 2, 2, 256, 128), BF),
        shape((3, 2, 4, 2, 2, UNITS, 128), BF),
        shape((4, 128, D), BF),
        shape((2, 8, 128, SEQ), BF),
        shape((4, 512, HD), BF),
        shape((4, 4, 2, 128, HD), BF),
        shape((4, 4, 2, 128, HD), BF),
        shape((512, 512), BF),
        shape((4, 128, D), BF),
    ]
    vmem = [shape((4, 1, 512), F32), shape((128, D), F32), shape((8, D), F32)]
    return pl.pallas_call(
        kernel_attend,
        name="attend",
        in_specs=[anywhere(), anywhere(), pl.BlockSpec(memory_space=pltpu.SMEM)]
        + [anywhere()] * 7
        + [in_vmem()] * 2
        + [anywhere()],
        out_specs=[anywhere()] * (len(hbm) + len(vmem)),
        out_shape=hbm + vmem,
        scratch_shapes=[
            pltpu.VMEM((4, 1, 512), F32),
            pltpu.VMEM((128, D), F32),
            pltpu.VMEM((8, D), F32),
            pltpu.VMEM((4, 2, 128, D), BF),
            pltpu.VMEM((4, 2, 128, D), BF),
            pltpu.VMEM((3, 2, 4, 2, 2, 128, 256), BF),
            pltpu.VMEM((2, 4, 2, 2, 256, 128), BF),
            pltpu.VMEM((3, 2, 4, 2, 2, UNITS, 128), BF),
            pltpu.VMEM((2, 4, 2, 128, HD), F32),
            pltpu.VMEM((4, 2, 128, 512), F32),
            pltpu.VMEM((4, 512, HD), BF),
            pltpu.VMEM((4, 4, 2, 128, HD), BF),
            pltpu.VMEM((4, 4, 2, 128, HD), BF),
            pltpu.VMEM((512, 512), BF),
            pltpu.VMEM((4, 128, D), BF),
            pltpu.VMEM((4, 128, D), BF),
            pltpu.VMEM((4, 128, D), BF),
            pltpu.VMEM((128, D // 2), BF),
            pltpu.VMEM((128, D // 2), BF),
            pltpu.VMEM((128, D), BF),
            pltpu.VMEM((128, D), BF),
            pltpu.VMEM((2, 8, 128, SEQ), BF),
            pltpu.VMEM((4, 2, 1, 256), F32),
            pltpu.VMEM((4, 2, 1, 256), F32),
            pltpu.VMEM((4, 2, HD, 256), F32),
            pltpu.VMEM((4, 8, 128), F32),
            pltpu.VMEM((4, 8, 128), F32),
            pltpu.VMEM((2, 4, 2, 8, 128), F32),
            pltpu.SemaphoreType.DMA((140,)),
            pltpu.SemaphoreType.DMA((140,)),
            pltpu.SemaphoreType.DMA((32,)),
        ],
        compiler_params=pltpu.CompilerParams(
            collective_id=0, has_side_effects=True, vmem_limit_bytes=VMEM_BYTES
        ),
    )(tokens, cotangent, starts, *weights, gain_attn, gain_mlp, tables)


def rope_tables():
    half = HD // 2
    freq = np.exp(np.arange(half, dtype=np.float32) * np.float32(-2.0 * math.log(10000.0) / HD))
    order = np.array(
        [
            [[(2 * pair + (zl + other) % 2) * 128 + np.arange(128) for other in range(2)] for pair in range(4)]
            for zl in range(2)
        ]
    )
    angle = order.astype(np.float32)[..., None] * freq.astype(np.float32)
    cosine, sine = np.cos(angle.astype(np.float64)), np.sin(angle.astype(np.float64))
    both = np.stack(
        [np.concatenate([cosine, cosine], -1), np.concatenate([-sine, sine], -1)], axis=1
    )
    return both.astype(np.float32)
SUM_Y, SUM_CUT = 400, 208
ORDER_FEED = (
    "hs", "l2", "g00", "u00", "f00", "g01", "u01", "f01", "b00", "ds.go", "g10", "u10", "f10",
    "g11", "u11", "f11", "b10", "b11", "t1", "t0", "ds.r", "cs", "ds.l", "gr1a", "gr1b", "s1z.go",
    "s1y.go", "gr0a", "gr0b", "s0z.go", "s0y.go", "ds.far", "bn", "t2", "dx.go", "fd0", "s1y.r",
    "s1y.l", "s1z.r", "fd1", "gr2a", "dx.r", "dx.l", "gr2b", "s0y.r", "s0y.l", "dg", "s1z.far",
    "s1z.k", "dx.near", "s0z.r", "s1y.far", "s1y.k", "dx.far", "dk", "s0y.far", "s0y.k",
    "s0z.far", "s0z.k",
)


def fold_view(ref, me, lead, axis, row, rows, cut):
    head = (ALL,) * lead

    def view(slot, part):
        start, size = row, rows
        if part == 0:
            size = cut
        if part == 1:
            start, size = row + cut, rows - cut
        if axis == "y":
            where = (ALL, slot, ALL)
        else:
            where = (lax.rem(slot, 2), ALL, lax.div(slot, 2))
        return ref.at[head + where + (pl.ds(start, size), ALL)]

    return view


def kernel_feed(
    h_in, cot_in, mlp_in, y_hbm, gains_hbm,
    part_out, dattn_out, fold_y_out, fold_z_out, down_out, dy_hbm, gain_hbm,
    y_in, gains_in, dy_out, gain_out,
    w_mlp, h_two, cot, gate_s, up_s, act_s, d_gate, d_up, act, flipped, flipped_far,
    h_far, cot_far, part, near_left, near_right, whole_left, whole_right, d_attn, out_part,
    *rest,
):
    bufs, (send, recv, local) = list(rest[:-3]), rest[-3:]
    bufs = [tuple(bufs[a:b]) for a, b in ((0, 4), (4, 7), (7, 11), (11, 14))]
    me = place()
    wire = Wire(send, recv, local)
    parts = {}

    def load(zl):
        for which in range(3):
            parts[which, zl] = wire.move(mlp_in.at[which, zl], w_mlp.at[which, zl])

    loads = [wire.move(h_in, h_two)]
    load(0)
    loads.append(wire.move(cot_in, cot))
    greet(me, False)
    plan = Plan()
    at = types.SimpleNamespace()
    kept = []

    def keep(source, target):
        kept.append(wire.move(source, target))

    def whole(which, zl):
        return jnp.concatenate(
            [
                w_mlp[which, zl, y, zh, core]
                for y in range(4)
                for zh in range(2)
                for core in range(2)
            ],
            axis=1,
        )

    def share(source, target):
        return [
            wire.put(
                source.at[:, :, pl.ds(pl.multiple_of((block * 2 + 1 - me.core) * 128, 128), 128)],
                target.at[block],
                sibling(me),
            )
            for block in range(8)
        ]

    def share_h():
        at.h_puts = share(h_two, h_far)

    def share_cot():
        at.cot_puts = share(cot, cot_far)

    one, far, three = rem4(me.x + 1), rem4(me.x + 2), rem4(me.x + 3)
    batches = ((far, one), (three, me.x))

    def rows_of_batch(ref, batch):
        return jnp.concatenate([ref[slot] for slot in batches[batch]], axis=0)

    def gate(batch, zl):
        def run():
            gate_s[...] = dot_nt(rows_of_batch(h_two, batch), whole(0, zl))

        return run

    def up(batch, zl):
        def run():
            up_s[...] = dot_nt(rows_of_batch(h_two, batch), whole(1, zl))

        return run

    def forward(batch, zl):
        def inner(index, carry):
            place_of, rest = lax.div(index, 4), lax.rem(index, 4)
            first, second = batches[batch]
            slot = first + place_of * (second - first)
            source = pl.ds(pl.multiple_of(index * 32, 32), 32)
            span = pl.ds(pl.multiple_of(rest * 32, 32), 32)
            gate, up, d_act = gate_s[source, :], up_s[source, :], act_s[source, :]
            sigma = 1.0 / (1.0 + jnp.exp(-gate))
            act[zl, slot, span, :] = (gate * sigma * up).astype(BF)
            d_gate[zl, slot, span, :] = (
                d_act * up * sigma * (1.0 + gate * (1.0 - sigma))
            ).astype(BF)
            d_up[zl, slot, span, :] = (d_act * gate * sigma).astype(BF)
            return carry

        def run():
            act_s[...] = dot_nt(rows_of_batch(cot, batch), whole(2, zl))
            lax.fori_loop(0, 8, inner, 0)

        return run

    def back_h(batch):
        def body(block, carry):
            y, zh = lax.div(block, 2), lax.rem(block, 2)
            total = None
            for which, left in ((0, d_gate), (1, d_up)):
                for zl in range(2):
                    weight = jnp.concatenate(
                        [w_mlp[which, zl, y, zh, 0], w_mlp[which, zl, y, zh, 1]], axis=1
                    )
                    rows = jnp.concatenate([left[zl, slot] for slot in batches[batch]], axis=0)
                    term = dot_nn(rows, weight)
                    total = term if total is None else total + term
            result = total.astype(BF)
            column = pl.ds(pl.multiple_of(block * 256, 256), 256)
            for index, slot in enumerate(batches[batch]):
                part[slot, :, column] = result[index * 128 : index * 128 + 128]
            return carry

        return body

    def add(target, term):
        add_into(target, [term])

    total = RingSum(
        wire, me, "x", columns_of(part), near_left, near_right, whole_left, whole_right,
        split_columns, add,
    )

    def back_first(half):
        def run():
            lax.fori_loop(half * 4, half * 4 + 4, back_h(0), 0)
            total.start_near(half)
            if half:
                total.start_whole(1)

        return run

    def back_second(half):
        def run():
            lax.fori_loop(half * 4, half * 4 + 4, back_h(1), 0)
            if half == 0:
                total.start_whole(0)

        return run

    plan.add("hs", share_h, lambda: [loads[0]], rank=3)
    plan.add("cs", share_cot, lambda: [loads[1]], rank=3)
    def load_rest():
        load(1)
        at.late = [wire.move(y_hbm, y_in), wire.move(gains_hbm, gains_in)]

    plan.add("l2", load_rest, lambda: [loads[0], parts[0, 0], parts[1, 0]], rank=0)
    before = ("l2",)
    for batch in range(2):
        for zl in range(2):
            name = "%d%d" % (batch, zl)
            plan.add("g" + name, gate(batch, zl), lambda zl=zl: [loads[0], parts[0, zl]], before, 2)
            plan.add("u" + name, up(batch, zl), lambda zl=zl: [parts[1, zl]], ("g" + name,), 2)
            plan.add(
                "f" + name, forward(batch, zl), lambda zl=zl: [loads[1], parts[2, zl]], ("u" + name,), 2
            )
            before = ("f" + name,)
        if batch == 0:
            plan.add("b00", back_first(0), after=before, rank=2)
            plan.add("ds.go", back_first(1), after=("b00",), rank=2)
            before = ("ds.go",)
    plan.add("b10", back_second(0), after=before, rank=2)
    plan.add("b11", back_second(1), after=("b10",), rank=2)
    total.plan(plan, "ds", (), 0, go=False)
    plan.steps["ds.l"].after += ("b11",)
    plan.steps["ds.far"].after += ("b10",)

    at.far = {}

    def turn_over(which, source):
        def run():
            for zl in range(2):
                flipped[which, zl] = source[zl].reshape(512, UNITS).T
            at.far[which] = wire.put(flipped.at[which], flipped_far.at[which], sibling(me))

        return run

    for which, source in enumerate((d_gate, d_up, act)):
        plan.add("t%d" % which, turn_over(which, source), after=("b11",), rank=2 + which * 0.2)

    def forward_down(block, carry):
        y, zh = lax.div(block, 2), lax.rem(block, 2)
        result = None
        for zl in range(2):
            weight = jnp.concatenate([w_mlp[2, zl, y, zh, 0], w_mlp[2, zl, y, zh, 1]], axis=1)
            term = dot_nn(act[zl].reshape(512, UNITS), weight)
            result = term if result is None else result + term
        out_part[:, :, pl.ds(pl.multiple_of(block * 256, 256), 256)] = result.astype(BF).reshape(4, 128, 256)
        return carry

    def down_rest():
        lax.fori_loop(4, 8, forward_down, 0)
        keep(out_part, part_out)

    plan.add("fd0", lambda: lax.fori_loop(0, 4, forward_down, 0), after=("t2",), rank=4)
    plan.add("fd1", down_rest, after=("fd0",), rank=4)

    def grad(which, rows, rows_far):
        def body(index, carry):
            zl, pair = lax.div(index, 2), lax.rem(index, 2)
            mine = jnp.concatenate(
                [
                    rows[:, :, pl.ds(pl.multiple_of(((pair * 4 + k) * 2 + me.core) * 128, 128), 128)]
                    .reshape(512, 128)
                    for k in range(4)
                ],
                axis=1,
            )
            other = jnp.concatenate(
                [rows_far[pair * 4 + k].reshape(512, 128) for k in range(4)], axis=1
            )
            result = dot_nn(flipped[which, zl], mine) + dot_nn(flipped_far[which, zl], other)
            result = result.astype(BF)
            for k in range(4):
                w_mlp[which, zl, pair * 2 + k // 2, k % 2, 0] = result[:, k * 128 : k * 128 + 128]
            return carry

        return body

    sums = []

    def start_sums(which):
        ref = w_mlp.at[which, :, :, :, 0]
        pair = [
            RingSum(wire, me, "y", fold_view(ref, me, 0, "y", 0, SUM_Y, SUM_CUT), *bufs[2 * which],
                    split_rows(SUM_CUT), add),
            PairSum(wire, me, fold_view(ref, me, 0, "z", SUM_Y, UNITS - SUM_Y, 0),
                    *bufs[2 * which + 1], add),
        ]
        for item, out, axis in zip(pair, (fold_y_out, fold_z_out), "yz"):
            name = "s%d%s" % (which, axis)
            item.plan(plan, name, ("gr%db" % which,), 1)
            plan.add(name + ".k", close_sum(item, out.at[which]), after=(name + ".far",), rank=3)

    def close_sum(item, out):
        def run():
            mine = item.part(item.at, None)
            add_into(mine, list(item.whole))
            keep(mine, out)

        return run

    rows_of_step = ((h_two, h_far), (h_two, h_far), (cot, cot_far))
    for which in range(3):
        body = grad(which, *rows_of_step[which])

        def waits(which=which):
            return [at.far[which]] + (at.cot_puts if which == 2 else at.h_puts)

        before = ("t%d" % which, "cs", "hs") + (("fd1",) if which == 2 else ())
        plan.add("gr%da" % which, lambda body=body: lax.fori_loop(0, 2, body, 0), waits, before, 3)
        plan.add(
            "gr%db" % which, lambda body=body: lax.fori_loop(2, 4, body, 0),
            after=("gr%da" % which,), rank=3,
        )
        if which < 2:
            start_sums(which)
    plan.add("dg", lambda: keep(w_mlp.at[2, :, :, :, 0], down_out), after=("gr2b",), rank=2)

    def back_norm(index, carry):
        span = pl.ds(pl.multiple_of(index * 16, 16), 16)
        d_h = (
            part[me.x, span, :].astype(F32)
            + whole_left[span, :].astype(F32)
            + whole_right[span, :].astype(F32)
        )
        value = y_in[span, :]
        scale = lax.rsqrt(jnp.mean(value * value, axis=-1, keepdims=True) + EPS)
        normed = value * scale
        e_two = d_h * gains_in[1:2, :]
        inner = jnp.mean(e_two * normed, axis=-1, keepdims=True)
        d_y = cot[me.x, span, :].astype(F32) + scale * (e_two - normed * inner)
        dy_out[span, :] = d_y
        d_attn[me.x, span, :] = d_y.astype(BF)
        return carry + jnp.sum(d_h * normed, axis=0, keepdims=True)

    def back_all():
        gain_out[...] = lax.fori_loop(0, 8, back_norm, jnp.zeros((1, D), F32))
        keep(dy_out, dy_hbm)
        keep(gain_out, gain_hbm)

    plan.add("bn", back_all, lambda: at.late, ("ds.far",), 0)
    Ring(wire, me, "x", rows_of(d_attn)).plan(plan, "dx", ("bn",), 0)
    plan.add("dk", lambda: keep(d_attn, dattn_out), after=("dx.far",), rank=0)
    plan.go(ORDER_FEED)
    for copy in kept:
        copy.wait()
    wire.drain()


def fold_shapes(lead, count, rows, cut, columns):
    return [
        pltpu.VMEM((*lead, *count, cut, columns), BF),
        pltpu.VMEM((*lead, *count, rows - cut, columns), BF),
        pltpu.VMEM((*lead, *count, rows, columns), BF),
        pltpu.VMEM((*lead, *count, rows, columns), BF),
    ]


def call_feed(h_two, cot, mlp, y_one, gains):
    shape = jax.ShapeDtypeStruct
    bufs = (
        fold_shapes((), (2, 2), SUM_Y, SUM_CUT, 128)
        + [pltpu.VMEM((4, UNITS - SUM_Y, 128), BF)] * 3
    ) * 2
    return pl.pallas_call(
        kernel_feed,
        name="feed",
        in_specs=[anywhere()] * 5,
        out_specs=[anywhere()] * 7,
        out_shape=[
            shape((4, 128, D), BF),
            shape((4, 128, D), BF),
            shape((2, 2, 2, SUM_Y, 128), BF),
            shape((2, 4, UNITS - SUM_Y, 128), BF),
            shape((2, 4, 2, UNITS, 128), BF),
            shape((128, D), F32),
            shape((1, D), F32),
        ],
        scratch_shapes=[
            pltpu.VMEM((128, D), F32),
            pltpu.VMEM((8, D), F32),
            pltpu.VMEM((128, D), F32),
            pltpu.VMEM((1, D), F32),
            pltpu.VMEM((3, 2, 4, 2, 2, UNITS, 128), BF),
            pltpu.VMEM((4, 128, D), BF),
            pltpu.VMEM((4, 128, D), BF),
            pltpu.VMEM((256, UNITS), F32),
            pltpu.VMEM((256, UNITS), F32),
            pltpu.VMEM((256, UNITS), F32),
            pltpu.VMEM((2, 4, 128, UNITS), BF),
            pltpu.VMEM((2, 4, 128, UNITS), BF),
            pltpu.VMEM((2, 4, 128, UNITS), BF),
            pltpu.VMEM((3, 2, UNITS, 512), BF),
            pltpu.VMEM((3, 2, UNITS, 512), BF),
            pltpu.VMEM((8, 4, 128, 128), BF),
            pltpu.VMEM((8, 4, 128, 128), BF),
            pltpu.VMEM((4, 128, D), BF),
            pltpu.VMEM((128, D // 2), BF),
            pltpu.VMEM((128, D // 2), BF),
            pltpu.VMEM((128, D), BF),
            pltpu.VMEM((128, D), BF),
            pltpu.VMEM((4, 128, D), BF),
            pltpu.VMEM((4, 128, D), BF),
        ]
        + bufs
        + [
            pltpu.SemaphoreType.DMA((100,)),
            pltpu.SemaphoreType.DMA((100,)),
            pltpu.SemaphoreType.DMA((24,)),
        ],
        compiler_params=pltpu.CompilerParams(
            collective_id=1, has_side_effects=True, vmem_limit_bytes=VMEM_BYTES
        ),
    )(h_two, cot, mlp, y_one, gains)
BACK_GROUPS = (3, 4, 4, 3, 3, 4, 4, 3, 3, 4, 4, 3, 3, 4)
ORDER_BACK = (
    "bias", "l2", "dh", "os.go", "l3", "my.b.go", "ba0", "wy.a.go", "ba2", "my.b.r", "wz.a.go",
    "mz.b.go", "bh0", "bh1", "wy.a.r", "mz.b.r", "wz.a.r", "wy.a.l", "gq0", "gq1", "qy.a.go",
    "qz.a.go", "as", "wy.a.far", "ax", "dl0", "mx", "my.b.far", "my.k", "dn1", "mz.b.l", "ht",
    "os.l", "os.r", "go", "dl1", "qy.a.l", "mz.", "az", "qy.a.r", "qz.a.r", "oz.a.go", "wz.a.far",
    "oy.a.go", "wy.b.go", "dn0", "ds.go", "ds.l", "mz.b.far", "mz.k", "oz.a.r", "os.far", "fo",
    "my.", "ay", "qy.a.far", "qy.b.go", "wy.b.r", "oy.a.l", "oy.a.r", "ds.r", "wz.b.go", "m.",
    "a.", "qz.a.far", "qz.b.go", "qy.b.r", "oy.a.far", "oy.b.go", "oz.a.far", "oz.b.go", "wz.b.r",
    "wz.b.l", "qz.b.r", "gk", "wy.b.far", "wy.k", "qz.b.l", "oz.b.r", "oy.b.r", "oz.b.l",
    "ds.far", "bn", "wz.b.far", "qy.b.far", "qy.k", "wz.k", "qz.b.far", "qz.k", "oz.b.far",
    "oz.k", "oy.b.far", "oy.k",
)
O_Y, O_CUT, O_REST = 192, 96, 32
Q_Y, Q_CUT, Q_REST = 80, 48, 16
DN_Y, DN_CUT, DN_REST = 448, 224, 128


class Fold:
    def __init__(self, wire, me, cut, view_one, axes, bufs, view_two, bufs_two):
        def add(target, term):
            add_into(target, [term])

        self.wire, self.me, self.add, self.split = wire, me, add, split_rows(cut)
        self.one = None
        if view_one is not None:
            self.one = self.sum(axes[0], view_one, bufs)
        self.two = self.sum(axes[1], view_two, bufs_two)

    def sum(self, axis, view, bufs):
        if axis == "z":
            return PairSum(self.wire, self.me, view, *bufs, self.add)
        return RingSum(self.wire, self.me, "y", view, *bufs, self.split, self.add)

    def turn(self):
        add_into(self.one.part(self.one.at, None), list(self.one.whole))
        self.two.start()

    def close(self, result, keep):
        add_into(self.two.part(self.two.at, None), list(self.two.whole), result)
        keep()

    def plan(self, plan, name, waits, after, rank, result, keep):
        if self.one is None:
            self.two.plan(plan, name + ".b", after, rank)
            plan.steps[name + ".b.go"].waits = waits
        else:
            self.one.plan(plan, name + ".a", after, rank)
            plan.steps[name + ".a.go"].waits = waits
            self.two.plan(plan, name + ".b", (name + ".a.far",), rank)
            plan.steps[name + ".b.go"].run = self.turn
        plan.add(name + ".k", lambda: self.close(result, keep), after=(name + ".b.far",), rank=rank + 0.5)


def crossed_view(ref, me, lead, axis, row, rows, cut):
    head = (ALL,) * lead

    def view(slot, part):
        start, size = row, rows
        if part == 0:
            size = cut
        if part == 1:
            start, size = row + cut, rows - cut
        if axis == "z":
            where = (lax.rem(slot, 2), me.y, lax.div(slot, 2))
        else:
            where = (me.zl, slot, me.zh)
        return ref.at[head + where + (pl.ds(start, size), ALL)]

    return view


def held_view(ref, lead, axis, rows, cut):
    head = (ALL,) * lead

    def view(slot, part):
        start, size = 0, rows
        if part == 0:
            size = cut
        if part == 1:
            start, size = cut, rows - cut
        where = (lax.rem(slot, 2), lax.div(slot, 2)) if axis == "z" else (slot,)
        return ref.at[head + where + (pl.ds(start, size), ALL)]

    return view


def kernel_back(
    start_in, tokens_hbm, dattn_hbm, part_hbm, qkv_hbm, wo_hbm, query_hbm, keys_hbm, values_hbm,
    heads_hbm, lse_hbm, turned_hbm, tables_hbm, gains_hbm, y_hbm, dy_hbm, gain_hbm, fold_y_hbm,
    fold_z_hbm, down_hbm,
    result_hbm, grad_tokens_hbm, g_qkv_hbm, g_o_hbm, g_mlp_hbm, g_gains_hbm,
    query_in, keys_in, values_in, heads_in, lse_in, gains_in, y_in, dy_in, gain_in,
    result_out, tokens_out, g_qkv_out, g_o_out, g_mlp_out, gains_out,
    w_qkv, w_o, d_attn, out_part, tables, bias, tok, turned, d_heads, d_query, d_keys, d_values,
    d_query_far, d_keys_far, d_values_far, sum_keys, sum_values, heads_t, heads_t_far, attn_far,
    d_h, far_one, side_left, side_right, last_z,
    near_left, near_right, whole_left, whole_right,
    out_near_left, out_near_right, out_whole_left, out_whole_right,
    fold_y, fold_z, g_down, gain_x, gain_z, gain_c, along_s, along_a, along_b, along_c, gain_t, along_t,
    *rest,
):
    bufs, (send, recv, local) = list(rest[:-3]), rest[-3:]
    groups = []
    for size in BACK_GROUPS:
        groups.append(tuple(bufs[:size]))
        bufs = bufs[size:]
    me = place()
    wire = Wire(send, recv, local)
    loads = {}

    def load(*items):
        for name, source, target in items:
            loads[name] = wire.move(source, target)

    def load_second():
        load(
            ("fold_y", fold_y_hbm, fold_y),
            ("fold_z", fold_z_hbm, fold_z),
            ("gain", gain_hbm, gain_in),
            ("heads", heads_hbm, heads_in),
            ("down", down_hbm, g_down),
        )

    def load_third():
        load(
            ("qkv", qkv_hbm, w_qkv),
            ("turned", turned_hbm, turned),
            ("y", y_hbm, y_in),
            ("dy", dy_hbm, dy_in),
            ("tok", tokens_hbm, tok),
            ("gains", gains_hbm, gains_in),
        )

    load(
        ("attn", dattn_hbm, d_attn),
        ("o", wo_hbm, w_o),
        ("query", query_hbm, query_in),
        ("keys", keys_hbm, keys_in),
        ("values", values_hbm, values_in),
        ("lse", lse_hbm, lse_in),
        ("tables", tables_hbm.at[me.zl], tables),
        ("part", part_hbm, out_part),
    )
    kept = []

    def keep(source, target):
        kept.append(wire.move(source, target))

    greet(me, True)
    plan = Plan()
    at = types.SimpleNamespace()
    one, far, three = rem4(me.x + 1), rem4(me.x + 2), rem4(me.x + 3)
    right, left = near(me, "x", 1), near(me, "x", 3)

    def add(target, term):
        add_into(target, [term])

    def loaded(*names):
        return lambda: [loads[name] for name in names]

    def share_attn():
        at.attn = [
            wire.put(
                d_attn.at[:, :, pl.ds(pl.multiple_of((block * 2 + 1 - me.core) * 128, 128), 128)],
                attn_far.at[block],
                sibling(me),
            )
            for block in range(8)
        ]

    def share_heads():
        heads_t[...] = heads_in[...].T
        at.heads = wire.put(heads_t, heads_t_far, sibling(me))

    plan.add("l2", load_second, loaded("attn", "o"), rank=0)
    plan.add("l3", load_third, loaded("query", "keys", "values", "lse", "tables"), ("l2",), 0)
    plan.add("as", share_attn, loaded("attn"), rank=1.5)
    plan.add("ht", share_heads, loaded("heads"), ("l2",), 1.5)

    total = RingSum(
        wire, me, "x", columns_of(out_part), out_near_left, out_near_right, out_whole_left,
        out_whole_right, split_columns, add,
    )
    total.plan(plan, "os", (), 1)
    plan.steps["os.go"].waits = loaded("part")

    def finish_out(index, carry):
        span = pl.ds(pl.multiple_of(index * 16, 16), 16)
        result_out[span, :] = (
            y_in[span, :]
            + (
                out_part[me.x, span, :].astype(F32)
                + out_whole_left[span, :].astype(F32)
                + out_whole_right[span, :].astype(F32)
            )
        ).astype(BF)
        return carry

    def finish_result():
        lax.fori_loop(0, 8, finish_out, 0)
        keep(result_out, result_hbm)

    plan.add("fo", finish_result, loaded("y"), ("os.far", "l3"), 6)

    def back_heads(zl, carry):
        weight = jnp.concatenate(
            [w_o[zl, y, zh, c] for y in range(4) for zh in range(2) for c in range(2)], axis=1
        )
        result = dot_nt(d_attn[...].reshape(512, D), weight).astype(BF)
        d_heads[zl * 2] = result[:, 0:HD]
        d_heads[zl * 2 + 1] = result[:, HD : 2 * HD]
        return carry

    plan.add("dh", lambda: lax.fori_loop(0, 2, back_heads, 0), loaded("attn", "o"), rank=2)
    plan.add("bias", lambda: fill_bias(bias, me, start_in[0]), rank=1)

    def back_attend(head, carry):
        for half, pairs in ((1, 4), (0, 3)):
            span = pairs * 256
            rows = slice(half * 256, half * 256 + 256)
            key = keys_in[head, 0:pairs].reshape(span, HD)
            value = values_in[head, 0:pairs].reshape(span, HD)
            query, d_head = query_in[head, rows, :], d_heads[head, rows, :]
            scores = dot_nt(key, query) * SCALE + bias[0:pairs, :, :, rows].reshape(span, 256)
            probs = jnp.exp(scores - lse_in[head, :, rows])
            d_probs = dot_nt(value, d_head)
            delta = jnp.sum(probs * d_probs, axis=0, keepdims=True)
            d_scores = (probs * (d_probs - delta) * SCALE).astype(BF)
            d_key = dot_nn(d_scores, query)
            d_value = dot_nn(probs.astype(BF), d_head)
            if half == 1:
                sum_keys[...] = d_key
                sum_values[...] = d_value
            else:
                sum_keys[0:span, :] += d_key
                sum_values[0:span, :] += d_value
            raw = dot_tn(key, d_scores).T
            cosine = tables[0, 2 * half : 2 * half + 2, 0].reshape(256, HD)
            sine = tables[1, 2 * half : 2 * half + 2, 0].reshape(256, HD)
            column = pl.ds(pl.multiple_of(head * HD, HD), HD)
            d_query[rows, column] = turn(raw, cosine, -sine).astype(BF)
        cosine, sine = tables[0].reshape(SEQ, HD), tables[1].reshape(SEQ, HD)
        d_keys[:, column] = turn(sum_keys[...], cosine, -sine).astype(BF)
        d_values[:, column] = sum_values[...].astype(BF)
        return carry

    def attend_rest():
        lax.fori_loop(2, 4, back_attend, 0)
        at.grads = [
            wire.put(d_query, d_query_far, sibling(me)),
            wire.put(d_keys, d_keys_far, sibling(me)),
            wire.put(d_values, d_values_far, sibling(me)),
        ]

    plan.add(
        "ba0", lambda: lax.fori_loop(0, 2, back_attend, 0),
        loaded("query", "keys", "values", "lse", "tables"), ("dh", "bias"), 2,
    )
    plan.add("ba2", attend_rest, after=("ba0",), rank=2)

    def back_h(block, carry):
        y, zh = lax.div(block, 2), lax.rem(block, 2)

        def weight(which):
            return jnp.concatenate(
                [w_qkv[which, 0, y, zh].reshape(256, 256), w_qkv[which, 1, y, zh].reshape(256, 256)],
                axis=1,
            )

        column = pl.ds(pl.multiple_of(block * 256, 256), 256)
        both = dot_nt(d_keys[...], weight(1)) + dot_nt(d_values[...], weight(2))
        both = both.reshape(4, 2, 128, 256)
        own = dot_nt(d_query[...], weight(0)).reshape(4, 128, 256) + both[:, 0]
        d_h[:, 0, :, column] = own.astype(BF)
        d_h[:, 1, :, column] = both[:, 1].astype(BF)
        return carry

    own = RingSum(
        wire, me, "x",
        lambda slot, half: d_h.at[slot, 0] if half is None else d_h.at[slot, 0, :, pl.ds(half * 1024, 1024)],
        near_left, near_right, whole_left, whole_right, split_columns, add,
    )
    at.far_z, at.sides, at.last = {}, {}, {}

    def cut(ref, half):
        return ref.at[:, pl.ds(half * 1024, 1024)]

    def back_half(half):
        def run():
            lax.fori_loop(half * 4, half * 4 + 4, back_h, 0)
            at.far_z[half] = wire.put(cut(d_h.at[far, 1], half), cut(far_one, half), partner(me))
            at.sides[half] = [
                wire.put(cut(d_h.at[one, 1], half), cut(side_left, half), right),
                wire.put(cut(d_h.at[three, 1], half), cut(side_right, half), left),
            ]
            own.start_whole(half)

        return run

    def near_half(half):
        def run():
            add_into(cut(d_h.at[far, 0], half), [cut(far_one, half)])
            own.start_near(half)

        return run

    def last_half(half):
        def run():
            add_into(cut(d_h.at[me.x, 1], half), [cut(side_left, half), cut(side_right, half)])
            at.last[half] = wire.put(cut(d_h.at[me.x, 1], half), cut(last_z, half), partner(me))

        return run

    plan.add("bh0", back_half(0), loaded("qkv"), ("ba2", "l3"), 2)
    plan.add("bh1", back_half(1), after=("bh0",), rank=2)
    for half in range(2):
        name = "%d" % half
        plan.add("dn" + name, near_half(half), lambda half=half: [at.far_z[half]], ("bh" + name,), 0)
        plan.add("dl" + name, last_half(half), lambda half=half: at.sides[half], ("bh" + name,), 0.5)
    plan.add("ds.go", lambda: None, after=("dn0", "dn1"), rank=0)
    own.plan(plan, "ds", (), 0, go=False)

    def grad_o(index, carry):
        zl, y = lax.div(index, 4), lax.rem(index, 4)
        mine = jnp.concatenate(
            [
                d_attn[:, :, pl.ds(pl.multiple_of(((y * 2 + zh) * 2 + me.core) * 128, 128), 128)]
                .reshape(512, 128)
                for zh in range(2)
            ],
            axis=1,
        )
        other = jnp.concatenate(
            [attn_far[y * 2 + zh].reshape(512, 128) for zh in range(2)], axis=1
        )
        rows = pl.ds(pl.multiple_of(zl * 256, 256), 256)
        result = (dot_nn(heads_t[rows, :], mine) + dot_nn(heads_t_far[rows, :], other)).astype(BF)
        w_o[zl, y, 0, 0] = result[:, 0:128]
        w_o[zl, y, 1, 0] = result[:, 128:256]
        return carry

    plan.add("go", lambda: lax.fori_loop(0, 8, grad_o, 0), lambda: [at.heads, *at.attn], ("as", "ht", "dh"), 3)

    def blocks(which, pair):
        return turned[which, pl.ds(pair * 4, 4)].reshape(512, SEQ)

    def own_rows(value):
        return jnp.concatenate([value[:, i * 256 : i * 256 + 128] for i in range(4)], axis=1)

    def grad_qkv(index, carry):
        zl, pair = lax.div(index, 2), lax.rem(index, 2)
        column = pl.ds(pl.multiple_of(zl * 256, 256), 256)
        mine, other = blocks(0, pair), blocks(1, pair)
        query_grad = dot_nn(own_rows(mine), d_query[:, column])
        query_grad = query_grad + dot_nn(own_rows(other), d_query_far[:, column])
        key_grad = dot_nn(mine, d_keys[:, column]) + dot_nn(other, d_keys_far[:, column])
        value_grad = dot_nn(mine, d_values[:, column]) + dot_nn(other, d_values_far[:, column])
        along = jnp.where(zl == 0, 0.0, along_s[pair])
        for which, result in enumerate((query_grad, key_grad, value_grad)):
            weight = w_qkv[which, zl, pl.ds(pair * 2, 2), :, me.core].reshape(512, 256)
            product = weight.astype(F32) * result
            along = along + product[:, 0:128] + product[:, 128:256]
            w_qkv[which, zl, pl.ds(pair * 2, 2), :, 0] = result.astype(BF).reshape(2, 2, 128, 256)
        along_s[pair] = along
        return carry

    plan.add(
        "gq0", lambda: lax.fori_loop(0, 2, grad_qkv, 0),
        lambda: [loads["turned"], *at.grads], ("bh1",), 3,
    )
    plan.add("gq1", lambda: lax.fori_loop(2, 4, grad_qkv, 0), after=("gq0",), rank=3)

    g_qkv, g_o = w_qkv.at[:, :, :, :, 0], w_o.at[:, :, :, 0]
    rest = UNITS - SUM_Y
    for name, fold, waits, after, rank, result, target, where in (
        ("my", Fold(wire, me, 0, None, ("y", "z"), None, held_view(fold_y, 1, "z", SUM_Y, 0), groups[0]),
         loaded("fold_y"), ("l2",), 1.2, g_mlp_out, g_mlp_hbm, (pl.ds(0, 2), pl.ds(0, SUM_Y), ALL)),
        ("mz", Fold(wire, me, 144, None, ("z", "y"), None, held_view(fold_z, 1, "y", rest, 144), groups[1]),
         loaded("fold_z"), ("l2",), 1.2, g_mlp_out, g_mlp_hbm, (pl.ds(0, 2), pl.ds(SUM_Y, UNITS - SUM_Y), ALL)),
        ("oy", Fold(wire, me, O_CUT, fold_view(g_o, me, 0, "y", 0, O_Y, O_CUT), ("y", "z"), groups[2],
                    crossed_view(g_o, me, 0, "z", 0, O_Y, 0), groups[3]),
         tuple, ("go",), 1.4, g_o_out, g_o_hbm, (pl.ds(0, O_Y), ALL)),
        ("oz", Fold(wire, me, O_REST, fold_view(g_o, me, 0, "z", O_Y, 256 - O_Y, 0), ("z", "y"), groups[4],
                    crossed_view(g_o, me, 0, "y", O_Y, 256 - O_Y, O_REST), groups[5]),
         tuple, ("go",), 1.4, g_o_out, g_o_hbm, (pl.ds(O_Y, 256 - O_Y), ALL)),
        ("qy", Fold(wire, me, Q_CUT, fold_view(g_qkv, me, 1, "y", 0, Q_Y, Q_CUT), ("y", "z"), groups[6],
                    crossed_view(g_qkv, me, 1, "z", 0, Q_Y, 0), groups[7]),
         tuple, ("gq1",), 1, g_qkv_out, g_qkv_hbm, (ALL, pl.ds(0, Q_Y), ALL)),
        ("qz", Fold(wire, me, Q_REST, fold_view(g_qkv, me, 1, "z", Q_Y, 128 - Q_Y, 0), ("z", "y"),
                    groups[8], crossed_view(g_qkv, me, 1, "y", Q_Y, 128 - Q_Y, Q_REST), groups[9]),
         tuple, ("gq1",), 1, g_qkv_out, g_qkv_hbm, (ALL, pl.ds(Q_Y, 128 - Q_Y), ALL)),
        ("wy", Fold(wire, me, DN_CUT, fold_view(g_down, me, 0, "y", 0, DN_Y, DN_CUT), ("y", "z"),
                    groups[10], crossed_view(g_down, me, 0, "z", 0, DN_Y, 0), groups[11]),
         loaded("down"), ("l2",), 1.3, g_mlp_out, g_mlp_hbm, (2, pl.ds(0, DN_Y), ALL)),
        ("wz", Fold(wire, me, DN_REST, fold_view(g_down, me, 0, "z", DN_Y, UNITS - DN_Y, 0), ("z", "y"),
                    groups[12], crossed_view(g_down, me, 0, "y", DN_Y, UNITS - DN_Y, DN_REST), groups[13]),
         loaded("down"), ("l2",), 1.3, g_mlp_out, g_mlp_hbm, (2, pl.ds(DN_Y, UNITS - DN_Y), ALL)),
    ):
        fold.plan(
            plan, name, waits, after, rank, result.at[where],
            lambda result=result, target=target, where=where: keep(result.at[where], target.at[where]),
        )

    def back_norm(index, carry):
        span = pl.ds(pl.multiple_of(index * 16, 16), 16)
        d_h_one = (
            d_h[me.x, 0, span, :].astype(F32)
            + whole_left[span, :].astype(F32)
            + whole_right[span, :].astype(F32)
            + last_z[span, :].astype(F32)
        )
        value = tok[span, :].astype(F32)
        scale = lax.rsqrt(jnp.mean(value * value, axis=-1, keepdims=True) + EPS)
        normed = value * scale
        e_one = d_h_one * gains_in[0:1, :]
        inner = jnp.mean(e_one * normed, axis=-1, keepdims=True)
        tokens_out[span, :] = (dy_in[span, :] + scale * (e_one - normed * inner)).astype(BF)
        return carry

    def feed_x():
        for block in range(16):
            gain_x[me.x, block : block + 1, :] = gain_in[0:1, block * 128 : block * 128 + 128]
        at.feed = Meet(wire, me, "x", gain_x).copies

    def feed_z():
        gain_z[me.z] = gain_x[0] + gain_x[1] + gain_x[2] + gain_x[3]
        at.feed = Meet(wire, me, "z", gain_z).copies

    def feed_y():
        gain_c[me.core, me.y] = gain_z[0] + gain_z[1] + gain_z[2] + gain_z[3]
        at.feed = MeetCores(wire, me, gain_c).copies

    def feed_all():
        total = gain_c[0, 0]
        for core, y in ((0, 1), (0, 2), (0, 3), (1, 0), (1, 1), (1, 2), (1, 3)):
            total = total + gain_c[core, y]
        gain_t[...] = total
        row = (me.y * 2 + me.zh) * 2 + me.core
        gains_out[1:2, :] = gain_t[pl.ds(row, 1), :]

    plan.add("mx", feed_x, loaded("gain"), ("l2",), 1)
    plan.add("mz.", feed_z, lambda: at.feed, ("mx",), 1)
    plan.add("my.", feed_y, lambda: at.feed, ("mz.",), 1)
    plan.add("m.", feed_all, lambda: at.feed, ("my.",), 1)

    def along_x():
        ones = jnp.ones((8, 128), F32)
        for pair in range(2):
            line = lax.dot_general(
                ones, along_s[pair], (((1,), (1,)), ((), ())), precision=lax.Precision.HIGHEST,
                preferred_element_type=F32,
            )
            for k in range(4):
                along_a[me.x, pair * 4 + k : pair * 4 + k + 1, :] = line[0:1, k * 128 : k * 128 + 128]
        at.along = Meet(wire, me, "x", along_a).copies

    def along_z():
        along_b[me.z] = along_a[0] + along_a[1] + along_a[2] + along_a[3]
        at.along = Meet(wire, me, "z", along_b).copies

    def along_y():
        along_c[me.y] = along_b[0] + along_b[1] + along_b[2] + along_b[3]
        at.along = Meet(wire, me, "y", along_c).copies

    def along_all():
        along_t[...] = along_c[0] + along_c[1] + along_c[2] + along_c[3]
        row = me.y * 2 + me.zh
        column = pl.ds(pl.multiple_of((row * 2 + me.core) * 128, 128), 128)
        gains_out[0:1, :] = along_t[pl.ds(row, 1), :] / gains_in[0:1, column]

    plan.add("ax", along_x, after=("gq1",), rank=1)
    plan.add("az", along_z, lambda: at.along, ("ax",), 1)
    plan.add("ay", along_y, lambda: at.along, ("az",), 1)
    plan.add("a.", along_all, lambda: [*loaded("gains")(), *at.along], ("ay",), 1)
    plan.add("gk", lambda: keep(gains_out, g_gains_hbm), after=("a.", "m."), rank=2)

    def back_all():
        lax.fori_loop(0, 8, back_norm, 0)
        keep(tokens_out, grad_tokens_hbm)

    plan.add(
        "bn", back_all,
        lambda: [*loaded("tok", "dy", "gains")(), at.last[0], at.last[1]], ("ds.far", "dl0", "dl1"), 0,
    )
    plan.go(ORDER_BACK)
    for copy in kept:
        copy.wait()
    wire.drain()


def call_back(starts, tokens, d_attn, out_part, qkv, w_out, query, keys, values, heads, lse, turned,
              tables, gains, y_one, d_y, gain_two, fold_y, fold_z, down):
    shape = jax.ShapeDtypeStruct

    def three(*dims):
        return [pltpu.VMEM(dims, BF)] * 3

    rest = UNITS - SUM_Y
    bufs = (
        three(2, SUM_Y, 128)
        + fold_shapes((2,), (), rest, 144, 128)
        + fold_shapes((), (2, 2), O_Y, O_CUT, 128)
        + three(O_Y, 128)
        + three(4, 256 - O_Y, 128)
        + fold_shapes((), (), 256 - O_Y, O_REST, 128)
        + fold_shapes((3,), (2, 2), Q_Y, Q_CUT, 256)
        + three(3, Q_Y, 256)
        + three(3, 4, 128 - Q_Y, 256)
        + fold_shapes((3,), (), 128 - Q_Y, Q_REST, 256)
        + fold_shapes((), (2, 2), DN_Y, DN_CUT, 128)
        + three(DN_Y, 128)
        + three(4, UNITS - DN_Y, 128)
        + fold_shapes((), (), UNITS - DN_Y, DN_REST, 128)
    )
    return pl.pallas_call(
        kernel_back,
        name="back",
        in_specs=[pl.BlockSpec(memory_space=pltpu.SMEM)] + [anywhere()] * 19,
        out_specs=[anywhere()] * 6,
        out_shape=[
            shape((128, D), BF),
            shape((128, D), BF),
            shape((3, 128, 256), F32),
            shape((256, 128), F32),
            shape((3, UNITS, 128), F32),
            shape((2, 128), F32),
        ],
        scratch_shapes=[
            pltpu.VMEM((4, 512, HD), BF),
            pltpu.VMEM((4, 4, 2, 128, HD), BF),
            pltpu.VMEM((4, 4, 2, 128, HD), BF),
            pltpu.VMEM((512, 512), BF),
            pltpu.VMEM((4, 1, 512), F32),
            pltpu.VMEM((8, D), F32),
            pltpu.VMEM((128, D), F32),
            pltpu.VMEM((128, D), F32),
            pltpu.VMEM((1, D), F32),
            pltpu.VMEM((128, D), BF),
            pltpu.VMEM((128, D), BF),
            pltpu.VMEM((3, 128, 256), F32),
            pltpu.VMEM((256, 128), F32),
            pltpu.VMEM((3, UNITS, 128), F32),
            pltpu.VMEM((2, 128), F32),
            pltpu.VMEM((3, 2, 4, 2, 2, 128, 256), BF),
            pltpu.VMEM((2, 4, 2, 2, 256, 128), BF),
            pltpu.VMEM((4, 128, D), BF),
            pltpu.VMEM((4, 128, D), BF),
            pltpu.VMEM((2, 4, 2, 128, HD), F32),
            pltpu.VMEM((4, 2, 128, 512), F32),
            pltpu.VMEM((128, D), BF),
            pltpu.VMEM((2, 8, 128, SEQ), BF),
            pltpu.VMEM((4, 512, HD), BF),
            pltpu.VMEM((512, 512), BF),
            pltpu.VMEM((SEQ, 512), BF),
            pltpu.VMEM((SEQ, 512), BF),
            pltpu.VMEM((512, 512), BF),
            pltpu.VMEM((SEQ, 512), BF),
            pltpu.VMEM((SEQ, 512), BF),
            pltpu.VMEM((SEQ, HD), F32),
            pltpu.VMEM((SEQ, HD), F32),
            pltpu.VMEM((512, 512), BF),
            pltpu.VMEM((512, 512), BF),
            pltpu.VMEM((8, 4, 128, 128), BF),
            pltpu.VMEM((4, 2, 128, D), BF),
        ]
        + [pltpu.VMEM((128, D), BF)] * 4
        + [
            pltpu.VMEM((128, D // 2), BF),
            pltpu.VMEM((128, D // 2), BF),
            pltpu.VMEM((128, D), BF),
            pltpu.VMEM((128, D), BF),
        ]
        * 2
        + [
            pltpu.VMEM((2, 2, 2, SUM_Y, 128), BF),
            pltpu.VMEM((2, 4, UNITS - SUM_Y, 128), BF),
            pltpu.VMEM((2, 4, 2, UNITS, 128), BF),
            pltpu.VMEM((4, 16, 128), F32),
            pltpu.VMEM((4, 16, 128), F32),
            pltpu.VMEM((2, 4, 16, 128), F32),
            pltpu.VMEM((2, 512, 128), F32),
            pltpu.VMEM((4, 8, 128), F32),
            pltpu.VMEM((4, 8, 128), F32),
            pltpu.VMEM((4, 8, 128), F32),
            pltpu.VMEM((16, 128), F32),
            pltpu.VMEM((8, 128), F32),
        ]
        + bufs
        + [
            pltpu.SemaphoreType.DMA((140,)),
            pltpu.SemaphoreType.DMA((140,)),
            pltpu.SemaphoreType.DMA((40,)),
        ],
        compiler_params=pltpu.CompilerParams(
            collective_id=2, has_side_effects=True, vmem_limit_bytes=VMEM_BYTES
        ),
    )(starts, tokens, d_attn, out_part, qkv, w_out, query, keys, values, heads, lse, turned,
      tables, gains, y_one, d_y, gain_two, fold_y, fold_z, down)


def kernel_settle(result_in, tokens_in, qkv_in, o_in, mlp_in, gains_in,
                  result, tokens, query, key, value, out, gate, up, down, attn, feed):
    tp = lax.axis_index("tensor")
    result[...] = result_in[...]
    tokens[...] = tokens_in[...]
    for index, target in enumerate((query, key, value)):
        target[...] = qkv_in[index]
    out[...] = o_in[...]
    for index, target in enumerate((gate, up, down)):
        target[...] = mlp_in[index]
    for index, target in enumerate((attn, feed)):
        row = gains_in[index : index + 1, :]
        target[...] = pltpu.roll(row, lax.rem(128 - tp * 16, 128), 1)[:, 0:16]


def call_settle(*arrays):
    shape = jax.ShapeDtypeStruct
    return pl.pallas_call(
        kernel_settle,
        name="settle",
        in_specs=[in_vmem()] * 6,
        out_specs=[in_vmem()] * 11,
        out_shape=[shape((128, D), BF)] * 2
        + [shape((128, 256), F32)] * 3
        + [shape((256, 128), F32)]
        + [shape((UNITS, 128), F32)] * 3
        + [shape((1, 16), F32)] * 2,
        compiler_params=pltpu.CompilerParams(vmem_limit_bytes=VMEM_BYTES),
    )(*arrays)


def on_device(tables, tokens, starts, w_query, w_key, w_value, w_out, w_gate, w_up, w_down,
              gain_attn, gain_mlp, cotangent):
    weights = (w_query, w_key, w_value, w_out, w_gate.T, w_up.T, w_down)
    (qkv, w_o, mlp, cot, turned, query, keys, values, heads, h_two, lse, y_one, gains) = call_attend(
        tokens, cotangent, starts, weights, gain_attn.reshape(1, 16), gain_mlp.reshape(1, 16), tables
    )
    out_part, d_attn, fold_y, fold_z, down, d_y, gain_two = call_feed(h_two, cot, mlp, y_one, gains)
    sums = call_back(
        starts, tokens, d_attn, out_part, qkv, w_o, query, keys, values, heads, lse, turned,
        tables, gains, y_one, d_y, gain_two, fold_y, fold_z, down,
    )
    result, grad_tokens, query, key, value, out, gate, up, down, attn, feed = call_settle(*sums)
    return (
        result, grad_tokens, query, key, value, out, gate.T, up.T, down,
        attn.reshape(16), feed.reshape(16),
    )


def solution(mesh):
    both = ("dp", "tensor")
    rows, wide, tall = P(both, None), P("dp", "tensor"), P("tensor", "dp")
    in_specs = (
        rows, P("dp"), wide, wide, wide, tall, wide, wide, tall, P(both), P(both), rows,
    )
    out_specs = (
        rows, rows, wide, wide, wide, tall, wide, wide, tall, P(both), P(both),
    )
    return jax.shard_map(
        functools.partial(on_device, rope_tables()), mesh=mesh, in_specs=in_specs,
        out_specs=out_specs, check_vma=False,
    )
```

```python
import functools
import math
import types

import jax
import jax.numpy as jnp
import numpy as np
from jax import lax
from jax.experimental import pallas as pl
from jax.experimental.pallas import tpu as pltpu
from jax.sharding import PartitionSpec as P

HD = 128
PIECE = 256
EPS = 1e-05
NEG = -1e30
SCALE = HD ** (-0.5)
D = 2048
SEQ = 1024
UNITS = 688
BF = jnp.bfloat16
F32 = jnp.float32
MESH = pl.DeviceIdType.MESH
VMEM_BYTES = 60 * 1024 * 1024
ALL = slice(None)


def dot_nn(left, right):
    return jnp.dot(left, right, preferred_element_type=F32)


def dot_nt(left, right):
    return lax.dot_general(left, right, (((1,), (1,)), ((), ())), preferred_element_type=F32)


def dot_tn(left, right):
    return lax.dot_general(left, right, (((0,), (0,)), ((), ())), preferred_element_type=F32)


def rem4(value):
    return lax.rem(value, 4)


def place():
    dp = lax.axis_index("dp")
    tp = lax.axis_index("tensor")
    zh = lax.rem(lax.div(dp, 2), 2)
    zl = lax.rem(tp, 2)
    return types.SimpleNamespace(
        y=lax.div(dp, 4), zh=zh, zl=zl, z=zh * 2 + zl, x=lax.div(tp, 2), core=lax.rem(dp, 2)
    )


def device(me, **moved):
    at = types.SimpleNamespace(**{**vars(me), **moved})
    zh, zl = lax.div(at.z, 2), lax.rem(at.z, 2)
    return (at.y * 4 + zh * 2 + at.core, at.x * 2 + zl)


def near(me, axis, step):
    return device(me, **{axis: rem4(getattr(me, axis) + step)})


def sibling(me):
    return device(me, core=1 - me.core)


def partner(me):
    return device(me, z=me.zh * 2 + 1 - me.zl)


def across(me):
    return device(me, z=rem4(me.z + 3 + 2 * me.zl))


def greet(me, wide, meanwhile=()):
    others = [near(me, axis, step) for axis in ("x", "y", "z") for step in (1, 3)] + [sibling(me)]
    if wide:
        others += [near(me, axis, 2) for axis in ("x", "y", "z")]
        others += [crossed(me, step) for step in (1, 2, 3)]
    barrier = pltpu.get_barrier_semaphore()
    for other in others:
        pl.semaphore_signal(barrier, inc=1, device_id=other, device_id_type=MESH)
    for copy in meanwhile:
        copy.wait()
    pl.semaphore_wait(barrier, len(others))


def crossed(me, step):
    return device(me, y=rem4(me.y + step), core=1 - me.core)


class Plan:
    def __init__(self):
        self.steps = {}

    def add(self, name, run, waits=tuple, after=(), rank=5):
        self.steps[name] = types.SimpleNamespace(run=run, waits=waits, after=after, rank=rank)

    def go(self, order):
        assert sorted(order) == sorted(self.steps)
        for name in order:
            step = self.steps[name]
            for copy in step.waits():
                copy.wait_recv()
            step.run()


class Once:
    def __init__(self, copy, remote):
        self.copy, self.remote = copy, remote
        self.received = self.left = False

    def wait_recv(self):
        if not self.received:
            self.received = True
            if self.remote:
                self.copy.wait_recv()
            else:
                self.copy.wait()

    wait = wait_recv

    def wait_send(self):
        if not self.left:
            self.left = True
            self.copy.wait_send()


class Wire:
    def __init__(self, send, recv, local):
        self.send, self.recv, self.local = send, recv, local
        self.used, self.used_local = 0, 0
        self.sent = []

    def put(self, source, target, to):
        index = self.used
        self.used += 1
        assert index < self.send.shape[0]
        copy = pltpu.make_async_remote_copy(
            src_ref=source,
            dst_ref=target,
            send_sem=self.send.at[index],
            recv_sem=self.recv.at[index],
            device_id=to,
            device_id_type=MESH,
        )
        copy.start()
        copy = Once(copy, True)
        self.sent.append(copy)
        return copy

    def move(self, source, target):
        index = self.used_local
        self.used_local += 1
        assert index < self.local.shape[0]
        copy = pltpu.make_async_copy(source, target, self.local.at[index])
        copy.start()
        return Once(copy, False)

    def drain(self):
        for copy in self.sent:
            copy.wait_send()
        self.sent = []


class Ring:
    def __init__(self, wire, me, axis, view):
        self.wire, self.view = wire, view
        self.at = getattr(me, axis)
        self.right, self.left = near(me, axis, 1), near(me, axis, 3)

    def put(self, slot, part, to):
        piece = self.view(slot, part)
        return self.wire.put(piece, piece, to)

    def start(self):
        self.right_one = self.put(self.at, 0, self.right)
        self.left_one = self.put(self.at, 1, self.left)
        self.right_two = self.put(self.at, 1, self.right)
        self.left_two = self.put(self.at, 0, self.left)

    def start_half(self, half):
        if half == 0:
            self.right_one = self.put(self.at, 0, self.right)
            self.left_two = self.put(self.at, 0, self.left)
        else:
            self.left_one = self.put(self.at, 1, self.left)
            self.right_two = self.put(self.at, 1, self.right)

    def plan(self, plan, name, after, rank):
        plan.add(name + ".go", self.start, after=after, rank=rank)
        plan.add(name + ".r", self.relay_right, lambda: [self.right_one], (name + ".go",), rank)
        plan.add(name + ".l", self.relay_left, lambda: [self.left_one], (name + ".go",), rank)
        plan.add(
            name + ".near", lambda: None, lambda: [self.right_two, self.left_two],
            (name + ".r", name + ".l"), rank,
        )
        plan.add(
            name + ".far", lambda: None, lambda: [self.far_right, self.far_left], (name + ".near",), rank
        )

    def relay_right(self):
        self.far_right = self.put(rem4(self.at + 3), 0, self.right)

    def relay_left(self):
        self.far_left = self.put(rem4(self.at + 1), 1, self.left)

    def copies(self):
        return [
            self.right_one, self.left_one, self.right_two, self.left_two, self.far_right, self.far_left
        ]

    def closed(self):
        return rem4(self.at + 3), rem4(self.at + 1)


class Direct:
    def __init__(self, wire, me, view):
        self.wire, self.view, self.me, self.at = wire, view, me, me.z

    def start(self):
        piece = self.view(self.at, None)
        others = (partner(self.me), across(self.me), near(self.me, "z", 2))
        self.copies = [self.wire.put(piece, piece, other) for other in others]

    def plan(self, plan, name, after, rank):
        plan.add(name + ".go", self.start, after=after, rank=rank)
        plan.add(name + ".far", lambda: None, lambda: self.copies, (name + ".go",), rank)


class PairRing:
    def __init__(self, wire, me, view):
        self.wire, self.view, self.me = wire, view, me
        self.at = me.z
        self.mate, self.beyond = me.zh * 2 + 1 - me.zl, rem4(me.z + 3 + 2 * me.zl)

    def put(self, slot, to):
        piece = self.view(slot, None)
        return self.wire.put(piece, piece, to)

    def start(self):
        self.to_mate = self.put(self.at, partner(self.me))
        self.to_beyond = self.put(self.at, across(self.me))

    def plan(self, plan, name, after, rank):
        plan.add(name + ".go", self.start, after=after, rank=rank)
        plan.add(name + ".r", self.relay, lambda: [self.to_mate], (name + ".go",), rank)
        plan.add(name + ".near", lambda: None, lambda: [self.to_beyond], (name + ".r",), rank)
        plan.add(name + ".far", lambda: None, lambda: [self.far], (name + ".near",), rank)

    def relay(self):
        self.far = self.put(self.mate, across(self.me))

    def copies(self):
        return [self.to_mate, self.to_beyond, self.far]

    def closed(self):
        return self.mate, self.beyond


class Meet:
    def __init__(self, wire, me, axis, ref):
        piece = ref.at[getattr(me, axis)]
        self.copies = [wire.put(piece, piece, near(me, axis, step)) for step in (1, 2, 3)]


class MeetCores:
    def __init__(self, wire, me, ref):
        piece = ref.at[me.core, me.y]
        others = [near(me, "y", step) for step in (1, 2, 3)] + [sibling(me)]
        others += [crossed(me, step) for step in (1, 2, 3)]
        self.copies = [wire.put(piece, piece, other) for other in others]


class RingSum:
    def __init__(self, wire, me, axis, part, from_left, from_right, whole_left, whole_right, split, add):
        self.wire, self.part, self.split, self.add = wire, part, split, add
        self.at = getattr(me, axis)
        self.right, self.left = near(me, axis, 1), near(me, axis, 3)
        self.near_bufs = (from_left, from_right)
        self.whole = (whole_left, whole_right)

    def start_near(self, half):
        piece = self.part(rem4(self.at + 2), half)
        to = self.left if half else self.right
        copy = self.wire.put(piece, self.near_bufs[half], to)
        if half:
            self.second = copy
        else:
            self.first = copy

    def start_whole(self, half):
        if half:
            self.right_whole = self.wire.put(
                self.part(rem4(self.at + 1), 1), self.split(self.whole[0], 1), self.right
            )
        else:
            self.left_whole = self.wire.put(
                self.part(rem4(self.at + 3), 0), self.split(self.whole[1], 0), self.left
            )

    def start(self, halves=(0, 1)):
        for half in halves:
            self.start_near(half)
        if 1 in halves:
            self.start_whole(1)
            self.start_whole(0)

    def plan(self, plan, name, after, rank, go=True):
        if go:
            plan.add(name + ".go", self.start, after=after, rank=rank)
        plan.add(name + ".r", self.relay_right, lambda: [self.first], (name + ".go",), rank)
        plan.add(name + ".l", self.relay_left, lambda: [self.second], (name + ".go",), rank)
        plan.add(
            name + ".far",
            lambda: None,
            lambda: [self.left_whole, self.right_whole, self.to_right, self.to_left],
            (name + ".r", name + ".l"),
            rank,
        )

    def relay_right(self):
        after = rem4(self.at + 1)
        self.add(self.part(after, 0), self.near_bufs[0])
        self.to_right = self.wire.put(self.part(after, 0), self.split(self.whole[0], 0), self.right)

    def relay_left(self):
        before = rem4(self.at + 3)
        self.add(self.part(before, 1), self.near_bufs[1])
        self.to_left = self.wire.put(self.part(before, 1), self.split(self.whole[1], 1), self.left)


class PairSum:
    def __init__(self, wire, me, part, from_beyond, for_mate, from_mate, add):
        self.wire, self.me, self.part, self.add = wire, me, part, add
        self.at = me.z
        self.mate, self.beyond = me.zh * 2 + 1 - me.zl, rem4(me.z + 3 + 2 * me.zl)
        self.for_mate, self.whole = for_mate, (from_beyond, from_mate)

    def start(self):
        far = rem4(self.at + 2)
        self.first = self.wire.put(self.part(far, None), self.for_mate, across(self.me))
        self.second = self.wire.put(self.part(self.beyond, None), self.whole[0], across(self.me))

    def plan(self, plan, name, after, rank):
        plan.add(name + ".go", self.start, after=after, rank=rank)
        plan.add(name + ".r", self.relay, lambda: [self.first], (name + ".go",), rank)
        plan.add(
            name + ".far", lambda: None, lambda: [self.second, self.to_mate], (name + ".r",), rank
        )

    def relay(self):
        self.add(self.part(self.mate, None), self.for_mate)
        self.to_mate = self.wire.put(self.part(self.mate, None), self.whole[1], partner(self.me))


def split_columns(ref, half):
    return ref.at[:, pl.ds(half * (D // 2), D // 2)]


def split_rows(cut):
    def split(ref, half):
        rows = ref.shape[-2]
        span = pl.ds(0, cut) if half == 0 else pl.ds(cut, rows - cut)
        return ref.at[(ALL,) * (len(ref.shape) - 2) + (span, ALL)]

    return split


class Spread:
    def __init__(self, wire, me, ref, lead, row, rows, first, cut, cuts=(ALL,), kind=PairRing):
        self.wire, self.me = wire, me
        head = (ALL,) * lead

        def view(y, z, part, low=ALL):
            zl, zh = (low, ALL) if z is None else (lax.rem(z, 2), lax.div(z, 2))
            start, size = row, rows
            if part == 0:
                size = cut
            if part == 1:
                start, size = row + cut, rows - cut
            yy = ALL if y is None else y
            return ref.at[head + (zl, yy, zh, me.core, pl.ds(start, size), ALL)]

        if first == "y":
            self.one = Ring(wire, me, "y", lambda slot, part: view(slot, me.z, part))
            self.twos = [PairRing(wire, me, lambda slot, part: view(None, slot, part))]
        else:
            self.one = kind(wire, me, lambda slot, part: view(me.y, slot, part))
            self.twos = [
                Ring(wire, me, "y", lambda slot, part, low=low: view(slot, None, part, low))
                for low in cuts
            ]

    def plan(self, plan, name, after, turn_after, rank):
        self.one.plan(plan, name + ".a", after, rank)
        self.plan_second(plan, name, (name + ".a.far", *turn_after), rank)

    def plan_second(self, plan, name, done, rank):
        done = list(done)
        self.shared = []
        for index, two in enumerate(self.twos):
            tail = str(index) if len(self.twos) > 1 else ""
            self.plan_two(plan, two, name, tail, tuple(done), rank + 0.01 * index)
            done += [name + ".b" + tail + ".r", name + ".b" + tail + ".l"] if tail else []

    def plan_two(self, plan, two, name, tail, after, rank):
        shared = []

        def share(slots):
            for slot in slots:
                piece = two.view(slot, None)
                shared.append(self.wire.put(piece, piece, sibling(self.me)))
            self.shared += shared[-len(slots) :]

        def go():
            two.start()
            share([two.at])

        step = name + ".b" + tail
        two.plan(plan, step, after, rank)
        plan.steps[step + ".go"].run = go
        plan.add(name + ".s" + tail, lambda: share(two.closed()), after=(step + ".near",), rank=rank)
        plan.add(
            name + ".t" + tail, lambda: share([rem4(two.at + 2)]),
            after=(name + ".s" + tail, step + ".far"), rank=rank,
        )
        plan.add(name + ".all" + tail, lambda: None, lambda: shared, (name + ".t" + tail,), rank)
MLP_Y, MLP_CUT, MLP_REST = 288, 144, 208
QKV_Y, QY_CUT, QZ_CUT = 32, 16, 48
QZ_KIND = PairRing
OUT_Y, OUT_CUT, OUT_REST = 64, 32, 96
MZ_AFTER, MZ_TURN = (), ()
MY_AFTER, MY_TURN = (), ()
ORDER_ATTEND = (
    "qz.a.go", "gx", "tz", "qy.a.go", "oy.a.go", "my.a.go", "tx.go", "bias", "qy.a.r", "qy.a.l",
    "gz", "qy.a.near", "oy.a.r", "oy.a.l", "oy.a.near", "qz.a.r", "qz.a.near", "my.a.r", "my.a.l",
    "my.a.near", "qy.a.far", "qy.b.go", "oz.a.go", "oy.a.far", "oy.b.go", "mz.a.go", "tx.r",
    "tx.l", "my.a.far", "qz.a.far", "qz.b0.go", "tx.near", "qz.b0.r", "qz.b0.l", "to", "gy",
    "qz.b0.near", "qz.s0", "tx.far", "tf", "qz.b1.go", "cx.go", "qy.b.r", "qy.b.near", "qy.s",
    "oz.a.r", "oz.a.near", "qz.b0.far", "qz.t0", "oy.b.r", "oy.b.near", "gains", "n1", "qz.all0",
    "oy.s", "n2", "n0", "qz.b1.r", "qz.b1.l", "qy.b.far", "qy.t", "n3", "mz.a.r", "mz.a.near",
    "oz.a.far", "oz.b.go", "qy.all", "proj0", "qz.b1.near", "qz.s1", "own0", "my.b.go",
    "qz.b1.far", "n4", "qz.t1", "oy.b.far", "oy.t", "oz.b.r", "oz.b.l", "rest0", "mz.a.far",
    "mz.b.go", "qz.all1", "rest1", "oy.all", "proj1", "cx.l", "own2", "n5", "last0", "cx.r",
    "oz.b.near", "oz.s", "oz.b.far", "att0", "cx.near", "wz.go", "oz.t", "last1", "att2",
    "oz.all", "po", "ys.go", "cx.far", "mz.b.r", "ck", "ht", "mz.b.l", "my.b.r", "my.b.near",
    "my.s", "flip", "wz.r", "flip2", "wz.near", "mz.b.near", "mz.s", "ys.r", "wy.go", "ys.l",
    "flip3", "mz.b.far", "mz.t", "mz0", "wy.l", "wy.r", "my.b.far", "my.t", "my0", "wy.near",
    "mz.all", "mz1", "wz.far", "wz0", "my.all", "my1", "ys.far", "fin", "wy.far", "wy0",
)

UP_Y, UP_CUT, UP_REST = 320, 160, 176


def up_spreads(wire, me, ref):
    return (
        Spread(wire, me, ref, 0, UP_Y, UNITS - UP_Y, "z", UP_REST),
        Spread(wire, me, ref, 0, 0, UP_Y, "y", UP_CUT),
    )


def norm_rows(source, target, gain, rows, step=32):
    def body(index, carry):
        span = pl.ds(pl.multiple_of(index * step, step), step)
        value = source[span, :].astype(F32)
        scale = lax.rsqrt(jnp.mean(value * value, axis=-1, keepdims=True) + EPS)
        target[span, :] = (value * scale * gain).astype(BF)
        return carry

    lax.fori_loop(0, rows // step, body, 0)


def fill_bias(bias, me, start):
    row = lax.broadcasted_iota(jnp.int32, (128, 512), 0)
    column = lax.broadcasted_iota(jnp.int32, (128, 512), 1)
    query = lax.div(column, 128) * 256 + me.zl * 128 + lax.rem(column, 128)
    query_in = (query >= start) & (query < start + PIECE)

    def body(block, carry):
        pair, other = lax.div(block, 2), lax.rem(block, 2)
        parity = me.zl + other * (1 - 2 * me.zl)
        key = (pair * 2 + parity) * 128 + row
        key_in = (key >= start) & (key < start + PIECE)
        allowed = (key <= query) | (query_in & key_in)
        bias[pair, other] = jnp.where(allowed, 0.0, NEG)
        return carry

    lax.fori_loop(0, 8, body, 0)


def turn(field, cosine, sine):
    return field * cosine + pltpu.roll(field, HD // 2, 1) * sine


def add_into(target, terms, result=None):
    shape = target.shape
    lead, rows, columns = shape[:-2], shape[-2], shape[-1]
    step = rows
    while step * columns > 33000:
        step = next(s for s in range(step - 16, 0, -16) if rows % s == 0)
    cuts = rows // step
    result = target if result is None else result

    def body(index, carry):
        where, rest = [], lax.div(index, cuts)
        for extent in reversed(lead):
            where.insert(0, lax.rem(rest, extent))
            rest = lax.div(rest, extent)
        where = tuple(where) + (
            pl.ds(pl.multiple_of(lax.rem(index, cuts) * step, 16), step), ALL
        )
        total = target[where].astype(F32)
        for term in terms:
            total = total + term[where].astype(F32)
        result[where] = total.astype(result.dtype)
        return carry

    lax.fori_loop(0, math.prod(lead) * cuts, body, 0)


def columns_of(ref):
    def view(slot, half):
        if half is None:
            return ref.at[slot]
        return ref.at[slot, :, pl.ds(half * (D // 2), D // 2)]

    return view


def rows_of(ref):
    def view(slot, half):
        return ref.at[slot] if half is None else ref.at[slot, pl.ds(half * 64, 64)]

    return view


def kernel_attend(
    tokens_in, cotangent_in, start_in, query_w, key_w, value_w, out_w, gate_w, up_w, down_w,
    gain_one_in, gain_two_in, tables_in,
    qkv_out, wo_out, mlp_out, cot_out, turned_out, query_out, keys_out, values_out, heads_out,
    h_out, lse_hbm, y_hbm, gains_hbm,
    lse_out, y_out, gains_out, tok, h_one, w_qkv, w_o, w_mlp, tables, bias, query, keys, values, heads, cot, h_two,
    part, near_left, near_right, whole_left, whole_right,
    turned, heads_t, top_s, total_s, result_s, gain_x, gain_z, gain_c,
    send, recv, local,
):
    me = place()
    wire = Wire(send, recv, local)
    own = [wire.move(tokens_in, tok.at[me.x, 0])]
    for index, ref in enumerate((query_w, key_w, value_w)):
        own.append(wire.move(ref, w_qkv.at[index, me.zl, me.y, me.zh, me.core]))
    own.append(wire.move(out_w, w_o.at[me.zl, me.y, me.zh, me.core]))
    for index, ref in enumerate((gate_w, down_w, up_w)):
        own.append(wire.move(ref, w_mlp.at[index, me.zl, me.y, me.zh, me.core]))
    own.append(wire.move(tables_in.at[me.zl], tables))
    own.append(wire.move(cotangent_in, cot.at[me.x]))
    lane = lax.div(lax.broadcasted_iota(jnp.int32, (1, 128), 1), 16)
    tensor = me.x * 2 + me.zl
    gain_x[me.x] = jnp.concatenate(
        [
            jnp.where(lane == tensor, jnp.concatenate([ref[...]] * 8, axis=1), 0.0)
            for ref in (gain_one_in, gain_two_in)
        ]
        + [jnp.zeros((6, 128), F32)],
        axis=0,
    )
    greet(me, True, own)
    plan = Plan()
    at = types.SimpleNamespace()
    one, far, three = rem4(me.x + 1), rem4(me.x + 2), rem4(me.x + 3)
    kept = []

    def keep(source, target):
        kept.append(wire.move(source, target))

    def gains_x():
        at.gains = Meet(wire, me, "x", gain_x).copies

    def gains_z():
        gain_z[me.z] = gain_x[0] + gain_x[1] + gain_x[2] + gain_x[3]
        at.gains = Meet(wire, me, "z", gain_z).copies

    def gains_y():
        gain_c[me.core, me.y, 0] = gain_z[0] + gain_z[1]
        gain_c[me.core, me.y, 1] = gain_z[2] + gain_z[3]
        at.gains = MeetCores(wire, me, gain_c).copies

    def gains_all():
        for y in range(4):
            for zh in range(2):
                for core in range(2):
                    column = (y * 4 + zh * 2 + core) * 128
                    gains_out[:, column : column + 128] = gain_c[core, y, zh]

    plan.add("gx", gains_x, rank=0)
    plan.add("gz", gains_z, lambda: at.gains, ("gx",), 0)
    plan.add("gy", gains_y, lambda: at.gains, ("gz",), 0)
    plan.add("gains", gains_all, lambda: at.gains, ("gy",), 1)

    def tokens_z():
        at.rows_z = wire.put(tok.at[me.x, 0], tok.at[me.x, 1], partner(me))

    def tokens_on():
        at.on = [
            wire.put(tok.at[me.x, 1], tok.at[me.x, 1], near(me, "x", step)) for step in (1, 3)
        ]

    def tokens_far():
        at.far_z = wire.put(tok.at[far, 0], tok.at[far, 1], partner(me))

    Ring(
        wire, me, "x",
        lambda slot, half: tok.at[slot, 0] if half is None else tok.at[slot, 0, pl.ds(half * 64, 64)],
    ).plan(plan, "tx", (), 0)
    plan.add("tz", tokens_z, rank=0)
    plan.add("to", tokens_on, lambda: [at.rows_z], ("tz",), 0)
    plan.add("tf", tokens_far, after=("tx.far",), rank=0)

    def norm(*blocks):
        def run():
            for slot, p in blocks:
                norm_rows(tok.at[slot, p], h_one.at[slot, p], gains_out[0:1, :], 128)

        return run

    plan.add("n0", norm((me.x, 0)), after=("gains",), rank=2)
    plan.add("n1", norm((one, 0), (three, 0)), after=("gains", "tx.near"), rank=2)
    plan.add("n2", norm((far, 0)), after=("gains", "tx.far"), rank=2)
    plan.add("n3", norm((me.x, 1)), after=("gains", "to"), rank=3)
    plan.add("n4", norm((one, 1), (three, 1)), lambda: at.on, ("gains", "to"), 3)
    plan.add("n5", norm((far, 1)), lambda: [at.far_z], ("gains", "tf"), 2)

    Spread(wire, me, w_qkv, 1, QKV_Y, 128 - QKV_Y, "z", QZ_CUT, (0, 1), QZ_KIND).plan(plan, "qz", (), (), 1)
    Spread(wire, me, w_qkv, 1, 0, QKV_Y, "y", QY_CUT).plan(plan, "qy", (), (), 1)
    Spread(wire, me, w_o, 0, OUT_Y, 256 - OUT_Y, "z", OUT_REST).plan(plan, "oz", (), (), 1)
    Spread(wire, me, w_o, 0, 0, OUT_Y, "y", OUT_CUT).plan(plan, "oy", (), (), 1)
    both = w_mlp.at[pl.ds(0, 2)]
    mlp_z = Spread(wire, me, both, 1, MLP_Y, UNITS - MLP_Y, "z", MLP_REST)
    mlp_y = Spread(wire, me, both, 1, 0, MLP_Y, "y", MLP_CUT)
    mlp_z.plan(plan, "mz", (), (), 1.5)
    mlp_y.plan(plan, "my", (), (), 1.5)
    up_z, up_y = up_spreads(wire, me, w_mlp.at[2])
    up_z.one.plan(plan, "wz", (), 1.7)
    up_y.one.plan(plan, "wy", (), 1.7)

    def keep_up(*where):
        return lambda: keep(w_mlp.at[(2, *where)], mlp_out.at[(2, *where)])

    plan.add(
        "wz0", keep_up(ALL, me.y, ALL, me.core, pl.ds(UP_Y, UNITS - UP_Y), ALL),
        after=("wz.far",), rank=1.8,
    )
    plan.add(
        "wy0", keep_up(me.zl, ALL, me.zh, me.core, pl.ds(0, UP_Y), ALL), after=("wy.far",), rank=1.8
    )
    plan.add("bias", lambda: fill_bias(bias, me, start_in[0]), rank=6)

    def project(zl, carry):
        rows = h_one[:, 0].reshape(512, D)
        cosine, sine = tables[0, :, 0].reshape(512, HD), tables[1, :, 0].reshape(512, HD)
        raw = dot_nn(rows, w_qkv[0, zl].reshape(D, 256))
        for j in range(2):
            query[zl * 2 + j] = turn(raw[:, j * HD : (j + 1) * HD], cosine, sine).astype(BF)
        raw = dot_nn(rows, w_qkv[1, zl].reshape(D, 256))
        for j in range(2):
            keys[zl * 2 + j, :, 0] = (
                turn(raw[:, j * HD : (j + 1) * HD], cosine, sine).astype(BF).reshape(4, 128, HD)
            )
        raw = dot_nn(rows, w_qkv[2, zl].reshape(D, 256))
        for j in range(2):
            values[zl * 2 + j, :, 0] = raw[:, j * HD : (j + 1) * HD].astype(BF).reshape(4, 128, HD)
        return carry

    def project_other(zl, slots):
        rows = jnp.concatenate([h_one[slot, 1] for slot in slots], axis=0)
        cosine = jnp.concatenate([tables[0, slot, 1] for slot in slots], axis=0)
        sine = jnp.concatenate([tables[1, slot, 1] for slot in slots], axis=0)
        raw_k = dot_nn(rows, w_qkv[1, zl].reshape(D, 256))
        raw_v = dot_nn(rows, w_qkv[2, zl].reshape(D, 256))
        for j in range(2):
            key = turn(raw_k[:, j * HD : (j + 1) * HD], cosine, sine).astype(BF)
            value = raw_v[:, j * HD : (j + 1) * HD].astype(BF)
            for index, slot in enumerate(slots):
                keys[zl * 2 + j, slot, 1] = key[index * 128 : index * 128 + 128]
                values[zl * 2 + j, slot, 1] = value[index * 128 : index * 128 + 128]

    at.projected = at.rest = 0

    def keep_when_done():
        if at.projected == 2 and at.rest == 4:
            keep(w_qkv, qkv_out)
            keep(query, query_out)
            keep(keys, keys_out)
            keep(values, values_out)

    def project_half(zl):
        def run():
            lax.fori_loop(zl, zl + 1, project, 0)
            at.projected += 1
            keep_when_done()

        return run

    def other(zl, slots):
        def run():
            project_other(zl, slots)
            at.rest += 1
            keep_when_done()

        return run

    for zl in range(2):
        name = "%d" % zl
        plan.add(
            "proj" + name, project_half(zl), after=("n0", "n1", "n2", "qy.all", "qz.all" + name), rank=2 + 0.1 * zl
        )
        plan.add(
            "rest" + name, other(zl, (me.x, one, three)), after=("n3", "n4", "qy.all", "qz.all" + name),
            rank=2.2 + 0.1 * zl,
        )
        plan.add("last" + name, other(zl, (far,)), after=("n5", "qy.all", "qz.all" + name), rank=2.4 + 0.1 * zl)

    def attend_own(head, carry):
        for half, pairs in ((0, 3), (1, 4)):
            span = pairs * 128
            rows = slice(half * 256, half * 256 + 256)
            scores = dot_nt(keys[head, 0:pairs, 0].reshape(span, HD), query[head, rows, :]) * SCALE
            scores = scores + bias[0:pairs, 0, :, rows].reshape(span, 256)
            top = jnp.max(scores, axis=0, keepdims=True)
            expo = jnp.exp(scores - top)
            top_s[head, half] = top
            total_s[head, half] = jnp.sum(expo, axis=0, keepdims=True)
            value = values[head, 0:pairs, 0].reshape(span, HD)
            result_s[head, half] = dot_tn(value, expo.astype(BF))
        return carry

    def attend_other(head, carry):
        for half, pairs in ((0, 3), (1, 4)):
            span = pairs * 128
            rows = slice(half * 256, half * 256 + 256)
            scores = dot_nt(keys[head, 0:pairs, 1].reshape(span, HD), query[head, rows, :]) * SCALE
            scores = scores + bias[0:pairs, 1, :, rows].reshape(span, 256)
            before = top_s[head, half]
            top = jnp.maximum(before, jnp.max(scores, axis=0, keepdims=True))
            fade = jnp.exp(before - top)
            expo = jnp.exp(scores - top)
            total = total_s[head, half] * fade + jnp.sum(expo, axis=0, keepdims=True)
            value = values[head, 0:pairs, 1].reshape(span, HD)
            result = (result_s[head, half] * fade + dot_tn(value, expo.astype(BF))) * (1.0 / total)
            heads[rows, pl.ds(pl.multiple_of(head * HD, HD), HD)] = result.T.astype(BF)
            lse_out[head, :, rows] = top + jnp.log(total)
        return carry

    def attend_rest():
        lax.fori_loop(2, 4, attend_other, 0)
        keep(lse_out, lse_hbm)

    plan.add("own0", lambda: lax.fori_loop(0, 2, attend_own, 0), after=("proj0", "bias"), rank=2.5)
    plan.add("own2", lambda: lax.fori_loop(2, 4, attend_own, 0), after=("proj1", "bias"), rank=2.5)
    plan.add(
        "att0", lambda: lax.fori_loop(0, 2, attend_other, 0), after=("own0", "rest0", "last0"), rank=2.5
    )
    plan.add("att2", attend_rest, after=("own2", "rest1", "last1", "att0"), rank=2.6)

    def project_out(block, carry):
        y, zh = lax.div(block, 2), lax.rem(block, 2)
        weight = jnp.concatenate(
            [
                jnp.concatenate([w_o[zl, y, zh, 0], w_o[zl, y, zh, 1]], axis=1)
                for zl in range(2)
            ],
            axis=0,
        )
        result = dot_nn(heads[...], weight).astype(BF).reshape(4, 128, 256)
        part[:, :, pl.ds(pl.multiple_of(block * 256, 256), 256)] = result
        return carry

    total = RingSum(
        wire, me, "x", columns_of(part), near_left, near_right, whole_left, whole_right,
        split_columns, lambda target, term: add_into(target, [term]),
    )

    def out_one():
        keep(w_o, wo_out)
        lax.fori_loop(0, 4, project_out, 0)
        total.start((0,))

    def out_two():
        lax.fori_loop(4, 8, project_out, 0)
        total.start((1,))

    plan.add("po", out_one, after=("att0", "att2", "oz.all", "oy.all"), rank=2)
    plan.add("ys.go", out_two, after=("po",), rank=2)
    total.plan(plan, "ys", (), 1, go=False)

    def finish(index, carry):
        span = pl.ds(pl.multiple_of(index * 32, 32), 32)
        value = tok[me.x, 0, span, :].astype(F32) + (
            part[me.x, span, :].astype(F32)
            + whole_left[span, :].astype(F32)
            + whole_right[span, :].astype(F32)
        )
        scale = lax.rsqrt(jnp.mean(value * value, axis=-1, keepdims=True) + EPS)
        y_out[span, :] = value
        h_two[span, :] = (value * scale * gains_out[1:2, :]).astype(BF)
        return carry

    def finish_all():
        lax.fori_loop(0, 4, finish, 0)
        keep(h_two, h_out)
        keep(y_out, y_hbm)
        keep(gains_out, gains_hbm)

    plan.add("fin", finish_all, after=("ys.far",), rank=0)
    Ring(wire, me, "x", rows_of(cot)).plan(plan, "cx", (), 1.6)
    plan.add("ck", lambda: keep(cot, cot_out), after=("cx.far",), rank=1.8)

    def flip(block, carry):
        column = pl.ds(pl.multiple_of(block * 128, 128), 128)
        rows = h_one[:, :, :, column].reshape(SEQ, 128)
        turned[lax.rem(block, 2), lax.div(block, 2)] = rows.T
        return carry

    def turn_heads():
        heads_t[...] = heads[...].T
        keep(heads_t, heads_out)

    plan.add("ht", turn_heads, after=("att0", "att2"), rank=6)

    def flip_rest():
        lax.fori_loop(8, 16, flip, 0)
        keep(turned.at[me.core], turned_out.at[0])
        at.turned = wire.put(turned.at[1 - me.core], turned_out.at[1], sibling(me))

    plan.add("flip", lambda: lax.fori_loop(0, 8, flip, 0), after=("n0", "n1", "n2", "n3", "n4", "n5"), rank=7)
    plan.add("flip2", flip_rest, after=("flip",), rank=7)
    plan.add("flip3", lambda: None, lambda: [at.turned], ("flip2",), 9)

    def keep_mlp(mine, start, size):
        def run():
            core = me.core if mine else 1 - me.core
            piece = (pl.ds(0, 2), ALL, ALL, ALL, core, pl.ds(start, size), ALL)
            keep(w_mlp.at[piece], mlp_out.at[piece])

        return run

    plan.add("my0", keep_mlp(True, 0, MLP_Y), after=("my.t",), rank=1.8)
    plan.add("my1", keep_mlp(False, 0, MLP_Y), after=("my.all",), rank=1.8)
    plan.add("mz0", keep_mlp(True, MLP_Y, UNITS - MLP_Y), after=("mz.t",), rank=1.8)
    plan.add("mz1", keep_mlp(False, MLP_Y, UNITS - MLP_Y), after=("mz.all",), rank=1.8)

    plan.go(ORDER_ATTEND)
    for copy in kept:
        copy.wait()
    wire.drain()


def anywhere():
    return pl.BlockSpec(memory_space=pl.ANY)


def in_vmem():
    return pl.BlockSpec(memory_space=pltpu.VMEM)


def call_attend(tokens, cotangent, starts, weights, gain_attn, gain_mlp, tables):
    shape = jax.ShapeDtypeStruct
    hbm = [
        shape((3, 2, 4, 2, 2, 128, 256), BF),
        shape((2, 4, 2, 2, 256, 128), BF),
        shape((3, 2, 4, 2, 2, UNITS, 128), BF),
        shape((4, 128, D), BF),
        shape((2, 8, 128, SEQ), BF),
        shape((4, 512, HD), BF),
        shape((4, 4, 2, 128, HD), BF),
        shape((4, 4, 2, 128, HD), BF),
        shape((512, 512), BF),
        shape((128, D), BF),
    ]
    vmem = [shape((4, 1, 512), F32), shape((128, D), F32), shape((8, D), F32)]
    return pl.pallas_call(
        kernel_attend,
        name="attend",
        in_specs=[anywhere(), anywhere(), pl.BlockSpec(memory_space=pltpu.SMEM)]
        + [anywhere()] * 7
        + [in_vmem()] * 2
        + [anywhere()],
        out_specs=[anywhere()] * (len(hbm) + len(vmem)),
        out_shape=hbm + vmem,
        scratch_shapes=[
            pltpu.VMEM((4, 1, 512), F32),
            pltpu.VMEM((128, D), F32),
            pltpu.VMEM((8, D), F32),
            pltpu.VMEM((4, 2, 128, D), BF),
            pltpu.VMEM((4, 2, 128, D), BF),
            pltpu.VMEM((3, 2, 4, 2, 2, 128, 256), BF),
            pltpu.VMEM((2, 4, 2, 2, 256, 128), BF),
            pltpu.VMEM((3, 2, 4, 2, 2, UNITS, 128), BF),
            pltpu.VMEM((2, 4, 2, 128, HD), F32),
            pltpu.VMEM((4, 2, 128, 512), F32),
            pltpu.VMEM((4, 512, HD), BF),
            pltpu.VMEM((4, 4, 2, 128, HD), BF),
            pltpu.VMEM((4, 4, 2, 128, HD), BF),
            pltpu.VMEM((512, 512), BF),
            pltpu.VMEM((4, 128, D), BF),
            pltpu.VMEM((128, D), BF),
            pltpu.VMEM((4, 128, D), BF),
            pltpu.VMEM((128, D // 2), BF),
            pltpu.VMEM((128, D // 2), BF),
            pltpu.VMEM((128, D), BF),
            pltpu.VMEM((128, D), BF),
            pltpu.VMEM((2, 8, 128, SEQ), BF),
            pltpu.VMEM((512, 512), BF),
            pltpu.VMEM((4, 2, 1, 256), F32),
            pltpu.VMEM((4, 2, 1, 256), F32),
            pltpu.VMEM((4, 2, HD, 256), F32),
            pltpu.VMEM((4, 8, 128), F32),
            pltpu.VMEM((4, 8, 128), F32),
            pltpu.VMEM((2, 4, 2, 8, 128), F32),
            pltpu.SemaphoreType.DMA((140,)),
            pltpu.SemaphoreType.DMA((140,)),
            pltpu.SemaphoreType.DMA((32,)),
        ],
        compiler_params=pltpu.CompilerParams(
            collective_id=0, has_side_effects=True, vmem_limit_bytes=VMEM_BYTES
        ),
    )(tokens, cotangent, starts, *weights, gain_attn, gain_mlp, tables)


def rope_tables():
    half = HD // 2
    freq = np.exp(np.arange(half, dtype=np.float32) * np.float32(-2.0 * math.log(10000.0) / HD))
    order = np.array(
        [
            [[(2 * pair + (zl + other) % 2) * 128 + np.arange(128) for other in range(2)] for pair in range(4)]
            for zl in range(2)
        ]
    )
    angle = order.astype(np.float32)[..., None] * freq.astype(np.float32)
    cosine, sine = np.cos(angle.astype(np.float64)), np.sin(angle.astype(np.float64))
    both = np.stack(
        [np.concatenate([cosine, cosine], -1), np.concatenate([-sine, sine], -1)], axis=1
    )
    return both.astype(np.float32)
SUM_Y, SUM_CUT = 400, 208
ORDER_FEED = (
    "hx.go", "wy.b.go", "wz.b.go", "l2", "wz.b.r", "wz.b.l", "a10", "a11", "wy.b.r", "wy.b.near",
    "wy.s", "a01", "wz.b.near", "wz.s", "hx.r", "hx.l", "hx.near", "g10", "g11", "wz.b.far",
    "wz.t", "a00", "wz.all", "wy.b.far", "wy.t", "hx.far", "g00", "hs", "wy.all", "f00", "g01",
    "f01", "b00", "ds.go", "f10", "f11", "b10", "b11", "t1", "ds.r", "t0", "ds.l", "cs", "gr1a",
    "gr1b", "s1z.go", "s1y.go", "gr0a", "gr0b", "s0y.go", "ds.far", "bn", "dx.go", "s0z.go",
    "s1y.l", "s1y.r", "s1z.r", "t2", "fd0", "fd1", "dx.r", "gr2a", "s0y.l", "gr2b", "dg",
    "s1z.far", "s0y.r", "s1z.k", "dx.l", "dx.near", "s0z.r", "s1y.far", "s1y.k", "dx.far", "dk",
    "s0y.far", "s0y.k", "s0z.far", "s0z.k",
)


def fold_view(ref, me, lead, axis, row, rows, cut):
    head = (ALL,) * lead

    def view(slot, part):
        start, size = row, rows
        if part == 0:
            size = cut
        if part == 1:
            start, size = row + cut, rows - cut
        if axis == "y":
            where = (ALL, slot, ALL)
        else:
            where = (lax.rem(slot, 2), ALL, lax.div(slot, 2))
        return ref.at[head + where + (pl.ds(start, size), ALL)]

    return view


def kernel_feed(
    h_in, cot_in, mlp_in, y_hbm, gains_hbm,
    part_out, dattn_out, fold_y_out, fold_z_out, down_out, dy_hbm, gain_hbm,
    y_in, gains_in, dy_out, gain_out,
    w_mlp, h_two, cot, gate_s, up_s, act_s, d_gate, d_up, act, flipped, flipped_far,
    h_far, cot_far, part, near_left, near_right, whole_left, whole_right, d_attn, out_part,
    *rest,
):
    bufs, (send, recv, local) = list(rest[:-3]), rest[-3:]
    bufs = [tuple(bufs[a:b]) for a, b in ((0, 4), (4, 7), (7, 11), (11, 14))]
    me = place()
    wire = Wire(send, recv, local)
    parts = {}

    def load(zl):
        for which in range(2):
            parts[which, zl] = wire.move(mlp_in.at[which, zl], w_mlp.at[which, zl])

    def load_up(*where):
        return wire.move(mlp_in.at[(2, *where)], w_mlp.at[(2, *where)])

    loads = [wire.move(h_in, h_two.at[me.x])]
    ups = [
        load_up(ALL, me.y, ALL, me.core, pl.ds(UP_Y, UNITS - UP_Y), ALL),
        load_up(me.zl, ALL, me.zh, me.core, pl.ds(0, UP_Y), ALL),
    ]
    greet(me, False)
    plan = Plan()
    at = types.SimpleNamespace()
    kept = []

    def keep(source, target):
        kept.append(wire.move(source, target))

    def whole(which, zl):
        return jnp.concatenate(
            [
                w_mlp[which, zl, y, zh, core]
                for y in range(4)
                for zh in range(2)
                for core in range(2)
            ],
            axis=1,
        )

    def share(source, target):
        return [
            wire.put(
                source.at[:, :, pl.ds(pl.multiple_of((block * 2 + 1 - me.core) * 128, 128), 128)],
                target.at[block],
                sibling(me),
            )
            for block in range(8)
        ]

    def share_h():
        at.h_puts = share(h_two, h_far)

    def share_cot():
        at.cot_puts = share(cot, cot_far)

    one, far, three = rem4(me.x + 1), rem4(me.x + 2), rem4(me.x + 3)
    batches = ((far, one), (three, me.x))

    def rows_of_batch(ref, batch):
        return jnp.concatenate([ref[slot] for slot in batches[batch]], axis=0)

    def room(batch, zl):
        return zl if batch else 2

    def gate(batch, zl):
        def run():
            gate_s[room(batch, zl)] = dot_nt(rows_of_batch(h_two, batch), whole(0, zl))

        return run

    def back_act(batch, zl):
        def run():
            act_s[batch * 2 + zl] = dot_nt(rows_of_batch(cot, batch), whole(1, zl))

        return run

    def forward(batch, zl):
        def inner(index, carry):
            place_of, rest = lax.div(index, 4), lax.rem(index, 4)
            first, second = batches[batch]
            slot = first + place_of * (second - first)
            source = pl.ds(pl.multiple_of(index * 32, 32), 32)
            span = pl.ds(pl.multiple_of(rest * 32, 32), 32)
            gate, up = gate_s[room(batch, zl), source, :], up_s[source, :]
            d_act = act_s[batch * 2 + zl, source, :]
            sigma = 1.0 / (1.0 + jnp.exp(-gate))
            act[zl, slot, span, :] = (gate * sigma * up).astype(BF)
            d_gate[zl, slot, span, :] = (
                d_act * up * sigma * (1.0 + gate * (1.0 - sigma))
            ).astype(BF)
            d_up[zl, slot, span, :] = (d_act * gate * sigma).astype(BF)
            return carry

        def run():
            up_s[...] = dot_nt(rows_of_batch(h_two, batch), whole(2, zl))
            lax.fori_loop(0, 8, inner, 0)

        return run

    def back_h(batch):
        def body(block, carry):
            y, zh = lax.div(block, 2), lax.rem(block, 2)
            total = None
            for which, left in ((0, d_gate), (2, d_up)):
                for zl in range(2):
                    weight = jnp.concatenate(
                        [w_mlp[which, zl, y, zh, 0], w_mlp[which, zl, y, zh, 1]], axis=1
                    )
                    rows = jnp.concatenate([left[zl, slot] for slot in batches[batch]], axis=0)
                    term = dot_nn(rows, weight)
                    total = term if total is None else total + term
            result = total.astype(BF)
            column = pl.ds(pl.multiple_of(block * 256, 256), 256)
            for index, slot in enumerate(batches[batch]):
                part[slot, :, column] = result[index * 128 : index * 128 + 128]
            return carry

        return body

    def add(target, term):
        add_into(target, [term])

    total = RingSum(
        wire, me, "x", columns_of(part), near_left, near_right, whole_left, whole_right,
        split_columns, add,
    )

    def back_first(half):
        def run():
            lax.fori_loop(half * 4, half * 4 + 4, back_h(0), 0)
            total.start_near(half)
            if half:
                total.start_whole(1)

        return run

    def back_second(half):
        def run():
            lax.fori_loop(half * 4, half * 4 + 4, back_h(1), 0)
            if half == 0:
                total.start_whole(0)

        return run

    plan.add("hs", share_h, after=("hx.far",), rank=3)
    plan.add("cs", share_cot, lambda: [loads[1]], ("l2",), 3)
    def load_rest():
        load(0)
        load(1)
        loads.append(wire.move(cot_in, cot))
        at.late = [wire.move(y_hbm, y_in), wire.move(gains_hbm, gains_in)]

    plan.add("l2", load_rest, lambda: [loads[0], *ups], ("hx.go",), 0)
    Ring(wire, me, "x", rows_of(h_two)).plan(plan, "hx", (), 0)
    plan.steps["hx.go"].waits = lambda: [loads[0]]
    up_z, up_y = up_spreads(wire, me, w_mlp.at[2])
    up_z.plan_second(plan, "wz", (), 1)
    up_y.plan_second(plan, "wy", (), 1)
    plan.steps["wz.b.go"].waits = lambda: [ups[0]]
    plan.steps["wy.b.go"].waits = lambda: [ups[1]]
    for zl in range(2):
        for batch in range(2):
            name = "%d%d" % (batch, zl)
            plan.add(
                "a" + name, back_act(batch, zl), lambda zl=zl: [loads[1], parts[1, zl]], ("l2",),
                4 - 0.5 * batch,
            )
        plan.add("g1%d" % zl, gate(1, zl), lambda zl=zl: [parts[0, zl]], ("hx.near", "l2"), 3)
    before = ("hx.far", "l2")
    for zl in range(2):
        name = "0%d" % zl
        plan.add("g" + name, gate(0, zl), lambda zl=zl: [parts[0, zl]], before, 2)
        plan.add(
            "f" + name, forward(0, zl), after=("g" + name, "a" + name, "wz.all", "wy.all", *before),
            rank=2,
        )
        before = ("f" + name,)
    plan.add("b00", back_first(0), after=before, rank=2)
    plan.add("ds.go", back_first(1), after=("b00",), rank=2)
    plan.add("f10", forward(1, 0), after=("g10", "a10", "ds.go"), rank=2.1)
    plan.add("f11", forward(1, 1), after=("g11", "a11", "f10"), rank=2.1)
    before = ("f10", "f11")
    plan.add("b10", back_second(0), after=before, rank=2)
    plan.add("b11", back_second(1), after=("b10",), rank=2)
    total.plan(plan, "ds", (), 0, go=False)
    plan.steps["ds.l"].after += ("b11",)
    plan.steps["ds.far"].after += ("b10",)

    at.far = {}

    def turn_over(which, source):
        def run():
            for zl in range(2):
                flipped[which, zl] = source[zl].reshape(512, UNITS).T
            at.far[which] = wire.put(flipped.at[which], flipped_far.at[which], sibling(me))

        return run

    for which, source in enumerate((d_gate, d_up, act)):
        plan.add("t%d" % which, turn_over(which, source), after=("b11",), rank=2 + which * 0.2)

    def forward_down(block, carry):
        y, zh = lax.div(block, 2), lax.rem(block, 2)
        result = None
        for zl in range(2):
            weight = jnp.concatenate([w_mlp[1, zl, y, zh, 0], w_mlp[1, zl, y, zh, 1]], axis=1)
            term = dot_nn(act[zl].reshape(512, UNITS), weight)
            result = term if result is None else result + term
        out_part[:, :, pl.ds(pl.multiple_of(block * 256, 256), 256)] = result.astype(BF).reshape(4, 128, 256)
        return carry

    def down_rest():
        lax.fori_loop(4, 8, forward_down, 0)
        keep(out_part, part_out)

    plan.add("fd0", lambda: lax.fori_loop(0, 4, forward_down, 0), after=("t2",), rank=4)
    plan.add("fd1", down_rest, after=("fd0",), rank=4)

    places = (0, 2, 1)

    def grad(which, rows, rows_far):
        def body(index, carry):
            zl, pair = lax.div(index, 2), lax.rem(index, 2)
            mine = jnp.concatenate(
                [
                    rows[:, :, pl.ds(pl.multiple_of(((pair * 4 + k) * 2 + me.core) * 128, 128), 128)]
                    .reshape(512, 128)
                    for k in range(4)
                ],
                axis=1,
            )
            other = jnp.concatenate(
                [rows_far[pair * 4 + k].reshape(512, 128) for k in range(4)], axis=1
            )
            result = dot_nn(flipped[which, zl], mine) + dot_nn(flipped_far[which, zl], other)
            result = result.astype(BF)
            for k in range(4):
                w_mlp[places[which], zl, pair * 2 + k // 2, k % 2, 0] = result[:, k * 128 : k * 128 + 128]
            return carry

        return body

    sums = []

    def start_sums(which):
        ref = w_mlp.at[places[which], :, :, :, 0]
        pair = [
            RingSum(wire, me, "y", fold_view(ref, me, 0, "y", 0, SUM_Y, SUM_CUT), *bufs[2 * which],
                    split_rows(SUM_CUT), add),
            PairSum(wire, me, fold_view(ref, me, 0, "z", SUM_Y, UNITS - SUM_Y, 0),
                    *bufs[2 * which + 1], add),
        ]
        for item, out, axis in zip(pair, (fold_y_out, fold_z_out), "yz"):
            name = "s%d%s" % (which, axis)
            item.plan(plan, name, ("gr%db" % which,), 1)
            plan.add(name + ".k", close_sum(item, out.at[which]), after=(name + ".far",), rank=3)

    def close_sum(item, out):
        def run():
            mine = item.part(item.at, None)
            add_into(mine, list(item.whole))
            keep(mine, out)

        return run

    rows_of_step = ((h_two, h_far), (h_two, h_far), (cot, cot_far))
    for which in range(3):
        body = grad(which, *rows_of_step[which])

        def waits(which=which):
            return [at.far[which]] + (at.cot_puts if which == 2 else at.h_puts)

        before = ("t%d" % which, "cs", "hs") + (("fd1",) if which == 2 else ())

        def first(body=body, which=which):
            if which == 1:
                for spread in (up_z, up_y):
                    for copy in [*spread.twos[0].copies(), *spread.shared]:
                        copy.wait_send()
            lax.fori_loop(0, 2, body, 0)

        plan.add("gr%da" % which, first, waits, before, 3)
        plan.add(
            "gr%db" % which, lambda body=body: lax.fori_loop(2, 4, body, 0),
            after=("gr%da" % which,), rank=3,
        )
        if which < 2:
            start_sums(which)
    plan.add("dg", lambda: keep(w_mlp.at[1, :, :, :, 0], down_out), after=("gr2b",), rank=2)

    def back_norm(index, carry):
        span = pl.ds(pl.multiple_of(index * 16, 16), 16)
        d_h = (
            part[me.x, span, :].astype(F32)
            + whole_left[span, :].astype(F32)
            + whole_right[span, :].astype(F32)
        )
        value = y_in[span, :]
        scale = lax.rsqrt(jnp.mean(value * value, axis=-1, keepdims=True) + EPS)
        normed = value * scale
        e_two = d_h * gains_in[1:2, :]
        inner = jnp.mean(e_two * normed, axis=-1, keepdims=True)
        d_y = cot[me.x, span, :].astype(F32) + scale * (e_two - normed * inner)
        dy_out[span, :] = d_y
        d_attn[me.x, span, :] = d_y.astype(BF)
        return carry + jnp.sum(d_h * normed, axis=0, keepdims=True)

    def back_one():
        gain_out[...] = lax.fori_loop(0, 4, back_norm, jnp.zeros((1, D), F32))
        d_ring.start_half(0)

    def back_two():
        gain_out[...] += lax.fori_loop(4, 8, back_norm, jnp.zeros((1, D), F32))
        d_ring.start_half(1)
        keep(dy_out, dy_hbm)
        keep(gain_out, gain_hbm)

    d_ring = Ring(wire, me, "x", rows_of(d_attn))
    plan.add("bn", back_one, lambda: at.late, ("ds.far",), 0)
    d_ring.plan(plan, "dx", ("bn",), 0)
    plan.steps["dx.go"].run = back_two
    plan.add("dk", lambda: keep(d_attn, dattn_out), after=("dx.far",), rank=0)
    plan.go(ORDER_FEED)
    for copy in kept:
        copy.wait()
    wire.drain()


def fold_shapes(lead, count, rows, cut, columns):
    return [
        pltpu.VMEM((*lead, *count, cut, columns), BF),
        pltpu.VMEM((*lead, *count, rows - cut, columns), BF),
        pltpu.VMEM((*lead, *count, rows, columns), BF),
        pltpu.VMEM((*lead, *count, rows, columns), BF),
    ]


def call_feed(h_two, cot, mlp, y_one, gains):
    shape = jax.ShapeDtypeStruct
    bufs = (
        fold_shapes((), (2, 2), SUM_Y, SUM_CUT, 128)
        + [pltpu.VMEM((4, UNITS - SUM_Y, 128), BF)] * 3
    ) * 2
    return pl.pallas_call(
        kernel_feed,
        name="feed",
        in_specs=[anywhere()] * 5,
        out_specs=[anywhere()] * 7,
        out_shape=[
            shape((4, 128, D), BF),
            shape((4, 128, D), BF),
            shape((2, 2, 2, SUM_Y, 128), BF),
            shape((2, 4, UNITS - SUM_Y, 128), BF),
            shape((2, 4, 2, UNITS, 128), BF),
            shape((128, D), F32),
            shape((1, D), F32),
        ],
        scratch_shapes=[
            pltpu.VMEM((128, D), F32),
            pltpu.VMEM((8, D), F32),
            pltpu.VMEM((128, D), F32),
            pltpu.VMEM((1, D), F32),
            pltpu.VMEM((3, 2, 4, 2, 2, UNITS, 128), BF),
            pltpu.VMEM((4, 128, D), BF),
            pltpu.VMEM((4, 128, D), BF),
            pltpu.VMEM((3, 256, UNITS), F32),
            pltpu.VMEM((256, UNITS), F32),
            pltpu.VMEM((4, 256, UNITS), F32),
            pltpu.VMEM((2, 4, 128, UNITS), BF),
            pltpu.VMEM((2, 4, 128, UNITS), BF),
            pltpu.VMEM((2, 4, 128, UNITS), BF),
            pltpu.VMEM((3, 2, UNITS, 512), BF),
            pltpu.VMEM((3, 2, UNITS, 512), BF),
            pltpu.VMEM((8, 4, 128, 128), BF),
            pltpu.VMEM((8, 4, 128, 128), BF),
            pltpu.VMEM((4, 128, D), BF),
            pltpu.VMEM((128, D // 2), BF),
            pltpu.VMEM((128, D // 2), BF),
            pltpu.VMEM((128, D), BF),
            pltpu.VMEM((128, D), BF),
            pltpu.VMEM((4, 128, D), BF),
            pltpu.VMEM((4, 128, D), BF),
        ]
        + bufs
        + [
            pltpu.SemaphoreType.DMA((100,)),
            pltpu.SemaphoreType.DMA((100,)),
            pltpu.SemaphoreType.DMA((24,)),
        ],
        compiler_params=pltpu.CompilerParams(
            collective_id=1, has_side_effects=True, vmem_limit_bytes=VMEM_BYTES
        ),
    )(h_two, cot, mlp, y_one, gains)
BACK_GROUPS = (3, 4, 4, 3, 3, 4, 4, 3, 3, 4, 4, 3, 3, 4)
ORDER_BACK = (
    "bias", "l2", "dh", "os.go", "l3", "my.b.go", "ba0", "wy.a.go", "ba2", "my.b.r", "wz.a.go",
    "mz.b.go", "bh0", "bh1", "wy.a.r", "mz.b.r", "wz.a.r", "wy.a.l", "gq0", "gq1", "qy.a.go",
    "qz.a.go", "as", "wy.a.far", "ax", "dl0", "mx", "my.b.far", "my.k", "dn1", "mz.b.l", "ht",
    "os.l", "os.r", "go", "dl1", "qy.a.l", "mz.", "az", "qy.a.r", "qz.a.r", "oz.a.go", "wz.a.far",
    "oy.a.go", "wy.b.go", "dn0", "ds.go", "ds.l", "mz.b.far", "mz.k", "oz.a.r", "os.far", "fo",
    "my.", "ay", "qy.a.far", "qy.b.go", "wy.b.r", "oy.a.l", "oy.a.r", "ds.r", "wz.b.go", "m.",
    "a.", "qz.a.far", "qz.b.go", "qy.b.r", "oy.a.far", "oy.b.go", "oz.a.far", "oz.b.go", "wz.b.r",
    "wz.b.l", "qz.b.r", "gk", "wy.b.far", "wy.k", "qz.b.l", "oz.b.r", "oy.b.r", "oz.b.l",
    "ds.far", "bn", "wz.b.far", "qy.b.far", "qy.k", "wz.k", "qz.b.far", "qz.k", "oz.b.far",
    "oz.k", "oy.b.far", "oy.k",
)
O_Y, O_CUT, O_REST = 192, 96, 32
Q_Y, Q_CUT, Q_REST = 80, 48, 16
DN_Y, DN_CUT, DN_REST = 448, 224, 128


class Fold:
    def __init__(self, wire, me, cut, view_one, axes, bufs, view_two, bufs_two):
        def add(target, term):
            add_into(target, [term])

        self.wire, self.me, self.add, self.split = wire, me, add, split_rows(cut)
        self.one = None
        if view_one is not None:
            self.one = self.sum(axes[0], view_one, bufs)
        self.two = self.sum(axes[1], view_two, bufs_two)

    def sum(self, axis, view, bufs):
        if axis == "z":
            return PairSum(self.wire, self.me, view, *bufs, self.add)
        return RingSum(self.wire, self.me, "y", view, *bufs, self.split, self.add)

    def turn(self):
        add_into(self.one.part(self.one.at, None), list(self.one.whole))
        self.two.start()

    def close(self, result, keep):
        add_into(self.two.part(self.two.at, None), list(self.two.whole), result)
        keep()

    def plan(self, plan, name, waits, after, rank, result, keep):
        if self.one is None:
            self.two.plan(plan, name + ".b", after, rank)
            plan.steps[name + ".b.go"].waits = waits
        else:
            self.one.plan(plan, name + ".a", after, rank)
            plan.steps[name + ".a.go"].waits = waits
            self.two.plan(plan, name + ".b", (name + ".a.far",), rank)
            plan.steps[name + ".b.go"].run = self.turn
        plan.add(name + ".k", lambda: self.close(result, keep), after=(name + ".b.far",), rank=rank + 0.5)


def crossed_view(ref, me, lead, axis, row, rows, cut):
    head = (ALL,) * lead

    def view(slot, part):
        start, size = row, rows
        if part == 0:
            size = cut
        if part == 1:
            start, size = row + cut, rows - cut
        if axis == "z":
            where = (lax.rem(slot, 2), me.y, lax.div(slot, 2))
        else:
            where = (me.zl, slot, me.zh)
        return ref.at[head + where + (pl.ds(start, size), ALL)]

    return view


def held_view(ref, lead, axis, rows, cut):
    head = (ALL,) * lead

    def view(slot, part):
        start, size = 0, rows
        if part == 0:
            size = cut
        if part == 1:
            start, size = cut, rows - cut
        where = (lax.rem(slot, 2), lax.div(slot, 2)) if axis == "z" else (slot,)
        return ref.at[head + where + (pl.ds(start, size), ALL)]

    return view


def kernel_back(
    start_in, tokens_hbm, dattn_hbm, part_hbm, qkv_hbm, wo_hbm, query_hbm, keys_hbm, values_hbm,
    heads_hbm, lse_hbm, turned_hbm, tables_hbm, gains_hbm, y_hbm, dy_hbm, gain_hbm, fold_y_hbm,
    fold_z_hbm, down_hbm,
    result_hbm, grad_tokens_hbm, g_qkv_hbm, g_o_hbm, g_mlp_hbm, g_gains_hbm,
    query_in, keys_in, values_in, lse_in, gains_in, y_in, dy_in, gain_in,
    result_out, tokens_out, g_qkv_out, g_o_out, g_mlp_out, gains_out,
    w_qkv, w_o, d_attn, out_part, tables, bias, tok, turned, d_heads, d_query, d_keys, d_values,
    d_query_far, d_keys_far, d_values_far, sum_keys, sum_values, heads_t, heads_t_far, attn_far,
    d_h, far_one, side_left, side_right, last_z,
    near_left, near_right, whole_left, whole_right,
    out_near_left, out_near_right, out_whole_left, out_whole_right,
    fold_y, fold_z, g_down, gain_x, gain_z, gain_c, along_s, along_a, along_b, along_c, gain_t, along_t,
    *rest,
):
    bufs, (send, recv, local) = list(rest[:-3]), rest[-3:]
    groups = []
    for size in BACK_GROUPS:
        groups.append(tuple(bufs[:size]))
        bufs = bufs[size:]
    me = place()
    wire = Wire(send, recv, local)
    loads = {}

    def load(*items):
        for name, source, target in items:
            loads[name] = wire.move(source, target)

    def load_second():
        load(
            ("fold_y", fold_y_hbm, fold_y),
            ("fold_z", fold_z_hbm, fold_z),
            ("gain", gain_hbm, gain_in),
            ("heads", heads_hbm, heads_t),
            ("down", down_hbm, g_down),
        )

    def load_third():
        load(
            ("qkv", qkv_hbm, w_qkv),
            ("turned", turned_hbm, turned),
            ("y", y_hbm, y_in),
            ("dy", dy_hbm, dy_in),
            ("tok", tokens_hbm, tok),
            ("gains", gains_hbm, gains_in),
        )

    load(
        ("attn", dattn_hbm, d_attn),
        ("o", wo_hbm, w_o),
        ("query", query_hbm, query_in),
        ("keys", keys_hbm, keys_in),
        ("values", values_hbm, values_in),
        ("lse", lse_hbm, lse_in),
        ("tables", tables_hbm.at[me.zl], tables),
        ("part", part_hbm, out_part),
    )
    kept = []

    def keep(source, target):
        kept.append(wire.move(source, target))

    greet(me, True)
    plan = Plan()
    at = types.SimpleNamespace()
    one, far, three = rem4(me.x + 1), rem4(me.x + 2), rem4(me.x + 3)
    right, left = near(me, "x", 1), near(me, "x", 3)

    def add(target, term):
        add_into(target, [term])

    def loaded(*names):
        return lambda: [loads[name] for name in names]

    def share_attn():
        at.attn = [
            wire.put(
                d_attn.at[:, :, pl.ds(pl.multiple_of((block * 2 + 1 - me.core) * 128, 128), 128)],
                attn_far.at[block],
                sibling(me),
            )
            for block in range(8)
        ]

    def share_heads():
        at.heads = wire.put(heads_t, heads_t_far, sibling(me))

    plan.add("l2", load_second, loaded("attn", "o"), rank=0)
    plan.add("l3", load_third, loaded("query", "keys", "values", "lse", "tables"), ("l2",), 0)
    plan.add("as", share_attn, loaded("attn"), rank=1.5)
    plan.add("ht", share_heads, loaded("heads"), ("l2",), 1.5)

    total = RingSum(
        wire, me, "x", columns_of(out_part), out_near_left, out_near_right, out_whole_left,
        out_whole_right, split_columns, add,
    )
    total.plan(plan, "os", (), 1)
    plan.steps["os.go"].waits = loaded("part")

    def finish_out(index, carry):
        span = pl.ds(pl.multiple_of(index * 16, 16), 16)
        result_out[span, :] = (
            y_in[span, :]
            + (
                out_part[me.x, span, :].astype(F32)
                + out_whole_left[span, :].astype(F32)
                + out_whole_right[span, :].astype(F32)
            )
        ).astype(BF)
        return carry

    def finish_result():
        lax.fori_loop(0, 8, finish_out, 0)
        keep(result_out, result_hbm)

    plan.add("fo", finish_result, loaded("y"), ("os.far", "l3"), 6)

    def back_heads(zl, carry):
        weight = jnp.concatenate(
            [w_o[zl, y, zh, c] for y in range(4) for zh in range(2) for c in range(2)], axis=1
        )
        result = dot_nt(d_attn[...].reshape(512, D), weight).astype(BF)
        d_heads[zl * 2] = result[:, 0:HD]
        d_heads[zl * 2 + 1] = result[:, HD : 2 * HD]
        return carry

    plan.add("dh", lambda: lax.fori_loop(0, 2, back_heads, 0), loaded("attn", "o"), rank=2)
    plan.add("bias", lambda: fill_bias(bias, me, start_in[0]), rank=1)

    def back_attend(head, carry):
        for half, pairs in ((1, 4), (0, 3)):
            span = pairs * 256
            rows = slice(half * 256, half * 256 + 256)
            key = keys_in[head, 0:pairs].reshape(span, HD)
            value = values_in[head, 0:pairs].reshape(span, HD)
            query, d_head = query_in[head, rows, :], d_heads[head, rows, :]
            scores = dot_nt(key, query) * SCALE + bias[0:pairs, :, :, rows].reshape(span, 256)
            probs = jnp.exp(scores - lse_in[head, :, rows])
            d_probs = dot_nt(value, d_head)
            delta = jnp.sum(probs * d_probs, axis=0, keepdims=True)
            d_scores = (probs * (d_probs - delta) * SCALE).astype(BF)
            d_key = dot_nn(d_scores, query)
            d_value = dot_nn(probs.astype(BF), d_head)
            if half == 1:
                sum_keys[...] = d_key
                sum_values[...] = d_value
            else:
                sum_keys[0:span, :] += d_key
                sum_values[0:span, :] += d_value
            raw = dot_tn(key, d_scores).T
            cosine = tables[0, 2 * half : 2 * half + 2, 0].reshape(256, HD)
            sine = tables[1, 2 * half : 2 * half + 2, 0].reshape(256, HD)
            column = pl.ds(pl.multiple_of(head * HD, HD), HD)
            d_query[rows, column] = turn(raw, cosine, -sine).astype(BF)
        cosine, sine = tables[0].reshape(SEQ, HD), tables[1].reshape(SEQ, HD)
        d_keys[:, column] = turn(sum_keys[...], cosine, -sine).astype(BF)
        d_values[:, column] = sum_values[...].astype(BF)
        return carry

    def attend_rest():
        lax.fori_loop(2, 4, back_attend, 0)
        at.grads = [
            wire.put(d_query, d_query_far, sibling(me)),
            wire.put(d_keys, d_keys_far, sibling(me)),
            wire.put(d_values, d_values_far, sibling(me)),
        ]

    plan.add(
        "ba0", lambda: lax.fori_loop(0, 2, back_attend, 0),
        loaded("query", "keys", "values", "lse", "tables"), ("dh", "bias"), 2,
    )
    plan.add("ba2", attend_rest, after=("ba0",), rank=2)

    def back_h(block, carry):
        y, zh = lax.div(block, 2), lax.rem(block, 2)

        def weight(which):
            return jnp.concatenate(
                [w_qkv[which, 0, y, zh].reshape(256, 256), w_qkv[which, 1, y, zh].reshape(256, 256)],
                axis=1,
            )

        column = pl.ds(pl.multiple_of(block * 256, 256), 256)
        both = dot_nt(d_keys[...], weight(1)) + dot_nt(d_values[...], weight(2))
        both = both.reshape(4, 2, 128, 256)
        own = dot_nt(d_query[...], weight(0)).reshape(4, 128, 256) + both[:, 0]
        d_h[:, 0, :, column] = own.astype(BF)
        d_h[:, 1, :, column] = both[:, 1].astype(BF)
        return carry

    own = RingSum(
        wire, me, "x",
        lambda slot, half: d_h.at[slot, 0] if half is None else d_h.at[slot, 0, :, pl.ds(half * 1024, 1024)],
        near_left, near_right, whole_left, whole_right, split_columns, add,
    )
    at.far_z, at.sides, at.last = {}, {}, {}

    def cut(ref, half):
        return ref.at[:, pl.ds(half * 1024, 1024)]

    def back_half(half):
        def run():
            lax.fori_loop(half * 4, half * 4 + 4, back_h, 0)
            at.far_z[half] = wire.put(cut(d_h.at[far, 1], half), cut(far_one, half), partner(me))
            at.sides[half] = [
                wire.put(cut(d_h.at[one, 1], half), cut(side_left, half), right),
                wire.put(cut(d_h.at[three, 1], half), cut(side_right, half), left),
            ]
            own.start_whole(half)

        return run

    def near_half(half):
        def run():
            add_into(cut(d_h.at[far, 0], half), [cut(far_one, half)])
            own.start_near(half)

        return run

    def last_half(half):
        def run():
            add_into(cut(d_h.at[me.x, 1], half), [cut(side_left, half), cut(side_right, half)])
            at.last[half] = wire.put(cut(d_h.at[me.x, 1], half), cut(last_z, half), partner(me))

        return run

    plan.add("bh0", back_half(0), loaded("qkv"), ("ba2", "l3"), 2)
    plan.add("bh1", back_half(1), after=("bh0",), rank=2)
    for half in range(2):
        name = "%d" % half
        plan.add("dn" + name, near_half(half), lambda half=half: [at.far_z[half]], ("bh" + name,), 0)
        plan.add("dl" + name, last_half(half), lambda half=half: at.sides[half], ("bh" + name,), 0.5)
    plan.add("ds.go", lambda: None, after=("dn0", "dn1"), rank=0)
    own.plan(plan, "ds", (), 0, go=False)

    def grad_o(index, carry):
        zl, y = lax.div(index, 4), lax.rem(index, 4)
        mine = jnp.concatenate(
            [
                d_attn[:, :, pl.ds(pl.multiple_of(((y * 2 + zh) * 2 + me.core) * 128, 128), 128)]
                .reshape(512, 128)
                for zh in range(2)
            ],
            axis=1,
        )
        other = jnp.concatenate(
            [attn_far[y * 2 + zh].reshape(512, 128) for zh in range(2)], axis=1
        )
        rows = pl.ds(pl.multiple_of(zl * 256, 256), 256)
        result = (dot_nn(heads_t[rows, :], mine) + dot_nn(heads_t_far[rows, :], other)).astype(BF)
        w_o[zl, y, 0, 0] = result[:, 0:128]
        w_o[zl, y, 1, 0] = result[:, 128:256]
        return carry

    plan.add("go", lambda: lax.fori_loop(0, 8, grad_o, 0), lambda: [at.heads, *at.attn], ("as", "ht", "dh"), 3)

    def blocks(which, pair):
        return turned[which, pl.ds(pair * 4, 4)].reshape(512, SEQ)

    def own_rows(value):
        return jnp.concatenate([value[:, i * 256 : i * 256 + 128] for i in range(4)], axis=1)

    def grad_qkv(index, carry):
        zl, pair = lax.div(index, 2), lax.rem(index, 2)
        column = pl.ds(pl.multiple_of(zl * 256, 256), 256)
        mine, other = blocks(0, pair), blocks(1, pair)
        query_grad = dot_nn(own_rows(mine), d_query[:, column])
        query_grad = query_grad + dot_nn(own_rows(other), d_query_far[:, column])
        key_grad = dot_nn(mine, d_keys[:, column]) + dot_nn(other, d_keys_far[:, column])
        value_grad = dot_nn(mine, d_values[:, column]) + dot_nn(other, d_values_far[:, column])
        along = jnp.where(zl == 0, 0.0, along_s[pair])
        for which, result in enumerate((query_grad, key_grad, value_grad)):
            weight = w_qkv[which, zl, pl.ds(pair * 2, 2), :, me.core].reshape(512, 256)
            product = weight.astype(F32) * result
            along = along + product[:, 0:128] + product[:, 128:256]
            w_qkv[which, zl, pl.ds(pair * 2, 2), :, 0] = result.astype(BF).reshape(2, 2, 128, 256)
        along_s[pair] = along
        return carry

    plan.add(
        "gq0", lambda: lax.fori_loop(0, 2, grad_qkv, 0),
        lambda: [loads["turned"], *at.grads], ("bh1",), 3,
    )
    plan.add("gq1", lambda: lax.fori_loop(2, 4, grad_qkv, 0), after=("gq0",), rank=3)

    g_qkv, g_o = w_qkv.at[:, :, :, :, 0], w_o.at[:, :, :, 0]
    rest = UNITS - SUM_Y
    for name, fold, waits, after, rank, result, target, where in (
        ("my", Fold(wire, me, 0, None, ("y", "z"), None, held_view(fold_y, 1, "z", SUM_Y, 0), groups[0]),
         loaded("fold_y"), ("l2",), 1.2, g_mlp_out, g_mlp_hbm, (pl.ds(0, 2), pl.ds(0, SUM_Y), ALL)),
        ("mz", Fold(wire, me, 144, None, ("z", "y"), None, held_view(fold_z, 1, "y", rest, 144), groups[1]),
         loaded("fold_z"), ("l2",), 1.2, g_mlp_out, g_mlp_hbm, (pl.ds(0, 2), pl.ds(SUM_Y, UNITS - SUM_Y), ALL)),
        ("oy", Fold(wire, me, O_CUT, fold_view(g_o, me, 0, "y", 0, O_Y, O_CUT), ("y", "z"), groups[2],
                    crossed_view(g_o, me, 0, "z", 0, O_Y, 0), groups[3]),
         tuple, ("go",), 1.4, g_o_out, g_o_hbm, (pl.ds(0, O_Y), ALL)),
        ("oz", Fold(wire, me, O_REST, fold_view(g_o, me, 0, "z", O_Y, 256 - O_Y, 0), ("z", "y"), groups[4],
                    crossed_view(g_o, me, 0, "y", O_Y, 256 - O_Y, O_REST), groups[5]),
         tuple, ("go",), 1.4, g_o_out, g_o_hbm, (pl.ds(O_Y, 256 - O_Y), ALL)),
        ("qy", Fold(wire, me, Q_CUT, fold_view(g_qkv, me, 1, "y", 0, Q_Y, Q_CUT), ("y", "z"), groups[6],
                    crossed_view(g_qkv, me, 1, "z", 0, Q_Y, 0), groups[7]),
         tuple, ("gq1",), 1, g_qkv_out, g_qkv_hbm, (ALL, pl.ds(0, Q_Y), ALL)),
        ("qz", Fold(wire, me, Q_REST, fold_view(g_qkv, me, 1, "z", Q_Y, 128 - Q_Y, 0), ("z", "y"),
                    groups[8], crossed_view(g_qkv, me, 1, "y", Q_Y, 128 - Q_Y, Q_REST), groups[9]),
         tuple, ("gq1",), 1, g_qkv_out, g_qkv_hbm, (ALL, pl.ds(Q_Y, 128 - Q_Y), ALL)),
        ("wy", Fold(wire, me, DN_CUT, fold_view(g_down, me, 0, "y", 0, DN_Y, DN_CUT), ("y", "z"),
                    groups[10], crossed_view(g_down, me, 0, "z", 0, DN_Y, 0), groups[11]),
         loaded("down"), ("l2",), 1.3, g_mlp_out, g_mlp_hbm, (2, pl.ds(0, DN_Y), ALL)),
        ("wz", Fold(wire, me, DN_REST, fold_view(g_down, me, 0, "z", DN_Y, UNITS - DN_Y, 0), ("z", "y"),
                    groups[12], crossed_view(g_down, me, 0, "y", DN_Y, UNITS - DN_Y, DN_REST), groups[13]),
         loaded("down"), ("l2",), 1.3, g_mlp_out, g_mlp_hbm, (2, pl.ds(DN_Y, UNITS - DN_Y), ALL)),
    ):
        fold.plan(
            plan, name, waits, after, rank, result.at[where],
            lambda result=result, target=target, where=where: keep(result.at[where], target.at[where]),
        )

    def back_norm(index, carry):
        span = pl.ds(pl.multiple_of(index * 16, 16), 16)
        d_h_one = (
            d_h[me.x, 0, span, :].astype(F32)
            + whole_left[span, :].astype(F32)
            + whole_right[span, :].astype(F32)
            + last_z[span, :].astype(F32)
        )
        value = tok[span, :].astype(F32)
        scale = lax.rsqrt(jnp.mean(value * value, axis=-1, keepdims=True) + EPS)
        normed = value * scale
        e_one = d_h_one * gains_in[0:1, :]
        inner = jnp.mean(e_one * normed, axis=-1, keepdims=True)
        tokens_out[span, :] = (dy_in[span, :] + scale * (e_one - normed * inner)).astype(BF)
        return carry

    def feed_x():
        for block in range(16):
            gain_x[me.x, block : block + 1, :] = gain_in[0:1, block * 128 : block * 128 + 128]
        at.feed = Meet(wire, me, "x", gain_x).copies

    def feed_z():
        gain_z[me.z] = gain_x[0] + gain_x[1] + gain_x[2] + gain_x[3]
        at.feed = Meet(wire, me, "z", gain_z).copies

    def feed_y():
        gain_c[me.core, me.y] = gain_z[0] + gain_z[1] + gain_z[2] + gain_z[3]
        at.feed = MeetCores(wire, me, gain_c).copies

    def feed_all():
        total = gain_c[0, 0]
        for core, y in ((0, 1), (0, 2), (0, 3), (1, 0), (1, 1), (1, 2), (1, 3)):
            total = total + gain_c[core, y]
        gain_t[...] = total
        row = (me.y * 2 + me.zh) * 2 + me.core
        gains_out[1:2, :] = gain_t[pl.ds(row, 1), :]

    plan.add("mx", feed_x, loaded("gain"), ("l2",), 1)
    plan.add("mz.", feed_z, lambda: at.feed, ("mx",), 1)
    plan.add("my.", feed_y, lambda: at.feed, ("mz.",), 1)
    plan.add("m.", feed_all, lambda: at.feed, ("my.",), 1)

    def along_x():
        ones = jnp.ones((8, 128), F32)
        for pair in range(2):
            line = lax.dot_general(
                ones, along_s[pair], (((1,), (1,)), ((), ())), precision=lax.Precision.HIGHEST,
                preferred_element_type=F32,
            )
            for k in range(4):
                along_a[me.x, pair * 4 + k : pair * 4 + k + 1, :] = line[0:1, k * 128 : k * 128 + 128]
        at.along = Meet(wire, me, "x", along_a).copies

    def along_z():
        along_b[me.z] = along_a[0] + along_a[1] + along_a[2] + along_a[3]
        at.along = Meet(wire, me, "z", along_b).copies

    def along_y():
        along_c[me.y] = along_b[0] + along_b[1] + along_b[2] + along_b[3]
        at.along = Meet(wire, me, "y", along_c).copies

    def along_all():
        along_t[...] = along_c[0] + along_c[1] + along_c[2] + along_c[3]
        row = me.y * 2 + me.zh
        column = pl.ds(pl.multiple_of((row * 2 + me.core) * 128, 128), 128)
        gains_out[0:1, :] = along_t[pl.ds(row, 1), :] / gains_in[0:1, column]

    plan.add("ax", along_x, after=("gq1",), rank=1)
    plan.add("az", along_z, lambda: at.along, ("ax",), 1)
    plan.add("ay", along_y, lambda: at.along, ("az",), 1)
    plan.add("a.", along_all, lambda: [*loaded("gains")(), *at.along], ("ay",), 1)
    plan.add("gk", lambda: keep(gains_out, g_gains_hbm), after=("a.", "m."), rank=2)

    def back_all():
        lax.fori_loop(0, 8, back_norm, 0)
        keep(tokens_out, grad_tokens_hbm)

    plan.add(
        "bn", back_all,
        lambda: [*loaded("tok", "dy", "gains")(), at.last[0], at.last[1]], ("ds.far", "dl0", "dl1"), 0,
    )
    plan.go(ORDER_BACK)
    for copy in kept:
        copy.wait()
    wire.drain()


def call_back(starts, tokens, d_attn, out_part, qkv, w_out, query, keys, values, heads, lse, turned,
              tables, gains, y_one, d_y, gain_two, fold_y, fold_z, down):
    shape = jax.ShapeDtypeStruct

    def three(*dims):
        return [pltpu.VMEM(dims, BF)] * 3

    rest = UNITS - SUM_Y
    bufs = (
        three(2, SUM_Y, 128)
        + fold_shapes((2,), (), rest, 144, 128)
        + fold_shapes((), (2, 2), O_Y, O_CUT, 128)
        + three(O_Y, 128)
        + three(4, 256 - O_Y, 128)
        + fold_shapes((), (), 256 - O_Y, O_REST, 128)
        + fold_shapes((3,), (2, 2), Q_Y, Q_CUT, 256)
        + three(3, Q_Y, 256)
        + three(3, 4, 128 - Q_Y, 256)
        + fold_shapes((3,), (), 128 - Q_Y, Q_REST, 256)
        + fold_shapes((), (2, 2), DN_Y, DN_CUT, 128)
        + three(DN_Y, 128)
        + three(4, UNITS - DN_Y, 128)
        + fold_shapes((), (), UNITS - DN_Y, DN_REST, 128)
    )
    return pl.pallas_call(
        kernel_back,
        name="back",
        in_specs=[pl.BlockSpec(memory_space=pltpu.SMEM)] + [anywhere()] * 19,
        out_specs=[anywhere()] * 6,
        out_shape=[
            shape((128, D), BF),
            shape((128, D), BF),
            shape((3, 128, 256), F32),
            shape((256, 128), F32),
            shape((3, UNITS, 128), F32),
            shape((2, 128), F32),
        ],
        scratch_shapes=[
            pltpu.VMEM((4, 512, HD), BF),
            pltpu.VMEM((4, 4, 2, 128, HD), BF),
            pltpu.VMEM((4, 4, 2, 128, HD), BF),
            pltpu.VMEM((4, 1, 512), F32),
            pltpu.VMEM((8, D), F32),
            pltpu.VMEM((128, D), F32),
            pltpu.VMEM((128, D), F32),
            pltpu.VMEM((1, D), F32),
            pltpu.VMEM((128, D), BF),
            pltpu.VMEM((128, D), BF),
            pltpu.VMEM((3, 128, 256), F32),
            pltpu.VMEM((256, 128), F32),
            pltpu.VMEM((3, UNITS, 128), F32),
            pltpu.VMEM((2, 128), F32),
            pltpu.VMEM((3, 2, 4, 2, 2, 128, 256), BF),
            pltpu.VMEM((2, 4, 2, 2, 256, 128), BF),
            pltpu.VMEM((4, 128, D), BF),
            pltpu.VMEM((4, 128, D), BF),
            pltpu.VMEM((2, 4, 2, 128, HD), F32),
            pltpu.VMEM((4, 2, 128, 512), F32),
            pltpu.VMEM((128, D), BF),
            pltpu.VMEM((2, 8, 128, SEQ), BF),
            pltpu.VMEM((4, 512, HD), BF),
            pltpu.VMEM((512, 512), BF),
            pltpu.VMEM((SEQ, 512), BF),
            pltpu.VMEM((SEQ, 512), BF),
            pltpu.VMEM((512, 512), BF),
            pltpu.VMEM((SEQ, 512), BF),
            pltpu.VMEM((SEQ, 512), BF),
            pltpu.VMEM((SEQ, HD), F32),
            pltpu.VMEM((SEQ, HD), F32),
            pltpu.VMEM((512, 512), BF),
            pltpu.VMEM((512, 512), BF),
            pltpu.VMEM((8, 4, 128, 128), BF),
            pltpu.VMEM((4, 2, 128, D), BF),
        ]
        + [pltpu.VMEM((128, D), BF)] * 4
        + [
            pltpu.VMEM((128, D // 2), BF),
            pltpu.VMEM((128, D // 2), BF),
            pltpu.VMEM((128, D), BF),
            pltpu.VMEM((128, D), BF),
        ]
        * 2
        + [
            pltpu.VMEM((2, 2, 2, SUM_Y, 128), BF),
            pltpu.VMEM((2, 4, UNITS - SUM_Y, 128), BF),
            pltpu.VMEM((2, 4, 2, UNITS, 128), BF),
            pltpu.VMEM((4, 16, 128), F32),
            pltpu.VMEM((4, 16, 128), F32),
            pltpu.VMEM((2, 4, 16, 128), F32),
            pltpu.VMEM((2, 512, 128), F32),
            pltpu.VMEM((4, 8, 128), F32),
            pltpu.VMEM((4, 8, 128), F32),
            pltpu.VMEM((4, 8, 128), F32),
            pltpu.VMEM((16, 128), F32),
            pltpu.VMEM((8, 128), F32),
        ]
        + bufs
        + [
            pltpu.SemaphoreType.DMA((140,)),
            pltpu.SemaphoreType.DMA((140,)),
            pltpu.SemaphoreType.DMA((40,)),
        ],
        compiler_params=pltpu.CompilerParams(
            collective_id=2, has_side_effects=True, vmem_limit_bytes=VMEM_BYTES
        ),
    )(starts, tokens, d_attn, out_part, qkv, w_out, query, keys, values, heads, lse, turned,
      tables, gains, y_one, d_y, gain_two, fold_y, fold_z, down)


def kernel_settle(result_in, tokens_in, qkv_in, o_in, mlp_in, gains_in,
                  result, tokens, query, key, value, out, gate, up, down, attn, feed):
    tp = lax.axis_index("tensor")
    result[...] = result_in[...]
    tokens[...] = tokens_in[...]
    for index, target in enumerate((query, key, value)):
        target[...] = qkv_in[index]
    out[...] = o_in[...]
    for index, target in enumerate((gate, up, down)):
        target[...] = mlp_in[index]
    for index, target in enumerate((attn, feed)):
        row = gains_in[index : index + 1, :]
        target[...] = pltpu.roll(row, lax.rem(128 - tp * 16, 128), 1)[:, 0:16]


def call_settle(*arrays):
    shape = jax.ShapeDtypeStruct
    return pl.pallas_call(
        kernel_settle,
        name="settle",
        in_specs=[in_vmem()] * 6,
        out_specs=[in_vmem()] * 11,
        out_shape=[shape((128, D), BF)] * 2
        + [shape((128, 256), F32)] * 3
        + [shape((256, 128), F32)]
        + [shape((UNITS, 128), F32)] * 3
        + [shape((1, 16), F32)] * 2,
        compiler_params=pltpu.CompilerParams(vmem_limit_bytes=VMEM_BYTES),
    )(*arrays)


def on_device(tables, tokens, starts, w_query, w_key, w_value, w_out, w_gate, w_up, w_down,
              gain_attn, gain_mlp, cotangent):
    weights = (w_query, w_key, w_value, w_out, w_gate.T, w_up.T, w_down)
    (qkv, w_o, mlp, cot, turned, query, keys, values, heads, h_two, lse, y_one, gains) = call_attend(
        tokens, cotangent, starts, weights, gain_attn.reshape(1, 16), gain_mlp.reshape(1, 16), tables
    )
    out_part, d_attn, fold_y, fold_z, down, d_y, gain_two = call_feed(h_two, cot, mlp, y_one, gains)
    sums = call_back(
        starts, tokens, d_attn, out_part, qkv, w_o, query, keys, values, heads, lse, turned,
        tables, gains, y_one, d_y, gain_two, fold_y, fold_z, down,
    )
    result, grad_tokens, query, key, value, out, gate, up, down, attn, feed = call_settle(*sums)
    return (
        result, grad_tokens, query, key, value, out, gate.T, up.T, down,
        attn.reshape(16), feed.reshape(16),
    )


def solution(mesh):
    both = ("dp", "tensor")
    rows, wide, tall = P(both, None), P("dp", "tensor"), P("tensor", "dp")
    in_specs = (
        rows, P("dp"), wide, wide, wide, tall, wide, wide, tall, P(both), P(both), rows,
    )
    out_specs = (
        rows, rows, wide, wide, wide, tall, wide, wide, tall, P(both), P(both),
    )
    return jax.shard_map(
        functools.partial(on_device, rope_tables()), mesh=mesh, in_specs=in_specs,
        out_specs=out_specs, check_vma=False,
    )
```

```python
import functools
import math
import types

import jax
import jax.numpy as jnp
import numpy as np
from jax import lax
from jax.experimental import pallas as pl
from jax.experimental.pallas import tpu as pltpu
from jax.sharding import PartitionSpec as P

HD = 128
PIECE = 256
EPS = 1e-05
NEG = -1e30
SCALE = HD ** (-0.5)
D = 2048
SEQ = 1024
UNITS = 688
BF = jnp.bfloat16
F32 = jnp.float32
MESH = pl.DeviceIdType.MESH
VMEM_BYTES = 60 * 1024 * 1024
ALL = slice(None)


def dot_nn(left, right):
    return jnp.dot(left, right, preferred_element_type=F32)


def dot_nt(left, right):
    return lax.dot_general(left, right, (((1,), (1,)), ((), ())), preferred_element_type=F32)


def dot_tn(left, right):
    return lax.dot_general(left, right, (((0,), (0,)), ((), ())), preferred_element_type=F32)


def rem4(value):
    return lax.rem(value, 4)


def place():
    dp = lax.axis_index("dp")
    tp = lax.axis_index("tensor")
    zh = lax.rem(lax.div(dp, 2), 2)
    zl = lax.rem(tp, 2)
    return types.SimpleNamespace(
        y=lax.div(dp, 4), zh=zh, zl=zl, z=zh * 2 + zl, x=lax.div(tp, 2), core=lax.rem(dp, 2)
    )


def device(me, **moved):
    at = types.SimpleNamespace(**{**vars(me), **moved})
    zh, zl = lax.div(at.z, 2), lax.rem(at.z, 2)
    return (at.y * 4 + zh * 2 + at.core, at.x * 2 + zl)


def near(me, axis, step):
    return device(me, **{axis: rem4(getattr(me, axis) + step)})


def sibling(me):
    return device(me, core=1 - me.core)


def partner(me):
    return device(me, z=me.zh * 2 + 1 - me.zl)


def across(me):
    return device(me, z=rem4(me.z + 3 + 2 * me.zl))


def greet(me, wide, meanwhile=()):
    others = [near(me, axis, step) for axis in ("x", "y", "z") for step in (1, 3)] + [sibling(me)]
    if wide:
        others += [near(me, axis, 2) for axis in ("x", "y", "z")]
        others += [crossed(me, step) for step in (1, 2, 3)]
    barrier = pltpu.get_barrier_semaphore()
    for other in others:
        pl.semaphore_signal(barrier, inc=1, device_id=other, device_id_type=MESH)
    for copy in meanwhile:
        copy.wait()
    pl.semaphore_wait(barrier, len(others))


def crossed(me, step):
    return device(me, y=rem4(me.y + step), core=1 - me.core)


class Plan:
    def __init__(self):
        self.steps = {}

    def add(self, name, run, waits=tuple, after=(), rank=5):
        self.steps[name] = types.SimpleNamespace(run=run, waits=waits, after=after, rank=rank)

    def go(self, order):
        assert sorted(order) == sorted(self.steps)
        for name in order:
            step = self.steps[name]
            for copy in step.waits():
                copy.wait_recv()
            step.run()


class Once:
    def __init__(self, copy, remote):
        self.copy, self.remote = copy, remote
        self.received = self.left = False

    def wait_recv(self):
        if not self.received:
            self.received = True
            if self.remote:
                self.copy.wait_recv()
            else:
                self.copy.wait()

    wait = wait_recv

    def wait_send(self):
        if not self.left:
            self.left = True
            self.copy.wait_send()


class Wire:
    def __init__(self, send, recv, local):
        self.send, self.recv, self.local = send, recv, local
        self.used, self.used_local = 0, 0
        self.sent = []

    def put(self, source, target, to):
        index = self.used
        self.used += 1
        assert index < self.send.shape[0]
        copy = pltpu.make_async_remote_copy(
            src_ref=source,
            dst_ref=target,
            send_sem=self.send.at[index],
            recv_sem=self.recv.at[index],
            device_id=to,
            device_id_type=MESH,
        )
        copy.start()
        copy = Once(copy, True)
        self.sent.append(copy)
        return copy

    def move(self, source, target):
        index = self.used_local
        self.used_local += 1
        assert index < self.local.shape[0]
        copy = pltpu.make_async_copy(source, target, self.local.at[index])
        copy.start()
        return Once(copy, False)

    def drain(self):
        for copy in self.sent:
            copy.wait_send()
        self.sent = []


class Ring:
    def __init__(self, wire, me, axis, view):
        self.wire, self.view = wire, view
        self.at = getattr(me, axis)
        self.right, self.left = near(me, axis, 1), near(me, axis, 3)

    def put(self, slot, part, to):
        piece = self.view(slot, part)
        return self.wire.put(piece, piece, to)

    def start(self):
        self.right_one = self.put(self.at, 0, self.right)
        self.left_one = self.put(self.at, 1, self.left)
        self.right_two = self.put(self.at, 1, self.right)
        self.left_two = self.put(self.at, 0, self.left)

    def start_half(self, half):
        if half == 0:
            self.right_one = self.put(self.at, 0, self.right)
            self.left_two = self.put(self.at, 0, self.left)
        else:
            self.left_one = self.put(self.at, 1, self.left)
            self.right_two = self.put(self.at, 1, self.right)

    def plan(self, plan, name, after, rank):
        plan.add(name + ".go", self.start, after=after, rank=rank)
        plan.add(name + ".r", self.relay_right, lambda: [self.right_one], (name + ".go",), rank)
        plan.add(name + ".l", self.relay_left, lambda: [self.left_one], (name + ".go",), rank)
        plan.add(
            name + ".near", lambda: None, lambda: [self.right_two, self.left_two],
            (name + ".r", name + ".l"), rank,
        )
        plan.add(
            name + ".far", lambda: None, lambda: [self.far_right, self.far_left], (name + ".near",), rank
        )

    def relay_right(self):
        self.far_right = self.put(rem4(self.at + 3), 0, self.right)

    def relay_left(self):
        self.far_left = self.put(rem4(self.at + 1), 1, self.left)

    def copies(self):
        return [
            self.right_one, self.left_one, self.right_two, self.left_two, self.far_right, self.far_left
        ]

    def closed(self):
        return rem4(self.at + 3), rem4(self.at + 1)


class Direct:
    def __init__(self, wire, me, view):
        self.wire, self.view, self.me, self.at = wire, view, me, me.z

    def start(self):
        piece = self.view(self.at, None)
        others = (partner(self.me), across(self.me), near(self.me, "z", 2))
        self.copies = [self.wire.put(piece, piece, other) for other in others]

    def plan(self, plan, name, after, rank):
        plan.add(name + ".go", self.start, after=after, rank=rank)
        plan.add(name + ".far", lambda: None, lambda: self.copies, (name + ".go",), rank)


class PairRing:
    def __init__(self, wire, me, view):
        self.wire, self.view, self.me = wire, view, me
        self.at = me.z
        self.mate, self.beyond = me.zh * 2 + 1 - me.zl, rem4(me.z + 3 + 2 * me.zl)

    def put(self, slot, to):
        piece = self.view(slot, None)
        return self.wire.put(piece, piece, to)

    def start(self):
        self.to_mate = self.put(self.at, partner(self.me))
        self.to_beyond = self.put(self.at, across(self.me))

    def plan(self, plan, name, after, rank):
        plan.add(name + ".go", self.start, after=after, rank=rank)
        plan.add(name + ".r", self.relay, lambda: [self.to_mate], (name + ".go",), rank)
        plan.add(name + ".near", lambda: None, lambda: [self.to_beyond], (name + ".r",), rank)
        plan.add(name + ".far", lambda: None, lambda: [self.far], (name + ".near",), rank)

    def relay(self):
        self.far = self.put(self.mate, across(self.me))

    def copies(self):
        return [self.to_mate, self.to_beyond, self.far]

    def closed(self):
        return self.mate, self.beyond


class Meet:
    def __init__(self, wire, me, axis, ref):
        piece = ref.at[getattr(me, axis)]
        self.copies = [wire.put(piece, piece, near(me, axis, step)) for step in (1, 2, 3)]


class MeetCores:
    def __init__(self, wire, me, ref):
        piece = ref.at[me.core, me.y]
        others = [near(me, "y", step) for step in (1, 2, 3)] + [sibling(me)]
        others += [crossed(me, step) for step in (1, 2, 3)]
        self.copies = [wire.put(piece, piece, other) for other in others]


class RingSum:
    def __init__(self, wire, me, axis, part, from_left, from_right, whole_left, whole_right, split, add):
        self.wire, self.part, self.split, self.add = wire, part, split, add
        self.at = getattr(me, axis)
        self.right, self.left = near(me, axis, 1), near(me, axis, 3)
        self.near_bufs = (from_left, from_right)
        self.whole = (whole_left, whole_right)

    def start_near(self, half):
        piece = self.part(rem4(self.at + 2), half)
        to = self.left if half else self.right
        copy = self.wire.put(piece, self.near_bufs[half], to)
        if half:
            self.second = copy
        else:
            self.first = copy

    def start_whole(self, half):
        if half:
            self.right_whole = self.wire.put(
                self.part(rem4(self.at + 1), 1), self.split(self.whole[0], 1), self.right
            )
        else:
            self.left_whole = self.wire.put(
                self.part(rem4(self.at + 3), 0), self.split(self.whole[1], 0), self.left
            )

    def start(self, halves=(0, 1)):
        for half in halves:
            self.start_near(half)
        if 1 in halves:
            self.start_whole(1)
            self.start_whole(0)

    def plan(self, plan, name, after, rank, go=True):
        if go:
            plan.add(name + ".go", self.start, after=after, rank=rank)
        plan.add(name + ".r", self.relay_right, lambda: [self.first], (name + ".go",), rank)
        plan.add(name + ".l", self.relay_left, lambda: [self.second], (name + ".go",), rank)
        plan.add(
            name + ".far",
            lambda: None,
            lambda: [self.left_whole, self.right_whole, self.to_right, self.to_left],
            (name + ".r", name + ".l"),
            rank,
        )

    def relay_right(self):
        after = rem4(self.at + 1)
        self.add(self.part(after, 0), self.near_bufs[0])
        self.to_right = self.wire.put(self.part(after, 0), self.split(self.whole[0], 0), self.right)

    def relay_left(self):
        before = rem4(self.at + 3)
        self.add(self.part(before, 1), self.near_bufs[1])
        self.to_left = self.wire.put(self.part(before, 1), self.split(self.whole[1], 1), self.left)


class PairSum:
    def __init__(self, wire, me, part, from_beyond, for_mate, from_mate, add):
        self.wire, self.me, self.part, self.add = wire, me, part, add
        self.at = me.z
        self.mate, self.beyond = me.zh * 2 + 1 - me.zl, rem4(me.z + 3 + 2 * me.zl)
        self.for_mate, self.whole = for_mate, (from_beyond, from_mate)

    def start(self):
        far = rem4(self.at + 2)
        self.first = self.wire.put(self.part(far, None), self.for_mate, across(self.me))
        self.second = self.wire.put(self.part(self.beyond, None), self.whole[0], across(self.me))

    def plan(self, plan, name, after, rank):
        plan.add(name + ".go", self.start, after=after, rank=rank)
        plan.add(name + ".r", self.relay, lambda: [self.first], (name + ".go",), rank)
        plan.add(
            name + ".far", lambda: None, lambda: [self.second, self.to_mate], (name + ".r",), rank
        )

    def relay(self):
        self.add(self.part(self.mate, None), self.for_mate)
        self.to_mate = self.wire.put(self.part(self.mate, None), self.whole[1], partner(self.me))


def split_columns(ref, half):
    return ref.at[:, pl.ds(half * (D // 2), D // 2)]


def split_rows(cut):
    def split(ref, half):
        rows = ref.shape[-2]
        span = pl.ds(0, cut) if half == 0 else pl.ds(cut, rows - cut)
        return ref.at[(ALL,) * (len(ref.shape) - 2) + (span, ALL)]

    return split


class Spread:
    def __init__(self, wire, me, ref, lead, row, rows, first, cut, cuts=(ALL,), kind=PairRing):
        self.wire, self.me = wire, me
        head = (ALL,) * lead

        def view(y, z, part, low=ALL):
            zl, zh = (low, ALL) if z is None else (lax.rem(z, 2), lax.div(z, 2))
            start, size = row, rows
            if part == 0:
                size = cut
            if part == 1:
                start, size = row + cut, rows - cut
            yy = ALL if y is None else y
            return ref.at[head + (zl, yy, zh, me.core, pl.ds(start, size), ALL)]

        if first == "y":
            self.one = Ring(wire, me, "y", lambda slot, part: view(slot, me.z, part))
            self.twos = [PairRing(wire, me, lambda slot, part: view(None, slot, part))]
        else:
            self.one = kind(wire, me, lambda slot, part: view(me.y, slot, part))
            self.twos = [
                Ring(wire, me, "y", lambda slot, part, low=low: view(slot, None, part, low))
                for low in cuts
            ]

    def plan(self, plan, name, after, turn_after, rank):
        self.one.plan(plan, name + ".a", after, rank)
        self.plan_second(plan, name, (name + ".a.far", *turn_after), rank)

    def plan_second(self, plan, name, done, rank):
        done = list(done)
        self.shared = []
        for index, two in enumerate(self.twos):
            tail = str(index) if len(self.twos) > 1 else ""
            self.plan_two(plan, two, name, tail, tuple(done), rank + 0.01 * index)
            done += [name + ".b" + tail + ".r", name + ".b" + tail + ".l"] if tail else []

    def plan_two(self, plan, two, name, tail, after, rank):
        shared = []

        def share(slots):
            for slot in slots:
                piece = two.view(slot, None)
                shared.append(self.wire.put(piece, piece, sibling(self.me)))
            self.shared += shared[-len(slots) :]

        def go():
            two.start()
            share([two.at])

        step = name + ".b" + tail
        two.plan(plan, step, after, rank)
        plan.steps[step + ".go"].run = go
        plan.add(name + ".s" + tail, lambda: share(two.closed()), after=(step + ".near",), rank=rank)
        plan.add(
            name + ".t" + tail, lambda: share([rem4(two.at + 2)]),
            after=(name + ".s" + tail, step + ".far"), rank=rank,
        )
        plan.add(name + ".all" + tail, lambda: None, lambda: shared, (name + ".t" + tail,), rank)
MLP_Y, MLP_CUT, MLP_REST = 288, 144, 208
QKV_Y, QY_CUT, QZ_CUT = 32, 16, 48
QZ_KIND = PairRing
OUT_Y, OUT_CUT, OUT_REST = 64, 32, 96
MZ_AFTER, MZ_TURN = (), ()
MY_AFTER, MY_TURN = (), ()
ORDER_ATTEND = (
    "qz.a.go", "gx", "tz", "qy.a.go", "oy.a.go", "my.a.go", "tx.go", "bias", "qy.a.r", "qy.a.l",
    "gz", "qy.a.near", "oy.a.r", "oy.a.l", "oy.a.near", "qz.a.r", "qz.a.near", "my.a.r", "my.a.l",
    "my.a.near", "qy.a.far", "qy.b.go", "oz.a.go", "oy.a.far", "oy.b.go", "mz.a.go", "tx.r",
    "tx.l", "my.a.far", "qz.a.far", "qz.b0.go", "tx.near", "qz.b0.r", "qz.b0.l", "to", "gy",
    "qz.b0.near", "qz.s0", "tx.far", "tf", "qz.b1.go", "cx.go", "qy.b.r", "qy.b.near", "qy.s",
    "oz.a.r", "oz.a.near", "qz.b0.far", "qz.t0", "oy.b.r", "oy.b.near", "gains", "n1", "qz.all0",
    "oy.s", "n2", "n0", "qz.b1.r", "qz.b1.l", "qy.b.far", "qy.t", "n3", "mz.a.r", "mz.a.near",
    "oz.a.far", "oz.b.go", "qy.all", "proj0", "qz.b1.near", "qz.s1", "own0", "my.b.go",
    "qz.b1.far", "n4", "qz.t1", "oy.b.far", "oy.t", "oz.b.r", "oz.b.l", "rest0", "mz.a.far",
    "mz.b.go", "qz.all1", "rest1", "oy.all", "proj1", "cx.l", "own2", "n5", "last0", "cx.r",
    "oz.b.near", "oz.s", "oz.b.far", "att0", "cx.near", "wz.go", "oz.t", "last1", "att2",
    "oz.all", "po", "ys.go", "cx.far", "mz.b.r", "ck", "ht", "mz.b.l", "my.b.r", "my.b.near",
    "my.s", "flip", "wz.r", "flip2", "wz.near", "mz.b.near", "mz.s", "ys.r", "wy.go", "ys.l",
    "flip3", "mz.b.far", "mz.t", "mz0", "wy.l", "wy.r", "my.b.far", "my.t", "my0", "wy.near",
    "mz.all", "mz1", "wz.far", "wz0", "my.all", "my1", "ys.far", "fin", "wy.far", "wy0",
)

UP_Y, UP_CUT, UP_REST = 320, 160, 176


def up_spreads(wire, me, ref):
    return (
        Spread(wire, me, ref, 0, UP_Y, UNITS - UP_Y, "z", UP_REST),
        Spread(wire, me, ref, 0, 0, UP_Y, "y", UP_CUT),
    )


def norm_rows(source, target, gain, rows, step=32):
    def body(index, carry):
        span = pl.ds(pl.multiple_of(index * step, step), step)
        value = source[span, :].astype(F32)
        scale = lax.rsqrt(jnp.mean(value * value, axis=-1, keepdims=True) + EPS)
        target[span, :] = (value * scale * gain).astype(BF)
        return carry

    lax.fori_loop(0, rows // step, body, 0)


def fill_bias(bias, me, start):
    row = lax.broadcasted_iota(jnp.int32, (128, 512), 0)
    column = lax.broadcasted_iota(jnp.int32, (128, 512), 1)
    query = lax.div(column, 128) * 256 + me.zl * 128 + lax.rem(column, 128)
    query_in = (query >= start) & (query < start + PIECE)

    def body(block, carry):
        pair, other = lax.div(block, 2), lax.rem(block, 2)
        parity = me.zl + other * (1 - 2 * me.zl)
        key = (pair * 2 + parity) * 128 + row
        key_in = (key >= start) & (key < start + PIECE)
        allowed = (key <= query) | (query_in & key_in)
        bias[pair, other] = jnp.where(allowed, 0.0, NEG)
        return carry

    lax.fori_loop(0, 8, body, 0)


def turn(field, cosine, sine):
    return field * cosine + pltpu.roll(field, HD // 2, 1) * sine


def add_into(target, terms, result=None):
    shape = target.shape
    lead, rows, columns = shape[:-2], shape[-2], shape[-1]
    step = rows
    while step * columns > 33000:
        step = next(s for s in range(step - 16, 0, -16) if rows % s == 0)
    cuts = rows // step
    result = target if result is None else result

    def body(index, carry):
        where, rest = [], lax.div(index, cuts)
        for extent in reversed(lead):
            where.insert(0, lax.rem(rest, extent))
            rest = lax.div(rest, extent)
        where = tuple(where) + (
            pl.ds(pl.multiple_of(lax.rem(index, cuts) * step, 16), step), ALL
        )
        total = target[where].astype(F32)
        for term in terms:
            total = total + term[where].astype(F32)
        result[where] = total.astype(result.dtype)
        return carry

    lax.fori_loop(0, math.prod(lead) * cuts, body, 0)


def columns_of(ref):
    def view(slot, half):
        if half is None:
            return ref.at[slot]
        return ref.at[slot, :, pl.ds(half * (D // 2), D // 2)]

    return view


def rows_of(ref):
    def view(slot, half):
        return ref.at[slot] if half is None else ref.at[slot, pl.ds(half * 64, 64)]

    return view


def kernel_attend(
    tokens_in, cotangent_in, start_in, query_w, key_w, value_w, out_w, gate_w, up_w, down_w,
    gain_one_in, gain_two_in, tables_in,
    qkv_out, wo_out, mlp_out, cot_out, turned_out, query_out, keys_out, values_out, heads_out,
    h_out, lse_hbm, y_hbm, gains_hbm,
    lse_out, y_out, gains_out, tok, h_one, w_qkv, w_o, w_mlp, tables, bias, query, keys, values, heads, cot, h_two,
    part, near_left, near_right, whole_left, whole_right,
    turned, heads_t, top_s, total_s, result_s, gain_x, gain_z, gain_c,
    send, recv, local,
):
    me = place()
    wire = Wire(send, recv, local)
    own = [wire.move(tokens_in, tok.at[me.x, 0])]
    for index, ref in enumerate((query_w, key_w, value_w)):
        own.append(wire.move(ref, w_qkv.at[index, me.zl, me.y, me.zh, me.core]))
    own.append(wire.move(out_w, w_o.at[me.zl, me.y, me.zh, me.core]))
    for index, ref in enumerate((gate_w, down_w, up_w)):
        own.append(wire.move(ref, w_mlp.at[index, me.zl, me.y, me.zh, me.core]))
    own.append(wire.move(tables_in.at[me.zl], tables))
    own.append(wire.move(cotangent_in, cot.at[me.x]))
    lane = lax.div(lax.broadcasted_iota(jnp.int32, (1, 128), 1), 16)
    tensor = me.x * 2 + me.zl
    gain_x[me.x] = jnp.concatenate(
        [
            jnp.where(lane == tensor, jnp.concatenate([ref[...]] * 8, axis=1), 0.0)
            for ref in (gain_one_in, gain_two_in)
        ]
        + [jnp.zeros((6, 128), F32)],
        axis=0,
    )
    greet(me, True, own)
    plan = Plan()
    at = types.SimpleNamespace()
    one, far, three = rem4(me.x + 1), rem4(me.x + 2), rem4(me.x + 3)
    kept = []

    def keep(source, target):
        kept.append(wire.move(source, target))

    def gains_x():
        at.gains = Meet(wire, me, "x", gain_x).copies

    def gains_z():
        gain_z[me.z] = gain_x[0] + gain_x[1] + gain_x[2] + gain_x[3]
        at.gains = Meet(wire, me, "z", gain_z).copies

    def gains_y():
        gain_c[me.core, me.y, 0] = gain_z[0] + gain_z[1]
        gain_c[me.core, me.y, 1] = gain_z[2] + gain_z[3]
        at.gains = MeetCores(wire, me, gain_c).copies

    def gains_all():
        for y in range(4):
            for zh in range(2):
                for core in range(2):
                    column = (y * 4 + zh * 2 + core) * 128
                    gains_out[:, column : column + 128] = gain_c[core, y, zh]

    plan.add("gx", gains_x, rank=0)
    plan.add("gz", gains_z, lambda: at.gains, ("gx",), 0)
    plan.add("gy", gains_y, lambda: at.gains, ("gz",), 0)
    plan.add("gains", gains_all, lambda: at.gains, ("gy",), 1)

    def tokens_z():
        at.rows_z = wire.put(tok.at[me.x, 0], tok.at[me.x, 1], partner(me))

    def tokens_on():
        at.on = [
            wire.put(tok.at[me.x, 1], tok.at[me.x, 1], near(me, "x", step)) for step in (1, 3)
        ]

    def tokens_far():
        at.far_z = wire.put(tok.at[far, 0], tok.at[far, 1], partner(me))

    Ring(
        wire, me, "x",
        lambda slot, half: tok.at[slot, 0] if half is None else tok.at[slot, 0, pl.ds(half * 64, 64)],
    ).plan(plan, "tx", (), 0)
    plan.add("tz", tokens_z, rank=0)
    plan.add("to", tokens_on, lambda: [at.rows_z], ("tz",), 0)
    plan.add("tf", tokens_far, after=("tx.far",), rank=0)

    def norm(*blocks):
        def run():
            for slot, p in blocks:
                norm_rows(tok.at[slot, p], h_one.at[slot, p], gains_out[0:1, :], 128)

        return run

    plan.add("n0", norm((me.x, 0)), after=("gains",), rank=2)
    plan.add("n1", norm((one, 0), (three, 0)), after=("gains", "tx.near"), rank=2)
    plan.add("n2", norm((far, 0)), after=("gains", "tx.far"), rank=2)
    plan.add("n3", norm((me.x, 1)), after=("gains", "to"), rank=3)
    plan.add("n4", norm((one, 1), (three, 1)), lambda: at.on, ("gains", "to"), 3)
    plan.add("n5", norm((far, 1)), lambda: [at.far_z], ("gains", "tf"), 2)

    Spread(wire, me, w_qkv, 1, QKV_Y, 128 - QKV_Y, "z", QZ_CUT, (0, 1), QZ_KIND).plan(plan, "qz", (), (), 1)
    Spread(wire, me, w_qkv, 1, 0, QKV_Y, "y", QY_CUT).plan(plan, "qy", (), (), 1)
    Spread(wire, me, w_o, 0, OUT_Y, 256 - OUT_Y, "z", OUT_REST).plan(plan, "oz", (), (), 1)
    Spread(wire, me, w_o, 0, 0, OUT_Y, "y", OUT_CUT).plan(plan, "oy", (), (), 1)
    both = w_mlp.at[pl.ds(0, 2)]
    mlp_z = Spread(wire, me, both, 1, MLP_Y, UNITS - MLP_Y, "z", MLP_REST)
    mlp_y = Spread(wire, me, both, 1, 0, MLP_Y, "y", MLP_CUT)
    mlp_z.plan(plan, "mz", (), (), 1.5)
    mlp_y.plan(plan, "my", (), (), 1.5)
    up_z, up_y = up_spreads(wire, me, w_mlp.at[2])
    up_z.one.plan(plan, "wz", (), 1.7)
    up_y.one.plan(plan, "wy", (), 1.7)

    def keep_up(*where):
        return lambda: keep(w_mlp.at[(2, *where)], mlp_out.at[(2, *where)])

    plan.add(
        "wz0", keep_up(ALL, me.y, ALL, me.core, pl.ds(UP_Y, UNITS - UP_Y), ALL),
        after=("wz.far",), rank=1.8,
    )
    plan.add(
        "wy0", keep_up(me.zl, ALL, me.zh, me.core, pl.ds(0, UP_Y), ALL), after=("wy.far",), rank=1.8
    )
    plan.add("bias", lambda: fill_bias(bias, me, start_in[0]), rank=6)

    def project(zl, carry):
        rows = h_one[:, 0].reshape(512, D)
        cosine, sine = tables[0, :, 0].reshape(512, HD), tables[1, :, 0].reshape(512, HD)
        raw = dot_nn(rows, w_qkv[0, zl].reshape(D, 256))
        for j in range(2):
            query[zl * 2 + j] = turn(raw[:, j * HD : (j + 1) * HD], cosine, sine).astype(BF)
        raw = dot_nn(rows, w_qkv[1, zl].reshape(D, 256))
        for j in range(2):
            keys[zl * 2 + j, :, 0] = (
                turn(raw[:, j * HD : (j + 1) * HD], cosine, sine).astype(BF).reshape(4, 128, HD)
            )
        raw = dot_nn(rows, w_qkv[2, zl].reshape(D, 256))
        for j in range(2):
            values[zl * 2 + j, :, 0] = raw[:, j * HD : (j + 1) * HD].astype(BF).reshape(4, 128, HD)
        return carry

    def project_other(zl, slots):
        rows = jnp.concatenate([h_one[slot, 1] for slot in slots], axis=0)
        cosine = jnp.concatenate([tables[0, slot, 1] for slot in slots], axis=0)
        sine = jnp.concatenate([tables[1, slot, 1] for slot in slots], axis=0)
        raw_k = dot_nn(rows, w_qkv[1, zl].reshape(D, 256))
        raw_v = dot_nn(rows, w_qkv[2, zl].reshape(D, 256))
        for j in range(2):
            key = turn(raw_k[:, j * HD : (j + 1) * HD], cosine, sine).astype(BF)
            value = raw_v[:, j * HD : (j + 1) * HD].astype(BF)
            for index, slot in enumerate(slots):
                keys[zl * 2 + j, slot, 1] = key[index * 128 : index * 128 + 128]
                values[zl * 2 + j, slot, 1] = value[index * 128 : index * 128 + 128]

    at.projected = at.rest = 0

    def keep_when_done():
        if at.projected == 2 and at.rest == 4:
            keep(w_qkv, qkv_out)
            keep(query, query_out)
            keep(keys, keys_out)
            keep(values, values_out)

    def project_half(zl):
        def run():
            lax.fori_loop(zl, zl + 1, project, 0)
            at.projected += 1
            keep_when_done()

        return run

    def other(zl, slots):
        def run():
            project_other(zl, slots)
            at.rest += 1
            keep_when_done()

        return run

    for zl in range(2):
        name = "%d" % zl
        plan.add(
            "proj" + name, project_half(zl), after=("n0", "n1", "n2", "qy.all", "qz.all" + name), rank=2 + 0.1 * zl
        )
        plan.add(
            "rest" + name, other(zl, (me.x, one, three)), after=("n3", "n4", "qy.all", "qz.all" + name),
            rank=2.2 + 0.1 * zl,
        )
        plan.add("last" + name, other(zl, (far,)), after=("n5", "qy.all", "qz.all" + name), rank=2.4 + 0.1 * zl)

    def attend_own(head, carry):
        for half, pairs in ((0, 3), (1, 4)):
            span = pairs * 128
            rows = slice(half * 256, half * 256 + 256)
            scores = dot_nt(keys[head, 0:pairs, 0].reshape(span, HD), query[head, rows, :]) * SCALE
            scores = scores + bias[0:pairs, 0, :, rows].reshape(span, 256)
            top = jnp.max(scores, axis=0, keepdims=True)
            expo = jnp.exp(scores - top)
            top_s[head, half] = top
            total_s[head, half] = jnp.sum(expo, axis=0, keepdims=True)
            value = values[head, 0:pairs, 0].reshape(span, HD)
            result_s[head, half] = dot_tn(value, expo.astype(BF))
        return carry

    def attend_other(head, carry):
        for half, pairs in ((0, 3), (1, 4)):
            span = pairs * 128
            rows = slice(half * 256, half * 256 + 256)
            scores = dot_nt(keys[head, 0:pairs, 1].reshape(span, HD), query[head, rows, :]) * SCALE
            scores = scores + bias[0:pairs, 1, :, rows].reshape(span, 256)
            before = top_s[head, half]
            top = jnp.maximum(before, jnp.max(scores, axis=0, keepdims=True))
            fade = jnp.exp(before - top)
            expo = jnp.exp(scores - top)
            total = total_s[head, half] * fade + jnp.sum(expo, axis=0, keepdims=True)
            value = values[head, 0:pairs, 1].reshape(span, HD)
            result = (result_s[head, half] * fade + dot_tn(value, expo.astype(BF))) * (1.0 / total)
            heads[rows, pl.ds(pl.multiple_of(head * HD, HD), HD)] = result.T.astype(BF)
            lse_out[head, :, rows] = top + jnp.log(total)
        return carry

    def attend_rest():
        lax.fori_loop(2, 4, attend_other, 0)
        keep(lse_out, lse_hbm)

    plan.add("own0", lambda: lax.fori_loop(0, 2, attend_own, 0), after=("proj0", "bias"), rank=2.5)
    plan.add("own2", lambda: lax.fori_loop(2, 4, attend_own, 0), after=("proj1", "bias"), rank=2.5)
    plan.add(
        "att0", lambda: lax.fori_loop(0, 2, attend_other, 0), after=("own0", "rest0", "last0"), rank=2.5
    )
    plan.add("att2", attend_rest, after=("own2", "rest1", "last1", "att0"), rank=2.6)

    def project_out(block, carry):
        y, zh = lax.div(block, 2), lax.rem(block, 2)
        weight = jnp.concatenate(
            [
                jnp.concatenate([w_o[zl, y, zh, 0], w_o[zl, y, zh, 1]], axis=1)
                for zl in range(2)
            ],
            axis=0,
        )
        result = dot_nn(heads[...], weight).astype(BF).reshape(4, 128, 256)
        part[:, :, pl.ds(pl.multiple_of(block * 256, 256), 256)] = result
        return carry

    total = RingSum(
        wire, me, "x", columns_of(part), near_left, near_right, whole_left, whole_right,
        split_columns, lambda target, term: add_into(target, [term]),
    )

    def out_one():
        keep(w_o, wo_out)
        lax.fori_loop(0, 4, project_out, 0)
        total.start((0,))

    def out_two():
        lax.fori_loop(4, 8, project_out, 0)
        total.start((1,))

    plan.add("po", out_one, after=("att0", "att2", "oz.all", "oy.all"), rank=2)
    plan.add("ys.go", out_two, after=("po",), rank=2)
    total.plan(plan, "ys", (), 1, go=False)

    def finish(index, carry):
        span = pl.ds(pl.multiple_of(index * 32, 32), 32)
        value = tok[me.x, 0, span, :].astype(F32) + (
            part[me.x, span, :].astype(F32)
            + whole_left[span, :].astype(F32)
            + whole_right[span, :].astype(F32)
        )
        scale = lax.rsqrt(jnp.mean(value * value, axis=-1, keepdims=True) + EPS)
        y_out[span, :] = value
        h_two[span, :] = (value * scale * gains_out[1:2, :]).astype(BF)
        return carry

    def finish_all():
        lax.fori_loop(0, 4, finish, 0)
        keep(h_two, h_out)
        keep(y_out, y_hbm)
        keep(gains_out, gains_hbm)

    plan.add("fin", finish_all, after=("ys.far",), rank=0)
    Ring(wire, me, "x", rows_of(cot)).plan(plan, "cx", (), 1.6)
    plan.add("ck", lambda: keep(cot, cot_out), after=("cx.far",), rank=1.8)

    def flip(block, carry):
        column = pl.ds(pl.multiple_of(block * 128, 128), 128)
        rows = h_one[:, :, :, column].reshape(SEQ, 128)
        turned[lax.rem(block, 2), lax.div(block, 2)] = rows.T
        return carry

    def turn_heads():
        heads_t[...] = heads[...].T
        keep(heads_t, heads_out)

    plan.add("ht", turn_heads, after=("att0", "att2"), rank=6)

    def flip_rest():
        lax.fori_loop(8, 16, flip, 0)
        keep(turned.at[me.core], turned_out.at[0])
        at.turned = wire.put(turned.at[1 - me.core], turned_out.at[1], sibling(me))

    plan.add("flip", lambda: lax.fori_loop(0, 8, flip, 0), after=("n0", "n1", "n2", "n3", "n4", "n5"), rank=7)
    plan.add("flip2", flip_rest, after=("flip",), rank=7)
    plan.add("flip3", lambda: None, lambda: [at.turned], ("flip2",), 9)

    def keep_mlp(mine, start, size):
        def run():
            core = me.core if mine else 1 - me.core
            piece = (pl.ds(0, 2), ALL, ALL, ALL, core, pl.ds(start, size), ALL)
            keep(w_mlp.at[piece], mlp_out.at[piece])

        return run

    plan.add("my0", keep_mlp(True, 0, MLP_Y), after=("my.t",), rank=1.8)
    plan.add("my1", keep_mlp(False, 0, MLP_Y), after=("my.all",), rank=1.8)
    plan.add("mz0", keep_mlp(True, MLP_Y, UNITS - MLP_Y), after=("mz.t",), rank=1.8)
    plan.add("mz1", keep_mlp(False, MLP_Y, UNITS - MLP_Y), after=("mz.all",), rank=1.8)

    plan.go(ORDER_ATTEND)
    for copy in kept:
        copy.wait()
    wire.drain()


def anywhere():
    return pl.BlockSpec(memory_space=pl.ANY)


def in_vmem():
    return pl.BlockSpec(memory_space=pltpu.VMEM)


def call_attend(tokens, cotangent, starts, weights, gain_attn, gain_mlp, tables):
    shape = jax.ShapeDtypeStruct
    hbm = [
        shape((3, 2, 4, 2, 2, 128, 256), BF),
        shape((2, 4, 2, 2, 256, 128), BF),
        shape((3, 2, 4, 2, 2, UNITS, 128), BF),
        shape((4, 128, D), BF),
        shape((2, 8, 128, SEQ), BF),
        shape((4, 512, HD), BF),
        shape((4, 4, 2, 128, HD), BF),
        shape((4, 4, 2, 128, HD), BF),
        shape((512, 512), BF),
        shape((128, D), BF),
    ]
    vmem = [shape((4, 1, 512), F32), shape((128, D), F32), shape((8, D), F32)]
    return pl.pallas_call(
        kernel_attend,
        name="attend",
        in_specs=[anywhere(), anywhere(), pl.BlockSpec(memory_space=pltpu.SMEM)]
        + [anywhere()] * 7
        + [in_vmem()] * 2
        + [anywhere()],
        out_specs=[anywhere()] * (len(hbm) + len(vmem)),
        out_shape=hbm + vmem,
        scratch_shapes=[
            pltpu.VMEM((4, 1, 512), F32),
            pltpu.VMEM((128, D), F32),
            pltpu.VMEM((8, D), F32),
            pltpu.VMEM((4, 2, 128, D), BF),
            pltpu.VMEM((4, 2, 128, D), BF),
            pltpu.VMEM((3, 2, 4, 2, 2, 128, 256), BF),
            pltpu.VMEM((2, 4, 2, 2, 256, 128), BF),
            pltpu.VMEM((3, 2, 4, 2, 2, UNITS, 128), BF),
            pltpu.VMEM((2, 4, 2, 128, HD), F32),
            pltpu.VMEM((4, 2, 128, 512), F32),
            pltpu.VMEM((4, 512, HD), BF),
            pltpu.VMEM((4, 4, 2, 128, HD), BF),
            pltpu.VMEM((4, 4, 2, 128, HD), BF),
            pltpu.VMEM((512, 512), BF),
            pltpu.VMEM((4, 128, D), BF),
            pltpu.VMEM((128, D), BF),
            pltpu.VMEM((4, 128, D), BF),
            pltpu.VMEM((128, D // 2), BF),
            pltpu.VMEM((128, D // 2), BF),
            pltpu.VMEM((128, D), BF),
            pltpu.VMEM((128, D), BF),
            pltpu.VMEM((2, 8, 128, SEQ), BF),
            pltpu.VMEM((512, 512), BF),
            pltpu.VMEM((4, 2, 1, 256), F32),
            pltpu.VMEM((4, 2, 1, 256), F32),
            pltpu.VMEM((4, 2, HD, 256), F32),
            pltpu.VMEM((4, 8, 128), F32),
            pltpu.VMEM((4, 8, 128), F32),
            pltpu.VMEM((2, 4, 2, 8, 128), F32),
            pltpu.SemaphoreType.DMA((140,)),
            pltpu.SemaphoreType.DMA((140,)),
            pltpu.SemaphoreType.DMA((32,)),
        ],
        compiler_params=pltpu.CompilerParams(
            collective_id=0, has_side_effects=True, vmem_limit_bytes=VMEM_BYTES
        ),
    )(tokens, cotangent, starts, *weights, gain_attn, gain_mlp, tables)


def rope_tables():
    half = HD // 2
    freq = np.exp(np.arange(half, dtype=np.float32) * np.float32(-2.0 * math.log(10000.0) / HD))
    order = np.array(
        [
            [[(2 * pair + (zl + other) % 2) * 128 + np.arange(128) for other in range(2)] for pair in range(4)]
            for zl in range(2)
        ]
    )
    angle = order.astype(np.float32)[..., None] * freq.astype(np.float32)
    cosine, sine = np.cos(angle.astype(np.float64)), np.sin(angle.astype(np.float64))
    both = np.stack(
        [np.concatenate([cosine, cosine], -1), np.concatenate([-sine, sine], -1)], axis=1
    )
    return both.astype(np.float32)
SUM_Y, SUM_CUT = 400, 208
ORDER_FEED = (
    "hx.go", "wy.b.go", "wz.b.go", "l2", "wz.b.r", "wz.b.l", "hx.r", "hx.l", "wy.b.r",
    "wy.b.near", "wy.s", "wz.b.near", "wz.s", "a00", "cs", "a01", "a10", "hx.near", "g11",
    "wz.b.far", "wz.t", "g10", "a11", "wz.all", "wy.b.far", "wy.t", "hx.far", "g00", "hs",
    "wy.all", "f00", "g01", "f01", "b00", "ds.go", "f10", "f11", "t1", "b10", "b11", "gr1a",
    "gr1b", "s1y.go", "ds.r", "ds.l", "s1z.go", "t0", "t2", "fd0", "gr0a", "s1y.r", "s1y.l",
    "ds.far", "bn", "s1z.r", "gr0b", "s0y.go", "s0z.go", "dx.go", "fd1", "gr2a", "dx.r",
    "s1y.far", "s1y.k", "s1z.far", "s1z.k", "s0y.l", "s0y.r", "s0z.r", "dx.l", "dx.near", "gr2b",
    "dg", "s0y.far", "s0y.k", "dx.far", "dk", "s0z.far", "s0z.k",
)


def fold_view(ref, me, lead, axis, row, rows, cut):
    head = (ALL,) * lead

    def view(slot, part):
        start, size = row, rows
        if part == 0:
            size = cut
        if part == 1:
            start, size = row + cut, rows - cut
        if axis == "y":
            where = (ALL, slot, ALL)
        else:
            where = (lax.rem(slot, 2), ALL, lax.div(slot, 2))
        return ref.at[head + where + (pl.ds(start, size), ALL)]

    return view


def kernel_feed(
    h_in, cot_in, mlp_in, y_hbm, gains_hbm,
    part_out, dattn_out, fold_y_out, fold_z_out, down_out, dy_hbm, gain_hbm,
    y_in, gains_in, dy_out, gain_out,
    w_mlp, h_two, cot, gate_s, up_s, act_s, d_gate, d_up, act, flipped, flipped_far,
    h_far, cot_far, part, near_left, near_right, whole_left, whole_right, d_attn, out_part,
    *rest,
):
    bufs, (send, recv, local) = list(rest[:-3]), rest[-3:]
    bufs = [tuple(bufs[a:b]) for a, b in ((0, 4), (4, 7), (7, 11), (11, 14))]
    me = place()
    wire = Wire(send, recv, local)
    parts = {}

    def load(zl):
        for which in range(2):
            parts[which, zl] = wire.move(mlp_in.at[which, zl], w_mlp.at[which, zl])

    def load_up(*where):
        return wire.move(mlp_in.at[(2, *where)], w_mlp.at[(2, *where)])

    loads = [wire.move(h_in, h_two.at[me.x])]
    ups = [
        load_up(ALL, me.y, ALL, me.core, pl.ds(UP_Y, UNITS - UP_Y), ALL),
        load_up(me.zl, ALL, me.zh, me.core, pl.ds(0, UP_Y), ALL),
    ]
    greet(me, False)
    plan = Plan()
    at = types.SimpleNamespace()
    kept = []

    def keep(source, target):
        kept.append(wire.move(source, target))

    def whole(which, zl):
        return jnp.concatenate(
            [
                w_mlp[which, zl, y, zh, core]
                for y in range(4)
                for zh in range(2)
                for core in range(2)
            ],
            axis=1,
        )

    def share(source, target):
        return [
            wire.put(
                source.at[:, :, pl.ds(pl.multiple_of((block * 2 + 1 - me.core) * 128, 128), 128)],
                target.at[block],
                sibling(me),
            )
            for block in range(8)
        ]

    def share_h():
        at.h_puts = share(h_two, h_far)

    def share_cot():
        at.cot_puts = share(cot, cot_far)

    one, far, three = rem4(me.x + 1), rem4(me.x + 2), rem4(me.x + 3)
    batches = ((far, one), (three, me.x))

    def rows_of_batch(ref, batch):
        return jnp.concatenate([ref[slot] for slot in batches[batch]], axis=0)

    def room(batch, zl):
        return zl if batch else 2

    def gate(batch, zl):
        def run():
            gate_s[room(batch, zl)] = dot_nt(rows_of_batch(h_two, batch), whole(0, zl))

        return run

    def back_act(batch, zl):
        def run():
            act_s[batch * 2 + zl] = dot_nt(rows_of_batch(cot, batch), whole(1, zl))

        return run

    def forward(batch, zl):
        def inner(index, carry):
            place_of, rest = lax.div(index, 4), lax.rem(index, 4)
            first, second = batches[batch]
            slot = first + place_of * (second - first)
            source = pl.ds(pl.multiple_of(index * 32, 32), 32)
            span = pl.ds(pl.multiple_of(rest * 32, 32), 32)
            gate, up = gate_s[room(batch, zl), source, :], up_s[source, :]
            d_act = act_s[batch * 2 + zl, source, :]
            sigma = 1.0 / (1.0 + jnp.exp(-gate))
            act[zl, slot, span, :] = (gate * sigma * up).astype(BF)
            d_gate[zl, slot, span, :] = (
                d_act * up * sigma * (1.0 + gate * (1.0 - sigma))
            ).astype(BF)
            d_up[zl, slot, span, :] = (d_act * gate * sigma).astype(BF)
            return carry

        def run():
            up_s[...] = dot_nt(rows_of_batch(h_two, batch), whole(2, zl))
            lax.fori_loop(0, 8, inner, 0)

        return run

    def back_h(batch):
        def body(block, carry):
            y, zh = lax.div(block, 2), lax.rem(block, 2)
            total = None
            for which, left in ((0, d_gate), (2, d_up)):
                for zl in range(2):
                    weight = jnp.concatenate(
                        [w_mlp[which, zl, y, zh, 0], w_mlp[which, zl, y, zh, 1]], axis=1
                    )
                    rows = jnp.concatenate([left[zl, slot] for slot in batches[batch]], axis=0)
                    term = dot_nn(rows, weight)
                    total = term if total is None else total + term
            result = total.astype(BF)
            column = pl.ds(pl.multiple_of(block * 256, 256), 256)
            for index, slot in enumerate(batches[batch]):
                part[slot, :, column] = result[index * 128 : index * 128 + 128]
            return carry

        return body

    def add(target, term):
        add_into(target, [term])

    total = RingSum(
        wire, me, "x", columns_of(part), near_left, near_right, whole_left, whole_right,
        split_columns, add,
    )

    def back_first(half):
        def run():
            lax.fori_loop(half * 4, half * 4 + 4, back_h(0), 0)
            total.start_near(half)
            if half:
                total.start_whole(1)

        return run

    def back_second(half):
        def run():
            lax.fori_loop(half * 4, half * 4 + 4, back_h(1), 0)
            if half == 0:
                total.start_whole(0)

        return run

    plan.add("hs", share_h, after=("hx.far",), rank=3)
    plan.add("cs", share_cot, lambda: [loads[1]], ("l2",), 3)
    def load_rest():
        load(0)
        load(1)
        loads.append(wire.move(cot_in, cot))
        at.late = [wire.move(y_hbm, y_in), wire.move(gains_hbm, gains_in)]

    plan.add("l2", load_rest, lambda: [loads[0], *ups], ("hx.go",), 0)
    Ring(wire, me, "x", rows_of(h_two)).plan(plan, "hx", (), 0)
    plan.steps["hx.go"].waits = lambda: [loads[0]]
    up_z, up_y = up_spreads(wire, me, w_mlp.at[2])
    up_z.plan_second(plan, "wz", (), 1)
    up_y.plan_second(plan, "wy", (), 1)
    plan.steps["wz.b.go"].waits = lambda: [ups[0]]
    plan.steps["wy.b.go"].waits = lambda: [ups[1]]
    for zl in range(2):
        for batch in range(2):
            name = "%d%d" % (batch, zl)
            plan.add(
                "a" + name, back_act(batch, zl), lambda zl=zl: [loads[1], parts[1, zl]], ("l2",),
                4 - 0.5 * batch,
            )
        plan.add("g1%d" % zl, gate(1, zl), lambda zl=zl: [parts[0, zl]], ("hx.near", "l2"), 3)
    before = ("hx.far", "l2")
    for zl in range(2):
        name = "0%d" % zl
        plan.add("g" + name, gate(0, zl), lambda zl=zl: [parts[0, zl]], before, 2)
        plan.add(
            "f" + name, forward(0, zl), after=("g" + name, "a" + name, "wz.all", "wy.all", *before),
            rank=2,
        )
        before = ("f" + name,)
    plan.add("b00", back_first(0), after=before, rank=2)
    plan.add("ds.go", back_first(1), after=("b00",), rank=2)
    plan.add("f10", forward(1, 0), after=("g10", "a10", "ds.go"), rank=2.1)
    plan.add("f11", forward(1, 1), after=("g11", "a11", "f10"), rank=2.1)
    before = ("f10", "f11")
    plan.add("b10", back_second(0), after=before, rank=2)
    plan.add("b11", back_second(1), after=("b10",), rank=2)
    total.plan(plan, "ds", (), 0, go=False)
    plan.steps["ds.l"].after += ("b11",)
    plan.steps["ds.far"].after += ("b10",)

    at.far = {}

    def turn_over(which, source):
        def run():
            for zl in range(2):
                flipped[which, zl] = source[zl].reshape(512, UNITS).T
            at.far[which] = wire.put(flipped.at[which], flipped_far.at[which], sibling(me))

        return run

    for which, source in enumerate((d_gate, d_up, act)):
        early = which == 1
        plan.add(
            "t%d" % which, turn_over(which, source), after=("f11",) if early else ("b11",),
            rank=1.9 if early else 2 + which * 0.2,
        )

    def forward_down(block, carry):
        y, zh = lax.div(block, 2), lax.rem(block, 2)
        result = None
        for zl in range(2):
            weight = jnp.concatenate([w_mlp[1, zl, y, zh, 0], w_mlp[1, zl, y, zh, 1]], axis=1)
            term = dot_nn(act[zl].reshape(512, UNITS), weight)
            result = term if result is None else result + term
        out_part[:, :, pl.ds(pl.multiple_of(block * 256, 256), 256)] = result.astype(BF).reshape(4, 128, 256)
        return carry

    def down_rest():
        lax.fori_loop(4, 8, forward_down, 0)
        keep(out_part, part_out)

    plan.add("fd0", lambda: lax.fori_loop(0, 4, forward_down, 0), after=("t2",), rank=4)
    plan.add("fd1", down_rest, after=("fd0",), rank=4)

    places = (0, 2, 1)

    def grad(which, rows, rows_far):
        def body(index, carry):
            zl, pair = lax.div(index, 2), lax.rem(index, 2)
            mine = jnp.concatenate(
                [
                    rows[:, :, pl.ds(pl.multiple_of(((pair * 4 + k) * 2 + me.core) * 128, 128), 128)]
                    .reshape(512, 128)
                    for k in range(4)
                ],
                axis=1,
            )
            other = jnp.concatenate(
                [rows_far[pair * 4 + k].reshape(512, 128) for k in range(4)], axis=1
            )
            result = dot_nn(flipped[which, zl], mine) + dot_nn(flipped_far[which, zl], other)
            result = result.astype(BF)
            for k in range(4):
                w_mlp[places[which], zl, pair * 2 + k // 2, k % 2, 0] = result[:, k * 128 : k * 128 + 128]
            return carry

        return body

    sums = []

    def start_sums(which):
        ref = w_mlp.at[places[which], :, :, :, 0]
        pair = [
            RingSum(wire, me, "y", fold_view(ref, me, 0, "y", 0, SUM_Y, SUM_CUT), *bufs[2 * which],
                    split_rows(SUM_CUT), add),
            PairSum(wire, me, fold_view(ref, me, 0, "z", SUM_Y, UNITS - SUM_Y, 0),
                    *bufs[2 * which + 1], add),
        ]
        for item, out, axis in zip(pair, (fold_y_out, fold_z_out), "yz"):
            name = "s%d%s" % (which, axis)
            item.plan(plan, name, ("gr%db" % which,), 1)
            plan.add(name + ".k", close_sum(item, out.at[which]), after=(name + ".far",), rank=3)

    def close_sum(item, out):
        def run():
            mine = item.part(item.at, None)
            add_into(mine, list(item.whole))
            keep(mine, out)

        return run

    rows_of_step = ((h_two, h_far), (h_two, h_far), (cot, cot_far))
    for which in range(3):
        body = grad(which, *rows_of_step[which])

        def waits(which=which):
            return [at.far[which]] + (at.cot_puts if which == 2 else at.h_puts)

        before = ("t%d" % which, "cs", "hs") + (("fd1",) if which == 2 else ())

        def first(body=body, which=which):
            if which == 1:
                for spread in (up_z, up_y):
                    for copy in [*spread.twos[0].copies(), *spread.shared]:
                        copy.wait_send()
            lax.fori_loop(0, 2, body, 0)

        plan.add("gr%da" % which, first, waits, before, 3)
        plan.add(
            "gr%db" % which, lambda body=body: lax.fori_loop(2, 4, body, 0),
            after=("gr%da" % which,), rank=3,
        )
        if which < 2:
            start_sums(which)
    plan.add("dg", lambda: keep(w_mlp.at[1, :, :, :, 0], down_out), after=("gr2b",), rank=2)

    def back_norm(index, carry):
        span = pl.ds(pl.multiple_of(index * 16, 16), 16)
        d_h = (
            part[me.x, span, :].astype(F32)
            + whole_left[span, :].astype(F32)
            + whole_right[span, :].astype(F32)
        )
        value = y_in[span, :]
        scale = lax.rsqrt(jnp.mean(value * value, axis=-1, keepdims=True) + EPS)
        normed = value * scale
        e_two = d_h * gains_in[1:2, :]
        inner = jnp.mean(e_two * normed, axis=-1, keepdims=True)
        d_y = cot[me.x, span, :].astype(F32) + scale * (e_two - normed * inner)
        dy_out[span, :] = d_y
        d_attn[me.x, span, :] = d_y.astype(BF)
        return carry + jnp.sum(d_h * normed, axis=0, keepdims=True)

    def back_one():
        gain_out[...] = lax.fori_loop(0, 4, back_norm, jnp.zeros((1, D), F32))
        d_ring.start_half(0)

    def back_two():
        gain_out[...] += lax.fori_loop(4, 8, back_norm, jnp.zeros((1, D), F32))
        d_ring.start_half(1)
        keep(dy_out, dy_hbm)
        keep(gain_out, gain_hbm)

    d_ring = Ring(wire, me, "x", rows_of(d_attn))
    plan.add("bn", back_one, lambda: at.late, ("ds.far",), 0)
    d_ring.plan(plan, "dx", ("bn",), 0)
    plan.steps["dx.go"].run = back_two
    plan.add("dk", lambda: keep(d_attn, dattn_out), after=("dx.far",), rank=0)
    plan.go(ORDER_FEED)
    for copy in kept:
        copy.wait()
    wire.drain()


def fold_shapes(lead, count, rows, cut, columns):
    return [
        pltpu.VMEM((*lead, *count, cut, columns), BF),
        pltpu.VMEM((*lead, *count, rows - cut, columns), BF),
        pltpu.VMEM((*lead, *count, rows, columns), BF),
        pltpu.VMEM((*lead, *count, rows, columns), BF),
    ]


def call_feed(h_two, cot, mlp, y_one, gains):
    shape = jax.ShapeDtypeStruct
    bufs = (
        fold_shapes((), (2, 2), SUM_Y, SUM_CUT, 128)
        + [pltpu.VMEM((4, UNITS - SUM_Y, 128), BF)] * 3
    ) * 2
    return pl.pallas_call(
        kernel_feed,
        name="feed",
        in_specs=[anywhere()] * 5,
        out_specs=[anywhere()] * 7,
        out_shape=[
            shape((4, 128, D), BF),
            shape((4, 128, D), BF),
            shape((2, 2, 2, SUM_Y, 128), BF),
            shape((2, 4, UNITS - SUM_Y, 128), BF),
            shape((2, 4, 2, UNITS, 128), BF),
            shape((128, D), F32),
            shape((1, D), F32),
        ],
        scratch_shapes=[
            pltpu.VMEM((128, D), F32),
            pltpu.VMEM((8, D), F32),
            pltpu.VMEM((128, D), F32),
            pltpu.VMEM((1, D), F32),
            pltpu.VMEM((3, 2, 4, 2, 2, UNITS, 128), BF),
            pltpu.VMEM((4, 128, D), BF),
            pltpu.VMEM((4, 128, D), BF),
            pltpu.VMEM((3, 256, UNITS), F32),
            pltpu.VMEM((256, UNITS), F32),
            pltpu.VMEM((4, 256, UNITS), F32),
            pltpu.VMEM((2, 4, 128, UNITS), BF),
            pltpu.VMEM((2, 4, 128, UNITS), BF),
            pltpu.VMEM((2, 4, 128, UNITS), BF),
            pltpu.VMEM((3, 2, UNITS, 512), BF),
            pltpu.VMEM((3, 2, UNITS, 512), BF),
            pltpu.VMEM((8, 4, 128, 128), BF),
            pltpu.VMEM((8, 4, 128, 128), BF),
            pltpu.VMEM((4, 128, D), BF),
            pltpu.VMEM((128, D // 2), BF),
            pltpu.VMEM((128, D // 2), BF),
            pltpu.VMEM((128, D), BF),
            pltpu.VMEM((128, D), BF),
            pltpu.VMEM((4, 128, D), BF),
            pltpu.VMEM((4, 128, D), BF),
        ]
        + bufs
        + [
            pltpu.SemaphoreType.DMA((100,)),
            pltpu.SemaphoreType.DMA((100,)),
            pltpu.SemaphoreType.DMA((24,)),
        ],
        compiler_params=pltpu.CompilerParams(
            collective_id=1, has_side_effects=True, vmem_limit_bytes=VMEM_BYTES
        ),
    )(h_two, cot, mlp, y_one, gains)
BACK_GROUPS = (3, 4, 4, 3, 3, 4, 4, 3, 3, 4, 4, 3, 3, 4, 4)
ORDER_BACK = (
    "l2", "bias", "l3", "dh", "mz.b.go", "os.go", "wz.a.go", "wy.a.go", "ba0", "mz.b.l",
    "my.b.go", "ba2", "wz.a.r", "bh0", "wy.a.r", "wy.a.l", "mz.b.r", "bh1", "gq0", "qy.a0.go",
    "dl0", "ht", "wy.a.far", "wy.b.go", "mx", "gq1", "ax", "qz.a.go", "qy.a1.go", "qy.a0.l",
    "qy.a0.r", "dn0", "my.b.r", "dn1", "ds.go", "mz.b.far", "mz.k", "os.r", "os.l", "wz.a.far",
    "wy.b.r", "as", "qy.a1.r", "mz.", "qy.a1.l", "qz.a.r", "go", "oz.a.go", "az", "ds.r",
    "my.b.far", "my.k", "ds.l", "qy.a0.far", "oy.a.go", "wy.b.far", "wy.k", "oz.a.r", "my.",
    "dl1", "qy.a1.far", "qy.b.go", "os.far", "fo", "oy.a.r", "oy.a.l", "wz.b.go", "ay",
    "qz.a.far", "qz.b.go", "oz.a.far", "oz.b.go", "m.", "qy.b.r", "ds.far", "oy.a.far", "oy.b.go",
    "wz.b.r", "wz.b.l", "qz.b.r", "qz.b.l", "a.", "gk", "oz.b.r", "oz.b.l", "oy.b.r", "wz.b.far",
    "wz.k", "bn", "qz.b.far", "qz.k", "qy.b.far", "qy.k", "oz.b.far", "oz.k", "oy.b.far", "oy.k",
)
O_Y, O_CUT, O_REST = 192, 96, 32
Q_Y, Q_CUT, Q_REST = 96, 48, 16
DN_Y, DN_CUT, DN_REST = 448, 224, 128


class Fold:
    def __init__(self, wire, me, cut, view_one, axes, bufs, view_two, bufs_two):
        def add(target, term):
            add_into(target, [term])

        self.wire, self.me, self.add, self.split = wire, me, add, split_rows(cut)
        self.ones = []
        if view_one is not None:
            views, groups = (view_one, bufs) if isinstance(view_one, tuple) else ((view_one,), (bufs,))
            self.ones = [self.sum(axes[0], view, group) for view, group in zip(views, groups)]
        self.two = self.sum(axes[1], view_two, bufs_two)

    def sum(self, axis, view, bufs):
        if axis == "z":
            return PairSum(self.wire, self.me, view, *bufs, self.add)
        return RingSum(self.wire, self.me, "y", view, *bufs, self.split, self.add)

    def turn(self):
        for one in self.ones:
            add_into(one.part(one.at, None), list(one.whole))
        self.two.start()

    def close(self, result, keep):
        add_into(self.two.part(self.two.at, None), list(self.two.whole), result)
        keep()

    def plan(self, plan, name, waits, after, rank, result, keep):
        if not self.ones:
            self.two.plan(plan, name + ".b", after, rank)
            plan.steps[name + ".b.go"].waits = waits
        else:
            done = ()
            for index, one in enumerate(self.ones):
                step = name + ".a" + ("%d" % index if len(self.ones) > 1 else "")
                one.plan(plan, step, after[index : index + 1] if len(self.ones) > 1 else after, rank)
                plan.steps[step + ".go"].waits = waits
                done += (step + ".far",)
            self.two.plan(plan, name + ".b", done, rank)
            plan.steps[name + ".b.go"].run = self.turn
        plan.add(name + ".k", lambda: self.close(result, keep), after=(name + ".b.far",), rank=rank + 0.5)


def crossed_view(ref, me, lead, axis, row, rows, cut):
    head = (ALL,) * lead

    def view(slot, part):
        start, size = row, rows
        if part == 0:
            size = cut
        if part == 1:
            start, size = row + cut, rows - cut
        if axis == "z":
            where = (lax.rem(slot, 2), me.y, lax.div(slot, 2))
        else:
            where = (me.zl, slot, me.zh)
        return ref.at[head + where + (pl.ds(start, size), ALL)]

    return view


def held_view(ref, lead, axis, rows, cut):
    head = (ALL,) * lead

    def view(slot, part):
        start, size = 0, rows
        if part == 0:
            size = cut
        if part == 1:
            start, size = cut, rows - cut
        where = (lax.rem(slot, 2), lax.div(slot, 2)) if axis == "z" else (slot,)
        return ref.at[head + where + (pl.ds(start, size), ALL)]

    return view


def kernel_back(
    start_in, tokens_hbm, dattn_hbm, part_hbm, qkv_hbm, wo_hbm, query_hbm, keys_hbm, values_hbm,
    heads_hbm, lse_hbm, turned_hbm, tables_hbm, gains_hbm, y_hbm, dy_hbm, gain_hbm, fold_y_hbm,
    fold_z_hbm, down_hbm,
    result_hbm, grad_tokens_hbm, g_qkv_hbm, g_o_hbm, g_mlp_hbm, g_gains_hbm,
    query_in, keys_in, values_in, lse_in, gains_in, y_in, dy_in, gain_in,
    result_out, tokens_out, g_qkv_out, g_o_out, g_mlp_out, gains_out,
    w_qkv, w_o, d_attn, out_part, tables, bias, tok, turned, d_heads, d_query, d_keys, d_values,
    d_query_far, d_keys_far, d_values_far, sum_keys, sum_values, heads_t, heads_t_far, attn_far,
    d_h, far_one, side_left, side_right, last_z,
    near_left, near_right, whole_left, whole_right,
    out_near_left, out_near_right, out_whole_left, out_whole_right,
    fold_y, fold_z, g_down, gain_x, gain_z, gain_c, along_s, along_a, along_b, along_c, gain_t, along_t,
    *rest,
):
    bufs, (send, recv, local) = list(rest[:-3]), rest[-3:]
    groups = []
    for size in BACK_GROUPS:
        groups.append(tuple(bufs[:size]))
        bufs = bufs[size:]
    me = place()
    wire = Wire(send, recv, local)
    loads = {}

    def load(*items):
        for name, source, target in items:
            loads[name] = wire.move(source, target)

    def load_second():
        load(
            ("fold_y", fold_y_hbm, fold_y),
            ("fold_z", fold_z_hbm, fold_z),
            ("gain", gain_hbm, gain_in),
            ("heads", heads_hbm, heads_t),
            ("down", down_hbm, g_down),
        )

    def load_third():
        load(
            ("qkv", qkv_hbm, w_qkv),
            ("turned", turned_hbm, turned),
            ("y", y_hbm, y_in),
            ("dy", dy_hbm, dy_in),
            ("tok", tokens_hbm, tok),
            ("gains", gains_hbm, gains_in),
        )

    load(
        ("attn", dattn_hbm, d_attn),
        ("o", wo_hbm, w_o),
        ("query", query_hbm, query_in),
        ("keys", keys_hbm, keys_in),
        ("values", values_hbm, values_in),
        ("lse", lse_hbm, lse_in),
        ("tables", tables_hbm.at[me.zl], tables),
        ("part", part_hbm, out_part),
    )
    kept = []

    def keep(source, target):
        kept.append(wire.move(source, target))

    greet(me, True)
    plan = Plan()
    at = types.SimpleNamespace()
    one, far, three = rem4(me.x + 1), rem4(me.x + 2), rem4(me.x + 3)
    right, left = near(me, "x", 1), near(me, "x", 3)

    def add(target, term):
        add_into(target, [term])

    def loaded(*names):
        return lambda: [loads[name] for name in names]

    def share_attn():
        at.attn = [
            wire.put(
                d_attn.at[:, :, pl.ds(pl.multiple_of((block * 2 + 1 - me.core) * 128, 128), 128)],
                attn_far.at[block],
                sibling(me),
            )
            for block in range(8)
        ]

    def share_heads():
        at.heads = wire.put(heads_t, heads_t_far, sibling(me))

    plan.add("l2", load_second, loaded("attn", "o"), rank=0)
    plan.add("l3", load_third, loaded("query", "keys", "values", "lse", "tables"), ("l2",), 0)
    plan.add("as", share_attn, loaded("attn"), rank=1.5)
    plan.add("ht", share_heads, loaded("heads"), ("l2",), 1.5)

    total = RingSum(
        wire, me, "x", columns_of(out_part), out_near_left, out_near_right, out_whole_left,
        out_whole_right, split_columns, add,
    )
    total.plan(plan, "os", (), 1)
    plan.steps["os.go"].waits = loaded("part")

    def finish_out(index, carry):
        span = pl.ds(pl.multiple_of(index * 16, 16), 16)
        result_out[span, :] = (
            y_in[span, :]
            + (
                out_part[me.x, span, :].astype(F32)
                + out_whole_left[span, :].astype(F32)
                + out_whole_right[span, :].astype(F32)
            )
        ).astype(BF)
        return carry

    def finish_result():
        lax.fori_loop(0, 8, finish_out, 0)
        keep(result_out, result_hbm)

    plan.add("fo", finish_result, loaded("y"), ("os.far", "l3"), 6)

    def back_heads(zl, carry):
        weight = jnp.concatenate(
            [w_o[zl, y, zh, c] for y in range(4) for zh in range(2) for c in range(2)], axis=1
        )
        result = dot_nt(d_attn[...].reshape(512, D), weight).astype(BF)
        d_heads[zl * 2] = result[:, 0:HD]
        d_heads[zl * 2 + 1] = result[:, HD : 2 * HD]
        return carry

    plan.add("dh", lambda: lax.fori_loop(0, 2, back_heads, 0), loaded("attn", "o"), rank=2)
    plan.add("bias", lambda: fill_bias(bias, me, start_in[0]), rank=1)

    def back_attend(head, carry):
        for half, pairs in ((1, 4), (0, 3)):
            span = pairs * 256
            rows = slice(half * 256, half * 256 + 256)
            key = keys_in[head, 0:pairs].reshape(span, HD)
            value = values_in[head, 0:pairs].reshape(span, HD)
            query, d_head = query_in[head, rows, :], d_heads[head, rows, :]
            scores = dot_nt(key, query) * SCALE + bias[0:pairs, :, :, rows].reshape(span, 256)
            probs = jnp.exp(scores - lse_in[head, :, rows])
            d_probs = dot_nt(value, d_head)
            delta = jnp.sum(probs * d_probs, axis=0, keepdims=True)
            d_scores = (probs * (d_probs - delta) * SCALE).astype(BF)
            d_key = dot_nn(d_scores, query)
            d_value = dot_nn(probs.astype(BF), d_head)
            if half == 1:
                sum_keys[...] = d_key
                sum_values[...] = d_value
            else:
                sum_keys[0:span, :] += d_key
                sum_values[0:span, :] += d_value
            raw = dot_tn(key, d_scores).T
            cosine = tables[0, 2 * half : 2 * half + 2, 0].reshape(256, HD)
            sine = tables[1, 2 * half : 2 * half + 2, 0].reshape(256, HD)
            column = pl.ds(pl.multiple_of(head * HD, HD), HD)
            d_query[rows, column] = turn(raw, cosine, -sine).astype(BF)
        cosine, sine = tables[0].reshape(SEQ, HD), tables[1].reshape(SEQ, HD)
        d_keys[:, column] = turn(sum_keys[...], cosine, -sine).astype(BF)
        d_values[:, column] = sum_values[...].astype(BF)
        return carry

    def attend_rest():
        lax.fori_loop(2, 4, back_attend, 0)
        at.grads = [
            wire.put(d_query, d_query_far, sibling(me)),
            wire.put(d_keys, d_keys_far, sibling(me)),
            wire.put(d_values, d_values_far, sibling(me)),
        ]

    plan.add(
        "ba0", lambda: lax.fori_loop(0, 2, back_attend, 0),
        loaded("query", "keys", "values", "lse", "tables"), ("dh", "bias"), 2,
    )
    plan.add("ba2", attend_rest, after=("ba0",), rank=2)

    def back_h(block, carry):
        y, zh = lax.div(block, 2), lax.rem(block, 2)

        def weight(which):
            return jnp.concatenate(
                [w_qkv[which, 0, y, zh].reshape(256, 256), w_qkv[which, 1, y, zh].reshape(256, 256)],
                axis=1,
            )

        column = pl.ds(pl.multiple_of(block * 256, 256), 256)
        both = dot_nt(d_keys[...], weight(1)) + dot_nt(d_values[...], weight(2))
        both = both.reshape(4, 2, 128, 256)
        own = dot_nt(d_query[...], weight(0)).reshape(4, 128, 256) + both[:, 0]
        d_h[:, 0, :, column] = own.astype(BF)
        d_h[:, 1, :, column] = both[:, 1].astype(BF)
        return carry

    own = RingSum(
        wire, me, "x",
        lambda slot, half: d_h.at[slot, 0] if half is None else d_h.at[slot, 0, :, pl.ds(half * 1024, 1024)],
        near_left, near_right, whole_left, whole_right, split_columns, add,
    )
    at.far_z, at.sides, at.last = {}, {}, {}

    def cut(ref, half):
        return ref.at[:, pl.ds(half * 1024, 1024)]

    def back_half(half):
        def run():
            lax.fori_loop(half * 4, half * 4 + 4, back_h, 0)
            at.far_z[half] = wire.put(cut(d_h.at[far, 1], half), cut(far_one, half), partner(me))
            at.sides[half] = [
                wire.put(cut(d_h.at[one, 1], half), cut(side_left, half), right),
                wire.put(cut(d_h.at[three, 1], half), cut(side_right, half), left),
            ]
            own.start_whole(half)

        return run

    def near_half(half):
        def run():
            add_into(cut(d_h.at[far, 0], half), [cut(far_one, half)])
            own.start_near(half)

        return run

    def last_half(half):
        def run():
            add_into(cut(d_h.at[me.x, 1], half), [cut(side_left, half), cut(side_right, half)])
            at.last[half] = wire.put(cut(d_h.at[me.x, 1], half), cut(last_z, half), partner(me))

        return run

    plan.add("bh0", back_half(0), loaded("qkv"), ("ba2", "l3"), 2)
    plan.add("bh1", back_half(1), after=("bh0",), rank=2)
    for half in range(2):
        name = "%d" % half
        plan.add("dn" + name, near_half(half), lambda half=half: [at.far_z[half]], ("bh" + name,), 0)
        plan.add("dl" + name, last_half(half), lambda half=half: at.sides[half], ("bh" + name,), 0.5)
    plan.add("ds.go", lambda: None, after=("dn0", "dn1"), rank=0)
    own.plan(plan, "ds", (), 0, go=False)

    def grad_o(index, carry):
        zl, y = lax.div(index, 4), lax.rem(index, 4)
        mine = jnp.concatenate(
            [
                d_attn[:, :, pl.ds(pl.multiple_of(((y * 2 + zh) * 2 + me.core) * 128, 128), 128)]
                .reshape(512, 128)
                for zh in range(2)
            ],
            axis=1,
        )
        other = jnp.concatenate(
            [attn_far[y * 2 + zh].reshape(512, 128) for zh in range(2)], axis=1
        )
        rows = pl.ds(pl.multiple_of(zl * 256, 256), 256)
        result = (dot_nn(heads_t[rows, :], mine) + dot_nn(heads_t_far[rows, :], other)).astype(BF)
        w_o[zl, y, 0, 0] = result[:, 0:128]
        w_o[zl, y, 1, 0] = result[:, 128:256]
        return carry

    plan.add("go", lambda: lax.fori_loop(0, 8, grad_o, 0), lambda: [at.heads, *at.attn], ("as", "ht", "dh"), 3)

    def blocks(which, pair):
        return turned[which, pl.ds(pair * 4, 4)].reshape(512, SEQ)

    def own_rows(value):
        return jnp.concatenate([value[:, i * 256 : i * 256 + 128] for i in range(4)], axis=1)

    def grad_qkv(index, carry):
        zl, pair = lax.div(index, 2), lax.rem(index, 2)
        column = pl.ds(pl.multiple_of(zl * 256, 256), 256)
        mine, other = blocks(0, pair), blocks(1, pair)
        query_grad = dot_nn(own_rows(mine), d_query[:, column])
        query_grad = query_grad + dot_nn(own_rows(other), d_query_far[:, column])
        key_grad = dot_nn(mine, d_keys[:, column]) + dot_nn(other, d_keys_far[:, column])
        value_grad = dot_nn(mine, d_values[:, column]) + dot_nn(other, d_values_far[:, column])
        along = jnp.where(zl == 0, 0.0, along_s[pair])
        for which, result in enumerate((query_grad, key_grad, value_grad)):
            weight = w_qkv[which, zl, pl.ds(pair * 2, 2), :, me.core].reshape(512, 256)
            product = weight.astype(F32) * result
            along = along + product[:, 0:128] + product[:, 128:256]
            w_qkv[which, zl, pl.ds(pair * 2, 2), :, 0] = result.astype(BF).reshape(2, 2, 128, 256)
        along_s[pair] = along
        return carry

    plan.add(
        "gq0", lambda: lax.fori_loop(0, 2, grad_qkv, 0),
        lambda: [loads["turned"], *at.grads], ("bh1",), 3,
    )
    plan.add("gq1", lambda: lax.fori_loop(2, 4, grad_qkv, 0), after=("gq0",), rank=3)

    g_qkv, g_o = w_qkv.at[:, :, :, :, 0], w_o.at[:, :, :, 0]
    rest = UNITS - SUM_Y

    def low_view(zl):
        def view(slot, part):
            span = {None: (0, Q_Y), 0: (0, Q_CUT), 1: (Q_CUT, Q_Y - Q_CUT)}[part]
            return g_qkv.at[:, zl, slot, :, pl.ds(*span), :]

        return view

    for name, fold, waits, after, rank, result, target, where in (
        ("my", Fold(wire, me, 0, None, ("y", "z"), None, held_view(fold_y, 1, "z", SUM_Y, 0), groups[0]),
         loaded("fold_y"), ("l2",), 1.2, g_mlp_out, g_mlp_hbm, (pl.ds(0, 2), pl.ds(0, SUM_Y), ALL)),
        ("mz", Fold(wire, me, 144, None, ("z", "y"), None, held_view(fold_z, 1, "y", rest, 144), groups[1]),
         loaded("fold_z"), ("l2",), 1.2, g_mlp_out, g_mlp_hbm, (pl.ds(0, 2), pl.ds(SUM_Y, UNITS - SUM_Y), ALL)),
        ("oy", Fold(wire, me, O_CUT, fold_view(g_o, me, 0, "y", 0, O_Y, O_CUT), ("y", "z"), groups[2],
                    crossed_view(g_o, me, 0, "z", 0, O_Y, 0), groups[3]),
         tuple, ("go",), 1.4, g_o_out, g_o_hbm, (pl.ds(0, O_Y), ALL)),
        ("oz", Fold(wire, me, O_REST, fold_view(g_o, me, 0, "z", O_Y, 256 - O_Y, 0), ("z", "y"), groups[4],
                    crossed_view(g_o, me, 0, "y", O_Y, 256 - O_Y, O_REST), groups[5]),
         tuple, ("go",), 1.4, g_o_out, g_o_hbm, (pl.ds(O_Y, 256 - O_Y), ALL)),
        ("qy", Fold(wire, me, Q_CUT, (low_view(0), low_view(1)), ("y", "z"), (groups[6], groups[14]),
                    crossed_view(g_qkv, me, 1, "z", 0, Q_Y, 0), groups[7]),
         tuple, ("gq0", "gq1"), 1, g_qkv_out, g_qkv_hbm, (ALL, pl.ds(0, Q_Y), ALL)),
        ("qz", Fold(wire, me, Q_REST, fold_view(g_qkv, me, 1, "z", Q_Y, 128 - Q_Y, 0), ("z", "y"),
                    groups[8], crossed_view(g_qkv, me, 1, "y", Q_Y, 128 - Q_Y, Q_REST), groups[9]),
         tuple, ("gq1",), 1, g_qkv_out, g_qkv_hbm, (ALL, pl.ds(Q_Y, 128 - Q_Y), ALL)),
        ("wy", Fold(wire, me, DN_CUT, fold_view(g_down, me, 0, "y", 0, DN_Y, DN_CUT), ("y", "z"),
                    groups[10], crossed_view(g_down, me, 0, "z", 0, DN_Y, 0), groups[11]),
         loaded("down"), ("l2",), 1.3, g_mlp_out, g_mlp_hbm, (2, pl.ds(0, DN_Y), ALL)),
        ("wz", Fold(wire, me, DN_REST, fold_view(g_down, me, 0, "z", DN_Y, UNITS - DN_Y, 0), ("z", "y"),
                    groups[12], crossed_view(g_down, me, 0, "y", DN_Y, UNITS - DN_Y, DN_REST), groups[13]),
         loaded("down"), ("l2",), 1.3, g_mlp_out, g_mlp_hbm, (2, pl.ds(DN_Y, UNITS - DN_Y), ALL)),
    ):
        fold.plan(
            plan, name, waits, after, rank, result.at[where],
            lambda result=result, target=target, where=where: keep(result.at[where], target.at[where]),
        )

    def back_norm(index, carry):
        span = pl.ds(pl.multiple_of(index * 16, 16), 16)
        d_h_one = (
            d_h[me.x, 0, span, :].astype(F32)
            + whole_left[span, :].astype(F32)
            + whole_right[span, :].astype(F32)
            + last_z[span, :].astype(F32)
        )
        value = tok[span, :].astype(F32)
        scale = lax.rsqrt(jnp.mean(value * value, axis=-1, keepdims=True) + EPS)
        normed = value * scale
        e_one = d_h_one * gains_in[0:1, :]
        inner = jnp.mean(e_one * normed, axis=-1, keepdims=True)
        tokens_out[span, :] = (dy_in[span, :] + scale * (e_one - normed * inner)).astype(BF)
        return carry

    def feed_x():
        for block in range(16):
            gain_x[me.x, block : block + 1, :] = gain_in[0:1, block * 128 : block * 128 + 128]
        at.feed = Meet(wire, me, "x", gain_x).copies

    def feed_z():
        gain_z[me.z] = gain_x[0] + gain_x[1] + gain_x[2] + gain_x[3]
        at.feed = Meet(wire, me, "z", gain_z).copies

    def feed_y():
        gain_c[me.core, me.y] = gain_z[0] + gain_z[1] + gain_z[2] + gain_z[3]
        at.feed = MeetCores(wire, me, gain_c).copies

    def feed_all():
        total = gain_c[0, 0]
        for core, y in ((0, 1), (0, 2), (0, 3), (1, 0), (1, 1), (1, 2), (1, 3)):
            total = total + gain_c[core, y]
        gain_t[...] = total
        row = (me.y * 2 + me.zh) * 2 + me.core
        gains_out[1:2, :] = gain_t[pl.ds(row, 1), :]

    plan.add("mx", feed_x, loaded("gain"), ("l2",), 1)
    plan.add("mz.", feed_z, lambda: at.feed, ("mx",), 1)
    plan.add("my.", feed_y, lambda: at.feed, ("mz.",), 1)
    plan.add("m.", feed_all, lambda: at.feed, ("my.",), 1)

    def along_x():
        ones = jnp.ones((8, 128), F32)
        for pair in range(2):
            line = lax.dot_general(
                ones, along_s[pair], (((1,), (1,)), ((), ())), precision=lax.Precision.HIGHEST,
                preferred_element_type=F32,
            )
            for k in range(4):
                along_a[me.x, pair * 4 + k : pair * 4 + k + 1, :] = line[0:1, k * 128 : k * 128 + 128]
        at.along = Meet(wire, me, "x", along_a).copies

    def along_z():
        along_b[me.z] = along_a[0] + along_a[1] + along_a[2] + along_a[3]
        at.along = Meet(wire, me, "z", along_b).copies

    def along_y():
        along_c[me.y] = along_b[0] + along_b[1] + along_b[2] + along_b[3]
        at.along = Meet(wire, me, "y", along_c).copies

    def along_all():
        along_t[...] = along_c[0] + along_c[1] + along_c[2] + along_c[3]
        row = me.y * 2 + me.zh
        column = pl.ds(pl.multiple_of((row * 2 + me.core) * 128, 128), 128)
        gains_out[0:1, :] = along_t[pl.ds(row, 1), :] / gains_in[0:1, column]

    plan.add("ax", along_x, after=("gq1",), rank=1)
    plan.add("az", along_z, lambda: at.along, ("ax",), 1)
    plan.add("ay", along_y, lambda: at.along, ("az",), 1)
    plan.add("a.", along_all, lambda: [*loaded("gains")(), *at.along], ("ay",), 1)
    plan.add("gk", lambda: keep(gains_out, g_gains_hbm), after=("a.", "m."), rank=2)

    def back_all():
        lax.fori_loop(0, 8, back_norm, 0)
        keep(tokens_out, grad_tokens_hbm)

    plan.add(
        "bn", back_all,
        lambda: [*loaded("tok", "dy", "gains")(), at.last[0], at.last[1]], ("ds.far", "dl0", "dl1"), 0,
    )
    plan.go(ORDER_BACK)
    for copy in kept:
        copy.wait()
    wire.drain()


def call_back(starts, tokens, d_attn, out_part, qkv, w_out, query, keys, values, heads, lse, turned,
              tables, gains, y_one, d_y, gain_two, fold_y, fold_z, down):
    shape = jax.ShapeDtypeStruct

    def three(*dims):
        return [pltpu.VMEM(dims, BF)] * 3

    rest = UNITS - SUM_Y
    bufs = (
        three(2, SUM_Y, 128)
        + fold_shapes((2,), (), rest, 144, 128)
        + fold_shapes((), (2, 2), O_Y, O_CUT, 128)
        + three(O_Y, 128)
        + three(4, 256 - O_Y, 128)
        + fold_shapes((), (), 256 - O_Y, O_REST, 128)
        + fold_shapes((3,), (2,), Q_Y, Q_CUT, 256)
        + three(3, Q_Y, 256)
        + three(3, 4, 128 - Q_Y, 256)
        + fold_shapes((3,), (), 128 - Q_Y, Q_REST, 256)
        + fold_shapes((), (2, 2), DN_Y, DN_CUT, 128)
        + three(DN_Y, 128)
        + three(4, UNITS - DN_Y, 128)
        + fold_shapes((), (), UNITS - DN_Y, DN_REST, 128)
        + fold_shapes((3,), (2,), Q_Y, Q_CUT, 256)
    )
    return pl.pallas_call(
        kernel_back,
        name="back",
        in_specs=[pl.BlockSpec(memory_space=pltpu.SMEM)] + [anywhere()] * 19,
        out_specs=[anywhere()] * 6,
        out_shape=[
            shape((128, D), BF),
            shape((128, D), BF),
            shape((3, 128, 256), F32),
            shape((256, 128), F32),
            shape((3, UNITS, 128), F32),
            shape((2, 128), F32),
        ],
        scratch_shapes=[
            pltpu.VMEM((4, 512, HD), BF),
            pltpu.VMEM((4, 4, 2, 128, HD), BF),
            pltpu.VMEM((4, 4, 2, 128, HD), BF),
            pltpu.VMEM((4, 1, 512), F32),
            pltpu.VMEM((8, D), F32),
            pltpu.VMEM((128, D), F32),
            pltpu.VMEM((128, D), F32),
            pltpu.VMEM((1, D), F32),
            pltpu.VMEM((128, D), BF),
            pltpu.VMEM((128, D), BF),
            pltpu.VMEM((3, 128, 256), F32),
            pltpu.VMEM((256, 128), F32),
            pltpu.VMEM((3, UNITS, 128), F32),
            pltpu.VMEM((2, 128), F32),
            pltpu.VMEM((3, 2, 4, 2, 2, 128, 256), BF),
            pltpu.VMEM((2, 4, 2, 2, 256, 128), BF),
            pltpu.VMEM((4, 128, D), BF),
            pltpu.VMEM((4, 128, D), BF),
            pltpu.VMEM((2, 4, 2, 128, HD), F32),
            pltpu.VMEM((4, 2, 128, 512), F32),
            pltpu.VMEM((128, D), BF),
            pltpu.VMEM((2, 8, 128, SEQ), BF),
            pltpu.VMEM((4, 512, HD), BF),
            pltpu.VMEM((512, 512), BF),
            pltpu.VMEM((SEQ, 512), BF),
            pltpu.VMEM((SEQ, 512), BF),
            pltpu.VMEM((512, 512), BF),
            pltpu.VMEM((SEQ, 512), BF),
            pltpu.VMEM((SEQ, 512), BF),
            pltpu.VMEM((SEQ, HD), F32),
            pltpu.VMEM((SEQ, HD), F32),
            pltpu.VMEM((512, 512), BF),
            pltpu.VMEM((512, 512), BF),
            pltpu.VMEM((8, 4, 128, 128), BF),
            pltpu.VMEM((4, 2, 128, D), BF),
        ]
        + [pltpu.VMEM((128, D), BF)] * 4
        + [
            pltpu.VMEM((128, D // 2), BF),
            pltpu.VMEM((128, D // 2), BF),
            pltpu.VMEM((128, D), BF),
            pltpu.VMEM((128, D), BF),
        ]
        * 2
        + [
            pltpu.VMEM((2, 2, 2, SUM_Y, 128), BF),
            pltpu.VMEM((2, 4, UNITS - SUM_Y, 128), BF),
            pltpu.VMEM((2, 4, 2, UNITS, 128), BF),
            pltpu.VMEM((4, 16, 128), F32),
            pltpu.VMEM((4, 16, 128), F32),
            pltpu.VMEM((2, 4, 16, 128), F32),
            pltpu.VMEM((2, 512, 128), F32),
            pltpu.VMEM((4, 8, 128), F32),
            pltpu.VMEM((4, 8, 128), F32),
            pltpu.VMEM((4, 8, 128), F32),
            pltpu.VMEM((16, 128), F32),
            pltpu.VMEM((8, 128), F32),
        ]
        + bufs
        + [
            pltpu.SemaphoreType.DMA((140,)),
            pltpu.SemaphoreType.DMA((140,)),
            pltpu.SemaphoreType.DMA((40,)),
        ],
        compiler_params=pltpu.CompilerParams(
            collective_id=2, has_side_effects=True, vmem_limit_bytes=VMEM_BYTES
        ),
    )(starts, tokens, d_attn, out_part, qkv, w_out, query, keys, values, heads, lse, turned,
      tables, gains, y_one, d_y, gain_two, fold_y, fold_z, down)


def kernel_settle(*refs):
    arrays, results, held, (row_s, send, recv) = refs[:6], refs[6:17], refs[17:23], refs[23:]
    tp = lax.axis_index("tensor")
    copies = [
        pltpu.make_async_copy(source, target, recv.at[index])
        for index, (source, target) in enumerate(zip(arrays, held))
    ]
    for copy in copies:
        copy.start()
    outs = []

    def give(source, index):
        copy = pltpu.make_async_copy(source, results[index], send.at[index])
        copy.start()
        outs.append(copy)

    copies[5].wait()
    for index in range(2):
        row = held[5][index : index + 1, :]
        row_s[index] = pltpu.roll(row, lax.rem(128 - tp * 16, 128), 1)[:, 0:16]
    for index in range(2):
        give(row_s.at[index], 9 + index)
    for index in range(2):
        copies[index].wait()
        give(held[index], index)
    copies[4].wait()
    for index in range(3):
        give(held[4].at[index], 6 + index)
    copies[2].wait()
    for index in range(3):
        give(held[2].at[index], 2 + index)
    copies[3].wait()
    give(held[3], 5)
    for copy in outs:
        copy.wait()


def call_settle(*arrays):
    shape = jax.ShapeDtypeStruct
    return pl.pallas_call(
        kernel_settle,
        name="settle",
        in_specs=[anywhere()] * 6,
        out_specs=[anywhere()] * 11,
        out_shape=[shape((128, D), BF)] * 2
        + [shape((128, 256), F32)] * 3
        + [shape((256, 128), F32)]
        + [shape((UNITS, 128), F32)] * 3
        + [shape((1, 16), F32)] * 2,
        scratch_shapes=[
            pltpu.VMEM((128, D), BF),
            pltpu.VMEM((128, D), BF),
            pltpu.VMEM((3, 128, 256), F32),
            pltpu.VMEM((256, 128), F32),
            pltpu.VMEM((3, UNITS, 128), F32),
            pltpu.VMEM((2, 128), F32),
            pltpu.VMEM((2, 1, 16), F32),
            pltpu.SemaphoreType.DMA((11,)),
            pltpu.SemaphoreType.DMA((6,)),
        ],
        compiler_params=pltpu.CompilerParams(vmem_limit_bytes=VMEM_BYTES),
    )(*arrays)


def on_device(tables, tokens, starts, w_query, w_key, w_value, w_out, w_gate, w_up, w_down,
              gain_attn, gain_mlp, cotangent):
    weights = (w_query, w_key, w_value, w_out, w_gate.T, w_up.T, w_down)
    (qkv, w_o, mlp, cot, turned, query, keys, values, heads, h_two, lse, y_one, gains) = call_attend(
        tokens, cotangent, starts, weights, gain_attn.reshape(1, 16), gain_mlp.reshape(1, 16), tables
    )
    out_part, d_attn, fold_y, fold_z, down, d_y, gain_two = call_feed(h_two, cot, mlp, y_one, gains)
    sums = call_back(
        starts, tokens, d_attn, out_part, qkv, w_o, query, keys, values, heads, lse, turned,
        tables, gains, y_one, d_y, gain_two, fold_y, fold_z, down,
    )
    result, grad_tokens, query, key, value, out, gate, up, down, attn, feed = call_settle(*sums)
    return (
        result, grad_tokens, query, key, value, out, gate.T, up.T, down,
        attn.reshape(16), feed.reshape(16),
    )


def solution(mesh):
    both = ("dp", "tensor")
    rows, wide, tall = P(both, None), P("dp", "tensor"), P("tensor", "dp")
    in_specs = (
        rows, P("dp"), wide, wide, wide, tall, wide, wide, tall, P(both), P(both), rows,
    )
    out_specs = (
        rows, rows, wide, wide, wide, tall, wide, wide, tall, P(both), P(both),
    )
    return jax.shard_map(
        functools.partial(on_device, rope_tables()), mesh=mesh, in_specs=in_specs,
        out_specs=out_specs, check_vma=False,
    )
```

```python
import functools
import math
import types

import jax
import jax.numpy as jnp
import numpy as np
from jax import lax
from jax.experimental import pallas as pl
from jax.experimental.pallas import tpu as pltpu
from jax.sharding import PartitionSpec as P

HD = 128
PIECE = 256
EPS = 1e-05
NEG = -1e30
SCALE = HD ** (-0.5)
D = 2048
SEQ = 1024
UNITS = 688
BF = jnp.bfloat16
F32 = jnp.float32
MESH = pl.DeviceIdType.MESH
VMEM_BYTES = 60 * 1024 * 1024
ALL = slice(None)


def dot_nn(left, right):
    return jnp.dot(left, right, preferred_element_type=F32)


def dot_nt(left, right):
    return lax.dot_general(left, right, (((1,), (1,)), ((), ())), preferred_element_type=F32)


def dot_tn(left, right):
    return lax.dot_general(left, right, (((0,), (0,)), ((), ())), preferred_element_type=F32)


def rem4(value):
    return lax.rem(value, 4)


def place():
    dp = lax.axis_index("dp")
    tp = lax.axis_index("tensor")
    zh = lax.rem(lax.div(dp, 2), 2)
    zl = lax.rem(tp, 2)
    return types.SimpleNamespace(
        y=lax.div(dp, 4), zh=zh, zl=zl, z=zh * 2 + zl, x=lax.div(tp, 2), core=lax.rem(dp, 2)
    )


def device(me, **moved):
    at = types.SimpleNamespace(**{**vars(me), **moved})
    zh, zl = lax.div(at.z, 2), lax.rem(at.z, 2)
    return (at.y * 4 + zh * 2 + at.core, at.x * 2 + zl)


def near(me, axis, step):
    return device(me, **{axis: rem4(getattr(me, axis) + step)})


def sibling(me):
    return device(me, core=1 - me.core)


def partner(me):
    return device(me, z=me.zh * 2 + 1 - me.zl)


def across(me):
    return device(me, z=rem4(me.z + 3 + 2 * me.zl))


def greet(me, wide, meanwhile=(), early=None):
    others = [near(me, axis, step) for axis in ("x", "y", "z") for step in (1, 3)] + [sibling(me)]
    if wide:
        others += [near(me, axis, 2) for axis in ("x", "y", "z")]
        others += [crossed(me, step) for step in (1, 2, 3)]
    barrier = pltpu.get_barrier_semaphore()
    for other in others:
        pl.semaphore_signal(barrier, inc=1, device_id=other, device_id_type=MESH)
    for copy in meanwhile:
        copy.wait()
    if early is not None:
        early()
    pl.semaphore_wait(barrier, len(others))


def crossed(me, step):
    return device(me, y=rem4(me.y + step), core=1 - me.core)


class Plan:
    def __init__(self):
        self.steps = {}

    def add(self, name, run, waits=tuple, after=(), rank=5):
        self.steps[name] = types.SimpleNamespace(run=run, waits=waits, after=after, rank=rank)

    def go(self, order):
        assert sorted(order) == sorted(self.steps)
        for name in order:
            step = self.steps[name]
            for copy in step.waits():
                copy.wait_recv()
            step.run()


class Once:
    def __init__(self, copy, remote):
        self.copy, self.remote = copy, remote
        self.received = self.left = False

    def wait_recv(self):
        if not self.received:
            self.received = True
            if self.remote:
                self.copy.wait_recv()
            else:
                self.copy.wait()

    wait = wait_recv

    def wait_send(self):
        if not self.left:
            self.left = True
            self.copy.wait_send()


class Wire:
    def __init__(self, send, recv, local):
        self.send, self.recv, self.local = send, recv, local
        self.used, self.used_local = 0, 0
        self.sent = []

    def put(self, source, target, to):
        index = self.used
        self.used += 1
        assert index < self.send.shape[0]
        copy = pltpu.make_async_remote_copy(
            src_ref=source,
            dst_ref=target,
            send_sem=self.send.at[index],
            recv_sem=self.recv.at[index],
            device_id=to,
            device_id_type=MESH,
        )
        copy.start()
        copy = Once(copy, True)
        self.sent.append(copy)
        return copy

    def move(self, source, target):
        index = self.used_local
        self.used_local += 1
        assert index < self.local.shape[0]
        copy = pltpu.make_async_copy(source, target, self.local.at[index])
        copy.start()
        return Once(copy, False)

    def drain(self):
        for copy in self.sent:
            copy.wait_send()
        self.sent = []


class Ring:
    def __init__(self, wire, me, axis, view):
        self.wire, self.view = wire, view
        self.at = getattr(me, axis)
        self.right, self.left = near(me, axis, 1), near(me, axis, 3)

    def put(self, slot, part, to):
        piece = self.view(slot, part)
        return self.wire.put(piece, piece, to)

    def start(self):
        self.right_one = self.put(self.at, 0, self.right)
        self.left_one = self.put(self.at, 1, self.left)
        self.right_two = self.put(self.at, 1, self.right)
        self.left_two = self.put(self.at, 0, self.left)

    def start_half(self, half):
        if half == 0:
            self.right_one = self.put(self.at, 0, self.right)
            self.left_two = self.put(self.at, 0, self.left)
        else:
            self.left_one = self.put(self.at, 1, self.left)
            self.right_two = self.put(self.at, 1, self.right)

    def plan(self, plan, name, after, rank):
        plan.add(name + ".go", self.start, after=after, rank=rank)
        plan.add(name + ".r", self.relay_right, lambda: [self.right_one], (name + ".go",), rank)
        plan.add(name + ".l", self.relay_left, lambda: [self.left_one], (name + ".go",), rank)
        plan.add(
            name + ".near", lambda: None, lambda: [self.right_two, self.left_two],
            (name + ".r", name + ".l"), rank,
        )
        plan.add(
            name + ".far", lambda: None, lambda: [self.far_right, self.far_left], (name + ".near",), rank
        )

    def relay_right(self):
        self.far_right = self.put(rem4(self.at + 3), 0, self.right)

    def relay_left(self):
        self.far_left = self.put(rem4(self.at + 1), 1, self.left)

    def copies(self):
        return [
            self.right_one, self.left_one, self.right_two, self.left_two, self.far_right, self.far_left
        ]

    def closed(self):
        return rem4(self.at + 3), rem4(self.at + 1)


class Direct:
    def __init__(self, wire, me, view):
        self.wire, self.view, self.me, self.at = wire, view, me, me.z

    def start(self):
        piece = self.view(self.at, None)
        others = (partner(self.me), across(self.me), near(self.me, "z", 2))
        self.copies = [self.wire.put(piece, piece, other) for other in others]

    def plan(self, plan, name, after, rank):
        plan.add(name + ".go", self.start, after=after, rank=rank)
        plan.add(name + ".far", lambda: None, lambda: self.copies, (name + ".go",), rank)


class PairRing:
    def __init__(self, wire, me, view):
        self.wire, self.view, self.me = wire, view, me
        self.at = me.z
        self.mate, self.beyond = me.zh * 2 + 1 - me.zl, rem4(me.z + 3 + 2 * me.zl)

    def put(self, slot, to):
        piece = self.view(slot, None)
        return self.wire.put(piece, piece, to)

    def start(self):
        self.to_mate = self.put(self.at, partner(self.me))
        self.to_beyond = self.put(self.at, across(self.me))

    def plan(self, plan, name, after, rank):
        plan.add(name + ".go", self.start, after=after, rank=rank)
        plan.add(name + ".r", self.relay, lambda: [self.to_mate], (name + ".go",), rank)
        plan.add(name + ".near", lambda: None, lambda: [self.to_beyond], (name + ".r",), rank)
        plan.add(name + ".far", lambda: None, lambda: [self.far], (name + ".near",), rank)

    def relay(self):
        self.far = self.put(self.mate, across(self.me))

    def copies(self):
        return [self.to_mate, self.to_beyond, self.far]

    def closed(self):
        return self.mate, self.beyond


class Meet:
    def __init__(self, wire, me, axis, ref):
        piece = ref.at[getattr(me, axis)]
        self.copies = [wire.put(piece, piece, near(me, axis, step)) for step in (1, 2, 3)]


class MeetCores:
    def __init__(self, wire, me, ref):
        piece = ref.at[me.core, me.y]
        others = [near(me, "y", step) for step in (1, 2, 3)] + [sibling(me)]
        others += [crossed(me, step) for step in (1, 2, 3)]
        self.copies = [wire.put(piece, piece, other) for other in others]


class RingSum:
    def __init__(self, wire, me, axis, part, from_left, from_right, whole_left, whole_right, split, add):
        self.wire, self.part, self.split, self.add = wire, part, split, add
        self.at = getattr(me, axis)
        self.right, self.left = near(me, axis, 1), near(me, axis, 3)
        self.near_bufs = (from_left, from_right)
        self.whole = (whole_left, whole_right)

    def start_near(self, half):
        piece = self.part(rem4(self.at + 2), half)
        to = self.left if half else self.right
        copy = self.wire.put(piece, self.near_bufs[half], to)
        if half:
            self.second = copy
        else:
            self.first = copy

    def start_whole(self, half):
        if half:
            self.right_whole = self.wire.put(
                self.part(rem4(self.at + 1), 1), self.split(self.whole[0], 1), self.right
            )
        else:
            self.left_whole = self.wire.put(
                self.part(rem4(self.at + 3), 0), self.split(self.whole[1], 0), self.left
            )

    def start(self, halves=(0, 1)):
        for half in halves:
            self.start_near(half)
        if 1 in halves:
            self.start_whole(1)
            self.start_whole(0)

    def plan(self, plan, name, after, rank, go=True):
        if go:
            plan.add(name + ".go", self.start, after=after, rank=rank)
        plan.add(name + ".r", self.relay_right, lambda: [self.first], (name + ".go",), rank)
        plan.add(name + ".l", self.relay_left, lambda: [self.second], (name + ".go",), rank)
        plan.add(
            name + ".far",
            lambda: None,
            lambda: [self.left_whole, self.right_whole, self.to_right, self.to_left],
            (name + ".r", name + ".l"),
            rank,
        )

    def relay_right(self):
        after = rem4(self.at + 1)
        self.add(self.part(after, 0), self.near_bufs[0])
        self.to_right = self.wire.put(self.part(after, 0), self.split(self.whole[0], 0), self.right)

    def relay_left(self):
        before = rem4(self.at + 3)
        self.add(self.part(before, 1), self.near_bufs[1])
        self.to_left = self.wire.put(self.part(before, 1), self.split(self.whole[1], 1), self.left)


class PairSum:
    def __init__(self, wire, me, part, from_beyond, for_mate, from_mate, add):
        self.wire, self.me, self.part, self.add = wire, me, part, add
        self.at = me.z
        self.mate, self.beyond = me.zh * 2 + 1 - me.zl, rem4(me.z + 3 + 2 * me.zl)
        self.for_mate, self.whole = for_mate, (from_beyond, from_mate)

    def start(self):
        far = rem4(self.at + 2)
        self.first = self.wire.put(self.part(far, None), self.for_mate, across(self.me))
        self.second = self.wire.put(self.part(self.beyond, None), self.whole[0], across(self.me))

    def plan(self, plan, name, after, rank):
        plan.add(name + ".go", self.start, after=after, rank=rank)
        plan.add(name + ".r", self.relay, lambda: [self.first], (name + ".go",), rank)
        plan.add(
            name + ".far", lambda: None, lambda: [self.second, self.to_mate], (name + ".r",), rank
        )

    def relay(self):
        self.add(self.part(self.mate, None), self.for_mate)
        self.to_mate = self.wire.put(self.part(self.mate, None), self.whole[1], partner(self.me))


def split_columns(ref, half):
    return ref.at[:, pl.ds(half * (D // 2), D // 2)]


def split_rows(cut):
    def split(ref, half):
        rows = ref.shape[-2]
        span = pl.ds(0, cut) if half == 0 else pl.ds(cut, rows - cut)
        return ref.at[(ALL,) * (len(ref.shape) - 2) + (span, ALL)]

    return split


class Spread:
    def __init__(self, wire, me, ref, lead, row, rows, first, cut, cuts=(ALL,), kind=PairRing, ring=False):
        self.wire, self.me = wire, me
        head = (ALL,) * lead

        def view(y, z, part, low=ALL):
            zl, zh = (low, ALL) if z is None else (lax.rem(z, 2), lax.div(z, 2))
            start, size = row, rows
            if part == 0:
                size = cut
            if part == 1:
                start, size = row + cut, rows - cut
            yy = ALL if y is None else y
            return ref.at[head + (zl, yy, zh, me.core, pl.ds(start, size), ALL)]

        if first == "y":
            self.one = Ring(wire, me, "y", lambda slot, part: view(slot, me.z, part))
            across_z = lambda slot, part: view(None, slot, part)
            self.twos = [
                Ring(wire, me, "z", across_z) if ring else PairRing(wire, me, across_z)
            ]
        else:
            self.one = kind(wire, me, lambda slot, part: view(me.y, slot, part))
            self.twos = [
                Ring(wire, me, "y", lambda slot, part, low=low: view(slot, None, part, low))
                for low in cuts
            ]

    def plan(self, plan, name, after, turn_after, rank):
        self.one.plan(plan, name + ".a", after, rank)
        self.plan_second(plan, name, (name + ".a.far", *turn_after), rank)

    def plan_second(self, plan, name, done, rank):
        done = list(done)
        self.shared = []
        for index, two in enumerate(self.twos):
            tail = str(index) if len(self.twos) > 1 else ""
            self.plan_two(plan, two, name, tail, tuple(done), rank + 0.01 * index)
            done += [name + ".b" + tail + ".r", name + ".b" + tail + ".l"] if tail else []

    def plan_two(self, plan, two, name, tail, after, rank):
        shared = []

        def share(slots):
            for slot in slots:
                piece = two.view(slot, None)
                shared.append(self.wire.put(piece, piece, sibling(self.me)))
            self.shared += shared[-len(slots) :]

        def go():
            two.start()
            share([two.at])

        step = name + ".b" + tail
        two.plan(plan, step, after, rank)
        plan.steps[step + ".go"].run = go
        plan.add(name + ".s" + tail, lambda: share(two.closed()), after=(step + ".near",), rank=rank)
        plan.add(
            name + ".t" + tail, lambda: share([rem4(two.at + 2)]),
            after=(name + ".s" + tail, step + ".far"), rank=rank,
        )
        plan.add(name + ".all" + tail, lambda: None, lambda: shared, (name + ".t" + tail,), rank)
MLP_Y, MLP_CUT, MLP_REST = 288, 144, 208
QKV_Y, QY_CUT, QZ_CUT = 32, 16, 48
QZ_KIND = PairRing
OUT_Y, OUT_CUT, OUT_REST = 64, 32, 96
MZ_AFTER, MZ_TURN = (), ()
MY_AFTER, MY_TURN = (), ()
ORDER_ATTEND = (
    "qz.a.go", "gx", "tz", "qy.a.go", "oy.a.go", "my.a.go", "tx.go", "bias", "qy.a.r", "qy.a.l",
    "gz", "qy.a.near", "oy.a.r", "oy.a.l", "oy.a.near", "qz.a.r", "qz.a.near", "my.a.r", "my.a.l",
    "my.a.near", "qy.a.far", "qy.b.go", "oz.a.go", "oy.a.far", "oy.b.go", "mz.a.go", "tx.r",
    "tx.l", "my.a.far", "qz.a.far", "qz.b0.go", "tx.near", "qz.b0.r", "qz.b0.l", "to", "gy",
    "qz.b0.near", "qz.s0", "tx.far", "tf", "qz.b1.go", "cx.go", "qy.b.r", "qy.b.near", "qy.s",
    "oz.a.r", "oz.a.near", "qz.b0.far", "qz.t0", "oy.b.r", "oy.b.near", "gains", "n1", "qz.all0",
    "oy.s", "n2", "n0", "qz.b1.r", "qz.b1.l", "qy.b.far", "qy.t", "n3", "mz.a.r", "mz.a.near",
    "oz.a.far", "oz.b.go", "qy.all", "proj0", "qz.b1.near", "qz.s1", "own0", "my.b.go",
    "qz.b1.far", "n4", "qz.t1", "oy.b.far", "oy.t", "oz.b.r", "oz.b.l", "rest0", "mz.a.far",
    "mz.b.go", "qz.all1", "rest1", "oy.all", "proj1", "cx.l", "own2", "n5", "last0", "cx.r",
    "oz.b.near", "oz.s", "oz.b.far", "att0", "cx.near", "wz.go", "oz.t", "last1", "att2",
    "oz.all", "po", "ys.go", "cx.far", "mz.b.r", "ck", "ht", "mz.b.l", "my.b.r", "my.b.near",
    "my.s", "flip", "wz.r", "flip2", "wz.near", "mz.b.near", "mz.s", "ys.r", "wy.go", "ys.l",
    "flip3", "mz.b.far", "mz.t", "mz0", "wy.l", "wy.r", "my.b.far", "my.t", "my0", "wy.near",
    "mz.all", "mz1", "wz.far", "wz0", "my.all", "my1", "ys.far", "fin", "wy.far", "wy0",
)

UP_Y, UP_CUT, UP_REST = 320, 160, 176


def up_spreads(wire, me, ref):
    return (
        Spread(wire, me, ref, 0, UP_Y, UNITS - UP_Y, "z", UP_REST),
        Spread(wire, me, ref, 0, 0, UP_Y, "y", UP_CUT, ring=True),
    )


def norm_rows(source, target, gain, rows, step=32):
    def body(index, carry):
        span = pl.ds(pl.multiple_of(index * step, step), step)
        value = source[span, :].astype(F32)
        scale = lax.rsqrt(jnp.mean(value * value, axis=-1, keepdims=True) + EPS)
        target[span, :] = (value * scale * gain).astype(BF)
        return carry

    lax.fori_loop(0, rows // step, body, 0)


def fill_bias(bias, me, start):
    row = lax.broadcasted_iota(jnp.int32, (128, 512), 0)
    column = lax.broadcasted_iota(jnp.int32, (128, 512), 1)
    query = lax.div(column, 128) * 256 + me.zl * 128 + lax.rem(column, 128)
    query_in = (query >= start) & (query < start + PIECE)

    def body(block, carry):
        pair, other = lax.div(block, 2), lax.rem(block, 2)
        parity = me.zl + other * (1 - 2 * me.zl)
        key = (pair * 2 + parity) * 128 + row
        key_in = (key >= start) & (key < start + PIECE)
        allowed = (key <= query) | (query_in & key_in)
        bias[pair, other] = jnp.where(allowed, 0.0, NEG)
        return carry

    lax.fori_loop(0, 8, body, 0)


def turn(field, cosine, sine):
    return field * cosine + pltpu.roll(field, HD // 2, 1) * sine


def add_into(target, terms, result=None):
    shape = target.shape
    lead, rows, columns = shape[:-2], shape[-2], shape[-1]
    step = rows
    while step * columns > 33000:
        step = next(s for s in range(step - 16, 0, -16) if rows % s == 0)
    cuts = rows // step
    result = target if result is None else result

    def body(index, carry):
        where, rest = [], lax.div(index, cuts)
        for extent in reversed(lead):
            where.insert(0, lax.rem(rest, extent))
            rest = lax.div(rest, extent)
        where = tuple(where) + (
            pl.ds(pl.multiple_of(lax.rem(index, cuts) * step, 16), step), ALL
        )
        total = target[where].astype(F32)
        for term in terms:
            total = total + term[where].astype(F32)
        result[where] = total.astype(result.dtype)
        return carry

    lax.fori_loop(0, math.prod(lead) * cuts, body, 0)


def columns_of(ref):
    def view(slot, half):
        if half is None:
            return ref.at[slot]
        return ref.at[slot, :, pl.ds(half * (D // 2), D // 2)]

    return view


def rows_of(ref):
    def view(slot, half):
        return ref.at[slot] if half is None else ref.at[slot, pl.ds(half * 64, 64)]

    return view


def kernel_attend(
    tokens_in, cotangent_in, start_in, query_w, key_w, value_w, out_w, gate_w, up_w, down_w,
    gain_one_in, gain_two_in, tables_in,
    qkv_out, wo_out, mlp_out, cot_out, turned_out, query_out, keys_out, values_out, heads_out,
    h_out, lse_hbm, y_hbm, gains_hbm,
    lse_out, y_out, gains_out, tok, h_one, w_qkv, w_o, w_mlp, tables, bias, query, keys, values, heads, cot, h_two,
    part, near_left, near_right, whole_left, whole_right,
    turned, heads_t, top_s, total_s, result_s, gain_x, gain_z, gain_c,
    send, recv, local,
):
    me = place()
    wire = Wire(send, recv, local)
    own = [wire.move(tokens_in, tok.at[me.x, 0])]
    for index, ref in enumerate((query_w, key_w, value_w)):
        own.append(wire.move(ref, w_qkv.at[index, me.zl, me.y, me.zh, me.core]))
    own.append(wire.move(out_w, w_o.at[me.zl, me.y, me.zh, me.core]))
    for index, ref in enumerate((gate_w, down_w, up_w)):
        own.append(wire.move(ref, w_mlp.at[index, me.zl, me.y, me.zh, me.core]))
    own.append(wire.move(tables_in.at[me.zl], tables))
    own.append(wire.move(cotangent_in, cot.at[me.x]))
    lane = lax.div(lax.broadcasted_iota(jnp.int32, (1, 128), 1), 16)
    tensor = me.x * 2 + me.zl
    gain_x[me.x] = jnp.concatenate(
        [
            jnp.where(lane == tensor, jnp.concatenate([ref[...]] * 8, axis=1), 0.0)
            for ref in (gain_one_in, gain_two_in)
        ]
        + [jnp.zeros((6, 128), F32)],
        axis=0,
    )
    greet(me, True, own)
    plan = Plan()
    at = types.SimpleNamespace()
    one, far, three = rem4(me.x + 1), rem4(me.x + 2), rem4(me.x + 3)
    kept = []

    def keep(source, target):
        kept.append(wire.move(source, target))

    def gains_x():
        at.gains = Meet(wire, me, "x", gain_x).copies

    def gains_z():
        gain_z[me.z] = gain_x[0] + gain_x[1] + gain_x[2] + gain_x[3]
        at.gains = Meet(wire, me, "z", gain_z).copies

    def gains_y():
        gain_c[me.core, me.y, 0] = gain_z[0] + gain_z[1]
        gain_c[me.core, me.y, 1] = gain_z[2] + gain_z[3]
        at.gains = MeetCores(wire, me, gain_c).copies

    def gains_all():
        for y in range(4):
            for zh in range(2):
                for core in range(2):
                    column = (y * 4 + zh * 2 + core) * 128
                    gains_out[:, column : column + 128] = gain_c[core, y, zh]

    plan.add("gx", gains_x, rank=0)
    plan.add("gz", gains_z, lambda: at.gains, ("gx",), 0)
    plan.add("gy", gains_y, lambda: at.gains, ("gz",), 0)
    plan.add("gains", gains_all, lambda: at.gains, ("gy",), 1)

    def tokens_z():
        at.rows_z = wire.put(tok.at[me.x, 0], tok.at[me.x, 1], partner(me))

    def tokens_on():
        at.on = [
            wire.put(tok.at[me.x, 1], tok.at[me.x, 1], near(me, "x", step)) for step in (1, 3)
        ]

    def tokens_far():
        at.far_z = wire.put(tok.at[far, 0], tok.at[far, 1], partner(me))

    Ring(
        wire, me, "x",
        lambda slot, half: tok.at[slot, 0] if half is None else tok.at[slot, 0, pl.ds(half * 64, 64)],
    ).plan(plan, "tx", (), 0)
    plan.add("tz", tokens_z, rank=0)
    plan.add("to", tokens_on, lambda: [at.rows_z], ("tz",), 0)
    plan.add("tf", tokens_far, after=("tx.far",), rank=0)

    def norm(*blocks):
        def run():
            for slot, p in blocks:
                norm_rows(tok.at[slot, p], h_one.at[slot, p], gains_out[0:1, :], 128)

        return run

    plan.add("n0", norm((me.x, 0)), after=("gains",), rank=2)
    plan.add("n1", norm((one, 0), (three, 0)), after=("gains", "tx.near"), rank=2)
    plan.add("n2", norm((far, 0)), after=("gains", "tx.far"), rank=2)
    plan.add("n3", norm((me.x, 1)), after=("gains", "to"), rank=3)
    plan.add("n4", norm((one, 1), (three, 1)), lambda: at.on, ("gains", "to"), 3)
    plan.add("n5", norm((far, 1)), lambda: [at.far_z], ("gains", "tf"), 2)

    Spread(wire, me, w_qkv, 1, QKV_Y, 128 - QKV_Y, "z", QZ_CUT, (0, 1), QZ_KIND).plan(plan, "qz", (), (), 1)
    Spread(wire, me, w_qkv, 1, 0, QKV_Y, "y", QY_CUT).plan(plan, "qy", (), (), 1)
    Spread(wire, me, w_o, 0, OUT_Y, 256 - OUT_Y, "z", OUT_REST).plan(plan, "oz", (), (), 1)
    Spread(wire, me, w_o, 0, 0, OUT_Y, "y", OUT_CUT).plan(plan, "oy", (), (), 1)
    both = w_mlp.at[pl.ds(0, 2)]
    mlp_z = Spread(wire, me, both, 1, MLP_Y, UNITS - MLP_Y, "z", MLP_REST)
    mlp_y = Spread(wire, me, both, 1, 0, MLP_Y, "y", MLP_CUT)
    mlp_z.plan(plan, "mz", (), (), 1.5)
    mlp_y.plan(plan, "my", (), (), 1.5)
    up_z, up_y = up_spreads(wire, me, w_mlp.at[2])
    up_z.one.plan(plan, "wz", (), 1.7)
    up_y.one.plan(plan, "wy", (), 1.7)

    def keep_up(*where):
        return lambda: keep(w_mlp.at[(2, *where)], mlp_out.at[(2, *where)])

    plan.add(
        "wz0", keep_up(ALL, me.y, ALL, me.core, pl.ds(UP_Y, UNITS - UP_Y), ALL),
        after=("wz.far",), rank=1.8,
    )
    plan.add(
        "wy0", keep_up(me.zl, ALL, me.zh, me.core, pl.ds(0, UP_Y), ALL), after=("wy.far",), rank=1.8
    )
    plan.add("bias", lambda: fill_bias(bias, me, start_in[0]), rank=6)

    def project(zl, carry):
        rows = h_one[:, 0].reshape(512, D)
        cosine, sine = tables[0, :, 0].reshape(512, HD), tables[1, :, 0].reshape(512, HD)
        raw = dot_nn(rows, w_qkv[0, zl].reshape(D, 256))
        for j in range(2):
            query[zl * 2 + j] = turn(raw[:, j * HD : (j + 1) * HD], cosine, sine).astype(BF)
        raw = dot_nn(rows, w_qkv[1, zl].reshape(D, 256))
        for j in range(2):
            keys[zl * 2 + j, :, 0] = (
                turn(raw[:, j * HD : (j + 1) * HD], cosine, sine).astype(BF).reshape(4, 128, HD)
            )
        raw = dot_nn(rows, w_qkv[2, zl].reshape(D, 256))
        for j in range(2):
            values[zl * 2 + j, :, 0] = raw[:, j * HD : (j + 1) * HD].astype(BF).reshape(4, 128, HD)
        return carry

    def project_other(zl, slots):
        rows = jnp.concatenate([h_one[slot, 1] for slot in slots], axis=0)
        cosine = jnp.concatenate([tables[0, slot, 1] for slot in slots], axis=0)
        sine = jnp.concatenate([tables[1, slot, 1] for slot in slots], axis=0)
        raw_k = dot_nn(rows, w_qkv[1, zl].reshape(D, 256))
        raw_v = dot_nn(rows, w_qkv[2, zl].reshape(D, 256))
        for j in range(2):
            key = turn(raw_k[:, j * HD : (j + 1) * HD], cosine, sine).astype(BF)
            value = raw_v[:, j * HD : (j + 1) * HD].astype(BF)
            for index, slot in enumerate(slots):
                keys[zl * 2 + j, slot, 1] = key[index * 128 : index * 128 + 128]
                values[zl * 2 + j, slot, 1] = value[index * 128 : index * 128 + 128]

    at.projected = at.rest = 0

    def keep_when_done():
        if at.projected == 2 and at.rest == 4:
            keep(w_qkv, qkv_out)
            keep(query, query_out)
            keep(keys, keys_out)
            keep(values, values_out)

    def project_half(zl):
        def run():
            lax.fori_loop(zl, zl + 1, project, 0)
            at.projected += 1
            keep_when_done()

        return run

    def other(zl, slots):
        def run():
            project_other(zl, slots)
            at.rest += 1
            keep_when_done()

        return run

    for zl in range(2):
        name = "%d" % zl
        plan.add(
            "proj" + name, project_half(zl), after=("n0", "n1", "n2", "qy.all", "qz.all" + name), rank=2 + 0.1 * zl
        )
        plan.add(
            "rest" + name, other(zl, (me.x, one, three)), after=("n3", "n4", "qy.all", "qz.all" + name),
            rank=2.2 + 0.1 * zl,
        )
        plan.add("last" + name, other(zl, (far,)), after=("n5", "qy.all", "qz.all" + name), rank=2.4 + 0.1 * zl)

    def attend_own(head, carry):
        for half, pairs in ((0, 3), (1, 4)):
            span = pairs * 128
            rows = slice(half * 256, half * 256 + 256)
            scores = dot_nt(keys[head, 0:pairs, 0].reshape(span, HD), query[head, rows, :]) * SCALE
            scores = scores + bias[0:pairs, 0, :, rows].reshape(span, 256)
            top = jnp.max(scores, axis=0, keepdims=True)
            expo = jnp.exp(scores - top)
            top_s[head, half] = top
            total_s[head, half] = jnp.sum(expo, axis=0, keepdims=True)
            value = values[head, 0:pairs, 0].reshape(span, HD)
            result_s[head, half] = dot_tn(value, expo.astype(BF))
        return carry

    def attend_other(head, carry):
        for half, pairs in ((0, 3), (1, 4)):
            span = pairs * 128
            rows = slice(half * 256, half * 256 + 256)
            scores = dot_nt(keys[head, 0:pairs, 1].reshape(span, HD), query[head, rows, :]) * SCALE
            scores = scores + bias[0:pairs, 1, :, rows].reshape(span, 256)
            before = top_s[head, half]
            top = jnp.maximum(before, jnp.max(scores, axis=0, keepdims=True))
            fade = jnp.exp(before - top)
            expo = jnp.exp(scores - top)
            total = total_s[head, half] * fade + jnp.sum(expo, axis=0, keepdims=True)
            value = values[head, 0:pairs, 1].reshape(span, HD)
            result = (result_s[head, half] * fade + dot_tn(value, expo.astype(BF))) * (1.0 / total)
            heads[rows, pl.ds(pl.multiple_of(head * HD, HD), HD)] = result.T.astype(BF)
            lse_out[head, :, rows] = top + jnp.log(total)
        return carry

    def attend_rest():
        lax.fori_loop(2, 4, attend_other, 0)
        keep(lse_out, lse_hbm)

    plan.add("own0", lambda: lax.fori_loop(0, 2, attend_own, 0), after=("proj0", "bias"), rank=2.5)
    plan.add("own2", lambda: lax.fori_loop(2, 4, attend_own, 0), after=("proj1", "bias"), rank=2.5)
    plan.add(
        "att0", lambda: lax.fori_loop(0, 2, attend_other, 0), after=("own0", "rest0", "last0"), rank=2.5
    )
    plan.add("att2", attend_rest, after=("own2", "rest1", "last1", "att0"), rank=2.6)

    def project_out(block, carry):
        y, zh = lax.div(block, 2), lax.rem(block, 2)
        weight = jnp.concatenate(
            [
                jnp.concatenate([w_o[zl, y, zh, 0], w_o[zl, y, zh, 1]], axis=1)
                for zl in range(2)
            ],
            axis=0,
        )
        result = dot_nn(heads[...], weight).astype(BF).reshape(4, 128, 256)
        part[:, :, pl.ds(pl.multiple_of(block * 256, 256), 256)] = result
        return carry

    total = RingSum(
        wire, me, "x", columns_of(part), near_left, near_right, whole_left, whole_right,
        split_columns, lambda target, term: add_into(target, [term]),
    )

    def out_one():
        keep(w_o, wo_out)
        lax.fori_loop(0, 4, project_out, 0)
        total.start((0,))

    def out_two():
        lax.fori_loop(4, 8, project_out, 0)
        total.start((1,))

    plan.add("po", out_one, after=("att0", "att2", "oz.all", "oy.all"), rank=2)
    plan.add("ys.go", out_two, after=("po",), rank=2)
    total.plan(plan, "ys", (), 1, go=False)

    def finish(index, carry):
        span = pl.ds(pl.multiple_of(index * 32, 32), 32)
        value = tok[me.x, 0, span, :].astype(F32) + (
            part[me.x, span, :].astype(F32)
            + whole_left[span, :].astype(F32)
            + whole_right[span, :].astype(F32)
        )
        scale = lax.rsqrt(jnp.mean(value * value, axis=-1, keepdims=True) + EPS)
        y_out[span, :] = value
        h_two[span, :] = (value * scale * gains_out[1:2, :]).astype(BF)
        return carry

    def finish_all():
        lax.fori_loop(0, 4, finish, 0)
        keep(h_two, h_out)
        keep(y_out, y_hbm)
        keep(gains_out, gains_hbm)

    plan.add("fin", finish_all, after=("ys.far",), rank=0)
    Ring(wire, me, "x", rows_of(cot)).plan(plan, "cx", (), 1.6)
    plan.add("ck", lambda: keep(cot, cot_out), after=("cx.far",), rank=1.8)

    def flip(block, carry):
        column = pl.ds(pl.multiple_of(block * 128, 128), 128)
        rows = h_one[:, :, :, column].reshape(SEQ, 128)
        turned[lax.rem(block, 2), lax.div(block, 2)] = rows.T
        return carry

    def turn_heads():
        heads_t[...] = heads[...].T
        keep(heads_t, heads_out)

    plan.add("ht", turn_heads, after=("att0", "att2"), rank=6)

    def flip_rest():
        lax.fori_loop(8, 16, flip, 0)
        keep(turned.at[me.core], turned_out.at[0])
        at.turned = wire.put(turned.at[1 - me.core], turned_out.at[1], sibling(me))

    plan.add("flip", lambda: lax.fori_loop(0, 8, flip, 0), after=("n0", "n1", "n2", "n3", "n4", "n5"), rank=7)
    plan.add("flip2", flip_rest, after=("flip",), rank=7)
    plan.add("flip3", lambda: None, lambda: [at.turned], ("flip2",), 9)

    def keep_mlp(mine, start, size):
        def run():
            core = me.core if mine else 1 - me.core
            piece = (pl.ds(0, 2), ALL, ALL, ALL, core, pl.ds(start, size), ALL)
            keep(w_mlp.at[piece], mlp_out.at[piece])

        return run

    plan.add("my0", keep_mlp(True, 0, MLP_Y), after=("my.t",), rank=1.8)
    plan.add("my1", keep_mlp(False, 0, MLP_Y), after=("my.all",), rank=1.8)
    plan.add("mz0", keep_mlp(True, MLP_Y, UNITS - MLP_Y), after=("mz.t",), rank=1.8)
    plan.add("mz1", keep_mlp(False, MLP_Y, UNITS - MLP_Y), after=("mz.all",), rank=1.8)

    plan.go(ORDER_ATTEND)
    for copy in kept:
        copy.wait()
    wire.drain()


def anywhere():
    return pl.BlockSpec(memory_space=pl.ANY)


def in_vmem():
    return pl.BlockSpec(memory_space=pltpu.VMEM)


def call_attend(tokens, cotangent, starts, weights, gain_attn, gain_mlp, tables):
    shape = jax.ShapeDtypeStruct
    hbm = [
        shape((3, 2, 4, 2, 2, 128, 256), BF),
        shape((2, 4, 2, 2, 256, 128), BF),
        shape((3, 2, 4, 2, 2, UNITS, 128), BF),
        shape((4, 128, D), BF),
        shape((2, 8, 128, SEQ), BF),
        shape((4, 512, HD), BF),
        shape((4, 4, 2, 128, HD), BF),
        shape((4, 4, 2, 128, HD), BF),
        shape((512, 512), BF),
        shape((128, D), BF),
    ]
    vmem = [shape((4, 1, 512), F32), shape((128, D), F32), shape((8, D), F32)]
    return pl.pallas_call(
        kernel_attend,
        name="attend",
        in_specs=[anywhere(), anywhere(), pl.BlockSpec(memory_space=pltpu.SMEM)]
        + [anywhere()] * 7
        + [in_vmem()] * 2
        + [anywhere()],
        out_specs=[anywhere()] * (len(hbm) + len(vmem)),
        out_shape=hbm + vmem,
        scratch_shapes=[
            pltpu.VMEM((4, 1, 512), F32),
            pltpu.VMEM((128, D), F32),
            pltpu.VMEM((8, D), F32),
            pltpu.VMEM((4, 2, 128, D), BF),
            pltpu.VMEM((4, 2, 128, D), BF),
            pltpu.VMEM((3, 2, 4, 2, 2, 128, 256), BF),
            pltpu.VMEM((2, 4, 2, 2, 256, 128), BF),
            pltpu.VMEM((3, 2, 4, 2, 2, UNITS, 128), BF),
            pltpu.VMEM((2, 4, 2, 128, HD), F32),
            pltpu.VMEM((4, 2, 128, 512), F32),
            pltpu.VMEM((4, 512, HD), BF),
            pltpu.VMEM((4, 4, 2, 128, HD), BF),
            pltpu.VMEM((4, 4, 2, 128, HD), BF),
            pltpu.VMEM((512, 512), BF),
            pltpu.VMEM((4, 128, D), BF),
            pltpu.VMEM((128, D), BF),
            pltpu.VMEM((4, 128, D), BF),
            pltpu.VMEM((128, D // 2), BF),
            pltpu.VMEM((128, D // 2), BF),
            pltpu.VMEM((128, D), BF),
            pltpu.VMEM((128, D), BF),
            pltpu.VMEM((2, 8, 128, SEQ), BF),
            pltpu.VMEM((512, 512), BF),
            pltpu.VMEM((4, 2, 1, 256), F32),
            pltpu.VMEM((4, 2, 1, 256), F32),
            pltpu.VMEM((4, 2, HD, 256), F32),
            pltpu.VMEM((4, 8, 128), F32),
            pltpu.VMEM((4, 8, 128), F32),
            pltpu.VMEM((2, 4, 2, 8, 128), F32),
            pltpu.SemaphoreType.DMA((140,)),
            pltpu.SemaphoreType.DMA((140,)),
            pltpu.SemaphoreType.DMA((32,)),
        ],
        compiler_params=pltpu.CompilerParams(
            collective_id=0, has_side_effects=True, vmem_limit_bytes=VMEM_BYTES
        ),
    )(tokens, cotangent, starts, *weights, gain_attn, gain_mlp, tables)


def rope_tables():
    half = HD // 2
    freq = np.exp(np.arange(half, dtype=np.float32) * np.float32(-2.0 * math.log(10000.0) / HD))
    order = np.array(
        [
            [[(2 * pair + (zl + other) % 2) * 128 + np.arange(128) for other in range(2)] for pair in range(4)]
            for zl in range(2)
        ]
    )
    angle = order.astype(np.float32)[..., None] * freq.astype(np.float32)
    cosine, sine = np.cos(angle.astype(np.float64)), np.sin(angle.astype(np.float64))
    both = np.stack(
        [np.concatenate([cosine, cosine], -1), np.concatenate([-sine, sine], -1)], axis=1
    )
    return both.astype(np.float32)
SUM_Y, SUM_CUT, SUM_REST = 352, 176, 176
ORDER_FEED = (
    "hx.go", "l2", "wz.b.go", "wy.b.go", "cs", "a11", "wz.b.l", "a01", "hx.l", "hx.r", "wy.b.l",
    "wy.b.r", "wz.b.r", "a00", "wy.b.near", "wy.s", "wz.b.near", "wz.s", "hx.near", "g11",
    "wy.b.far", "wy.t", "g10", "wz.b.far", "wz.t", "wy.all", "a10", "wz.all", "hx.far", "g00",
    "f00", "g01", "f01", "b00", "ds.go", "f10", "f11", "b10", "hs", "ds.r", "t1", "b11", "t0",
    "ds.l", "gr1a", "gr1b", "s1z.go", "s1y.go", "gr0a", "gr0b", "ds.far", "bn", "s0y.go", "s1z.l",
    "s1z.r", "s1y.r", "s1y.l", "dx.go", "s0z.go", "t2", "fd0", "s1z.far", "s1z.k", "s0y.r",
    "dx.r", "fd1", "s0z.l", "s0z.r", "s0y.l", "dx.l", "dx.near", "gr2a", "gr2b", "s1y.far",
    "s1y.k", "dg", "s0z.far", "s0z.k", "s0y.far", "s0y.k", "dx.far", "dk",
)


def fold_view(ref, me, lead, axis, row, rows, cut):
    head = (ALL,) * lead

    def view(slot, part):
        start, size = row, rows
        if part == 0:
            size = cut
        if part == 1:
            start, size = row + cut, rows - cut
        if axis == "y":
            where = (ALL, slot, ALL)
        else:
            where = (lax.rem(slot, 2), ALL, lax.div(slot, 2))
        return ref.at[head + where + (pl.ds(start, size), ALL)]

    return view


def kernel_feed(
    h_in, cot_in, mlp_in, y_hbm, gains_hbm,
    part_out, dattn_out, fold_y_out, fold_z_out, down_out, dy_hbm, gain_hbm,
    y_in, gains_in, dy_out, gain_out,
    w_mlp, h_two, cot, gate_s, up_s, act_s, d_gate, d_up, act, flipped, flipped_far,
    h_far, cot_far, part, near_left, near_right, whole_left, whole_right, d_attn, out_part,
    *rest,
):
    bufs, (send, recv, local) = list(rest[:-3]), rest[-3:]
    bufs = [tuple(bufs[a:b]) for a, b in ((0, 4), (4, 8), (8, 12), (12, 16))]
    me = place()
    wire = Wire(send, recv, local)
    parts = {}

    def load(zl):
        for which in range(2):
            parts[which, zl] = wire.move(mlp_in.at[which, zl], w_mlp.at[which, zl])

    def load_up(*where):
        return wire.move(mlp_in.at[(2, *where)], w_mlp.at[(2, *where)])

    loads = [wire.move(h_in, h_two.at[me.x])]
    ups = [
        load_up(ALL, me.y, ALL, me.core, pl.ds(UP_Y, UNITS - UP_Y), ALL),
        load_up(me.zl, ALL, me.zh, me.core, pl.ds(0, UP_Y), ALL),
    ]
    greet(me, False)
    plan = Plan()
    at = types.SimpleNamespace()
    kept = []

    def keep(source, target):
        kept.append(wire.move(source, target))

    def whole(which, zl):
        return jnp.concatenate(
            [
                w_mlp[which, zl, y, zh, core]
                for y in range(4)
                for zh in range(2)
                for core in range(2)
            ],
            axis=1,
        )

    def share(source, target):
        return [
            wire.put(
                source.at[:, :, pl.ds(pl.multiple_of((block * 2 + 1 - me.core) * 128, 128), 128)],
                target.at[block],
                sibling(me),
            )
            for block in range(8)
        ]

    def share_h():
        at.h_puts = share(h_two, h_far)

    def share_cot():
        at.cot_puts = share(cot, cot_far)

    one, far, three = rem4(me.x + 1), rem4(me.x + 2), rem4(me.x + 3)
    batches = ((far, one), (three, me.x))

    def rows_of_batch(ref, batch):
        return jnp.concatenate([ref[slot] for slot in batches[batch]], axis=0)

    def room(batch, zl):
        return zl if batch else 2

    def gate(batch, zl):
        def run():
            gate_s[room(batch, zl)] = dot_nt(rows_of_batch(h_two, batch), whole(0, zl))

        return run

    def back_act(batch, zl):
        def run():
            act_s[batch * 2 + zl] = dot_nt(rows_of_batch(cot, batch), whole(1, zl))

        return run

    def forward(batch, zl):
        def inner(index, carry):
            place_of, rest = lax.div(index, 4), lax.rem(index, 4)
            first, second = batches[batch]
            slot = first + place_of * (second - first)
            source = pl.ds(pl.multiple_of(index * 32, 32), 32)
            span = pl.ds(pl.multiple_of(rest * 32, 32), 32)
            gate, up = gate_s[room(batch, zl), source, :], up_s[source, :]
            d_act = act_s[batch * 2 + zl, source, :]
            sigma = 1.0 / (1.0 + jnp.exp(-gate))
            act[zl, slot, span, :] = (gate * sigma * up).astype(BF)
            d_gate[zl, slot, span, :] = (
                d_act * up * sigma * (1.0 + gate * (1.0 - sigma))
            ).astype(BF)
            d_up[zl, slot, span, :] = (d_act * gate * sigma).astype(BF)
            return carry

        def run():
            up_s[...] = dot_nt(rows_of_batch(h_two, batch), whole(2, zl))
            lax.fori_loop(0, 8, inner, 0)

        return run

    def back_h(batch):
        def body(block, carry):
            y, zh = lax.div(block, 2), lax.rem(block, 2)
            total = None
            for which, left in ((0, d_gate), (2, d_up)):
                for zl in range(2):
                    weight = jnp.concatenate(
                        [w_mlp[which, zl, y, zh, 0], w_mlp[which, zl, y, zh, 1]], axis=1
                    )
                    rows = jnp.concatenate([left[zl, slot] for slot in batches[batch]], axis=0)
                    term = dot_nn(rows, weight)
                    total = term if total is None else total + term
            result = total.astype(BF)
            column = pl.ds(pl.multiple_of(block * 256, 256), 256)
            for index, slot in enumerate(batches[batch]):
                part[slot, :, column] = result[index * 128 : index * 128 + 128]
            return carry

        return body

    def add(target, term):
        add_into(target, [term])

    total = RingSum(
        wire, me, "x", columns_of(part), near_left, near_right, whole_left, whole_right,
        split_columns, add,
    )

    def back_first(half):
        def run():
            lax.fori_loop(half * 4, half * 4 + 4, back_h(0), 0)
            total.start_near(half)
            if half:
                total.start_whole(1)

        return run

    def back_second(half):
        def run():
            lax.fori_loop(half * 4, half * 4 + 4, back_h(1), 0)
            if half == 0:
                total.start_whole(0)

        return run

    plan.add("hs", share_h, after=("hx.far",), rank=3)
    plan.add("cs", share_cot, lambda: [loads[1]], ("l2",), 3)
    def load_rest():
        load(0)
        load(1)
        loads.append(wire.move(cot_in, cot))
        at.late = [wire.move(y_hbm, y_in), wire.move(gains_hbm, gains_in)]

    plan.add("l2", load_rest, lambda: [loads[0], *ups], ("hx.go",), 0)
    Ring(wire, me, "x", rows_of(h_two)).plan(plan, "hx", (), 0)
    plan.steps["hx.go"].waits = lambda: [loads[0]]
    up_z, up_y = up_spreads(wire, me, w_mlp.at[2])
    up_z.plan_second(plan, "wz", (), 1)
    up_y.plan_second(plan, "wy", (), 1)
    plan.steps["wz.b.go"].waits = lambda: [ups[0]]
    plan.steps["wy.b.go"].waits = lambda: [ups[1]]
    for zl in range(2):
        for batch in range(2):
            name = "%d%d" % (batch, zl)
            plan.add(
                "a" + name, back_act(batch, zl), lambda zl=zl: [loads[1], parts[1, zl]], ("l2",),
                4 - 0.5 * batch,
            )
        plan.add("g1%d" % zl, gate(1, zl), lambda zl=zl: [parts[0, zl]], ("hx.near", "l2"), 3)
    before = ("hx.far", "l2")
    for zl in range(2):
        name = "0%d" % zl
        plan.add("g" + name, gate(0, zl), lambda zl=zl: [parts[0, zl]], before, 2)
        plan.add(
            "f" + name, forward(0, zl), after=("g" + name, "a" + name, "wz.all", "wy.all", *before),
            rank=2,
        )
        before = ("f" + name,)
    plan.add("b00", back_first(0), after=before, rank=2)
    plan.add("ds.go", back_first(1), after=("b00",), rank=2)
    plan.add("f10", forward(1, 0), after=("g10", "a10", "ds.go"), rank=2.1)
    plan.add("f11", forward(1, 1), after=("g11", "a11", "f10"), rank=2.1)
    before = ("f10", "f11")
    plan.add("b10", back_second(0), after=before, rank=2)
    plan.add("b11", back_second(1), after=("b10",), rank=2)
    total.plan(plan, "ds", (), 0, go=False)
    plan.steps["ds.l"].after += ("b11",)
    plan.steps["ds.far"].after += ("b10",)

    at.far = {}

    def turn_over(which, source):
        def run():
            for zl in range(2):
                flipped[which, zl] = source[zl].reshape(512, UNITS).T
            at.far[which] = wire.put(flipped.at[which], flipped_far.at[which], sibling(me))

        return run

    for which, source in enumerate((d_gate, d_up, act)):
        early = which == 1
        plan.add(
            "t%d" % which, turn_over(which, source), after=("f11",) if early else ("b11",),
            rank=1.9 if early else 2 + which * 0.2,
        )

    def forward_down(block, carry):
        y, zh = lax.div(block, 2), lax.rem(block, 2)
        result = None
        for zl in range(2):
            weight = jnp.concatenate([w_mlp[1, zl, y, zh, 0], w_mlp[1, zl, y, zh, 1]], axis=1)
            term = dot_nn(act[zl].reshape(512, UNITS), weight)
            result = term if result is None else result + term
        out_part[:, :, pl.ds(pl.multiple_of(block * 256, 256), 256)] = result.astype(BF).reshape(4, 128, 256)
        return carry

    def down_rest():
        lax.fori_loop(4, 8, forward_down, 0)
        keep(out_part, part_out)

    plan.add("fd0", lambda: lax.fori_loop(0, 4, forward_down, 0), after=("t2",), rank=4)
    plan.add("fd1", down_rest, after=("fd0",), rank=4)

    places = (0, 2, 1)

    def grad(which, rows, rows_far):
        def body(index, carry):
            zl, pair = lax.div(index, 2), lax.rem(index, 2)
            mine = jnp.concatenate(
                [
                    rows[:, :, pl.ds(pl.multiple_of(((pair * 4 + k) * 2 + me.core) * 128, 128), 128)]
                    .reshape(512, 128)
                    for k in range(4)
                ],
                axis=1,
            )
            other = jnp.concatenate(
                [rows_far[pair * 4 + k].reshape(512, 128) for k in range(4)], axis=1
            )
            result = dot_nn(flipped[which, zl], mine) + dot_nn(flipped_far[which, zl], other)
            result = result.astype(BF)
            for k in range(4):
                w_mlp[places[which], zl, pair * 2 + k // 2, k % 2, 0] = result[:, k * 128 : k * 128 + 128]
            return carry

        return body

    sums = []

    def start_sums(which):
        ref = w_mlp.at[places[which], :, :, :, 0]
        pair = [
            RingSum(wire, me, "y", fold_view(ref, me, 0, "y", 0, SUM_Y, SUM_CUT), *bufs[2 * which],
                    split_rows(SUM_CUT), add),
            RingSum(wire, me, "z", fold_view(ref, me, 0, "z", SUM_Y, UNITS - SUM_Y, SUM_REST),
                    *bufs[2 * which + 1], split_rows(SUM_REST), add),
        ]
        for item, out, axis in zip(pair, (fold_y_out, fold_z_out), "yz"):
            name = "s%d%s" % (which, axis)
            item.plan(plan, name, ("gr%db" % which,), 1)
            plan.add(name + ".k", close_sum(item, out.at[which]), after=(name + ".far",), rank=3)

    def close_sum(item, out):
        def run():
            mine = item.part(item.at, None)
            add_into(mine, list(item.whole))
            keep(mine, out)

        return run

    rows_of_step = ((h_two, h_far), (h_two, h_far), (cot, cot_far))
    for which in range(3):
        body = grad(which, *rows_of_step[which])

        def waits(which=which):
            return [at.far[which]] + (at.cot_puts if which == 2 else at.h_puts)

        before = ("t%d" % which, "cs", "hs") + (("fd1",) if which == 2 else ())

        def first(body=body, which=which):
            if which == 1:
                for spread in (up_z, up_y):
                    for copy in [*spread.twos[0].copies(), *spread.shared]:
                        copy.wait_send()
            lax.fori_loop(0, 2, body, 0)

        plan.add("gr%da" % which, first, waits, before, 3)
        plan.add(
            "gr%db" % which, lambda body=body: lax.fori_loop(2, 4, body, 0),
            after=("gr%da" % which,), rank=3,
        )
        if which < 2:
            start_sums(which)
    plan.add("dg", lambda: keep(w_mlp.at[1, :, :, :, 0], down_out), after=("gr2b",), rank=2)

    def back_norm(index, carry):
        span = pl.ds(pl.multiple_of(index * 16, 16), 16)
        d_h = (
            part[me.x, span, :].astype(F32)
            + whole_left[span, :].astype(F32)
            + whole_right[span, :].astype(F32)
        )
        value = y_in[span, :]
        scale = lax.rsqrt(jnp.mean(value * value, axis=-1, keepdims=True) + EPS)
        normed = value * scale
        e_two = d_h * gains_in[1:2, :]
        inner = jnp.mean(e_two * normed, axis=-1, keepdims=True)
        d_y = cot[me.x, span, :].astype(F32) + scale * (e_two - normed * inner)
        dy_out[span, :] = d_y
        d_attn[me.x, span, :] = d_y.astype(BF)
        return carry + jnp.sum(d_h * normed, axis=0, keepdims=True)

    def back_one():
        gain_out[...] = lax.fori_loop(0, 4, back_norm, jnp.zeros((1, D), F32))
        d_ring.start_half(0)

    def back_two():
        gain_out[...] += lax.fori_loop(4, 8, back_norm, jnp.zeros((1, D), F32))
        d_ring.start_half(1)
        keep(dy_out, dy_hbm)
        keep(gain_out, gain_hbm)

    d_ring = Ring(wire, me, "x", rows_of(d_attn))
    plan.add("bn", back_one, lambda: at.late, ("ds.far",), 0)
    d_ring.plan(plan, "dx", ("bn",), 0)
    plan.steps["dx.go"].run = back_two
    plan.add("dk", lambda: keep(d_attn, dattn_out), after=("dx.far",), rank=0)
    plan.go(ORDER_FEED)
    for copy in kept:
        copy.wait()
    wire.drain()


def fold_shapes(lead, count, rows, cut, columns):
    return [
        pltpu.VMEM((*lead, *count, cut, columns), BF),
        pltpu.VMEM((*lead, *count, rows - cut, columns), BF),
        pltpu.VMEM((*lead, *count, rows, columns), BF),
        pltpu.VMEM((*lead, *count, rows, columns), BF),
    ]


def call_feed(h_two, cot, mlp, y_one, gains):
    shape = jax.ShapeDtypeStruct
    bufs = (
        fold_shapes((), (2, 2), SUM_Y, SUM_CUT, 128)
        + fold_shapes((), (4,), UNITS - SUM_Y, SUM_REST, 128)
    ) * 2
    return pl.pallas_call(
        kernel_feed,
        name="feed",
        in_specs=[anywhere()] * 5,
        out_specs=[anywhere()] * 7,
        out_shape=[
            shape((4, 128, D), BF),
            shape((4, 128, D), BF),
            shape((2, 2, 2, SUM_Y, 128), BF),
            shape((2, 4, UNITS - SUM_Y, 128), BF),
            shape((2, 4, 2, UNITS, 128), BF),
            shape((128, D), F32),
            shape((1, D), F32),
        ],
        scratch_shapes=[
            pltpu.VMEM((128, D), F32),
            pltpu.VMEM((8, D), F32),
            pltpu.VMEM((128, D), F32),
            pltpu.VMEM((1, D), F32),
            pltpu.VMEM((3, 2, 4, 2, 2, UNITS, 128), BF),
            pltpu.VMEM((4, 128, D), BF),
            pltpu.VMEM((4, 128, D), BF),
            pltpu.VMEM((3, 256, UNITS), F32),
            pltpu.VMEM((256, UNITS), F32),
            pltpu.VMEM((4, 256, UNITS), F32),
            pltpu.VMEM((2, 4, 128, UNITS), BF),
            pltpu.VMEM((2, 4, 128, UNITS), BF),
            pltpu.VMEM((2, 4, 128, UNITS), BF),
            pltpu.VMEM((3, 2, UNITS, 512), BF),
            pltpu.VMEM((3, 2, UNITS, 512), BF),
            pltpu.VMEM((8, 4, 128, 128), BF),
            pltpu.VMEM((8, 4, 128, 128), BF),
            pltpu.VMEM((4, 128, D), BF),
            pltpu.VMEM((128, D // 2), BF),
            pltpu.VMEM((128, D // 2), BF),
            pltpu.VMEM((128, D), BF),
            pltpu.VMEM((128, D), BF),
            pltpu.VMEM((4, 128, D), BF),
            pltpu.VMEM((4, 128, D), BF),
        ]
        + bufs
        + [
            pltpu.SemaphoreType.DMA((100,)),
            pltpu.SemaphoreType.DMA((100,)),
            pltpu.SemaphoreType.DMA((24,)),
        ],
        compiler_params=pltpu.CompilerParams(
            collective_id=1, has_side_effects=True, vmem_limit_bytes=VMEM_BYTES
        ),
    )(h_two, cot, mlp, y_one, gains)
BACK_GROUPS = (3, 4, 4, 3, 3, 4, 4, 3, 3, 4, 4, 3, 3, 4, 4)
ORDER_BACK = (
    "l2", "ba0", "my.b.go", "mz.b.go", "wy.a.go", "os.go", "mx", "ht", "l3", "wz.a.go", "ba2",
    "mz.b.r", "my.b.r", "bh0", "bh1", "gq0", "qy.a0.go", "gq1", "dl0", "qz.a.go", "qy.a1.go",
    "wy.a.r", "mz.", "qy.a0.l", "my.b.far", "my.k", "qy.a0.r", "os.l", "ax", "wy.a.l", "dn0",
    "mz.b.l", "dn1", "ds.go", "os.r", "as", "wz.a.r", "qy.a1.l", "qy.a1.r", "go", "oy.a.go",
    "dl1", "qz.a.r", "oz.a.go", "wz.a.far", "wz.b.go", "ds.r", "my.", "wy.a.far", "wy.b.go", "az",
    "oz.a.r", "qy.a0.far", "mz.b.far", "mz.k", "qy.a1.far", "qy.b.go", "os.far", "fo", "wy.b.r",
    "oy.a.l", "ds.l", "oy.a.r", "wz.b.l", "wz.b.r", "qz.a.far", "qz.b.go", "ay", "m.", "qy.b.r",
    "oy.a.far", "oy.b.go", "oz.a.far", "oz.b.go", "wz.b.far", "wz.k", "qz.b.r", "qz.b.l",
    "wy.b.far", "wy.k", "oz.b.r", "oz.b.l", "oy.b.r", "ds.far", "bn", "a.", "gk", "qy.b.far",
    "qy.k", "qz.b.far", "qz.k", "oz.b.far", "oz.k", "oy.b.far", "oy.k",
)
O_Y, O_CUT, O_REST = 160, 80, 48
Q_Y, Q_CUT, Q_REST = 80, 48, 16
DN_Y, DN_CUT, DN_REST = 448, 224, 128


class Fold:
    def __init__(self, wire, me, cut, view_one, axes, bufs, view_two, bufs_two):
        def add(target, term):
            add_into(target, [term])

        self.wire, self.me, self.add, self.split = wire, me, add, split_rows(cut)
        self.ones = []
        if view_one is not None:
            views, groups = (view_one, bufs) if isinstance(view_one, tuple) else ((view_one,), (bufs,))
            self.ones = [self.sum(axes[0], view, group) for view, group in zip(views, groups)]
        self.two = self.sum(axes[1], view_two, bufs_two)

    def sum(self, axis, view, bufs):
        if axis == "z":
            return PairSum(self.wire, self.me, view, *bufs, self.add)
        return RingSum(self.wire, self.me, "y", view, *bufs, self.split, self.add)

    def turn(self):
        for one in self.ones:
            add_into(one.part(one.at, None), list(one.whole))
        self.two.start()

    def close(self, result, keep):
        add_into(self.two.part(self.two.at, None), list(self.two.whole), result)
        keep()

    def plan(self, plan, name, waits, after, rank, result, keep):
        if not self.ones:
            self.two.plan(plan, name + ".b", after, rank)
            plan.steps[name + ".b.go"].waits = waits
        else:
            done = ()
            for index, one in enumerate(self.ones):
                step = name + ".a" + ("%d" % index if len(self.ones) > 1 else "")
                one.plan(plan, step, after[index : index + 1] if len(self.ones) > 1 else after, rank)
                plan.steps[step + ".go"].waits = waits
                done += (step + ".far",)
            self.two.plan(plan, name + ".b", done, rank)
            plan.steps[name + ".b.go"].run = self.turn
        plan.add(name + ".k", lambda: self.close(result, keep), after=(name + ".b.far",), rank=rank + 0.5)


def crossed_view(ref, me, lead, axis, row, rows, cut):
    head = (ALL,) * lead

    def view(slot, part):
        start, size = row, rows
        if part == 0:
            size = cut
        if part == 1:
            start, size = row + cut, rows - cut
        if axis == "z":
            where = (lax.rem(slot, 2), me.y, lax.div(slot, 2))
        else:
            where = (me.zl, slot, me.zh)
        return ref.at[head + where + (pl.ds(start, size), ALL)]

    return view


def held_view(ref, lead, axis, rows, cut):
    head = (ALL,) * lead

    def view(slot, part):
        start, size = 0, rows
        if part == 0:
            size = cut
        if part == 1:
            start, size = cut, rows - cut
        where = (lax.rem(slot, 2), lax.div(slot, 2)) if axis == "z" else (slot,)
        return ref.at[head + where + (pl.ds(start, size), ALL)]

    return view


def kernel_back(
    start_in, tokens_hbm, dattn_hbm, part_hbm, qkv_hbm, wo_hbm, query_hbm, keys_hbm, values_hbm,
    heads_hbm, lse_hbm, turned_hbm, tables_hbm, gains_hbm, y_hbm, dy_hbm, gain_hbm, fold_y_hbm,
    fold_z_hbm, down_hbm,
    result_hbm, grad_tokens_hbm, g_qkv_hbm, g_o_hbm, g_mlp_hbm, g_gains_hbm,
    query_in, keys_in, values_in, lse_in, gains_in, y_in, dy_in, gain_in,
    result_out, tokens_out, g_qkv_out, g_o_out, g_mlp_out, gains_out,
    w_qkv, w_o, d_attn, out_part, tables, bias, tok, turned, d_heads, d_query, d_keys, d_values,
    d_query_far, d_keys_far, d_values_far, sum_keys, sum_values, heads_t, heads_t_far, attn_far,
    d_h, far_one, side_left, side_right, last_z,
    near_left, near_right, whole_left, whole_right,
    out_near_left, out_near_right, out_whole_left, out_whole_right,
    fold_y, fold_z, g_down, gain_x, gain_z, gain_c, along_s, along_a, along_b, along_c, gain_t, along_t,
    *rest,
):
    bufs, (send, recv, local) = list(rest[:-3]), rest[-3:]
    groups = []
    for size in BACK_GROUPS:
        groups.append(tuple(bufs[:size]))
        bufs = bufs[size:]
    me = place()
    wire = Wire(send, recv, local)
    loads = {}

    def load(*items):
        for name, source, target in items:
            loads[name] = wire.move(source, target)

    def load_second():
        load(
            ("fold_y", fold_y_hbm, fold_y),
            ("fold_z", fold_z_hbm, fold_z),
            ("gain", gain_hbm, gain_in),
            ("heads", heads_hbm, heads_t),
            ("down", down_hbm, g_down),
        )

    def load_third():
        load(
            ("qkv", qkv_hbm, w_qkv),
            ("turned", turned_hbm, turned),
            ("y", y_hbm, y_in),
            ("dy", dy_hbm, dy_in),
            ("tok", tokens_hbm, tok),
            ("gains", gains_hbm, gains_in),
        )

    load(
        ("attn", dattn_hbm, d_attn),
        ("o", wo_hbm, w_o),
        ("query", query_hbm, query_in),
        ("keys", keys_hbm, keys_in),
        ("values", values_hbm, values_in),
        ("lse", lse_hbm, lse_in),
        ("tables", tables_hbm.at[me.zl], tables),
        ("part", part_hbm, out_part),
    )
    kept = []

    def keep(source, target):
        kept.append(wire.move(source, target))

    def back_heads(zl, carry):
        weight = jnp.concatenate(
            [w_o[zl, y, zh, c] for y in range(4) for zh in range(2) for c in range(2)], axis=1
        )
        result = dot_nt(d_attn[...].reshape(512, D), weight).astype(BF)
        d_heads[zl * 2] = result[:, 0:HD]
        d_heads[zl * 2 + 1] = result[:, HD : 2 * HD]
        return carry

    def early():
        fill_bias(bias, me, start_in[0])
        loads["attn"].wait()
        loads["o"].wait()
        lax.fori_loop(0, 2, back_heads, 0)

    greet(me, True, (), early)
    plan = Plan()
    at = types.SimpleNamespace()
    one, far, three = rem4(me.x + 1), rem4(me.x + 2), rem4(me.x + 3)
    right, left = near(me, "x", 1), near(me, "x", 3)

    def add(target, term):
        add_into(target, [term])

    def loaded(*names):
        return lambda: [loads[name] for name in names]

    def share_attn():
        at.attn = [
            wire.put(
                d_attn.at[:, :, pl.ds(pl.multiple_of((block * 2 + 1 - me.core) * 128, 128), 128)],
                attn_far.at[block],
                sibling(me),
            )
            for block in range(8)
        ]

    def share_heads():
        at.heads = wire.put(heads_t, heads_t_far, sibling(me))

    plan.add("l2", load_second, loaded("attn", "o"), rank=0)
    plan.add("l3", load_third, loaded("query", "keys", "values", "lse", "tables"), ("l2",), 0)
    plan.add("as", share_attn, loaded("attn"), rank=1.5)
    plan.add("ht", share_heads, loaded("heads"), ("l2",), 1.5)

    total = RingSum(
        wire, me, "x", columns_of(out_part), out_near_left, out_near_right, out_whole_left,
        out_whole_right, split_columns, add,
    )
    total.plan(plan, "os", (), 1)
    plan.steps["os.go"].waits = loaded("part")

    def finish_out(index, carry):
        span = pl.ds(pl.multiple_of(index * 16, 16), 16)
        result_out[span, :] = (
            y_in[span, :]
            + (
                out_part[me.x, span, :].astype(F32)
                + out_whole_left[span, :].astype(F32)
                + out_whole_right[span, :].astype(F32)
            )
        ).astype(BF)
        return carry

    def finish_result():
        lax.fori_loop(0, 8, finish_out, 0)
        keep(result_out, result_hbm)

    plan.add("fo", finish_result, loaded("y"), ("os.far", "l3"), 6)

    def back_attend(head, carry):
        for half, pairs in ((1, 4), (0, 3)):
            span = pairs * 256
            rows = slice(half * 256, half * 256 + 256)
            key = keys_in[head, 0:pairs].reshape(span, HD)
            value = values_in[head, 0:pairs].reshape(span, HD)
            query, d_head = query_in[head, rows, :], d_heads[head, rows, :]
            scores = dot_nt(key, query) * SCALE + bias[0:pairs, :, :, rows].reshape(span, 256)
            probs = jnp.exp(scores - lse_in[head, :, rows])
            d_probs = dot_nt(value, d_head)
            delta = jnp.sum(probs * d_probs, axis=0, keepdims=True)
            d_scores = (probs * (d_probs - delta) * SCALE).astype(BF)
            d_key = dot_nn(d_scores, query)
            d_value = dot_nn(probs.astype(BF), d_head)
            if half == 1:
                sum_keys[...] = d_key
                sum_values[...] = d_value
            else:
                sum_keys[0:span, :] += d_key
                sum_values[0:span, :] += d_value
            raw = dot_tn(key, d_scores).T
            cosine = tables[0, 2 * half : 2 * half + 2, 0].reshape(256, HD)
            sine = tables[1, 2 * half : 2 * half + 2, 0].reshape(256, HD)
            column = pl.ds(pl.multiple_of(head * HD, HD), HD)
            d_query[rows, column] = turn(raw, cosine, -sine).astype(BF)
        cosine, sine = tables[0].reshape(SEQ, HD), tables[1].reshape(SEQ, HD)
        d_keys[:, column] = turn(sum_keys[...], cosine, -sine).astype(BF)
        d_values[:, column] = sum_values[...].astype(BF)
        return carry

    def attend_rest():
        lax.fori_loop(2, 4, back_attend, 0)
        at.grads = [
            wire.put(d_query, d_query_far, sibling(me)),
            wire.put(d_keys, d_keys_far, sibling(me)),
            wire.put(d_values, d_values_far, sibling(me)),
        ]

    plan.add(
        "ba0", lambda: lax.fori_loop(0, 2, back_attend, 0),
        loaded("query", "keys", "values", "lse", "tables"), (), 2,
    )
    plan.add("ba2", attend_rest, after=("ba0",), rank=2)

    def back_h(block, carry):
        y, zh = lax.div(block, 2), lax.rem(block, 2)

        def weight(which):
            return jnp.concatenate(
                [w_qkv[which, 0, y, zh].reshape(256, 256), w_qkv[which, 1, y, zh].reshape(256, 256)],
                axis=1,
            )

        column = pl.ds(pl.multiple_of(block * 256, 256), 256)
        both = dot_nt(d_keys[...], weight(1)) + dot_nt(d_values[...], weight(2))
        both = both.reshape(4, 2, 128, 256)
        own = dot_nt(d_query[...], weight(0)).reshape(4, 128, 256) + both[:, 0]
        d_h[:, 0, :, column] = own.astype(BF)
        d_h[:, 1, :, column] = both[:, 1].astype(BF)
        return carry

    own = RingSum(
        wire, me, "x",
        lambda slot, half: d_h.at[slot, 0] if half is None else d_h.at[slot, 0, :, pl.ds(half * 1024, 1024)],
        near_left, near_right, whole_left, whole_right, split_columns, add,
    )
    at.far_z, at.sides, at.last = {}, {}, {}

    def cut(ref, half):
        return ref.at[:, pl.ds(half * 1024, 1024)]

    def back_half(half):
        def run():
            lax.fori_loop(half * 4, half * 4 + 4, back_h, 0)
            at.far_z[half] = wire.put(cut(d_h.at[far, 1], half), cut(far_one, half), partner(me))
            at.sides[half] = [
                wire.put(cut(d_h.at[one, 1], half), cut(side_left, half), right),
                wire.put(cut(d_h.at[three, 1], half), cut(side_right, half), left),
            ]
            own.start_whole(half)

        return run

    def near_half(half):
        def run():
            add_into(cut(d_h.at[far, 0], half), [cut(far_one, half)])
            own.start_near(half)

        return run

    def last_half(half):
        def run():
            add_into(cut(d_h.at[me.x, 1], half), [cut(side_left, half), cut(side_right, half)])
            at.last[half] = wire.put(cut(d_h.at[me.x, 1], half), cut(last_z, half), partner(me))

        return run

    plan.add("bh0", back_half(0), loaded("qkv"), ("ba2", "l3"), 2)
    plan.add("bh1", back_half(1), after=("bh0",), rank=2)
    for half in range(2):
        name = "%d" % half
        plan.add("dn" + name, near_half(half), lambda half=half: [at.far_z[half]], ("bh" + name,), 0)
        plan.add("dl" + name, last_half(half), lambda half=half: at.sides[half], ("bh" + name,), 0.5)
    plan.add("ds.go", lambda: None, after=("dn0", "dn1"), rank=0)
    own.plan(plan, "ds", (), 0, go=False)

    def grad_o(index, carry):
        zl, y = lax.div(index, 4), lax.rem(index, 4)
        mine = jnp.concatenate(
            [
                d_attn[:, :, pl.ds(pl.multiple_of(((y * 2 + zh) * 2 + me.core) * 128, 128), 128)]
                .reshape(512, 128)
                for zh in range(2)
            ],
            axis=1,
        )
        other = jnp.concatenate(
            [attn_far[y * 2 + zh].reshape(512, 128) for zh in range(2)], axis=1
        )
        rows = pl.ds(pl.multiple_of(zl * 256, 256), 256)
        result = (dot_nn(heads_t[rows, :], mine) + dot_nn(heads_t_far[rows, :], other)).astype(BF)
        w_o[zl, y, 0, 0] = result[:, 0:128]
        w_o[zl, y, 1, 0] = result[:, 128:256]
        return carry

    plan.add("go", lambda: lax.fori_loop(0, 8, grad_o, 0), lambda: [at.heads, *at.attn], ("as", "ht"), 3)

    def blocks(which, pair):
        return turned[which, pl.ds(pair * 4, 4)].reshape(512, SEQ)

    def own_rows(value):
        return jnp.concatenate([value[:, i * 256 : i * 256 + 128] for i in range(4)], axis=1)

    def grad_qkv(index, carry):
        zl, pair = lax.div(index, 2), lax.rem(index, 2)
        column = pl.ds(pl.multiple_of(zl * 256, 256), 256)
        mine, other = blocks(0, pair), blocks(1, pair)
        query_grad = dot_nn(own_rows(mine), d_query[:, column])
        query_grad = query_grad + dot_nn(own_rows(other), d_query_far[:, column])
        key_grad = dot_nn(mine, d_keys[:, column]) + dot_nn(other, d_keys_far[:, column])
        value_grad = dot_nn(mine, d_values[:, column]) + dot_nn(other, d_values_far[:, column])
        along = jnp.where(zl == 0, 0.0, along_s[pair])
        for which, result in enumerate((query_grad, key_grad, value_grad)):
            weight = w_qkv[which, zl, pl.ds(pair * 2, 2), :, me.core].reshape(512, 256)
            product = weight.astype(F32) * result
            along = along + product[:, 0:128] + product[:, 128:256]
            w_qkv[which, zl, pl.ds(pair * 2, 2), :, 0] = result.astype(BF).reshape(2, 2, 128, 256)
        along_s[pair] = along
        return carry

    plan.add(
        "gq0", lambda: lax.fori_loop(0, 2, grad_qkv, 0),
        lambda: [loads["turned"], *at.grads], ("bh1",), 3,
    )
    plan.add("gq1", lambda: lax.fori_loop(2, 4, grad_qkv, 0), after=("gq0",), rank=3)

    g_qkv, g_o = w_qkv.at[:, :, :, :, 0], w_o.at[:, :, :, 0]
    rest = UNITS - SUM_Y

    def low_view(zl):
        def view(slot, part):
            span = {None: (0, Q_Y), 0: (0, Q_CUT), 1: (Q_CUT, Q_Y - Q_CUT)}[part]
            return g_qkv.at[:, zl, slot, :, pl.ds(*span), :]

        return view

    for name, fold, waits, after, rank, result, target, where in (
        ("my", Fold(wire, me, 0, None, ("y", "z"), None, held_view(fold_y, 1, "z", SUM_Y, 0), groups[0]),
         loaded("fold_y"), ("l2",), 1.2, g_mlp_out, g_mlp_hbm, (pl.ds(0, 2), pl.ds(0, SUM_Y), ALL)),
        ("mz", Fold(wire, me, 144, None, ("z", "y"), None, held_view(fold_z, 1, "y", rest, 144), groups[1]),
         loaded("fold_z"), ("l2",), 1.2, g_mlp_out, g_mlp_hbm, (pl.ds(0, 2), pl.ds(SUM_Y, UNITS - SUM_Y), ALL)),
        ("oy", Fold(wire, me, O_CUT, fold_view(g_o, me, 0, "y", 0, O_Y, O_CUT), ("y", "z"), groups[2],
                    crossed_view(g_o, me, 0, "z", 0, O_Y, 0), groups[3]),
         tuple, ("go",), 1.4, g_o_out, g_o_hbm, (pl.ds(0, O_Y), ALL)),
        ("oz", Fold(wire, me, O_REST, fold_view(g_o, me, 0, "z", O_Y, 256 - O_Y, 0), ("z", "y"), groups[4],
                    crossed_view(g_o, me, 0, "y", O_Y, 256 - O_Y, O_REST), groups[5]),
         tuple, ("go",), 1.4, g_o_out, g_o_hbm, (pl.ds(O_Y, 256 - O_Y), ALL)),
        ("qy", Fold(wire, me, Q_CUT, (low_view(0), low_view(1)), ("y", "z"), (groups[6], groups[14]),
                    crossed_view(g_qkv, me, 1, "z", 0, Q_Y, 0), groups[7]),
         tuple, ("gq0", "gq1"), 1, g_qkv_out, g_qkv_hbm, (ALL, pl.ds(0, Q_Y), ALL)),
        ("qz", Fold(wire, me, Q_REST, fold_view(g_qkv, me, 1, "z", Q_Y, 128 - Q_Y, 0), ("z", "y"),
                    groups[8], crossed_view(g_qkv, me, 1, "y", Q_Y, 128 - Q_Y, Q_REST), groups[9]),
         tuple, ("gq1",), 1, g_qkv_out, g_qkv_hbm, (ALL, pl.ds(Q_Y, 128 - Q_Y), ALL)),
        ("wy", Fold(wire, me, DN_CUT, fold_view(g_down, me, 0, "y", 0, DN_Y, DN_CUT), ("y", "z"),
                    groups[10], crossed_view(g_down, me, 0, "z", 0, DN_Y, 0), groups[11]),
         loaded("down"), ("l2",), 1.3, g_mlp_out, g_mlp_hbm, (2, pl.ds(0, DN_Y), ALL)),
        ("wz", Fold(wire, me, DN_REST, fold_view(g_down, me, 0, "z", DN_Y, UNITS - DN_Y, 0), ("z", "y"),
                    groups[12], crossed_view(g_down, me, 0, "y", DN_Y, UNITS - DN_Y, DN_REST), groups[13]),
         loaded("down"), ("l2",), 1.3, g_mlp_out, g_mlp_hbm, (2, pl.ds(DN_Y, UNITS - DN_Y), ALL)),
    ):
        fold.plan(
            plan, name, waits, after, rank, result.at[where],
            lambda result=result, target=target, where=where: keep(result.at[where], target.at[where]),
        )

    def back_norm(index, carry):
        span = pl.ds(pl.multiple_of(index * 16, 16), 16)
        d_h_one = (
            d_h[me.x, 0, span, :].astype(F32)
            + whole_left[span, :].astype(F32)
            + whole_right[span, :].astype(F32)
            + last_z[span, :].astype(F32)
        )
        value = tok[span, :].astype(F32)
        scale = lax.rsqrt(jnp.mean(value * value, axis=-1, keepdims=True) + EPS)
        normed = value * scale
        e_one = d_h_one * gains_in[0:1, :]
        inner = jnp.mean(e_one * normed, axis=-1, keepdims=True)
        tokens_out[span, :] = (dy_in[span, :] + scale * (e_one - normed * inner)).astype(BF)
        return carry

    def feed_x():
        for block in range(16):
            gain_x[me.x, block : block + 1, :] = gain_in[0:1, block * 128 : block * 128 + 128]
        at.feed = Meet(wire, me, "x", gain_x).copies

    def feed_z():
        gain_z[me.z] = gain_x[0] + gain_x[1] + gain_x[2] + gain_x[3]
        at.feed = Meet(wire, me, "z", gain_z).copies

    def feed_y():
        gain_c[me.core, me.y] = gain_z[0] + gain_z[1] + gain_z[2] + gain_z[3]
        at.feed = MeetCores(wire, me, gain_c).copies

    def feed_all():
        total = gain_c[0, 0]
        for core, y in ((0, 1), (0, 2), (0, 3), (1, 0), (1, 1), (1, 2), (1, 3)):
            total = total + gain_c[core, y]
        gain_t[...] = total
        row = (me.y * 2 + me.zh) * 2 + me.core
        gains_out[1:2, :] = gain_t[pl.ds(row, 1), :]

    plan.add("mx", feed_x, loaded("gain"), ("l2",), 1)
    plan.add("mz.", feed_z, lambda: at.feed, ("mx",), 1)
    plan.add("my.", feed_y, lambda: at.feed, ("mz.",), 1)
    plan.add("m.", feed_all, lambda: at.feed, ("my.",), 1)

    def along_x():
        ones = jnp.ones((8, 128), F32)
        for pair in range(2):
            line = lax.dot_general(
                ones, along_s[pair], (((1,), (1,)), ((), ())), precision=lax.Precision.HIGHEST,
                preferred_element_type=F32,
            )
            for k in range(4):
                along_a[me.x, pair * 4 + k : pair * 4 + k + 1, :] = line[0:1, k * 128 : k * 128 + 128]
        at.along = Meet(wire, me, "x", along_a).copies

    def along_z():
        along_b[me.z] = along_a[0] + along_a[1] + along_a[2] + along_a[3]
        at.along = Meet(wire, me, "z", along_b).copies

    def along_y():
        along_c[me.y] = along_b[0] + along_b[1] + along_b[2] + along_b[3]
        at.along = Meet(wire, me, "y", along_c).copies

    def along_all():
        along_t[...] = along_c[0] + along_c[1] + along_c[2] + along_c[3]
        row = me.y * 2 + me.zh
        column = pl.ds(pl.multiple_of((row * 2 + me.core) * 128, 128), 128)
        gains_out[0:1, :] = along_t[pl.ds(row, 1), :] / gains_in[0:1, column]

    plan.add("ax", along_x, after=("gq1",), rank=1)
    plan.add("az", along_z, lambda: at.along, ("ax",), 1)
    plan.add("ay", along_y, lambda: at.along, ("az",), 1)
    plan.add("a.", along_all, lambda: [*loaded("gains")(), *at.along], ("ay",), 1)
    plan.add("gk", lambda: keep(gains_out, g_gains_hbm), after=("a.", "m."), rank=2)

    def back_all():
        lax.fori_loop(0, 8, back_norm, 0)
        keep(tokens_out, grad_tokens_hbm)

    plan.add(
        "bn", back_all,
        lambda: [*loaded("tok", "dy", "gains")(), at.last[0], at.last[1]], ("ds.far", "dl0", "dl1"), 0,
    )
    plan.go(ORDER_BACK)
    for copy in kept:
        copy.wait()
    wire.drain()


def call_back(starts, tokens, d_attn, out_part, qkv, w_out, query, keys, values, heads, lse, turned,
              tables, gains, y_one, d_y, gain_two, fold_y, fold_z, down):
    shape = jax.ShapeDtypeStruct

    def three(*dims):
        return [pltpu.VMEM(dims, BF)] * 3

    rest = UNITS - SUM_Y
    bufs = (
        three(2, SUM_Y, 128)
        + fold_shapes((2,), (), rest, 144, 128)
        + fold_shapes((), (2, 2), O_Y, O_CUT, 128)
        + three(O_Y, 128)
        + three(4, 256 - O_Y, 128)
        + fold_shapes((), (), 256 - O_Y, O_REST, 128)
        + fold_shapes((3,), (2,), Q_Y, Q_CUT, 256)
        + three(3, Q_Y, 256)
        + three(3, 4, 128 - Q_Y, 256)
        + fold_shapes((3,), (), 128 - Q_Y, Q_REST, 256)
        + fold_shapes((), (2, 2), DN_Y, DN_CUT, 128)
        + three(DN_Y, 128)
        + three(4, UNITS - DN_Y, 128)
        + fold_shapes((), (), UNITS - DN_Y, DN_REST, 128)
        + fold_shapes((3,), (2,), Q_Y, Q_CUT, 256)
    )
    return pl.pallas_call(
        kernel_back,
        name="back",
        in_specs=[pl.BlockSpec(memory_space=pltpu.SMEM)] + [anywhere()] * 19,
        out_specs=[anywhere()] * 6,
        out_shape=[
            shape((128, D), BF),
            shape((128, D), BF),
            shape((3, 128, 256), F32),
            shape((256, 128), F32),
            shape((3, UNITS, 128), F32),
            shape((2, 128), F32),
        ],
        scratch_shapes=[
            pltpu.VMEM((4, 512, HD), BF),
            pltpu.VMEM((4, 4, 2, 128, HD), BF),
            pltpu.VMEM((4, 4, 2, 128, HD), BF),
            pltpu.VMEM((4, 1, 512), F32),
            pltpu.VMEM((8, D), F32),
            pltpu.VMEM((128, D), F32),
            pltpu.VMEM((128, D), F32),
            pltpu.VMEM((1, D), F32),
            pltpu.VMEM((128, D), BF),
            pltpu.VMEM((128, D), BF),
            pltpu.VMEM((3, 128, 256), F32),
            pltpu.VMEM((256, 128), F32),
            pltpu.VMEM((3, UNITS, 128), F32),
            pltpu.VMEM((2, 128), F32),
            pltpu.VMEM((3, 2, 4, 2, 2, 128, 256), BF),
            pltpu.VMEM((2, 4, 2, 2, 256, 128), BF),
            pltpu.VMEM((4, 128, D), BF),
            pltpu.VMEM((4, 128, D), BF),
            pltpu.VMEM((2, 4, 2, 128, HD), F32),
            pltpu.VMEM((4, 2, 128, 512), F32),
            pltpu.VMEM((128, D), BF),
            pltpu.VMEM((2, 8, 128, SEQ), BF),
            pltpu.VMEM((4, 512, HD), BF),
            pltpu.VMEM((512, 512), BF),
            pltpu.VMEM((SEQ, 512), BF),
            pltpu.VMEM((SEQ, 512), BF),
            pltpu.VMEM((512, 512), BF),
            pltpu.VMEM((SEQ, 512), BF),
            pltpu.VMEM((SEQ, 512), BF),
            pltpu.VMEM((SEQ, HD), F32),
            pltpu.VMEM((SEQ, HD), F32),
            pltpu.VMEM((512, 512), BF),
            pltpu.VMEM((512, 512), BF),
            pltpu.VMEM((8, 4, 128, 128), BF),
            pltpu.VMEM((4, 2, 128, D), BF),
        ]
        + [pltpu.VMEM((128, D), BF)] * 4
        + [
            pltpu.VMEM((128, D // 2), BF),
            pltpu.VMEM((128, D // 2), BF),
            pltpu.VMEM((128, D), BF),
            pltpu.VMEM((128, D), BF),
        ]
        * 2
        + [
            pltpu.VMEM((2, 2, 2, SUM_Y, 128), BF),
            pltpu.VMEM((2, 4, UNITS - SUM_Y, 128), BF),
            pltpu.VMEM((2, 4, 2, UNITS, 128), BF),
            pltpu.VMEM((4, 16, 128), F32),
            pltpu.VMEM((4, 16, 128), F32),
            pltpu.VMEM((2, 4, 16, 128), F32),
            pltpu.VMEM((2, 512, 128), F32),
            pltpu.VMEM((4, 8, 128), F32),
            pltpu.VMEM((4, 8, 128), F32),
            pltpu.VMEM((4, 8, 128), F32),
            pltpu.VMEM((16, 128), F32),
            pltpu.VMEM((8, 128), F32),
        ]
        + bufs
        + [
            pltpu.SemaphoreType.DMA((140,)),
            pltpu.SemaphoreType.DMA((140,)),
            pltpu.SemaphoreType.DMA((40,)),
        ],
        compiler_params=pltpu.CompilerParams(
            collective_id=2, has_side_effects=True, vmem_limit_bytes=VMEM_BYTES
        ),
    )(starts, tokens, d_attn, out_part, qkv, w_out, query, keys, values, heads, lse, turned,
      tables, gains, y_one, d_y, gain_two, fold_y, fold_z, down)


def kernel_settle(*refs):
    arrays, results, held, (row_s, send, recv) = refs[:6], refs[6:17], refs[17:23], refs[23:]
    tp = lax.axis_index("tensor")
    copies = [
        pltpu.make_async_copy(source, target, recv.at[index])
        for index, (source, target) in enumerate(zip(arrays, held))
    ]
    for copy in copies:
        copy.start()
    outs = []

    def give(source, index):
        copy = pltpu.make_async_copy(source, results[index], send.at[index])
        copy.start()
        outs.append(copy)

    copies[5].wait()
    for index in range(2):
        row = held[5][index : index + 1, :]
        row_s[index] = pltpu.roll(row, lax.rem(128 - tp * 16, 128), 1)[:, 0:16]
    for index in range(2):
        give(row_s.at[index], 9 + index)
    for index in range(2):
        copies[index].wait()
        give(held[index], index)
    copies[4].wait()
    for index in range(3):
        give(held[4].at[index], 6 + index)
    copies[2].wait()
    for index in range(3):
        give(held[2].at[index], 2 + index)
    copies[3].wait()
    give(held[3], 5)
    for copy in outs:
        copy.wait()


def call_settle(*arrays):
    shape = jax.ShapeDtypeStruct
    return pl.pallas_call(
        kernel_settle,
        name="settle",
        in_specs=[anywhere()] * 6,
        out_specs=[anywhere()] * 11,
        out_shape=[shape((128, D), BF)] * 2
        + [shape((128, 256), F32)] * 3
        + [shape((256, 128), F32)]
        + [shape((UNITS, 128), F32)] * 3
        + [shape((1, 16), F32)] * 2,
        scratch_shapes=[
            pltpu.VMEM((128, D), BF),
            pltpu.VMEM((128, D), BF),
            pltpu.VMEM((3, 128, 256), F32),
            pltpu.VMEM((256, 128), F32),
            pltpu.VMEM((3, UNITS, 128), F32),
            pltpu.VMEM((2, 128), F32),
            pltpu.VMEM((2, 1, 16), F32),
            pltpu.SemaphoreType.DMA((11,)),
            pltpu.SemaphoreType.DMA((6,)),
        ],
        compiler_params=pltpu.CompilerParams(vmem_limit_bytes=VMEM_BYTES),
    )(*arrays)


def on_device(tables, tokens, starts, w_query, w_key, w_value, w_out, w_gate, w_up, w_down,
              gain_attn, gain_mlp, cotangent):
    weights = (w_query, w_key, w_value, w_out, w_gate.T, w_up.T, w_down)
    (qkv, w_o, mlp, cot, turned, query, keys, values, heads, h_two, lse, y_one, gains) = call_attend(
        tokens, cotangent, starts, weights, gain_attn.reshape(1, 16), gain_mlp.reshape(1, 16), tables
    )
    out_part, d_attn, fold_y, fold_z, down, d_y, gain_two = call_feed(h_two, cot, mlp, y_one, gains)
    sums = call_back(
        starts, tokens, d_attn, out_part, qkv, w_o, query, keys, values, heads, lse, turned,
        tables, gains, y_one, d_y, gain_two, fold_y, fold_z, down,
    )
    result, grad_tokens, query, key, value, out, gate, up, down, attn, feed = call_settle(*sums)
    return (
        result, grad_tokens, query, key, value, out, gate.T, up.T, down,
        attn.reshape(16), feed.reshape(16),
    )


def solution(mesh):
    both = ("dp", "tensor")
    rows, wide, tall = P(both, None), P("dp", "tensor"), P("tensor", "dp")
    in_specs = (
        rows, P("dp"), wide, wide, wide, tall, wide, wide, tall, P(both), P(both), rows,
    )
    out_specs = (
        rows, rows, wide, wide, wide, tall, wide, wide, tall, P(both), P(both),
    )
    return jax.shard_map(
        functools.partial(on_device, rope_tables()), mesh=mesh, in_specs=in_specs,
        out_specs=out_specs, check_vma=False,
    )
```

```python
import functools
import math
import types

import jax
import jax.numpy as jnp
import numpy as np
from jax import lax
from jax.experimental import pallas as pl
from jax.experimental.pallas import tpu as pltpu
from jax.sharding import PartitionSpec as P

HD = 128
PIECE = 256
EPS = 1e-05
NEG = -1e30
SCALE = HD ** (-0.5)
D = 2048
SEQ = 1024
UNITS = 688
BF = jnp.bfloat16
F32 = jnp.float32
MESH = pl.DeviceIdType.MESH
VMEM_BYTES = 60 * 1024 * 1024
ALL = slice(None)


def dot_nn(left, right):
    return jnp.dot(left, right, preferred_element_type=F32)


def dot_nt(left, right):
    return lax.dot_general(left, right, (((1,), (1,)), ((), ())), preferred_element_type=F32)


def dot_tn(left, right):
    return lax.dot_general(left, right, (((0,), (0,)), ((), ())), preferred_element_type=F32)


def rem4(value):
    return lax.rem(value, 4)


def place():
    dp = lax.axis_index("dp")
    tp = lax.axis_index("tensor")
    zh = lax.rem(lax.div(dp, 2), 2)
    zl = lax.rem(tp, 2)
    return types.SimpleNamespace(
        y=lax.div(dp, 4), zh=zh, zl=zl, z=zh * 2 + zl, x=lax.div(tp, 2), core=lax.rem(dp, 2)
    )


def device(me, **moved):
    at = types.SimpleNamespace(**{**vars(me), **moved})
    zh, zl = lax.div(at.z, 2), lax.rem(at.z, 2)
    return (at.y * 4 + zh * 2 + at.core, at.x * 2 + zl)


def near(me, axis, step):
    return device(me, **{axis: rem4(getattr(me, axis) + step)})


def sibling(me):
    return device(me, core=1 - me.core)


def partner(me):
    return device(me, z=me.zh * 2 + 1 - me.zl)


def across(me):
    return device(me, z=rem4(me.z + 3 + 2 * me.zl))


def greet(me, wide, meanwhile=(), early=None):
    others = [near(me, axis, step) for axis in ("x", "y", "z") for step in (1, 3)] + [sibling(me)]
    if wide:
        others += [near(me, axis, 2) for axis in ("x", "y", "z")]
        others += [crossed(me, step) for step in (1, 2, 3)]
    barrier = pltpu.get_barrier_semaphore()
    for other in others:
        pl.semaphore_signal(barrier, inc=1, device_id=other, device_id_type=MESH)
    for copy in meanwhile:
        copy.wait()
    if early is not None:
        early()
    pl.semaphore_wait(barrier, len(others))


def crossed(me, step):
    return device(me, y=rem4(me.y + step), core=1 - me.core)


class Plan:
    def __init__(self):
        self.steps = {}

    def add(self, name, run, waits=tuple, after=(), rank=5):
        self.steps[name] = types.SimpleNamespace(run=run, waits=waits, after=after, rank=rank)

    def go(self, order):
        assert sorted(order) == sorted(self.steps)
        for name in order:
            step = self.steps[name]
            for copy in step.waits():
                copy.wait_recv()
            step.run()


class Once:
    def __init__(self, copy, remote):
        self.copy, self.remote = copy, remote
        self.received = self.left = False

    def wait_recv(self):
        if not self.received:
            self.received = True
            if self.remote:
                self.copy.wait_recv()
            else:
                self.copy.wait()

    wait = wait_recv

    def wait_send(self):
        if not self.left:
            self.left = True
            self.copy.wait_send()


class Wire:
    def __init__(self, send, recv, local):
        self.send, self.recv, self.local = send, recv, local
        self.used, self.used_local = 0, 0
        self.sent = []

    def put(self, source, target, to):
        index = self.used
        self.used += 1
        assert index < self.send.shape[0]
        copy = pltpu.make_async_remote_copy(
            src_ref=source,
            dst_ref=target,
            send_sem=self.send.at[index],
            recv_sem=self.recv.at[index],
            device_id=to,
            device_id_type=MESH,
        )
        copy.start()
        copy = Once(copy, True)
        self.sent.append(copy)
        return copy

    def move(self, source, target):
        index = self.used_local
        self.used_local += 1
        assert index < self.local.shape[0]
        copy = pltpu.make_async_copy(source, target, self.local.at[index])
        copy.start()
        return Once(copy, False)

    def drain(self):
        for copy in self.sent:
            copy.wait_send()
        self.sent = []


class Ring:
    def __init__(self, wire, me, axis, view):
        self.wire, self.view = wire, view
        self.at = getattr(me, axis)
        self.right, self.left = near(me, axis, 1), near(me, axis, 3)

    def put(self, slot, part, to):
        piece = self.view(slot, part)
        return self.wire.put(piece, piece, to)

    def start(self):
        self.right_one = self.put(self.at, 0, self.right)
        self.left_one = self.put(self.at, 1, self.left)
        self.right_two = self.put(self.at, 1, self.right)
        self.left_two = self.put(self.at, 0, self.left)

    def start_half(self, half):
        if half == 0:
            self.right_one = self.put(self.at, 0, self.right)
            self.left_two = self.put(self.at, 0, self.left)
        else:
            self.left_one = self.put(self.at, 1, self.left)
            self.right_two = self.put(self.at, 1, self.right)

    def plan(self, plan, name, after, rank):
        plan.add(name + ".go", self.start, after=after, rank=rank)
        plan.add(name + ".r", self.relay_right, lambda: [self.right_one], (name + ".go",), rank)
        plan.add(name + ".l", self.relay_left, lambda: [self.left_one], (name + ".go",), rank)
        plan.add(
            name + ".near", lambda: None, lambda: [self.right_two, self.left_two],
            (name + ".r", name + ".l"), rank,
        )
        plan.add(
            name + ".far", lambda: None, lambda: [self.far_right, self.far_left], (name + ".near",), rank
        )

    def relay_right(self):
        self.far_right = self.put(rem4(self.at + 3), 0, self.right)

    def relay_left(self):
        self.far_left = self.put(rem4(self.at + 1), 1, self.left)

    def copies(self):
        return [
            self.right_one, self.left_one, self.right_two, self.left_two, self.far_right, self.far_left
        ]

    def closed(self):
        return rem4(self.at + 3), rem4(self.at + 1)


class Direct:
    def __init__(self, wire, me, view):
        self.wire, self.view, self.me, self.at = wire, view, me, me.z

    def start(self):
        piece = self.view(self.at, None)
        others = (partner(self.me), across(self.me), near(self.me, "z", 2))
        self.copies = [self.wire.put(piece, piece, other) for other in others]

    def plan(self, plan, name, after, rank):
        plan.add(name + ".go", self.start, after=after, rank=rank)
        plan.add(name + ".far", lambda: None, lambda: self.copies, (name + ".go",), rank)


class PairRing:
    def __init__(self, wire, me, view):
        self.wire, self.view, self.me = wire, view, me
        self.at = me.z
        self.mate, self.beyond = me.zh * 2 + 1 - me.zl, rem4(me.z + 3 + 2 * me.zl)

    def put(self, slot, to):
        piece = self.view(slot, None)
        return self.wire.put(piece, piece, to)

    def start(self):
        self.to_mate = self.put(self.at, partner(self.me))
        self.to_beyond = self.put(self.at, across(self.me))

    def plan(self, plan, name, after, rank):
        plan.add(name + ".go", self.start, after=after, rank=rank)
        plan.add(name + ".r", self.relay, lambda: [self.to_mate], (name + ".go",), rank)
        plan.add(name + ".near", lambda: None, lambda: [self.to_beyond], (name + ".r",), rank)
        plan.add(name + ".far", lambda: None, lambda: [self.far], (name + ".near",), rank)

    def relay(self):
        self.far = self.put(self.mate, across(self.me))

    def copies(self):
        return [self.to_mate, self.to_beyond, self.far]

    def closed(self):
        return self.mate, self.beyond


class Meet:
    def __init__(self, wire, me, axis, ref):
        piece = ref.at[getattr(me, axis)]
        self.copies = [wire.put(piece, piece, near(me, axis, step)) for step in (1, 2, 3)]


class MeetCores:
    def __init__(self, wire, me, ref):
        piece = ref.at[me.core, me.y]
        others = [near(me, "y", step) for step in (1, 2, 3)] + [sibling(me)]
        others += [crossed(me, step) for step in (1, 2, 3)]
        self.copies = [wire.put(piece, piece, other) for other in others]


class RingSum:
    def __init__(self, wire, me, axis, part, from_left, from_right, whole_left, whole_right, split, add):
        self.wire, self.part, self.split, self.add = wire, part, split, add
        self.at = getattr(me, axis)
        self.right, self.left = near(me, axis, 1), near(me, axis, 3)
        self.near_bufs = (from_left, from_right)
        self.whole = (whole_left, whole_right)

    def start_near(self, half):
        piece = self.part(rem4(self.at + 2), half)
        to = self.left if half else self.right
        copy = self.wire.put(piece, self.near_bufs[half], to)
        if half:
            self.second = copy
        else:
            self.first = copy

    def start_whole(self, half):
        if half:
            self.right_whole = self.wire.put(
                self.part(rem4(self.at + 1), 1), self.split(self.whole[0], 1), self.right
            )
        else:
            self.left_whole = self.wire.put(
                self.part(rem4(self.at + 3), 0), self.split(self.whole[1], 0), self.left
            )

    def start(self, halves=(0, 1)):
        for half in halves:
            self.start_near(half)
        if 1 in halves:
            self.start_whole(1)
            self.start_whole(0)

    def plan(self, plan, name, after, rank, go=True):
        if go:
            plan.add(name + ".go", self.start, after=after, rank=rank)
        plan.add(name + ".r", self.relay_right, lambda: [self.first], (name + ".go",), rank)
        plan.add(name + ".l", self.relay_left, lambda: [self.second], (name + ".go",), rank)
        plan.add(
            name + ".far",
            lambda: None,
            lambda: [self.left_whole, self.right_whole, self.to_right, self.to_left],
            (name + ".r", name + ".l"),
            rank,
        )

    def relay_right(self):
        after = rem4(self.at + 1)
        self.add(self.part(after, 0), self.near_bufs[0])
        self.to_right = self.wire.put(self.part(after, 0), self.split(self.whole[0], 0), self.right)

    def relay_left(self):
        before = rem4(self.at + 3)
        self.add(self.part(before, 1), self.near_bufs[1])
        self.to_left = self.wire.put(self.part(before, 1), self.split(self.whole[1], 1), self.left)


class PairSum:
    def __init__(self, wire, me, part, from_beyond, for_mate, from_mate, add):
        self.wire, self.me, self.part, self.add = wire, me, part, add
        self.at = me.z
        self.mate, self.beyond = me.zh * 2 + 1 - me.zl, rem4(me.z + 3 + 2 * me.zl)
        self.for_mate, self.whole = for_mate, (from_beyond, from_mate)

    def start(self):
        far = rem4(self.at + 2)
        self.first = self.wire.put(self.part(far, None), self.for_mate, across(self.me))
        self.second = self.wire.put(self.part(self.beyond, None), self.whole[0], across(self.me))

    def plan(self, plan, name, after, rank):
        plan.add(name + ".go", self.start, after=after, rank=rank)
        plan.add(name + ".r", self.relay, lambda: [self.first], (name + ".go",), rank)
        plan.add(
            name + ".far", lambda: None, lambda: [self.second, self.to_mate], (name + ".r",), rank
        )

    def relay(self):
        self.add(self.part(self.mate, None), self.for_mate)
        self.to_mate = self.wire.put(self.part(self.mate, None), self.whole[1], partner(self.me))


def split_columns(ref, half):
    return ref.at[:, pl.ds(half * (D // 2), D // 2)]


def split_rows(cut):
    def split(ref, half):
        rows = ref.shape[-2]
        span = pl.ds(0, cut) if half == 0 else pl.ds(cut, rows - cut)
        return ref.at[(ALL,) * (len(ref.shape) - 2) + (span, ALL)]

    return split


class Spread:
    def __init__(self, wire, me, ref, lead, row, rows, first, cut, cuts=(ALL,), kind=PairRing, ring=False):
        self.wire, self.me = wire, me
        head = (ALL,) * lead

        def view(y, z, part, low=ALL):
            zl, zh = (low, ALL) if z is None else (lax.rem(z, 2), lax.div(z, 2))
            start, size = row, rows
            if part == 0:
                size = cut
            if part == 1:
                start, size = row + cut, rows - cut
            yy = ALL if y is None else y
            return ref.at[head + (zl, yy, zh, me.core, pl.ds(start, size), ALL)]

        if first == "y":
            self.one = Ring(wire, me, "y", lambda slot, part: view(slot, me.z, part))
            across_z = lambda slot, part: view(None, slot, part)
            self.twos = [
                Ring(wire, me, "z", across_z) if ring else PairRing(wire, me, across_z)
            ]
        else:
            self.one = kind(wire, me, lambda slot, part: view(me.y, slot, part))
            self.twos = [
                Ring(wire, me, "y", lambda slot, part, low=low: view(slot, None, part, low))
                for low in cuts
            ]

    def plan(self, plan, name, after, turn_after, rank):
        self.one.plan(plan, name + ".a", after, rank)
        self.plan_second(plan, name, (name + ".a.far", *turn_after), rank)

    def plan_second(self, plan, name, done, rank):
        done = list(done)
        self.shared = []
        for index, two in enumerate(self.twos):
            tail = str(index) if len(self.twos) > 1 else ""
            self.plan_two(plan, two, name, tail, tuple(done), rank + 0.01 * index)
            done += [name + ".b" + tail + ".r", name + ".b" + tail + ".l"] if tail else []

    def plan_two(self, plan, two, name, tail, after, rank):
        shared = []

        def share(slots):
            for slot in slots:
                piece = two.view(slot, None)
                shared.append(self.wire.put(piece, piece, sibling(self.me)))
            self.shared += shared[-len(slots) :]

        def go():
            two.start()
            share([two.at])

        step = name + ".b" + tail
        two.plan(plan, step, after, rank)
        plan.steps[step + ".go"].run = go
        plan.add(name + ".s" + tail, lambda: share(two.closed()), after=(step + ".near",), rank=rank)
        plan.add(
            name + ".t" + tail, lambda: share([rem4(two.at + 2)]),
            after=(name + ".s" + tail, step + ".far"), rank=rank,
        )
        plan.add(name + ".all" + tail, lambda: None, lambda: shared, (name + ".t" + tail,), rank)
MLP_Y, MLP_CUT, MLP_REST = 288, 144, 208
QKV_Y, QY_CUT, QZ_CUT = 32, 16, 48
QZ_KIND = PairRing
OUT_Y, OUT_CUT, OUT_REST = 64, 32, 96
MZ_AFTER, MZ_TURN = (), ()
MY_AFTER, MY_TURN = (), ()
ORDER_ATTEND = (
    "qz.a.go", "gx", "tz", "qy.a.go", "oy.a.go", "my.a.go", "tx.go", "bias", "qy.a.r", "qy.a.l",
    "gz", "qy.a.near", "oy.a.r", "oy.a.l", "oy.a.near", "qz.a.r", "qz.a.near", "my.a.r", "my.a.l",
    "my.a.near", "qy.a.far", "qy.b.go", "oz.a.go", "oy.a.far", "oy.b.go", "mz.a.go", "tx.r",
    "tx.l", "my.a.far", "qz.a.far", "qz.b0.go", "tx.near", "qz.b0.r", "qz.b0.l", "to", "gy",
    "qz.b0.near", "qz.s0", "tx.far", "tf", "qz.b1.go", "cx.go", "qy.b.r", "qy.b.near", "qy.s",
    "oz.a.r", "oz.a.near", "qz.b0.far", "qz.t0", "oy.b.r", "oy.b.near", "gains", "n1", "qz.all0",
    "oy.s", "n2", "n0", "qz.b1.r", "qz.b1.l", "qy.b.far", "qy.t", "n3", "mz.a.r", "mz.a.near",
    "oz.a.far", "oz.b.go", "qy.all", "proj0", "qz.b1.near", "qz.s1", "own0", "my.b.go",
    "qz.b1.far", "n4", "qz.t1", "oy.b.far", "oy.t", "oz.b.r", "oz.b.l", "rest0", "mz.a.far",
    "mz.b.go", "qz.all1", "rest1", "oy.all", "proj1", "cx.l", "own2", "n5", "last0", "cx.r",
    "oz.b.near", "oz.s", "oz.b.far", "att0", "cx.near", "wz.go", "oz.t", "last1", "att2",
    "oz.all", "po", "ys.go", "cx.far", "mz.b.r", "ck", "ht", "mz.b.l", "my.b.r", "my.b.near",
    "my.s", "flip", "wz.r", "flip2", "wz.near", "mz.b.near", "mz.s", "ys.r", "wy.go", "ys.l",
    "flip3", "mz.b.far", "mz.t", "mz0", "wy.l", "wy.r", "my.b.far", "my.t", "my0", "wy.near",
    "mz.all", "mz1", "wz.far", "wz0", "my.all", "my1", "ys.far", "fin", "wy.far", "wy0",
)

UP_Y, UP_CUT, UP_REST = 320, 160, 176


def up_spreads(wire, me, ref):
    return (
        Spread(wire, me, ref, 0, UP_Y, UNITS - UP_Y, "z", UP_REST),
        Spread(wire, me, ref, 0, 0, UP_Y, "y", UP_CUT, ring=True),
    )


def norm_rows(source, target, gain, rows, step=32):
    def body(index, carry):
        span = pl.ds(pl.multiple_of(index * step, step), step)
        value = source[span, :].astype(F32)
        scale = lax.rsqrt(jnp.mean(value * value, axis=-1, keepdims=True) + EPS)
        target[span, :] = (value * scale * gain).astype(BF)
        return carry

    lax.fori_loop(0, rows // step, body, 0)


def fill_bias(bias, me, start):
    row = lax.broadcasted_iota(jnp.int32, (128, 512), 0)
    column = lax.broadcasted_iota(jnp.int32, (128, 512), 1)
    query = lax.div(column, 128) * 256 + me.zl * 128 + lax.rem(column, 128)
    query_in = (query >= start) & (query < start + PIECE)

    def body(block, carry):
        pair, other = lax.div(block, 2), lax.rem(block, 2)
        parity = me.zl + other * (1 - 2 * me.zl)
        key = (pair * 2 + parity) * 128 + row
        key_in = (key >= start) & (key < start + PIECE)
        allowed = (key <= query) | (query_in & key_in)
        bias[pair, other] = jnp.where(allowed, 0.0, NEG)
        return carry

    lax.fori_loop(0, 8, body, 0)


def turn(field, cosine, sine):
    return field * cosine + pltpu.roll(field, HD // 2, 1) * sine


def add_into(target, terms, result=None):
    shape = target.shape
    lead, rows, columns = shape[:-2], shape[-2], shape[-1]
    step = rows
    while step * columns > 33000:
        step = next(s for s in range(step - 16, 0, -16) if rows % s == 0)
    cuts = rows // step
    result = target if result is None else result

    def body(index, carry):
        where, rest = [], lax.div(index, cuts)
        for extent in reversed(lead):
            where.insert(0, lax.rem(rest, extent))
            rest = lax.div(rest, extent)
        where = tuple(where) + (
            pl.ds(pl.multiple_of(lax.rem(index, cuts) * step, 16), step), ALL
        )
        total = target[where].astype(F32)
        for term in terms:
            total = total + term[where].astype(F32)
        result[where] = total.astype(result.dtype)
        return carry

    lax.fori_loop(0, math.prod(lead) * cuts, body, 0)


def columns_of(ref):
    def view(slot, half):
        if half is None:
            return ref.at[slot]
        return ref.at[slot, :, pl.ds(half * (D // 2), D // 2)]

    return view


def rows_of(ref):
    def view(slot, half):
        return ref.at[slot] if half is None else ref.at[slot, pl.ds(half * 64, 64)]

    return view


def kernel_attend(
    tokens_in, cotangent_in, start_in, query_w, key_w, value_w, out_w, gate_w, up_w, down_w,
    gain_one_in, gain_two_in, tables_in,
    qkv_out, wo_out, mlp_out, cot_out, turned_out, query_out, keys_out, values_out, heads_out,
    h_out, lse_hbm, y_hbm, gains_hbm,
    lse_out, y_out, gains_out, tok, h_one, w_qkv, w_o, w_mlp, tables, bias, query, keys, values, heads, cot, h_two,
    part, near_left, near_right, whole_left, whole_right,
    turned, heads_t, top_s, total_s, result_s, gain_x, gain_z, gain_c,
    send, recv, local,
):
    me = place()
    wire = Wire(send, recv, local)
    own = [wire.move(tokens_in, tok.at[me.x, 0])]
    for index, ref in enumerate((query_w, key_w, value_w)):
        own.append(wire.move(ref, w_qkv.at[index, me.zl, me.y, me.zh, me.core]))
    own.append(wire.move(out_w, w_o.at[me.zl, me.y, me.zh, me.core]))
    for index, ref in enumerate((gate_w, down_w, up_w)):
        own.append(wire.move(ref, w_mlp.at[index, me.zl, me.y, me.zh, me.core]))
    own.append(wire.move(tables_in.at[me.zl], tables))
    own.append(wire.move(cotangent_in, cot.at[me.x]))
    lane = lax.div(lax.broadcasted_iota(jnp.int32, (1, 128), 1), 16)
    tensor = me.x * 2 + me.zl
    gain_x[me.x] = jnp.concatenate(
        [
            jnp.where(lane == tensor, jnp.concatenate([ref[...]] * 8, axis=1), 0.0)
            for ref in (gain_one_in, gain_two_in)
        ]
        + [jnp.zeros((6, 128), F32)],
        axis=0,
    )
    greet(me, True, own)
    plan = Plan()
    at = types.SimpleNamespace()
    one, far, three = rem4(me.x + 1), rem4(me.x + 2), rem4(me.x + 3)
    kept = []

    def keep(source, target):
        kept.append(wire.move(source, target))

    def gains_x():
        at.gains = Meet(wire, me, "x", gain_x).copies

    def gains_z():
        gain_z[me.z] = gain_x[0] + gain_x[1] + gain_x[2] + gain_x[3]
        at.gains = Meet(wire, me, "z", gain_z).copies

    def gains_y():
        gain_c[me.core, me.y, 0] = gain_z[0] + gain_z[1]
        gain_c[me.core, me.y, 1] = gain_z[2] + gain_z[3]
        at.gains = MeetCores(wire, me, gain_c).copies

    def gains_all():
        for y in range(4):
            for zh in range(2):
                for core in range(2):
                    column = (y * 4 + zh * 2 + core) * 128
                    gains_out[:, column : column + 128] = gain_c[core, y, zh]

    plan.add("gx", gains_x, rank=0)
    plan.add("gz", gains_z, lambda: at.gains, ("gx",), 0)
    plan.add("gy", gains_y, lambda: at.gains, ("gz",), 0)
    plan.add("gains", gains_all, lambda: at.gains, ("gy",), 1)

    def tokens_z():
        at.rows_z = wire.put(tok.at[me.x, 0], tok.at[me.x, 1], partner(me))

    def tokens_on():
        at.on = [
            wire.put(tok.at[me.x, 1], tok.at[me.x, 1], near(me, "x", step)) for step in (1, 3)
        ]

    def tokens_far():
        at.far_z = wire.put(tok.at[far, 0], tok.at[far, 1], partner(me))

    Ring(
        wire, me, "x",
        lambda slot, half: tok.at[slot, 0] if half is None else tok.at[slot, 0, pl.ds(half * 64, 64)],
    ).plan(plan, "tx", (), 0)
    plan.add("tz", tokens_z, rank=0)
    plan.add("to", tokens_on, lambda: [at.rows_z], ("tz",), 0)
    plan.add("tf", tokens_far, after=("tx.far",), rank=0)

    def norm(*blocks):
        def run():
            for slot, p in blocks:
                norm_rows(tok.at[slot, p], h_one.at[slot, p], gains_out[0:1, :], 128)

        return run

    plan.add("n0", norm((me.x, 0)), after=("gains",), rank=2)
    plan.add("n1", norm((one, 0), (three, 0)), after=("gains", "tx.near"), rank=2)
    plan.add("n2", norm((far, 0)), after=("gains", "tx.far"), rank=2)
    plan.add("n3", norm((me.x, 1)), after=("gains", "to"), rank=3)
    plan.add("n4", norm((one, 1), (three, 1)), lambda: at.on, ("gains", "to"), 3)
    plan.add("n5", norm((far, 1)), lambda: [at.far_z], ("gains", "tf"), 2)

    Spread(wire, me, w_qkv, 1, QKV_Y, 128 - QKV_Y, "z", QZ_CUT, (0, 1), QZ_KIND).plan(plan, "qz", (), (), 1)
    Spread(wire, me, w_qkv, 1, 0, QKV_Y, "y", QY_CUT).plan(plan, "qy", (), (), 1)
    Spread(wire, me, w_o, 0, OUT_Y, 256 - OUT_Y, "z", OUT_REST).plan(plan, "oz", (), (), 1)
    Spread(wire, me, w_o, 0, 0, OUT_Y, "y", OUT_CUT).plan(plan, "oy", (), (), 1)
    both = w_mlp.at[pl.ds(0, 2)]
    mlp_z = Spread(wire, me, both, 1, MLP_Y, UNITS - MLP_Y, "z", MLP_REST)
    mlp_y = Spread(wire, me, both, 1, 0, MLP_Y, "y", MLP_CUT)
    mlp_z.plan(plan, "mz", (), (), 1.5)
    mlp_y.plan(plan, "my", (), (), 1.5)
    up_z, up_y = up_spreads(wire, me, w_mlp.at[2])
    up_z.one.plan(plan, "wz", (), 1.7)
    up_y.one.plan(plan, "wy", (), 1.7)

    def keep_up(*where):
        return lambda: keep(w_mlp.at[(2, *where)], mlp_out.at[(2, *where)])

    plan.add(
        "wz0", keep_up(ALL, me.y, ALL, me.core, pl.ds(UP_Y, UNITS - UP_Y), ALL),
        after=("wz.far",), rank=1.8,
    )
    plan.add(
        "wy0", keep_up(me.zl, ALL, me.zh, me.core, pl.ds(0, UP_Y), ALL), after=("wy.far",), rank=1.8
    )
    plan.add("bias", lambda: fill_bias(bias, me, start_in[0]), rank=6)

    def project(zl, carry):
        rows = h_one[:, 0].reshape(512, D)
        cosine, sine = tables[0, :, 0].reshape(512, HD), tables[1, :, 0].reshape(512, HD)
        raw = dot_nn(rows, w_qkv[0, zl].reshape(D, 256))
        for j in range(2):
            query[zl * 2 + j] = turn(raw[:, j * HD : (j + 1) * HD], cosine, sine).astype(BF)
        raw = dot_nn(rows, w_qkv[1, zl].reshape(D, 256))
        for j in range(2):
            keys[zl * 2 + j, :, 0] = (
                turn(raw[:, j * HD : (j + 1) * HD], cosine, sine).astype(BF).reshape(4, 128, HD)
            )
        raw = dot_nn(rows, w_qkv[2, zl].reshape(D, 256))
        for j in range(2):
            values[zl * 2 + j, :, 0] = raw[:, j * HD : (j + 1) * HD].astype(BF).reshape(4, 128, HD)
        return carry

    def project_other(zl, slots):
        rows = jnp.concatenate([h_one[slot, 1] for slot in slots], axis=0)
        cosine = jnp.concatenate([tables[0, slot, 1] for slot in slots], axis=0)
        sine = jnp.concatenate([tables[1, slot, 1] for slot in slots], axis=0)
        raw_k = dot_nn(rows, w_qkv[1, zl].reshape(D, 256))
        raw_v = dot_nn(rows, w_qkv[2, zl].reshape(D, 256))
        for j in range(2):
            key = turn(raw_k[:, j * HD : (j + 1) * HD], cosine, sine).astype(BF)
            value = raw_v[:, j * HD : (j + 1) * HD].astype(BF)
            for index, slot in enumerate(slots):
                keys[zl * 2 + j, slot, 1] = key[index * 128 : index * 128 + 128]
                values[zl * 2 + j, slot, 1] = value[index * 128 : index * 128 + 128]

    at.projected = at.rest = 0

    def keep_when_done():
        if at.projected == 2 and at.rest == 4:
            keep(w_qkv, qkv_out)
            keep(query, query_out)
            keep(keys, keys_out)
            keep(values, values_out)

    def project_half(zl):
        def run():
            lax.fori_loop(zl, zl + 1, project, 0)
            at.projected += 1
            keep_when_done()

        return run

    def other(zl, slots):
        def run():
            project_other(zl, slots)
            at.rest += 1
            keep_when_done()

        return run

    for zl in range(2):
        name = "%d" % zl
        plan.add(
            "proj" + name, project_half(zl), after=("n0", "n1", "n2", "qy.all", "qz.all" + name), rank=2 + 0.1 * zl
        )
        plan.add(
            "rest" + name, other(zl, (me.x, one, three)), after=("n3", "n4", "qy.all", "qz.all" + name),
            rank=2.2 + 0.1 * zl,
        )
        plan.add("last" + name, other(zl, (far,)), after=("n5", "qy.all", "qz.all" + name), rank=2.4 + 0.1 * zl)

    def attend_own(head, carry):
        for half, pairs in ((0, 3), (1, 4)):
            span = pairs * 128
            rows = slice(half * 256, half * 256 + 256)
            scores = dot_nt(keys[head, 0:pairs, 0].reshape(span, HD), query[head, rows, :]) * SCALE
            scores = scores + bias[0:pairs, 0, :, rows].reshape(span, 256)
            top = jnp.max(scores, axis=0, keepdims=True)
            expo = jnp.exp(scores - top)
            top_s[head, half] = top
            total_s[head, half] = jnp.sum(expo, axis=0, keepdims=True)
            value = values[head, 0:pairs, 0].reshape(span, HD)
            result_s[head, half] = dot_tn(value, expo.astype(BF))
        return carry

    def attend_other(head, carry):
        for half, pairs in ((0, 3), (1, 4)):
            span = pairs * 128
            rows = slice(half * 256, half * 256 + 256)
            scores = dot_nt(keys[head, 0:pairs, 1].reshape(span, HD), query[head, rows, :]) * SCALE
            scores = scores + bias[0:pairs, 1, :, rows].reshape(span, 256)
            before = top_s[head, half]
            top = jnp.maximum(before, jnp.max(scores, axis=0, keepdims=True))
            fade = jnp.exp(before - top)
            expo = jnp.exp(scores - top)
            total = total_s[head, half] * fade + jnp.sum(expo, axis=0, keepdims=True)
            value = values[head, 0:pairs, 1].reshape(span, HD)
            result = (result_s[head, half] * fade + dot_tn(value, expo.astype(BF))) * (1.0 / total)
            heads[rows, pl.ds(pl.multiple_of(head * HD, HD), HD)] = result.T.astype(BF)
            lse_out[head, :, rows] = top + jnp.log(total)
        return carry

    def attend_rest():
        lax.fori_loop(2, 4, attend_other, 0)
        keep(lse_out, lse_hbm)

    plan.add("own0", lambda: lax.fori_loop(0, 2, attend_own, 0), after=("proj0", "bias"), rank=2.5)
    plan.add("own2", lambda: lax.fori_loop(2, 4, attend_own, 0), after=("proj1", "bias"), rank=2.5)
    plan.add(
        "att0", lambda: lax.fori_loop(0, 2, attend_other, 0), after=("own0", "rest0", "last0"), rank=2.5
    )
    plan.add("att2", attend_rest, after=("own2", "rest1", "last1", "att0"), rank=2.6)

    def project_out(block, carry):
        y, zh = lax.div(block, 2), lax.rem(block, 2)
        weight = jnp.concatenate(
            [
                jnp.concatenate([w_o[zl, y, zh, 0], w_o[zl, y, zh, 1]], axis=1)
                for zl in range(2)
            ],
            axis=0,
        )
        result = dot_nn(heads[...], weight).astype(BF).reshape(4, 128, 256)
        part[:, :, pl.ds(pl.multiple_of(block * 256, 256), 256)] = result
        return carry

    total = RingSum(
        wire, me, "x", columns_of(part), near_left, near_right, whole_left, whole_right,
        split_columns, lambda target, term: add_into(target, [term]),
    )

    def out_one():
        keep(w_o, wo_out)
        lax.fori_loop(0, 4, project_out, 0)
        total.start((0,))

    def out_two():
        lax.fori_loop(4, 8, project_out, 0)
        total.start((1,))

    plan.add("po", out_one, after=("att0", "att2", "oz.all", "oy.all"), rank=2)
    plan.add("ys.go", out_two, after=("po",), rank=2)
    total.plan(plan, "ys", (), 1, go=False)

    def finish(index, carry):
        span = pl.ds(pl.multiple_of(index * 32, 32), 32)
        value = tok[me.x, 0, span, :].astype(F32) + (
            part[me.x, span, :].astype(F32)
            + whole_left[span, :].astype(F32)
            + whole_right[span, :].astype(F32)
        )
        scale = lax.rsqrt(jnp.mean(value * value, axis=-1, keepdims=True) + EPS)
        y_out[span, :] = value
        h_two[span, :] = (value * scale * gains_out[1:2, :]).astype(BF)
        return carry

    def finish_all():
        lax.fori_loop(0, 4, finish, 0)
        keep(h_two, h_out)
        keep(y_out, y_hbm)
        keep(gains_out, gains_hbm)

    plan.add("fin", finish_all, after=("ys.far",), rank=0)
    Ring(wire, me, "x", rows_of(cot)).plan(plan, "cx", (), 1.6)
    plan.add("ck", lambda: keep(cot, cot_out), after=("cx.far",), rank=1.8)

    def flip(block, carry):
        column = pl.ds(pl.multiple_of(block * 128, 128), 128)
        rows = h_one[:, :, :, column].reshape(SEQ, 128)
        turned[lax.rem(block, 2), lax.div(block, 2)] = rows.T
        return carry

    def turn_heads():
        heads_t[...] = heads[...].T
        keep(heads_t, heads_out)

    plan.add("ht", turn_heads, after=("att0", "att2"), rank=6)

    def flip_rest():
        lax.fori_loop(8, 16, flip, 0)
        keep(turned.at[me.core], turned_out.at[0])
        at.turned = wire.put(turned.at[1 - me.core], turned_out.at[1], sibling(me))

    plan.add("flip", lambda: lax.fori_loop(0, 8, flip, 0), after=("n0", "n1", "n2", "n3", "n4", "n5"), rank=7)
    plan.add("flip2", flip_rest, after=("flip",), rank=7)
    plan.add("flip3", lambda: None, lambda: [at.turned], ("flip2",), 9)

    def keep_mlp(mine, start, size):
        def run():
            core = me.core if mine else 1 - me.core
            piece = (pl.ds(0, 2), ALL, ALL, ALL, core, pl.ds(start, size), ALL)
            keep(w_mlp.at[piece], mlp_out.at[piece])

        return run

    plan.add("my0", keep_mlp(True, 0, MLP_Y), after=("my.t",), rank=1.8)
    plan.add("my1", keep_mlp(False, 0, MLP_Y), after=("my.all",), rank=1.8)
    plan.add("mz0", keep_mlp(True, MLP_Y, UNITS - MLP_Y), after=("mz.t",), rank=1.8)
    plan.add("mz1", keep_mlp(False, MLP_Y, UNITS - MLP_Y), after=("mz.all",), rank=1.8)

    plan.go(ORDER_ATTEND)
    for copy in kept:
        copy.wait()
    wire.drain()


def anywhere():
    return pl.BlockSpec(memory_space=pl.ANY)


def in_vmem():
    return pl.BlockSpec(memory_space=pltpu.VMEM)


def call_attend(tokens, cotangent, starts, weights, gain_attn, gain_mlp, tables):
    shape = jax.ShapeDtypeStruct
    hbm = [
        shape((3, 2, 4, 2, 2, 128, 256), BF),
        shape((2, 4, 2, 2, 256, 128), BF),
        shape((3, 2, 4, 2, 2, UNITS, 128), BF),
        shape((4, 128, D), BF),
        shape((2, 8, 128, SEQ), BF),
        shape((4, 512, HD), BF),
        shape((4, 4, 2, 128, HD), BF),
        shape((4, 4, 2, 128, HD), BF),
        shape((512, 512), BF),
        shape((128, D), BF),
    ]
    vmem = [shape((4, 1, 512), F32), shape((128, D), F32), shape((8, D), F32)]
    return pl.pallas_call(
        kernel_attend,
        name="attend",
        in_specs=[anywhere(), anywhere(), pl.BlockSpec(memory_space=pltpu.SMEM)]
        + [anywhere()] * 7
        + [in_vmem()] * 2
        + [anywhere()],
        out_specs=[anywhere()] * (len(hbm) + len(vmem)),
        out_shape=hbm + vmem,
        scratch_shapes=[
            pltpu.VMEM((4, 1, 512), F32),
            pltpu.VMEM((128, D), F32),
            pltpu.VMEM((8, D), F32),
            pltpu.VMEM((4, 2, 128, D), BF),
            pltpu.VMEM((4, 2, 128, D), BF),
            pltpu.VMEM((3, 2, 4, 2, 2, 128, 256), BF),
            pltpu.VMEM((2, 4, 2, 2, 256, 128), BF),
            pltpu.VMEM((3, 2, 4, 2, 2, UNITS, 128), BF),
            pltpu.VMEM((2, 4, 2, 128, HD), F32),
            pltpu.VMEM((4, 2, 128, 512), F32),
            pltpu.VMEM((4, 512, HD), BF),
            pltpu.VMEM((4, 4, 2, 128, HD), BF),
            pltpu.VMEM((4, 4, 2, 128, HD), BF),
            pltpu.VMEM((512, 512), BF),
            pltpu.VMEM((4, 128, D), BF),
            pltpu.VMEM((128, D), BF),
            pltpu.VMEM((4, 128, D), BF),
            pltpu.VMEM((128, D // 2), BF),
            pltpu.VMEM((128, D // 2), BF),
            pltpu.VMEM((128, D), BF),
            pltpu.VMEM((128, D), BF),
            pltpu.VMEM((2, 8, 128, SEQ), BF),
            pltpu.VMEM((512, 512), BF),
            pltpu.VMEM((4, 2, 1, 256), F32),
            pltpu.VMEM((4, 2, 1, 256), F32),
            pltpu.VMEM((4, 2, HD, 256), F32),
            pltpu.VMEM((4, 8, 128), F32),
            pltpu.VMEM((4, 8, 128), F32),
            pltpu.VMEM((2, 4, 2, 8, 128), F32),
            pltpu.SemaphoreType.DMA((140,)),
            pltpu.SemaphoreType.DMA((140,)),
            pltpu.SemaphoreType.DMA((32,)),
        ],
        compiler_params=pltpu.CompilerParams(
            collective_id=0, has_side_effects=True, vmem_limit_bytes=VMEM_BYTES
        ),
    )(tokens, cotangent, starts, *weights, gain_attn, gain_mlp, tables)


def rope_tables():
    half = HD // 2
    freq = np.exp(np.arange(half, dtype=np.float32) * np.float32(-2.0 * math.log(10000.0) / HD))
    order = np.array(
        [
            [[(2 * pair + (zl + other) % 2) * 128 + np.arange(128) for other in range(2)] for pair in range(4)]
            for zl in range(2)
        ]
    )
    angle = order.astype(np.float32)[..., None] * freq.astype(np.float32)
    cosine, sine = np.cos(angle.astype(np.float64)), np.sin(angle.astype(np.float64))
    both = np.stack(
        [np.concatenate([cosine, cosine], -1), np.concatenate([-sine, sine], -1)], axis=1
    )
    return both.astype(np.float32)
SUM_Y, SUM_CUT, SUM_REST = 352, 176, 176
ORDER_FEED = (
    "hx.go", "l2", "wz.b.go", "wy.b.go", "cs", "a11", "wz.b.l", "a01", "hx.l", "hx.r", "wy.b.l",
    "wy.b.r", "wz.b.r", "a00", "wy.b.near", "wy.s", "wz.b.near", "wz.s", "hx.near", "g11",
    "wy.b.far", "wy.t", "g10", "wz.b.far", "wz.t", "wy.all", "a10", "wz.all", "hx.far", "g00",
    "f00", "g01", "f01", "b00", "ds.go", "f10", "f11", "b10", "hs", "ds.r", "t1", "b11", "t0",
    "ds.l", "gr1a", "gr1b", "s1z.go", "s1y.go", "gr0a", "gr0b", "ds.far", "bn", "s0y.go", "s1z.l",
    "s1z.r", "s1y.r", "s1y.l", "dx.go", "s0z.go", "t2", "fd0", "s1z.far", "s1z.k", "s0y.r",
    "dx.r", "fd1", "s0z.l", "s0z.r", "s0y.l", "dx.l", "dx.near", "gr2a", "gr2b", "s1y.far",
    "s1y.k", "dg", "s0z.far", "s0z.k", "s0y.far", "s0y.k", "dx.far", "dk",
)


def fold_view(ref, me, lead, axis, row, rows, cut):
    head = (ALL,) * lead

    def view(slot, part):
        start, size = row, rows
        if part == 0:
            size = cut
        if part == 1:
            start, size = row + cut, rows - cut
        if axis == "y":
            where = (ALL, slot, ALL)
        else:
            where = (lax.rem(slot, 2), ALL, lax.div(slot, 2))
        return ref.at[head + where + (pl.ds(start, size), ALL)]

    return view


def kernel_feed(
    h_in, cot_in, mlp_in, y_hbm, gains_hbm,
    part_out, dattn_out, fold_y_out, fold_z_out, down_out, dy_hbm, gain_hbm,
    y_in, gains_in, dy_out, gain_out,
    w_mlp, h_two, cot, gate_s, up_s, act_s, d_gate, d_up, act, flipped, flipped_far,
    h_far, cot_far, part, near_left, near_right, whole_left, whole_right, d_attn, out_part,
    *rest,
):
    bufs, (send, recv, local) = list(rest[:-3]), rest[-3:]
    bufs = [tuple(bufs[a:b]) for a, b in ((0, 4), (4, 8), (8, 12), (12, 16))]
    me = place()
    wire = Wire(send, recv, local)
    parts = {}

    def load(zl):
        for which in range(2):
            parts[which, zl] = wire.move(mlp_in.at[which, zl], w_mlp.at[which, zl])

    def load_up(*where):
        return wire.move(mlp_in.at[(2, *where)], w_mlp.at[(2, *where)])

    loads = [wire.move(h_in, h_two.at[me.x])]
    ups = [
        load_up(ALL, me.y, ALL, me.core, pl.ds(UP_Y, UNITS - UP_Y), ALL),
        load_up(me.zl, ALL, me.zh, me.core, pl.ds(0, UP_Y), ALL),
    ]
    greet(me, False)
    plan = Plan()
    at = types.SimpleNamespace()
    kept = []

    def keep(source, target):
        kept.append(wire.move(source, target))

    def whole(which, zl):
        return jnp.concatenate(
            [
                w_mlp[which, zl, y, zh, core]
                for y in range(4)
                for zh in range(2)
                for core in range(2)
            ],
            axis=1,
        )

    def share(source, target):
        return [
            wire.put(
                source.at[:, :, pl.ds(pl.multiple_of((block * 2 + 1 - me.core) * 128, 128), 128)],
                target.at[block],
                sibling(me),
            )
            for block in range(8)
        ]

    def share_h():
        at.h_puts = share(h_two, h_far)

    def share_cot():
        at.cot_puts = share(cot, cot_far)

    one, far, three = rem4(me.x + 1), rem4(me.x + 2), rem4(me.x + 3)
    batches = ((far, one), (three, me.x))

    def rows_of_batch(ref, batch):
        return jnp.concatenate([ref[slot] for slot in batches[batch]], axis=0)

    def room(batch, zl):
        return zl if batch else 2

    def gate(batch, zl):
        def run():
            gate_s[room(batch, zl)] = dot_nt(rows_of_batch(h_two, batch), whole(0, zl))

        return run

    def back_act(batch, zl):
        def run():
            act_s[batch * 2 + zl] = dot_nt(rows_of_batch(cot, batch), whole(1, zl))

        return run

    def forward(batch, zl):
        def inner(index, carry):
            place_of, rest = lax.div(index, 4), lax.rem(index, 4)
            first, second = batches[batch]
            slot = first + place_of * (second - first)
            source = pl.ds(pl.multiple_of(index * 32, 32), 32)
            span = pl.ds(pl.multiple_of(rest * 32, 32), 32)
            gate, up = gate_s[room(batch, zl), source, :], up_s[source, :]
            d_act = act_s[batch * 2 + zl, source, :]
            sigma = 1.0 / (1.0 + jnp.exp(-gate))
            act[zl, slot, span, :] = (gate * sigma * up).astype(BF)
            d_gate[zl, slot, span, :] = (
                d_act * up * sigma * (1.0 + gate * (1.0 - sigma))
            ).astype(BF)
            d_up[zl, slot, span, :] = (d_act * gate * sigma).astype(BF)
            return carry

        def run():
            up_s[...] = dot_nt(rows_of_batch(h_two, batch), whole(2, zl))
            lax.fori_loop(0, 8, inner, 0)

        return run

    def back_h(batch):
        def body(block, carry):
            y, zh = lax.div(block, 2), lax.rem(block, 2)
            total = None
            for which, left in ((0, d_gate), (2, d_up)):
                for zl in range(2):
                    weight = jnp.concatenate(
                        [w_mlp[which, zl, y, zh, 0], w_mlp[which, zl, y, zh, 1]], axis=1
                    )
                    rows = jnp.concatenate([left[zl, slot] for slot in batches[batch]], axis=0)
                    term = dot_nn(rows, weight)
                    total = term if total is None else total + term
            result = total.astype(BF)
            column = pl.ds(pl.multiple_of(block * 256, 256), 256)
            for index, slot in enumerate(batches[batch]):
                part[slot, :, column] = result[index * 128 : index * 128 + 128]
            return carry

        return body

    def add(target, term):
        add_into(target, [term])

    total = RingSum(
        wire, me, "x", columns_of(part), near_left, near_right, whole_left, whole_right,
        split_columns, add,
    )

    def back_first(half):
        def run():
            lax.fori_loop(half * 4, half * 4 + 4, back_h(0), 0)
            total.start_near(half)
            if half:
                total.start_whole(1)

        return run

    def back_second(half):
        def run():
            lax.fori_loop(half * 4, half * 4 + 4, back_h(1), 0)
            if half == 0:
                total.start_whole(0)

        return run

    plan.add("hs", share_h, after=("hx.far",), rank=3)
    plan.add("cs", share_cot, lambda: [loads[1]], ("l2",), 3)
    def load_rest():
        load(0)
        load(1)
        loads.append(wire.move(cot_in, cot))
        at.late = [wire.move(y_hbm, y_in), wire.move(gains_hbm, gains_in)]

    plan.add("l2", load_rest, lambda: [loads[0], *ups], ("hx.go",), 0)
    Ring(wire, me, "x", rows_of(h_two)).plan(plan, "hx", (), 0)
    plan.steps["hx.go"].waits = lambda: [loads[0]]
    up_z, up_y = up_spreads(wire, me, w_mlp.at[2])
    up_z.plan_second(plan, "wz", (), 1)
    up_y.plan_second(plan, "wy", (), 1)
    plan.steps["wz.b.go"].waits = lambda: [ups[0]]
    plan.steps["wy.b.go"].waits = lambda: [ups[1]]
    for zl in range(2):
        for batch in range(2):
            name = "%d%d" % (batch, zl)
            plan.add(
                "a" + name, back_act(batch, zl), lambda zl=zl: [loads[1], parts[1, zl]], ("l2",),
                4 - 0.5 * batch,
            )
        plan.add("g1%d" % zl, gate(1, zl), lambda zl=zl: [parts[0, zl]], ("hx.near", "l2"), 3)
    before = ("hx.far", "l2")
    for zl in range(2):
        name = "0%d" % zl
        plan.add("g" + name, gate(0, zl), lambda zl=zl: [parts[0, zl]], before, 2)
        plan.add(
            "f" + name, forward(0, zl), after=("g" + name, "a" + name, "wz.all", "wy.all", *before),
            rank=2,
        )
        before = ("f" + name,)
    plan.add("b00", back_first(0), after=before, rank=2)
    plan.add("ds.go", back_first(1), after=("b00",), rank=2)
    plan.add("f10", forward(1, 0), after=("g10", "a10", "ds.go"), rank=2.1)
    plan.add("f11", forward(1, 1), after=("g11", "a11", "f10"), rank=2.1)
    before = ("f10", "f11")
    plan.add("b10", back_second(0), after=before, rank=2)
    plan.add("b11", back_second(1), after=("b10",), rank=2)
    total.plan(plan, "ds", (), 0, go=False)
    plan.steps["ds.l"].after += ("b11",)
    plan.steps["ds.far"].after += ("b10",)

    at.far = {}

    def turn_over(which, source):
        def run():
            for zl in range(2):
                flipped[which, zl] = source[zl].reshape(512, UNITS).T
            at.far[which] = wire.put(flipped.at[which], flipped_far.at[which], sibling(me))

        return run

    for which, source in enumerate((d_gate, d_up, act)):
        early = which == 1
        plan.add(
            "t%d" % which, turn_over(which, source), after=("f11",) if early else ("b11",),
            rank=1.9 if early else 2 + which * 0.2,
        )

    def forward_down(block, carry):
        y, zh = lax.div(block, 2), lax.rem(block, 2)
        result = None
        for zl in range(2):
            weight = jnp.concatenate([w_mlp[1, zl, y, zh, 0], w_mlp[1, zl, y, zh, 1]], axis=1)
            term = dot_nn(act[zl].reshape(512, UNITS), weight)
            result = term if result is None else result + term
        out_part[:, :, pl.ds(pl.multiple_of(block * 256, 256), 256)] = result.astype(BF).reshape(4, 128, 256)
        return carry

    def down_rest():
        lax.fori_loop(4, 8, forward_down, 0)
        keep(out_part, part_out)

    plan.add("fd0", lambda: lax.fori_loop(0, 4, forward_down, 0), after=("t2",), rank=4)
    plan.add("fd1", down_rest, after=("fd0",), rank=4)

    places = (0, 2, 1)

    def grad(which, rows, rows_far):
        def body(index, carry):
            zl, pair = lax.div(index, 2), lax.rem(index, 2)
            mine = jnp.concatenate(
                [
                    rows[:, :, pl.ds(pl.multiple_of(((pair * 4 + k) * 2 + me.core) * 128, 128), 128)]
                    .reshape(512, 128)
                    for k in range(4)
                ],
                axis=1,
            )
            other = jnp.concatenate(
                [rows_far[pair * 4 + k].reshape(512, 128) for k in range(4)], axis=1
            )
            result = dot_nn(flipped[which, zl], mine) + dot_nn(flipped_far[which, zl], other)
            result = result.astype(BF)
            for k in range(4):
                w_mlp[places[which], zl, pair * 2 + k // 2, k % 2, 0] = result[:, k * 128 : k * 128 + 128]
            return carry

        return body

    sums = []

    def start_sums(which):
        ref = w_mlp.at[places[which], :, :, :, 0]
        pair = [
            RingSum(wire, me, "y", fold_view(ref, me, 0, "y", 0, SUM_Y, SUM_CUT), *bufs[2 * which],
                    split_rows(SUM_CUT), add),
            RingSum(wire, me, "z", fold_view(ref, me, 0, "z", SUM_Y, UNITS - SUM_Y, SUM_REST),
                    *bufs[2 * which + 1], split_rows(SUM_REST), add),
        ]
        for item, out, axis in zip(pair, (fold_y_out, fold_z_out), "yz"):
            name = "s%d%s" % (which, axis)
            item.plan(plan, name, ("gr%db" % which,), 1)
            plan.add(name + ".k", close_sum(item, out.at[which]), after=(name + ".far",), rank=3)

    def close_sum(item, out):
        def run():
            mine = item.part(item.at, None)
            add_into(mine, list(item.whole))
            keep(mine, out)

        return run

    rows_of_step = ((h_two, h_far), (h_two, h_far), (cot, cot_far))
    for which in range(3):
        body = grad(which, *rows_of_step[which])

        def waits(which=which):
            return [at.far[which]] + (at.cot_puts if which == 2 else at.h_puts)

        before = ("t%d" % which, "cs", "hs") + (("fd1",) if which == 2 else ())

        def first(body=body, which=which):
            if which == 1:
                for spread in (up_z, up_y):
                    for copy in [*spread.twos[0].copies(), *spread.shared]:
                        copy.wait_send()
            lax.fori_loop(0, 2, body, 0)

        plan.add("gr%da" % which, first, waits, before, 3)
        plan.add(
            "gr%db" % which, lambda body=body: lax.fori_loop(2, 4, body, 0),
            after=("gr%da" % which,), rank=3,
        )
        if which < 2:
            start_sums(which)
    plan.add("dg", lambda: keep(w_mlp.at[1, :, :, :, 0], down_out), after=("gr2b",), rank=2)

    def back_norm(index, carry):
        span = pl.ds(pl.multiple_of(index * 16, 16), 16)
        d_h = (
            part[me.x, span, :].astype(F32)
            + whole_left[span, :].astype(F32)
            + whole_right[span, :].astype(F32)
        )
        value = y_in[span, :]
        scale = lax.rsqrt(jnp.mean(value * value, axis=-1, keepdims=True) + EPS)
        normed = value * scale
        e_two = d_h * gains_in[1:2, :]
        inner = jnp.mean(e_two * normed, axis=-1, keepdims=True)
        d_y = cot[me.x, span, :].astype(F32) + scale * (e_two - normed * inner)
        dy_out[span, :] = d_y
        d_attn[me.x, span, :] = d_y.astype(BF)
        return carry + jnp.sum(d_h * normed, axis=0, keepdims=True)

    def back_one():
        gain_out[...] = lax.fori_loop(0, 4, back_norm, jnp.zeros((1, D), F32))
        d_ring.start_half(0)

    def back_two():
        gain_out[...] += lax.fori_loop(4, 8, back_norm, jnp.zeros((1, D), F32))
        d_ring.start_half(1)
        keep(dy_out, dy_hbm)
        keep(gain_out, gain_hbm)

    d_ring = Ring(wire, me, "x", rows_of(d_attn))
    plan.add("bn", back_one, lambda: at.late, ("ds.far",), 0)
    d_ring.plan(plan, "dx", ("bn",), 0)
    plan.steps["dx.go"].run = back_two
    plan.add("dk", lambda: keep(d_attn, dattn_out), after=("dx.far",), rank=0)
    plan.go(ORDER_FEED)
    for copy in kept:
        copy.wait()
    wire.drain()


def fold_shapes(lead, count, rows, cut, columns):
    return [
        pltpu.VMEM((*lead, *count, cut, columns), BF),
        pltpu.VMEM((*lead, *count, rows - cut, columns), BF),
        pltpu.VMEM((*lead, *count, rows, columns), BF),
        pltpu.VMEM((*lead, *count, rows, columns), BF),
    ]


def call_feed(h_two, cot, mlp, y_one, gains):
    shape = jax.ShapeDtypeStruct
    bufs = (
        fold_shapes((), (2, 2), SUM_Y, SUM_CUT, 128)
        + fold_shapes((), (4,), UNITS - SUM_Y, SUM_REST, 128)
    ) * 2
    return pl.pallas_call(
        kernel_feed,
        name="feed",
        in_specs=[anywhere()] * 5,
        out_specs=[anywhere()] * 7,
        out_shape=[
            shape((4, 128, D), BF),
            shape((4, 128, D), BF),
            shape((2, 2, 2, SUM_Y, 128), BF),
            shape((2, 4, UNITS - SUM_Y, 128), BF),
            shape((2, 4, 2, UNITS, 128), BF),
            shape((128, D), F32),
            shape((1, D), F32),
        ],
        scratch_shapes=[
            pltpu.VMEM((128, D), F32),
            pltpu.VMEM((8, D), F32),
            pltpu.VMEM((128, D), F32),
            pltpu.VMEM((1, D), F32),
            pltpu.VMEM((3, 2, 4, 2, 2, UNITS, 128), BF),
            pltpu.VMEM((4, 128, D), BF),
            pltpu.VMEM((4, 128, D), BF),
            pltpu.VMEM((3, 256, UNITS), F32),
            pltpu.VMEM((256, UNITS), F32),
            pltpu.VMEM((4, 256, UNITS), F32),
            pltpu.VMEM((2, 4, 128, UNITS), BF),
            pltpu.VMEM((2, 4, 128, UNITS), BF),
            pltpu.VMEM((2, 4, 128, UNITS), BF),
            pltpu.VMEM((3, 2, UNITS, 512), BF),
            pltpu.VMEM((3, 2, UNITS, 512), BF),
            pltpu.VMEM((8, 4, 128, 128), BF),
            pltpu.VMEM((8, 4, 128, 128), BF),
            pltpu.VMEM((4, 128, D), BF),
            pltpu.VMEM((128, D // 2), BF),
            pltpu.VMEM((128, D // 2), BF),
            pltpu.VMEM((128, D), BF),
            pltpu.VMEM((128, D), BF),
            pltpu.VMEM((4, 128, D), BF),
            pltpu.VMEM((4, 128, D), BF),
        ]
        + bufs
        + [
            pltpu.SemaphoreType.DMA((100,)),
            pltpu.SemaphoreType.DMA((100,)),
            pltpu.SemaphoreType.DMA((24,)),
        ],
        compiler_params=pltpu.CompilerParams(
            collective_id=1, has_side_effects=True, vmem_limit_bytes=VMEM_BYTES
        ),
    )(h_two, cot, mlp, y_one, gains)
BACK_GROUPS = (3, 4, 4, 3, 3, 4, 4, 3, 3, 4, 4, 3, 3, 4, 4)
ORDER_BACK = (
    "l2", "bias", "l3", "dh", "mz.b.go", "os.go", "wz.a.go", "wy.a.go", "ba0", "mz.b.l",
    "my.b.go", "ba2", "wz.a.r", "bh0", "wy.a.r", "wy.a.l", "mz.b.r", "bh1", "gq0", "qy.a0.go",
    "dl0", "ht", "wy.a.far", "wy.b.go", "mx", "gq1", "ax", "qz.a.go", "qy.a1.go", "qy.a0.l",
    "qy.a0.r", "dn0", "my.b.r", "dn1", "ds.go", "mz.b.far", "mz.k", "os.r", "os.l", "wz.a.far",
    "wy.b.r", "as", "qy.a1.r", "mz.", "qy.a1.l", "qz.a.r", "go", "oz.a.go", "az", "ds.r",
    "my.b.far", "my.k", "ds.l", "qy.a0.far", "oy.a.go", "wy.b.far", "wy.k", "oz.a.r", "my.",
    "dl1", "qy.a1.far", "qy.b.go", "os.far", "fo", "oy.a.r", "oy.a.l", "wz.b.go", "ay",
    "qz.a.far", "qz.b.go", "oz.a.far", "oz.b.go", "m.", "qy.b.r", "ds.far", "oy.a.far", "oy.b.go",
    "wz.b.r", "wz.b.l", "qz.b.r", "qz.b.l", "a.", "gk", "oz.b.r", "oz.b.l", "oy.b.r", "wz.b.far",
    "wz.k", "bn", "qz.b.far", "qz.k", "qy.b.far", "qy.k", "oz.b.far", "oz.k", "oy.b.far", "oy.k",
)
O_Y, O_CUT, O_REST = 192, 96, 32
Q_Y, Q_CUT, Q_REST = 96, 48, 16
DN_Y, DN_CUT, DN_REST = 448, 224, 128


class Fold:
    def __init__(self, wire, me, cut, view_one, axes, bufs, view_two, bufs_two):
        def add(target, term):
            add_into(target, [term])

        self.wire, self.me, self.add, self.split = wire, me, add, split_rows(cut)
        self.ones = []
        if view_one is not None:
            views, groups = (view_one, bufs) if isinstance(view_one, tuple) else ((view_one,), (bufs,))
            self.ones = [self.sum(axes[0], view, group) for view, group in zip(views, groups)]
        self.two = self.sum(axes[1], view_two, bufs_two)

    def sum(self, axis, view, bufs):
        if axis == "z":
            return PairSum(self.wire, self.me, view, *bufs, self.add)
        return RingSum(self.wire, self.me, "y", view, *bufs, self.split, self.add)

    def turn(self):
        for one in self.ones:
            add_into(one.part(one.at, None), list(one.whole))
        self.two.start()

    def close(self, result, keep):
        add_into(self.two.part(self.two.at, None), list(self.two.whole), result)
        keep()

    def plan(self, plan, name, waits, after, rank, result, keep):
        if not self.ones:
            self.two.plan(plan, name + ".b", after, rank)
            plan.steps[name + ".b.go"].waits = waits
        else:
            done = ()
            for index, one in enumerate(self.ones):
                step = name + ".a" + ("%d" % index if len(self.ones) > 1 else "")
                one.plan(plan, step, after[index : index + 1] if len(self.ones) > 1 else after, rank)
                plan.steps[step + ".go"].waits = waits
                done += (step + ".far",)
            self.two.plan(plan, name + ".b", done, rank)
            plan.steps[name + ".b.go"].run = self.turn
        plan.add(name + ".k", lambda: self.close(result, keep), after=(name + ".b.far",), rank=rank + 0.5)


def crossed_view(ref, me, lead, axis, row, rows, cut):
    head = (ALL,) * lead

    def view(slot, part):
        start, size = row, rows
        if part == 0:
            size = cut
        if part == 1:
            start, size = row + cut, rows - cut
        if axis == "z":
            where = (lax.rem(slot, 2), me.y, lax.div(slot, 2))
        else:
            where = (me.zl, slot, me.zh)
        return ref.at[head + where + (pl.ds(start, size), ALL)]

    return view


def held_view(ref, lead, axis, rows, cut):
    head = (ALL,) * lead

    def view(slot, part):
        start, size = 0, rows
        if part == 0:
            size = cut
        if part == 1:
            start, size = cut, rows - cut
        where = (lax.rem(slot, 2), lax.div(slot, 2)) if axis == "z" else (slot,)
        return ref.at[head + where + (pl.ds(start, size), ALL)]

    return view


def kernel_back(
    start_in, tokens_hbm, dattn_hbm, part_hbm, qkv_hbm, wo_hbm, query_hbm, keys_hbm, values_hbm,
    heads_hbm, lse_hbm, turned_hbm, tables_hbm, gains_hbm, y_hbm, dy_hbm, gain_hbm, fold_y_hbm,
    fold_z_hbm, down_hbm,
    result_hbm, grad_tokens_hbm, g_qkv_hbm, g_o_hbm, g_mlp_hbm, g_gains_hbm,
    query_in, keys_in, values_in, lse_in, gains_in, y_in, dy_in, gain_in,
    result_out, tokens_out, g_qkv_out, g_o_out, g_mlp_out, gains_out,
    w_qkv, w_o, d_attn, out_part, tables, bias, tok, turned, d_heads, d_query, d_keys, d_values,
    d_query_far, d_keys_far, d_values_far, sum_keys, sum_values, heads_t, heads_t_far, attn_far,
    d_h, far_one, side_left, side_right, last_z,
    near_left, near_right, whole_left, whole_right,
    out_near_left, out_near_right, out_whole_left, out_whole_right,
    fold_y, fold_z, g_down, gain_x, gain_z, gain_c, along_s, along_a, along_b, along_c, gain_t, along_t,
    *rest,
):
    bufs, (send, recv, local) = list(rest[:-3]), rest[-3:]
    groups = []
    for size in BACK_GROUPS:
        groups.append(tuple(bufs[:size]))
        bufs = bufs[size:]
    me = place()
    wire = Wire(send, recv, local)
    loads = {}

    def load(*items):
        for name, source, target in items:
            loads[name] = wire.move(source, target)

    def load_second():
        load(
            ("fold_y", fold_y_hbm, fold_y),
            ("fold_z", fold_z_hbm, fold_z),
            ("gain", gain_hbm, gain_in),
            ("heads", heads_hbm, heads_t),
            ("down", down_hbm, g_down),
        )

    def load_third():
        load(
            ("qkv", qkv_hbm, w_qkv),
            ("turned", turned_hbm, turned),
            ("y", y_hbm, y_in),
            ("dy", dy_hbm, dy_in),
            ("tok", tokens_hbm, tok),
            ("gains", gains_hbm, gains_in),
        )

    load(
        ("attn", dattn_hbm, d_attn),
        ("o", wo_hbm, w_o),
        ("query", query_hbm, query_in),
        ("keys", keys_hbm, keys_in),
        ("values", values_hbm, values_in),
        ("lse", lse_hbm, lse_in),
        ("tables", tables_hbm.at[me.zl], tables),
        ("part", part_hbm, out_part),
    )
    kept = []

    def keep(source, target):
        kept.append(wire.move(source, target))

    greet(me, True)
    plan = Plan()
    at = types.SimpleNamespace()
    one, far, three = rem4(me.x + 1), rem4(me.x + 2), rem4(me.x + 3)
    right, left = near(me, "x", 1), near(me, "x", 3)

    def add(target, term):
        add_into(target, [term])

    def loaded(*names):
        return lambda: [loads[name] for name in names]

    def share_attn():
        at.attn = [
            wire.put(
                d_attn.at[:, :, pl.ds(pl.multiple_of((block * 2 + 1 - me.core) * 128, 128), 128)],
                attn_far.at[block],
                sibling(me),
            )
            for block in range(8)
        ]

    def share_heads():
        at.heads = wire.put(heads_t, heads_t_far, sibling(me))

    plan.add("l2", load_second, loaded("attn", "o"), rank=0)
    plan.add("l3", load_third, loaded("query", "keys", "values", "lse", "tables"), ("l2",), 0)
    plan.add("as", share_attn, loaded("attn"), rank=1.5)
    plan.add("ht", share_heads, loaded("heads"), ("l2",), 1.5)

    total = RingSum(
        wire, me, "x", columns_of(out_part), out_near_left, out_near_right, out_whole_left,
        out_whole_right, split_columns, add,
    )
    total.plan(plan, "os", (), 1)
    plan.steps["os.go"].waits = loaded("part")

    def finish_out(index, carry):
        span = pl.ds(pl.multiple_of(index * 16, 16), 16)
        result_out[span, :] = (
            y_in[span, :]
            + (
                out_part[me.x, span, :].astype(F32)
                + out_whole_left[span, :].astype(F32)
                + out_whole_right[span, :].astype(F32)
            )
        ).astype(BF)
        return carry

    def finish_result():
        lax.fori_loop(0, 8, finish_out, 0)
        keep(result_out, result_hbm)

    plan.add("fo", finish_result, loaded("y"), ("os.far", "l3"), 6)

    def back_heads(zl, carry):
        weight = jnp.concatenate(
            [w_o[zl, y, zh, c] for y in range(4) for zh in range(2) for c in range(2)], axis=1
        )
        result = dot_nt(d_attn[...].reshape(512, D), weight).astype(BF)
        d_heads[zl * 2] = result[:, 0:HD]
        d_heads[zl * 2 + 1] = result[:, HD : 2 * HD]
        return carry

    plan.add("dh", lambda: lax.fori_loop(0, 2, back_heads, 0), loaded("attn", "o"), rank=2)
    plan.add("bias", lambda: fill_bias(bias, me, start_in[0]), rank=1)

    def back_attend(head, carry):
        for half, pairs in ((1, 4), (0, 3)):
            span = pairs * 256
            rows = slice(half * 256, half * 256 + 256)
            key = keys_in[head, 0:pairs].reshape(span, HD)
            value = values_in[head, 0:pairs].reshape(span, HD)
            query, d_head = query_in[head, rows, :], d_heads[head, rows, :]
            scores = dot_nt(key, query) * SCALE + bias[0:pairs, :, :, rows].reshape(span, 256)
            probs = jnp.exp(scores - lse_in[head, :, rows])
            d_probs = dot_nt(value, d_head)
            delta = jnp.sum(probs * d_probs, axis=0, keepdims=True)
            d_scores = (probs * (d_probs - delta) * SCALE).astype(BF)
            d_key = dot_nn(d_scores, query)
            d_value = dot_nn(probs.astype(BF), d_head)
            if half == 1:
                sum_keys[...] = d_key
                sum_values[...] = d_value
            else:
                sum_keys[0:span, :] += d_key
                sum_values[0:span, :] += d_value
            raw = dot_tn(key, d_scores).T
            cosine = tables[0, 2 * half : 2 * half + 2, 0].reshape(256, HD)
            sine = tables[1, 2 * half : 2 * half + 2, 0].reshape(256, HD)
            column = pl.ds(pl.multiple_of(head * HD, HD), HD)
            d_query[rows, column] = turn(raw, cosine, -sine).astype(BF)
        cosine, sine = tables[0].reshape(SEQ, HD), tables[1].reshape(SEQ, HD)
        d_keys[:, column] = turn(sum_keys[...], cosine, -sine).astype(BF)
        d_values[:, column] = sum_values[...].astype(BF)
        return carry

    def attend_rest():
        lax.fori_loop(2, 4, back_attend, 0)
        at.grads = [
            wire.put(d_query, d_query_far, sibling(me)),
            wire.put(d_keys, d_keys_far, sibling(me)),
            wire.put(d_values, d_values_far, sibling(me)),
        ]

    plan.add(
        "ba0", lambda: lax.fori_loop(0, 2, back_attend, 0),
        loaded("query", "keys", "values", "lse", "tables"), ("dh", "bias"), 2,
    )
    plan.add("ba2", attend_rest, after=("ba0",), rank=2)

    def back_h(block, carry):
        y, zh = lax.div(block, 2), lax.rem(block, 2)

        def weight(which):
            return jnp.concatenate(
                [w_qkv[which, 0, y, zh].reshape(256, 256), w_qkv[which, 1, y, zh].reshape(256, 256)],
                axis=1,
            )

        column = pl.ds(pl.multiple_of(block * 256, 256), 256)
        both = dot_nt(d_keys[...], weight(1)) + dot_nt(d_values[...], weight(2))
        both = both.reshape(4, 2, 128, 256)
        own = dot_nt(d_query[...], weight(0)).reshape(4, 128, 256) + both[:, 0]
        d_h[:, 0, :, column] = own.astype(BF)
        d_h[:, 1, :, column] = both[:, 1].astype(BF)
        return carry

    own = RingSum(
        wire, me, "x",
        lambda slot, half: d_h.at[slot, 0] if half is None else d_h.at[slot, 0, :, pl.ds(half * 1024, 1024)],
        near_left, near_right, whole_left, whole_right, split_columns, add,
    )
    at.far_z, at.sides, at.last = {}, {}, {}

    def cut(ref, half):
        return ref.at[:, pl.ds(half * 1024, 1024)]

    def back_half(half):
        def run():
            lax.fori_loop(half * 4, half * 4 + 4, back_h, 0)
            at.far_z[half] = wire.put(cut(d_h.at[far, 1], half), cut(far_one, half), partner(me))
            at.sides[half] = [
                wire.put(cut(d_h.at[one, 1], half), cut(side_left, half), right),
                wire.put(cut(d_h.at[three, 1], half), cut(side_right, half), left),
            ]
            own.start_whole(half)

        return run

    def near_half(half):
        def run():
            add_into(cut(d_h.at[far, 0], half), [cut(far_one, half)])
            own.start_near(half)

        return run

    def last_half(half):
        def run():
            add_into(cut(d_h.at[me.x, 1], half), [cut(side_left, half), cut(side_right, half)])
            at.last[half] = wire.put(cut(d_h.at[me.x, 1], half), cut(last_z, half), partner(me))

        return run

    plan.add("bh0", back_half(0), loaded("qkv"), ("ba2", "l3"), 2)
    plan.add("bh1", back_half(1), after=("bh0",), rank=2)
    for half in range(2):
        name = "%d" % half
        plan.add("dn" + name, near_half(half), lambda half=half: [at.far_z[half]], ("bh" + name,), 0)
        plan.add("dl" + name, last_half(half), lambda half=half: at.sides[half], ("bh" + name,), 0.5)
    plan.add("ds.go", lambda: None, after=("dn0", "dn1"), rank=0)
    own.plan(plan, "ds", (), 0, go=False)

    def grad_o(index, carry):
        zl, y = lax.div(index, 4), lax.rem(index, 4)
        mine = jnp.concatenate(
            [
                d_attn[:, :, pl.ds(pl.multiple_of(((y * 2 + zh) * 2 + me.core) * 128, 128), 128)]
                .reshape(512, 128)
                for zh in range(2)
            ],
            axis=1,
        )
        other = jnp.concatenate(
            [attn_far[y * 2 + zh].reshape(512, 128) for zh in range(2)], axis=1
        )
        rows = pl.ds(pl.multiple_of(zl * 256, 256), 256)
        result = (dot_nn(heads_t[rows, :], mine) + dot_nn(heads_t_far[rows, :], other)).astype(BF)
        w_o[zl, y, 0, 0] = result[:, 0:128]
        w_o[zl, y, 1, 0] = result[:, 128:256]
        return carry

    plan.add("go", lambda: lax.fori_loop(0, 8, grad_o, 0), lambda: [at.heads, *at.attn], ("as", "ht", "dh"), 3)

    def blocks(which, pair):
        return turned[which, pl.ds(pair * 4, 4)].reshape(512, SEQ)

    def own_rows(value):
        return jnp.concatenate([value[:, i * 256 : i * 256 + 128] for i in range(4)], axis=1)

    def grad_qkv(index, carry):
        zl, pair = lax.div(index, 2), lax.rem(index, 2)
        column = pl.ds(pl.multiple_of(zl * 256, 256), 256)
        mine, other = blocks(0, pair), blocks(1, pair)
        query_grad = dot_nn(own_rows(mine), d_query[:, column])
        query_grad = query_grad + dot_nn(own_rows(other), d_query_far[:, column])
        key_grad = dot_nn(mine, d_keys[:, column]) + dot_nn(other, d_keys_far[:, column])
        value_grad = dot_nn(mine, d_values[:, column]) + dot_nn(other, d_values_far[:, column])
        along = jnp.where(zl == 0, 0.0, along_s[pair])
        for which, result in enumerate((query_grad, key_grad, value_grad)):
            weight = w_qkv[which, zl, pl.ds(pair * 2, 2), :, me.core].reshape(512, 256)
            product = weight.astype(F32) * result
            along = along + product[:, 0:128] + product[:, 128:256]
            w_qkv[which, zl, pl.ds(pair * 2, 2), :, 0] = result.astype(BF).reshape(2, 2, 128, 256)
        along_s[pair] = along
        return carry

    plan.add(
        "gq0", lambda: lax.fori_loop(0, 2, grad_qkv, 0),
        lambda: [loads["turned"], *at.grads], ("bh1",), 3,
    )
    plan.add("gq1", lambda: lax.fori_loop(2, 4, grad_qkv, 0), after=("gq0",), rank=3)

    g_qkv, g_o = w_qkv.at[:, :, :, :, 0], w_o.at[:, :, :, 0]
    rest = UNITS - SUM_Y

    def low_view(zl):
        def view(slot, part):
            span = {None: (0, Q_Y), 0: (0, Q_CUT), 1: (Q_CUT, Q_Y - Q_CUT)}[part]
            return g_qkv.at[:, zl, slot, :, pl.ds(*span), :]

        return view

    for name, fold, waits, after, rank, result, target, where in (
        ("my", Fold(wire, me, 0, None, ("y", "z"), None, held_view(fold_y, 1, "z", SUM_Y, 0), groups[0]),
         loaded("fold_y"), ("l2",), 1.2, g_mlp_out, g_mlp_hbm, (pl.ds(0, 2), pl.ds(0, SUM_Y), ALL)),
        ("mz", Fold(wire, me, 144, None, ("z", "y"), None, held_view(fold_z, 1, "y", rest, 144), groups[1]),
         loaded("fold_z"), ("l2",), 1.2, g_mlp_out, g_mlp_hbm, (pl.ds(0, 2), pl.ds(SUM_Y, UNITS - SUM_Y), ALL)),
        ("oy", Fold(wire, me, O_CUT, fold_view(g_o, me, 0, "y", 0, O_Y, O_CUT), ("y", "z"), groups[2],
                    crossed_view(g_o, me, 0, "z", 0, O_Y, 0), groups[3]),
         tuple, ("go",), 1.4, g_o_out, g_o_hbm, (pl.ds(0, O_Y), ALL)),
        ("oz", Fold(wire, me, O_REST, fold_view(g_o, me, 0, "z", O_Y, 256 - O_Y, 0), ("z", "y"), groups[4],
                    crossed_view(g_o, me, 0, "y", O_Y, 256 - O_Y, O_REST), groups[5]),
         tuple, ("go",), 1.4, g_o_out, g_o_hbm, (pl.ds(O_Y, 256 - O_Y), ALL)),
        ("qy", Fold(wire, me, Q_CUT, (low_view(0), low_view(1)), ("y", "z"), (groups[6], groups[14]),
                    crossed_view(g_qkv, me, 1, "z", 0, Q_Y, 0), groups[7]),
         tuple, ("gq0", "gq1"), 1, g_qkv_out, g_qkv_hbm, (ALL, pl.ds(0, Q_Y), ALL)),
        ("qz", Fold(wire, me, Q_REST, fold_view(g_qkv, me, 1, "z", Q_Y, 128 - Q_Y, 0), ("z", "y"),
                    groups[8], crossed_view(g_qkv, me, 1, "y", Q_Y, 128 - Q_Y, Q_REST), groups[9]),
         tuple, ("gq1",), 1, g_qkv_out, g_qkv_hbm, (ALL, pl.ds(Q_Y, 128 - Q_Y), ALL)),
        ("wy", Fold(wire, me, DN_CUT, fold_view(g_down, me, 0, "y", 0, DN_Y, DN_CUT), ("y", "z"),
                    groups[10], crossed_view(g_down, me, 0, "z", 0, DN_Y, 0), groups[11]),
         loaded("down"), ("l2",), 1.3, g_mlp_out, g_mlp_hbm, (2, pl.ds(0, DN_Y), ALL)),
        ("wz", Fold(wire, me, DN_REST, fold_view(g_down, me, 0, "z", DN_Y, UNITS - DN_Y, 0), ("z", "y"),
                    groups[12], crossed_view(g_down, me, 0, "y", DN_Y, UNITS - DN_Y, DN_REST), groups[13]),
         loaded("down"), ("l2",), 1.3, g_mlp_out, g_mlp_hbm, (2, pl.ds(DN_Y, UNITS - DN_Y), ALL)),
    ):
        fold.plan(
            plan, name, waits, after, rank, result.at[where],
            lambda result=result, target=target, where=where: keep(result.at[where], target.at[where]),
        )

    def back_norm(index, carry):
        span = pl.ds(pl.multiple_of(index * 16, 16), 16)
        d_h_one = (
            d_h[me.x, 0, span, :].astype(F32)
            + whole_left[span, :].astype(F32)
            + whole_right[span, :].astype(F32)
            + last_z[span, :].astype(F32)
        )
        value = tok[span, :].astype(F32)
        scale = lax.rsqrt(jnp.mean(value * value, axis=-1, keepdims=True) + EPS)
        normed = value * scale
        e_one = d_h_one * gains_in[0:1, :]
        inner = jnp.mean(e_one * normed, axis=-1, keepdims=True)
        tokens_out[span, :] = (dy_in[span, :] + scale * (e_one - normed * inner)).astype(BF)
        return carry

    def feed_x():
        for block in range(16):
            gain_x[me.x, block : block + 1, :] = gain_in[0:1, block * 128 : block * 128 + 128]
        at.feed = Meet(wire, me, "x", gain_x).copies

    def feed_z():
        gain_z[me.z] = gain_x[0] + gain_x[1] + gain_x[2] + gain_x[3]
        at.feed = Meet(wire, me, "z", gain_z).copies

    def feed_y():
        gain_c[me.core, me.y] = gain_z[0] + gain_z[1] + gain_z[2] + gain_z[3]
        at.feed = MeetCores(wire, me, gain_c).copies

    def feed_all():
        total = gain_c[0, 0]
        for core, y in ((0, 1), (0, 2), (0, 3), (1, 0), (1, 1), (1, 2), (1, 3)):
            total = total + gain_c[core, y]
        gain_t[...] = total
        row = (me.y * 2 + me.zh) * 2 + me.core
        gains_out[1:2, :] = gain_t[pl.ds(row, 1), :]

    plan.add("mx", feed_x, loaded("gain"), ("l2",), 1)
    plan.add("mz.", feed_z, lambda: at.feed, ("mx",), 1)
    plan.add("my.", feed_y, lambda: at.feed, ("mz.",), 1)
    plan.add("m.", feed_all, lambda: at.feed, ("my.",), 1)

    def along_x():
        ones = jnp.ones((8, 128), F32)
        for pair in range(2):
            line = lax.dot_general(
                ones, along_s[pair], (((1,), (1,)), ((), ())), precision=lax.Precision.HIGHEST,
                preferred_element_type=F32,
            )
            for k in range(4):
                along_a[me.x, pair * 4 + k : pair * 4 + k + 1, :] = line[0:1, k * 128 : k * 128 + 128]
        at.along = Meet(wire, me, "x", along_a).copies

    def along_z():
        along_b[me.z] = along_a[0] + along_a[1] + along_a[2] + along_a[3]
        at.along = Meet(wire, me, "z", along_b).copies

    def along_y():
        along_c[me.y] = along_b[0] + along_b[1] + along_b[2] + along_b[3]
        at.along = Meet(wire, me, "y", along_c).copies

    def along_all():
        along_t[...] = along_c[0] + along_c[1] + along_c[2] + along_c[3]
        row = me.y * 2 + me.zh
        column = pl.ds(pl.multiple_of((row * 2 + me.core) * 128, 128), 128)
        gains_out[0:1, :] = along_t[pl.ds(row, 1), :] / gains_in[0:1, column]

    plan.add("ax", along_x, after=("gq1",), rank=1)
    plan.add("az", along_z, lambda: at.along, ("ax",), 1)
    plan.add("ay", along_y, lambda: at.along, ("az",), 1)
    plan.add("a.", along_all, lambda: [*loaded("gains")(), *at.along], ("ay",), 1)
    plan.add("gk", lambda: keep(gains_out, g_gains_hbm), after=("a.", "m."), rank=2)

    def back_all():
        lax.fori_loop(0, 8, back_norm, 0)
        keep(tokens_out, grad_tokens_hbm)

    plan.add(
        "bn", back_all,
        lambda: [*loaded("tok", "dy", "gains")(), at.last[0], at.last[1]], ("ds.far", "dl0", "dl1"), 0,
    )
    plan.go(ORDER_BACK)
    for copy in kept:
        copy.wait()
    wire.drain()


def call_back(starts, tokens, d_attn, out_part, qkv, w_out, query, keys, values, heads, lse, turned,
              tables, gains, y_one, d_y, gain_two, fold_y, fold_z, down):
    shape = jax.ShapeDtypeStruct

    def three(*dims):
        return [pltpu.VMEM(dims, BF)] * 3

    rest = UNITS - SUM_Y
    bufs = (
        three(2, SUM_Y, 128)
        + fold_shapes((2,), (), rest, 144, 128)
        + fold_shapes((), (2, 2), O_Y, O_CUT, 128)
        + three(O_Y, 128)
        + three(4, 256 - O_Y, 128)
        + fold_shapes((), (), 256 - O_Y, O_REST, 128)
        + fold_shapes((3,), (2,), Q_Y, Q_CUT, 256)
        + three(3, Q_Y, 256)
        + three(3, 4, 128 - Q_Y, 256)
        + fold_shapes((3,), (), 128 - Q_Y, Q_REST, 256)
        + fold_shapes((), (2, 2), DN_Y, DN_CUT, 128)
        + three(DN_Y, 128)
        + three(4, UNITS - DN_Y, 128)
        + fold_shapes((), (), UNITS - DN_Y, DN_REST, 128)
        + fold_shapes((3,), (2,), Q_Y, Q_CUT, 256)
    )
    return pl.pallas_call(
        kernel_back,
        name="back",
        in_specs=[pl.BlockSpec(memory_space=pltpu.SMEM)] + [anywhere()] * 19,
        out_specs=[anywhere()] * 6,
        out_shape=[
            shape((128, D), BF),
            shape((128, D), BF),
            shape((3, 128, 256), F32),
            shape((256, 128), F32),
            shape((3, UNITS, 128), F32),
            shape((2, 128), F32),
        ],
        scratch_shapes=[
            pltpu.VMEM((4, 512, HD), BF),
            pltpu.VMEM((4, 4, 2, 128, HD), BF),
            pltpu.VMEM((4, 4, 2, 128, HD), BF),
            pltpu.VMEM((4, 1, 512), F32),
            pltpu.VMEM((8, D), F32),
            pltpu.VMEM((128, D), F32),
            pltpu.VMEM((128, D), F32),
            pltpu.VMEM((1, D), F32),
            pltpu.VMEM((128, D), BF),
            pltpu.VMEM((128, D), BF),
            pltpu.VMEM((3, 128, 256), F32),
            pltpu.VMEM((256, 128), F32),
            pltpu.VMEM((3, UNITS, 128), F32),
            pltpu.VMEM((2, 128), F32),
            pltpu.VMEM((3, 2, 4, 2, 2, 128, 256), BF),
            pltpu.VMEM((2, 4, 2, 2, 256, 128), BF),
            pltpu.VMEM((4, 128, D), BF),
            pltpu.VMEM((4, 128, D), BF),
            pltpu.VMEM((2, 4, 2, 128, HD), F32),
            pltpu.VMEM((4, 2, 128, 512), F32),
            pltpu.VMEM((128, D), BF),
            pltpu.VMEM((2, 8, 128, SEQ), BF),
            pltpu.VMEM((4, 512, HD), BF),
            pltpu.VMEM((512, 512), BF),
            pltpu.VMEM((SEQ, 512), BF),
            pltpu.VMEM((SEQ, 512), BF),
            pltpu.VMEM((512, 512), BF),
            pltpu.VMEM((SEQ, 512), BF),
            pltpu.VMEM((SEQ, 512), BF),
            pltpu.VMEM((SEQ, HD), F32),
            pltpu.VMEM((SEQ, HD), F32),
            pltpu.VMEM((512, 512), BF),
            pltpu.VMEM((512, 512), BF),
            pltpu.VMEM((8, 4, 128, 128), BF),
            pltpu.VMEM((4, 2, 128, D), BF),
        ]
        + [pltpu.VMEM((128, D), BF)] * 4
        + [
            pltpu.VMEM((128, D // 2), BF),
            pltpu.VMEM((128, D // 2), BF),
            pltpu.VMEM((128, D), BF),
            pltpu.VMEM((128, D), BF),
        ]
        * 2
        + [
            pltpu.VMEM((2, 2, 2, SUM_Y, 128), BF),
            pltpu.VMEM((2, 4, UNITS - SUM_Y, 128), BF),
            pltpu.VMEM((2, 4, 2, UNITS, 128), BF),
            pltpu.VMEM((4, 16, 128), F32),
            pltpu.VMEM((4, 16, 128), F32),
            pltpu.VMEM((2, 4, 16, 128), F32),
            pltpu.VMEM((2, 512, 128), F32),
            pltpu.VMEM((4, 8, 128), F32),
            pltpu.VMEM((4, 8, 128), F32),
            pltpu.VMEM((4, 8, 128), F32),
            pltpu.VMEM((16, 128), F32),
            pltpu.VMEM((8, 128), F32),
        ]
        + bufs
        + [
            pltpu.SemaphoreType.DMA((140,)),
            pltpu.SemaphoreType.DMA((140,)),
            pltpu.SemaphoreType.DMA((40,)),
        ],
        compiler_params=pltpu.CompilerParams(
            collective_id=2, has_side_effects=True, vmem_limit_bytes=VMEM_BYTES
        ),
    )(starts, tokens, d_attn, out_part, qkv, w_out, query, keys, values, heads, lse, turned,
      tables, gains, y_one, d_y, gain_two, fold_y, fold_z, down)


def kernel_settle(*refs):
    arrays, results, held, (row_s, send, recv) = refs[:6], refs[6:17], refs[17:23], refs[23:]
    tp = lax.axis_index("tensor")
    copies = [
        pltpu.make_async_copy(source, target, recv.at[index])
        for index, (source, target) in enumerate(zip(arrays, held))
    ]
    for copy in copies:
        copy.start()
    outs = []

    def give(source, index):
        copy = pltpu.make_async_copy(source, results[index], send.at[index])
        copy.start()
        outs.append(copy)

    copies[5].wait()
    for index in range(2):
        row = held[5][index : index + 1, :]
        row_s[index] = pltpu.roll(row, lax.rem(128 - tp * 16, 128), 1)[:, 0:16]
    for index in range(2):
        give(row_s.at[index], 9 + index)
    for index in range(2):
        copies[index].wait()
        give(held[index], index)
    copies[4].wait()
    for index in range(3):
        give(held[4].at[index], 6 + index)
    copies[2].wait()
    for index in range(3):
        give(held[2].at[index], 2 + index)
    copies[3].wait()
    give(held[3], 5)
    for copy in outs:
        copy.wait()


def call_settle(*arrays):
    shape = jax.ShapeDtypeStruct
    return pl.pallas_call(
        kernel_settle,
        name="settle",
        in_specs=[anywhere()] * 6,
        out_specs=[anywhere()] * 11,
        out_shape=[shape((128, D), BF)] * 2
        + [shape((128, 256), F32)] * 3
        + [shape((256, 128), F32)]
        + [shape((UNITS, 128), F32)] * 3
        + [shape((1, 16), F32)] * 2,
        scratch_shapes=[
            pltpu.VMEM((128, D), BF),
            pltpu.VMEM((128, D), BF),
            pltpu.VMEM((3, 128, 256), F32),
            pltpu.VMEM((256, 128), F32),
            pltpu.VMEM((3, UNITS, 128), F32),
            pltpu.VMEM((2, 128), F32),
            pltpu.VMEM((2, 1, 16), F32),
            pltpu.SemaphoreType.DMA((11,)),
            pltpu.SemaphoreType.DMA((6,)),
        ],
        compiler_params=pltpu.CompilerParams(vmem_limit_bytes=VMEM_BYTES),
    )(*arrays)


def on_device(tables, tokens, starts, w_query, w_key, w_value, w_out, w_gate, w_up, w_down,
              gain_attn, gain_mlp, cotangent):
    weights = (w_query, w_key, w_value, w_out, w_gate.T, w_up.T, w_down)
    (qkv, w_o, mlp, cot, turned, query, keys, values, heads, h_two, lse, y_one, gains) = call_attend(
        tokens, cotangent, starts, weights, gain_attn.reshape(1, 16), gain_mlp.reshape(1, 16), tables
    )
    out_part, d_attn, fold_y, fold_z, down, d_y, gain_two = call_feed(h_two, cot, mlp, y_one, gains)
    sums = call_back(
        starts, tokens, d_attn, out_part, qkv, w_o, query, keys, values, heads, lse, turned,
        tables, gains, y_one, d_y, gain_two, fold_y, fold_z, down,
    )
    result, grad_tokens, query, key, value, out, gate, up, down, attn, feed = call_settle(*sums)
    return (
        result, grad_tokens, query, key, value, out, gate.T, up.T, down,
        attn.reshape(16), feed.reshape(16),
    )


def solution(mesh):
    both = ("dp", "tensor")
    rows, wide, tall = P(both, None), P("dp", "tensor"), P("tensor", "dp")
    in_specs = (
        rows, P("dp"), wide, wide, wide, tall, wide, wide, tall, P(both), P(both), rows,
    )
    out_specs = (
        rows, rows, wide, wide, wide, tall, wide, wide, tall, P(both), P(both),
    )
    return jax.shard_map(
        functools.partial(on_device, rope_tables()), mesh=mesh, in_specs=in_specs,
        out_specs=out_specs, check_vma=False,
    )
```
